32 devices in a mesh: ctx: 16 (over z, x, core), wsh: 2 (over y).
Axes of the slice: x: 2, y: 2, z: 4, core: 2. Of those that a mesh axis runs over, the one named last changes fastest.
Arguments:
- hidden_in: bfloat16 [2, 2, 8192, 768], P(None, 'wsh', 'ctx'), may hold values from -6 to 6
- segment_ids: int32 [2, 2, 8192], P(None, 'wsh'), may hold values from 0 to 10, never falling along the last dimension, each value on 1 to 1537 neighbouring positions
- out_grad: bfloat16 [2, 2, 8192, 768], P(None, 'wsh', 'ctx'), may hold values from -6 to 6
- query_w: bfloat16 [768, 384], P('wsh'), may hold values from -0.625 to 0.625
- query_b: bfloat16 [384], P('wsh'), may hold values from -3 to 3
- key_w: bfloat16 [768, 384], P('wsh'), may hold values from -0.21875 to 0.21875
- value_w: bfloat16 [768, 384], P('wsh'), may hold values from -0.21875 to 0.21875
- value_b: bfloat16 [384], P('wsh'), may hold values from -3 to 3
- depth_kernel: bfloat16 [9, 768], P(None, 'wsh'), may hold values from -2 to 2
- point_w: bfloat16 [768, 384], P('wsh'), may hold values from -0.21875 to 0.21875
- point_b: bfloat16 [384], P('wsh'), may hold values from -3 to 3
- kernel_w: bfloat16 [384, 54], P('wsh'), may hold values from -0.078125 to 0.078125
- kernel_b: bfloat16 [54], P('wsh'), may hold values from -3 to 3
- conv_w: bfloat16 [768, 384], P('wsh'), may hold values from -0.21875 to 0.21875
- conv_b: bfloat16 [384], P('wsh'), may hold values from -3 to 3
- output_w: bfloat16 [768, 768], P('wsh'), may hold values from -0.21875 to 0.21875
- output_b: bfloat16 [768], P('wsh'), may hold values from -3 to 3
- norm1_gain: bfloat16 [768], P('wsh'), may hold values from 0.5 to 1.5
- norm1_bias: bfloat16 [768], P('wsh'), may hold values from -3 to 3
- inner_w: bfloat16 [2, 384, 1536], P(None, 'wsh'), may hold values from -0.3125 to 0.3125
- inner_b: bfloat16 [3072], P('wsh'), may hold values from -3 to 3
- outer_w: bfloat16 [2, 1536, 384], P(None, 'wsh'), may hold values from -0.15625 to 0.15625
- outer_b: bfloat16 [768], P('wsh'), may hold values from -3 to 3
- norm2_gain: bfloat16 [768], P('wsh'), may hold values from 0.5 to 1.5
- norm2_bias: bfloat16 [768], P('wsh'), may hold values from -3 to 3
Outputs:
- output: bfloat16 [2, 2, 8192, 768], P(None, 'wsh', 'ctx')
- input_grad: float32 [2, 2, 8192, 768], P(None, 'wsh', 'ctx')
- grad_query_w: float32 [768, 384], P('wsh')
- grad_query_b: float32 [384], P('wsh')
- grad_key_w: float32 [768, 384], P('wsh')
- grad_value_w: float32 [768, 384], P('wsh')
- grad_value_b: float32 [384], P('wsh')
- grad_depth_kernel: float32 [9, 768], P(None, 'wsh')
- grad_point_w: float32 [768, 384], P('wsh')
- grad_point_b: float32 [384], P('wsh')
- grad_kernel_w: float32 [384, 54], P('wsh')
- grad_kernel_b: float32 [54], P('wsh')
- grad_conv_w: float32 [768, 384], P('wsh')
- grad_conv_b: float32 [384], P('wsh')
- grad_output_w: float32 [768, 768], P('wsh')
- grad_output_b: float32 [768], P('wsh')
- grad_norm1_gain: float32 [768], P('wsh')
- grad_norm1_bias: float32 [768], P('wsh')
- grad_inner_w: float32 [2, 384, 1536], P(None, 'wsh')
- grad_inner_b: float32 [3072], P('wsh')
- grad_outer_w: float32 [2, 1536, 384], P(None, 'wsh')
- grad_outer_b: float32 [768], P('wsh')
- grad_norm2_gain: float32 [768], P('wsh')
- grad_norm2_bias: float32 [768], P('wsh')
The draws below stay inside these ranges and needn't reach their ends.
Inputs may be any that keep to these rules, and one draw needn't show every extreme that they name: `segment_ids`: within each sequence the document numbers never fall; each document has 1 to 1537 tokens, and one has exactly 1537.
All inputs are finite; a program needn't handle non-finite values.
Results may differ from the reference program's by a relative error of at most 0.015.
The reference program's roundings to bfloat16 on the way count: a program that leaves them out, or rounds other values in their place, can miss the bound.
Values may be sent and summed in bfloat16 or wider, within the bound.
A program may use at most 256 MiB of HBM per device.

```python
import math
import jax
import jax.numpy as jnp
import numpy as np
from jax import lax

D = 768
HEADS = 6
HEAD_DIM = 64
KERNEL = 9
FF = 3072
GROUPS = 2
A = 384
MB = 2
B = 2
SEQ = 8192
DOC_MAX = 1537
DOCS = 11


def levels(rng, extent, cuts, smallest, high):
    factor_of, own = 1.0, jax.random.fold_in(rng, 6)
    for dim, parts in cuts:
        steps = jnp.exp(jax.random.uniform(jax.random.fold_in(own, dim), (parts,), jnp.float32, smallest / len(cuts), high / len(cuts)))
        factor_of = factor_of * jnp.repeat(steps, extent[dim] // parts).reshape([-1 if axis == dim else 1 for axis in range(len(extent))])
    return factor_of


def length_profile(amount, total, bound, skew):
    weights = [(1 << 20) // math.isqrt(grade ** skew) + 1 for grade in range(2, amount + 1)]
    rest, given = total - bound - (amount - 1), [1] * (amount - 1)
    while rest > 0:
        candidates = [i for i in range(amount - 1) if given[i] < bound]
        whole, budget = sum([weights[i] for i in candidates]), rest
        for i in candidates:
            more = min(bound - given[i], max(1, budget * weights[i] // whole), rest)
            given[i] = given[i] + more
            rest = rest - more
    return np.array([bound] + given)


def ragged(key, count, total, limit, skew):
    if count == 2:
        one = jax.random.randint(key, (), max(1, total - limit), min(limit, total - 1) + 1)
        return jnp.stack([one, total - one])
    sizes = jnp.asarray(length_profile(count, total, limit, skew), jnp.int32)
    twos = (count - 1) // 2
    giver, sink = sizes[1:1 + 2 * twos:2], sizes[2:2 + 2 * twos:2]
    room = jnp.minimum(giver - 1, limit - sink)
    passed = jax.random.randint(jax.random.fold_in(key, 1), (twos,), 0, 1 << 20) % (room + 1)
    sizes = sizes.at[1:1 + 2 * twos:2].set(giver - passed).at[2:2 + 2 * twos:2].set(sink + passed)
    return sizes[jax.random.permutation(jax.random.fold_in(key, 2), count)]


def scatter_about(rng, extent, scale, limit, shards=(), held_as=jnp.bfloat16):
    values = scale * jax.random.normal(rng, extent, jnp.float32)
    if shards:
        values = values * levels(rng, extent, shards, -0.22, 0.18)
    return jnp.clip(values, -limit, limit).astype(held_as)


def setup_inputs(seed: int = 0) -> dict:
    splits = jax.random.split(jax.random.key(seed), 26)
    return {
        "hidden_in": scatter_about(splits[0], (MB, B, SEQ, D), 1.0, 6.0, ((1, 2), (2, 16))),
        "segment_ids": jax.vmap(lambda own: jnp.searchsorted(jnp.cumsum(ragged(own, DOCS, SEQ, DOC_MAX, 1)), jnp.arange(SEQ), side="right"))(jax.random.split(splits[1], MB * B)).reshape((MB, B, SEQ)).astype(jnp.int32),
        "out_grad": scatter_about(splits[2], (MB, B, SEQ, D), 1.0, 6.0, ((1, 2), (2, 16))),
        "query_w": scatter_about(splits[3], (D, A), (D // 9) ** -0.5, 0.625, ((0, 2),)),
        "query_b": scatter_about(splits[4], (A,), 0.5, 3.0, ((0, 2),)),
        "key_w": scatter_about(splits[5], (D, A), D ** -0.5, 0.21875, ((0, 2),)),
        "value_w": scatter_about(splits[6], (D, A), D ** -0.5, 0.21875, ((0, 2),)),
        "value_b": scatter_about(splits[7], (A,), 0.5, 3.0, ((0, 2),)),
        "depth_kernel": scatter_about(splits[8], (KERNEL, D), KERNEL ** -0.5, 2.0, ((1, 2),)),
        "point_w": scatter_about(splits[9], (D, A), D ** -0.5, 0.21875, ((0, 2),)),
        "point_b": scatter_about(splits[10], (A,), 0.5, 3.0, ((0, 2),)),
        "kernel_w": scatter_about(splits[11], (A, HEADS * KERNEL), (16 * A) ** -0.5, 0.078125, ((0, 2),)),
        "kernel_b": scatter_about(splits[12], (HEADS * KERNEL,), 0.5, 3.0, ((0, 2),)),
        "conv_w": scatter_about(splits[13], (D, A), D ** -0.5, 0.21875, ((0, 2),)),
        "conv_b": scatter_about(splits[14], (A,), 0.5, 3.0, ((0, 2),)),
        "output_w": scatter_about(splits[15], (2 * A, D), (2 * A) ** -0.5, 0.21875, ((0, 2),)),
        "output_b": scatter_about(splits[16], (D,), 0.5, 3.0, ((0, 2),)),
        "norm1_gain": jnp.clip(1.0 + 0.1 * jax.random.normal(splits[17], (D,), jnp.float32), 0.5, 1.5).astype(jnp.bfloat16),
        "norm1_bias": scatter_about(splits[18], (D,), 0.5, 3.0, ((0, 2),)),
        "inner_w": scatter_about(splits[19], (GROUPS, D // GROUPS, FF // GROUPS), (D // GROUPS) ** -0.5, 0.3125, ((1, 2),)),
        "inner_b": scatter_about(splits[20], (FF,), 0.5, 3.0, ((0, 2),)),
        "outer_w": scatter_about(splits[21], (GROUPS, FF // GROUPS, D // GROUPS), (FF // GROUPS) ** -0.5, 0.15625, ((1, 2),)),
        "outer_b": scatter_about(splits[22], (D,), 0.5, 3.0, ((0, 2),)),
        "norm2_gain": jnp.clip(1.0 + 0.1 * jax.random.normal(splits[23], (D,), jnp.float32), 0.5, 1.5).astype(jnp.bfloat16),
        "norm2_bias": scatter_about(splits[24], (D,), 0.5, 3.0, ((0, 2),)),
    }


highest = lax.Precision.HIGHEST

@jax.custom_vjp
def low(v):
    return lax.optimization_barrier(v.astype(jnp.bfloat16)).astype(jnp.float32)

@jax.custom_vjp
def low_back(v):
    return v

def low_keep(v):
    return (low(v), None)

def low_pass(kept, grad):
    return (grad,)

def back_keep(v):
    return (v, None)

def back_low(kept, grad):
    return (low(grad),)
low.defvjp(low_keep, low_pass)
low_back.defvjp(back_keep, back_low)

def product(left, right):
    return jnp.dot(left, right, precision=highest, preferred_element_type=jnp.float32)

def layer_norm(values, gain, shift):
    center = values - lax.optimization_barrier(jnp.mean(values, axis=-1, keepdims=True))
    spread = lax.optimization_barrier(jnp.mean(center * center, axis=-1, keepdims=True))
    return center * lax.rsqrt(spread + 1e-05) * gain + shift

def attend(queries, keys_all, values_all, segs):
    length = queries.shape[0]
    block = math.gcd(length, 512)
    score_scale = HEAD_DIM ** (-0.5)
    key_heads = keys_all.reshape(length, HEADS, HEAD_DIM)
    value_heads = values_all.reshape(length, HEADS, HEAD_DIM)

    def one_block(inputs):
        query_part, seg_part = inputs
        query_heads = query_part.reshape(block, HEADS, HEAD_DIM)
        raw_scores = jnp.einsum('qhd,khd->hqk', query_heads, key_heads, precision=highest) * score_scale
        same_doc = seg_part[:, None] == segs[None, :]
        scores = low_back(jnp.where(same_doc[None], raw_scores, -1000000000.0))
        weights = low(jax.nn.softmax(scores, axis=-1))
        head_out = jnp.einsum('hqk,khd->qhd', weights, value_heads, precision=highest)
        return head_out.reshape(block, HEADS * HEAD_DIM)
    pieces = lax.map(jax.checkpoint(one_block), (queries.reshape(length // block, block, -1), segs.reshape(length // block, block)))
    return pieces.reshape(length, -1)

def forward_seq(tokens, segs, params):
    query_w, query_b, key_w, value_w, value_b, depth_kernel, point_w, point_b, kernel_w, kernel_b, conv_w, conv_b, output_w, output_b, norm1_gain, norm1_bias, inner_w, inner_b, outer_w, outer_b, norm2_gain, norm2_bias = params
    length = tokens.shape[0]
    half_taps = KERNEL // 2
    queries = low_back(low(product(tokens, query_w) + query_b))
    keys_all = low_back(low(product(tokens, key_w)))
    values_all = low_back(low(product(tokens, value_w) + value_b))
    seg_pad = jnp.pad(segs, (half_taps, half_taps), constant_values=-1)
    tok_pad = jnp.pad(tokens, ((half_taps, half_taps), (0, 0)))
    masks = [(seg_pad[offset:offset + length] == segs).astype(tokens.dtype)[:, None] for offset in range(KERNEL)]
    depth_sum = sum((depth_kernel[offset] * tok_pad[offset:offset + length] * masks[offset] for offset in range(KERNEL)))
    depth_low = low(depth_sum)
    span_keys = low_back(product(depth_low, point_w) + point_b)
    mixed_low = low(span_keys * queries)
    logits = low_back(product(mixed_low, kernel_w) + kernel_b)
    kernels = jax.nn.softmax(logits.reshape(length, HEADS, KERNEL), axis=-1)
    conv_vals = low_back(product(tokens, conv_w) + conv_b)
    conv_pad = jnp.pad(conv_vals, ((half_taps, half_taps), (0, 0))).reshape(length + 2 * half_taps, HEADS, HEAD_DIM)
    convolved = sum(((kernels[:, :, offset] * masks[offset])[:, :, None] * conv_pad[offset:offset + length] for offset in range(KERNEL)))
    attended = attend(queries, keys_all, values_all, segs)
    joined = low_back(low(jnp.concatenate([attended, convolved.reshape(length, -1)], axis=1)))
    branch = low_back(product(joined, output_w) + output_b)
    normed = layer_norm(branch + tokens, norm1_gain, norm1_bias)
    groups_in = low(normed).reshape(length, GROUPS, -1)
    inner_pre = low_back(jnp.einsum('ngd,gdf->ngf', groups_in, inner_w, precision=highest) + inner_b.reshape(GROUPS, -1))
    active = low(jax.nn.gelu(inner_pre, approximate=False))
    outer_out = low_back(jnp.einsum('ngf,gfd->ngd', active, outer_w, precision=highest) + outer_b.reshape(GROUPS, -1))
    return layer_norm(outer_out.reshape(length, -1) + normed, norm2_gain, norm2_bias)

def reference(hidden_in, segment_ids, out_grad, query_w, query_b, key_w, value_w, value_b, depth_kernel, point_w, point_b, kernel_w, kernel_b, conv_w, conv_b, output_w, output_b, norm1_gain, norm1_bias, inner_w, inner_b, outer_w, outer_b, norm2_gain, norm2_bias):
    params = tuple((weight.astype(jnp.float32) for weight in (query_w, query_b, key_w, value_w, value_b, depth_kernel, point_w, point_b, kernel_w, kernel_b, conv_w, conv_b, output_w, output_b, norm1_gain, norm1_bias, inner_w, inner_b, outer_w, outer_b, norm2_gain, norm2_bias)))
    seq_count = hidden_in.shape[0] * hidden_in.shape[1]
    tokens = hidden_in.astype(jnp.float32).reshape(seq_count, SEQ, D)
    segs = segment_ids.reshape(seq_count, SEQ)
    cotangents = out_grad.astype(jnp.float32).reshape(seq_count, SEQ, D)

    def one_seq(totals, inputs):
        tok_seq, seg_seq, cot_seq = inputs
        result, pull = jax.vjp(lambda tok_arg, par_arg: forward_seq(tok_arg, seg_seq, par_arg), tok_seq, params)
        grad_tok, grad_par = pull(cot_seq)
        return (jax.tree.map(jnp.add, totals, grad_par), (result.astype(jnp.bfloat16), grad_tok))
    totals, (results, grad_tokens) = lax.scan(one_seq, jax.tree.map(jnp.zeros_like, params), (tokens, segs, cotangents))
    return (results.reshape(hidden_in.shape), grad_tokens.reshape(hidden_in.shape), totals[0], totals[1], totals[2], totals[3], totals[4], totals[5], totals[6], totals[7], totals[8], totals[9], totals[10], totals[11], totals[12], totals[13], totals[14], totals[15], totals[16], totals[17], totals[18], totals[19], totals[20], totals[21])
```

```python
import functools

import jax
import jax.numpy as jnp
from jax import lax
from jax.experimental import pallas as pl
from jax.experimental.pallas import tpu as pltpu
from jax.sharding import PartitionSpec as P

HEADS = 6
HEAD_DIM = 64
KERNEL = 9
GROUPS = 2
HOPS = 2


def passed_along(shard, axis, by):
    count = lax.axis_size(axis)
    pairs = [(i, i + by) for i in range(count) if 0 <= i + by < count]
    return lax.ppermute(shard, axis, pairs)


def for_sending(shard):

    def short(part):
        return part.astype(jnp.bfloat16) if part.dtype == jnp.float32 else part

    return jax.tree.map(short, shard)


def with_halo(block, sides, width):
    for axis, dim in sides:
        count = lax.axis_size(axis)
        forward = [(i, i + 1) for i in range(count - 1)]
        backward = [(target, source) for source, target in forward]
        low = lax.ppermute(
            lax.slice_in_dim(block, block.shape[dim] - width, None, axis=dim), axis, forward
        )
        high = lax.ppermute(lax.slice_in_dim(block, 0, width, axis=dim), axis, backward)
        block = jnp.concatenate([low, block, high], axis=dim)
    return block


def layer_norm(values, gain, shift):
    center = values - jnp.mean(values, axis=-1, keepdims=True)
    spread = jnp.mean(center * center, axis=-1, keepdims=True)
    return center * lax.rsqrt(spread + 1e-05) * gain + shift


def gelu_exact(values):
    return jax.nn.gelu(values, approximate=False)


def kernel_softmax(values):
    return jax.nn.softmax(values, axis=-1)


def product(left, right):
    return jnp.dot(left, right, preferred_element_type=jnp.float32)


def product_tn(left, right):
    return jnp.einsum("na,nb->ab", left, right, preferred_element_type=jnp.float32)


def product_nt(left, right):
    return jnp.einsum("na,ba->nb", left, right, preferred_element_type=jnp.float32)


def column_sum(values):
    return jnp.sum(values.astype(jnp.float32), axis=0)


def placed_rows(term, before, after):
    widths = [(0, 0)] * term.ndim
    widths[1] = (before, after)
    return jnp.pad(term, widths)


TILE = 256
NEG = -1000000000.0
LANES = 128
HEADS_HERE = HEADS // 2


def rows_nt(left, right):
    return lax.dot_general(
        left, right, (((1,), (1,)), ((), ())), preferred_element_type=jnp.float32
    )


def lane_half(block, upper):
    lane = lax.broadcasted_iota(jnp.int32, block.shape, 1)
    keep = lane >= HEAD_DIM if upper else lane < HEAD_DIM
    return jnp.where(keep, block, jnp.zeros_like(block))


def same_document(segk_ref, segq_ref, j):
    cols = pl.ds(pl.multiple_of(j * TILE, TILE), TILE)
    row = segk_ref[0:1, cols]
    column = jnp.broadcast_to(row, (LANES, TILE)).T
    wide = jnp.concatenate([column] * (TILE // LANES), axis=1)
    return wide == segq_ref[0:1, :]


def load_queries(q_ref, qm_ref):
    scale = jnp.asarray(HEAD_DIM ** (-0.5), q_ref.dtype)
    first = q_ref[:, 0:LANES] * scale
    qm_ref[0] = lane_half(first, False)
    qm_ref[1] = lane_half(first, True)
    qm_ref[2] = lane_half(q_ref[:, LANES : 2 * LANES] * scale, False)


KEY_GROUP = (0, 0, 1)
VALUE_GROUP = (2, 2, 1)


def lane_group(group):
    return slice(group * LANES, (group + 1) * LANES)


def attend_kernel(bounds, q_ref, kv_ref, segk_ref, segq_ref, out_ref, outt_ref, lse_ref,
                  qm_ref, m_ref, l_ref, acc_ref, low_ref):
    tile = pl.program_id(0)
    load_queries(q_ref, qm_ref)
    m_ref[...] = jnp.full_like(m_ref, -jnp.inf)
    l_ref[...] = jnp.zeros_like(l_ref)
    acc_ref[...] = jnp.zeros_like(acc_ref)
    low_ref[...] = jnp.zeros_like(low_ref)

    def step(j, carry):
        rows = pl.ds(pl.multiple_of(j * TILE, TILE), TILE)
        same = same_document(segk_ref, segq_ref, j)
        values_t = kv_ref[rows, LANES : 3 * LANES].T
        value_rows = (2 * HEAD_DIM, 3 * HEAD_DIM, HEAD_DIM)
        for head in range(HEADS_HERE):
            keys = kv_ref[rows, lane_group(KEY_GROUP[head])]
            scores = jnp.where(same, rows_nt(keys, qm_ref[head]), NEG)
            old = m_ref[head : head + 1, :]
            top = jnp.maximum(old, jnp.max(scores, axis=0, keepdims=True))
            expo = jnp.exp(scores - top)
            alpha = jnp.exp(old - top)
            m_ref[head : head + 1, :] = top
            l_ref[head : head + 1, :] = l_ref[head : head + 1, :] * alpha + jnp.sum(
                expo, axis=0, keepdims=True
            )
            high = expo.astype(jnp.bfloat16)
            rest = (expo - high.astype(jnp.float32)).astype(jnp.bfloat16)
            span = slice(head * HEAD_DIM, (head + 1) * HEAD_DIM)
            vals = values_t[value_rows[head] : value_rows[head] + HEAD_DIM, :]
            acc_ref[span, :] = acc_ref[span, :] * alpha + jnp.dot(
                vals, high, preferred_element_type=jnp.float32
            )
            low_ref[span, :] = low_ref[span, :] * alpha + jnp.dot(
                vals, rest, preferred_element_type=jnp.float32
            )
        return carry

    lax.fori_loop(bounds[0, tile], bounds[1, tile], step, 0)
    lse_ref[...] = m_ref[...] + jnp.log(l_ref[...])
    used = HEADS_HERE * HEAD_DIM
    for head in range(HEADS_HERE):
        span = slice(head * HEAD_DIM, (head + 1) * HEAD_DIM)
        inv = 1.0 / l_ref[head : head + 1, :]
        acc_ref[span, :] = acc_ref[span, :] * inv
        low_ref[span, :] = low_ref[span, :] * inv
    outt_ref[...] = acc_ref[...] + low_ref[...]
    out_ref[...] = acc_ref[...].T.astype(jnp.bfloat16)


def attend(bounds, queries, window, seg_keys, seg_queries):
    rows, wide = queries.shape
    span, width = window.shape
    return pl.pallas_call(
        attend_kernel,
        grid_spec=pltpu.PrefetchScalarGridSpec(
            num_scalar_prefetch=1,
            grid=(rows // TILE,),
            in_specs=[
                pl.BlockSpec((TILE, wide), lambda i, b: (i, 0)),
                pl.BlockSpec((span, width), lambda i, b: (0, 0)),
                pl.BlockSpec((8, span), lambda i, b: (0, 0)),
                pl.BlockSpec((8, TILE), lambda i, b: (0, i)),
            ],
            out_specs=[
                pl.BlockSpec((TILE, wide), lambda i, b: (i, 0)),
                pl.BlockSpec((wide, TILE), lambda i, b: (0, i)),
                pl.BlockSpec((8, TILE), lambda i, b: (0, i)),
            ],
            scratch_shapes=[
                pltpu.VMEM((HEADS_HERE, TILE, LANES), jnp.bfloat16),
                pltpu.VMEM((8, TILE), jnp.float32),
                pltpu.VMEM((8, TILE), jnp.float32),
                pltpu.VMEM((wide, TILE), jnp.float32),
                pltpu.VMEM((wide, TILE), jnp.float32),
            ],
        ),
        out_shape=[
            jax.ShapeDtypeStruct((rows, wide), jnp.bfloat16),
            jax.ShapeDtypeStruct((wide, rows), jnp.float32),
            jax.ShapeDtypeStruct((8, rows), jnp.float32),
        ],
        compiler_params=pltpu.CompilerParams(vmem_limit_bytes=40 * 2**20),
        name="attend",
    )(bounds, queries, window, seg_keys, seg_queries)


def attend_back_kernel(bounds, q_ref, kv_ref, segk_ref, segq_ref, grad_ref, outt_ref, lse_ref,
                       dq_ref, dkv_ref, qm_ref, gm_ref, delta_ref, dq_acc, dkv_acc):
    tile = pl.program_id(0)

    @pl.when(tile == 0)
    def _():
        dkv_acc[...] = jnp.zeros_like(dkv_acc)

    load_queries(q_ref, qm_ref)
    gm_ref[0] = lane_half(grad_ref[:, 0:LANES], False)
    gm_ref[1] = lane_half(grad_ref[:, 0:LANES], True)
    gm_ref[2] = lane_half(grad_ref[:, LANES : 2 * LANES], True)
    grads_t = grad_ref[...].astype(jnp.float32).T
    grad_rows = (0, HEAD_DIM, 3 * HEAD_DIM)
    for head in range(HEADS_HERE):
        span = slice(head * HEAD_DIM, (head + 1) * HEAD_DIM)
        delta_ref[head : head + 1, :] = jnp.sum(
            grads_t[grad_rows[head] : grad_rows[head] + HEAD_DIM, :] * outt_ref[span, :],
            axis=0, keepdims=True,
        )
    dq_acc[...] = jnp.zeros_like(dq_acc)

    def step(j, carry):
        rows = pl.ds(pl.multiple_of(j * TILE, TILE), TILE)
        same = same_document(segk_ref, segq_ref, j)
        keys_t = kv_ref[rows, 0 : 2 * LANES].T
        sums = [dkv_acc[rows, lane_group(g)] for g in range(3)]
        for head in range(HEADS_HERE):
            span = slice(head * HEAD_DIM, (head + 1) * HEAD_DIM)
            keys = kv_ref[rows, lane_group(KEY_GROUP[head])]
            vals = kv_ref[rows, lane_group(VALUE_GROUP[head])]
            scores = rows_nt(keys, qm_ref[head])
            probs = jnp.where(same, jnp.exp(scores - lse_ref[head : head + 1, :]), 0.0)
            dprobs = rows_nt(vals, gm_ref[head])
            dscores = (probs * (dprobs - delta_ref[head : head + 1, :])).astype(jnp.bfloat16)
            dq_acc[span, :] += jnp.dot(
                keys_t[span, :], dscores, preferred_element_type=jnp.float32
            )
            sums[KEY_GROUP[head]] += jnp.dot(
                dscores, qm_ref[head], preferred_element_type=jnp.float32
            )
            sums[VALUE_GROUP[head]] += jnp.dot(
                probs.astype(jnp.bfloat16), gm_ref[head], preferred_element_type=jnp.float32
            )
        for g in range(3):
            dkv_acc[rows, lane_group(g)] = sums[g]
        return carry

    lax.fori_loop(bounds[0, tile], bounds[1, tile], step, 0)
    dq_ref[...] = (dq_acc[...].T * HEAD_DIM ** (-0.5)).astype(dq_ref.dtype)

    @pl.when(tile == pl.num_programs(0) - 1)
    def _():
        dkv_ref[...] = dkv_acc[...].astype(dkv_ref.dtype)


def attend_back(bounds, queries, window, seg_keys, seg_queries, grads, outt, lse):
    rows, wide = queries.shape
    span, width = window.shape
    return pl.pallas_call(
        attend_back_kernel,
        grid_spec=pltpu.PrefetchScalarGridSpec(
            num_scalar_prefetch=1,
            grid=(rows // TILE,),
            in_specs=[
                pl.BlockSpec((TILE, wide), lambda i, b: (i, 0)),
                pl.BlockSpec((span, width), lambda i, b: (0, 0)),
                pl.BlockSpec((8, span), lambda i, b: (0, 0)),
                pl.BlockSpec((8, TILE), lambda i, b: (0, i)),
                pl.BlockSpec((TILE, wide), lambda i, b: (i, 0)),
                pl.BlockSpec((wide, TILE), lambda i, b: (0, i)),
                pl.BlockSpec((8, TILE), lambda i, b: (0, i)),
            ],
            out_specs=[
                pl.BlockSpec((TILE, wide), lambda i, b: (i, 0)),
                pl.BlockSpec((span, width), lambda i, b: (0, 0)),
            ],
            scratch_shapes=[
                pltpu.VMEM((HEADS_HERE, TILE, LANES), jnp.bfloat16),
                pltpu.VMEM((HEADS_HERE, TILE, LANES), jnp.bfloat16),
                pltpu.VMEM((8, TILE), jnp.float32),
                pltpu.VMEM((wide, TILE), jnp.float32),
                pltpu.VMEM((span, width), jnp.float32),
            ],
        ),
        out_shape=[
            jax.ShapeDtypeStruct((rows, wide), jnp.bfloat16),
            jax.ShapeDtypeStruct((span, width), jnp.bfloat16),
        ],
        compiler_params=pltpu.CompilerParams(vmem_limit_bytes=48 * 2**20),
        name="attend_back",
    )(bounds, queries, window, seg_keys, seg_queries, grads, outt, lse)


def rolled(part):
    return jnp.concatenate([part[..., HEAD_DIM:], part[..., :HEAD_DIM]], axis=-1)


def joined_halves(lower, upper):
    return jnp.concatenate([lower[..., :HEAD_DIM], upper[..., HEAD_DIM:]], axis=-1)


def lanes_of(values):
    return [values[..., lane_group(g)] for g in range(3)]


def parts_of_queries(queries, upper):
    one, two, three = lanes_of(queries)
    swapped = rolled(two)
    first, second = (swapped, two) if upper else (two, swapped)
    return jnp.stack(
        [jnp.concatenate([one, first], axis=-1), jnp.concatenate([three, second], axis=-1)], axis=1
    ).reshape(TEAM, queries.shape[1], 2 * LANES)


def parts_of_keys(keys, values):
    k = lanes_of(keys)
    v = lanes_of(values)
    low = jnp.concatenate([k[0], joined_halves(k[1], rolled(v[1])), v[0]], axis=-1)
    high = jnp.concatenate([k[2], joined_halves(rolled(k[1]), v[1]), v[2]], axis=-1)
    return jnp.stack([low, high], axis=1).reshape(TEAM, keys.shape[1], 3 * LANES)


def natural_rows(parts):
    pairs = parts.reshape(TEAM // 2, 2, parts.shape[1], 2 * LANES)
    low, high = pairs[:, 0], pairs[:, 1]
    middle = joined_halves(low[..., LANES:], rolled(high[..., LANES:]))
    return jnp.concatenate([low[..., :LANES], middle, high[..., :LANES]], axis=-1)


def natural_keys(parts):
    pairs = parts.reshape(TEAM // 2, 2, parts.shape[1], 3 * LANES)
    low, high = lanes_of(pairs[:, 0]), lanes_of(pairs[:, 1])
    keys = jnp.concatenate([low[0], joined_halves(low[1], rolled(high[1])), high[0]], axis=-1)
    values = jnp.concatenate([low[2], joined_halves(rolled(low[1]), high[1]), high[2]], axis=-1)
    return keys, values


TEAM = 4


def flip(index, step):
    return index + step * (1 - 2 * lax.rem(lax.div(index, step), 2))


def mate(rank, offset):
    if offset % 2:
        rank = flip(rank, 1)
    if offset // 2:
        rank = flip(rank, 2)
    return rank


def greet(peers):
    barrier = pltpu.get_barrier_semaphore()
    for peer in peers:
        pl.semaphore_signal(
            barrier, inc=1, device_id=peer, device_id_type=pl.DeviceIdType.MESH
        )
    pl.semaphore_wait(barrier, len(peers))


def remote(src, dst, send, recv, peer):
    return pltpu.make_async_remote_copy(
        src_ref=src,
        dst_ref=dst,
        send_sem=send,
        recv_sem=recv,
        device_id=peer,
        device_id_type=pl.DeviceIdType.MESH,
    )


def shard_view(ref, part, rows, count):
    if len(ref.shape) == 3:
        return ref.at[:, pl.ds(part * rows, count), :]
    return ref.at[pl.ds(part * rows, count), :]


def gather_kernel(count, *refs):
    shards, fulls = refs[:count], refs[count : 2 * count]
    send_y, recv_y, send_c, recv_c, local = refs[2 * count :]
    me, side = lax.axis_index("ctx"), lax.axis_index("wsh")
    core = lax.rem(me, 2)
    twin, across = {"ctx": flip(me, 1)}, {"wsh": 1 - side}
    greet([twin, across])
    copies = []

    def half(ref, base, rows):
        view = pl.ds(pl.multiple_of(base + core * (rows // 2), 16), rows // 2)
        return ref.at[:, view, :] if len(ref.shape) == 3 else ref.at[view, :]

    def whole(ref, base, rows):
        view = pl.ds(pl.multiple_of(base, 16), rows)
        return ref.at[:, view, :] if len(ref.shape) == 3 else ref.at[view, :]

    for i in range(count):
        rows = shards[i].shape[-2]
        copy = remote(
            half(shards[i], 0, rows), half(fulls[i], side * rows, rows),
            send_y.at[i], recv_y.at[i], across,
        )
        copy.start()
        copies.append(copy)
    own = []
    for i in range(count):
        rows = shards[i].shape[-2]
        copy = pltpu.make_async_copy(shards[i], whole(fulls[i], side * rows, rows), local.at[i])
        copy.start()
        own.append(copy)
    passed = []
    for i in range(count):
        rows = shards[i].shape[-2]
        copies[i].wait_recv()
        came = half(fulls[i], (1 - side) * rows, rows)
        copy = remote(came, came, send_c.at[i], recv_c.at[i], twin)
        copy.start()
        passed.append(copy)
    for i in range(count):
        copies[i].wait_send()
        own[i].wait()
        passed[i].wait()


def gather_weights(shards):
    count = len(shards)
    fulls = [
        jax.ShapeDtypeStruct(s.shape[:-2] + (2 * s.shape[-2], s.shape[-1]), s.dtype) for s in shards
    ]
    return pl.pallas_call(
        functools.partial(gather_kernel, count),
        out_shape=fulls,
        in_specs=[pl.BlockSpec(memory_space=pl.ANY)] * count,
        out_specs=[pl.BlockSpec(memory_space=pl.ANY)] * count,
        scratch_shapes=[pltpu.SemaphoreType.DMA((count,))] * 5,
        compiler_params=pltpu.CompilerParams(collective_id=0, has_side_effects=True),
        name="gather_weights",
    )(*shards)


def spread_kernel(kv_ref, q_ref, win_ref, out_ref, send_kv, recv_kv, send_q, recv_q,
                  send_l, recv_l, send_r, recv_r):
    me = lax.axis_index("ctx")
    count = lax.axis_size("ctx")
    rank = lax.rem(me, TEAM)
    base = me - rank
    team = lax.div(me, TEAM)
    teams = count // TEAM
    block = kv_ref.shape[1]
    halo = (TEAM - 1) * block
    right, left = lax.rem(me + TEAM, count), lax.rem(me + count - TEAM, count)
    greet([{"ctx": base + mate(rank, o)} for o in range(1, TEAM)] + [{"ctx": right}, {"ctx": left}])

    def place(r):
        return win_ref.at[pl.ds(pl.multiple_of(halo + r * block, 16), block), :]

    kv_copies, q_copies = [], []
    own_kv = pltpu.make_async_copy(kv_ref.at[rank], place(rank), recv_kv.at[0])
    own_kv.start()
    own_q = pltpu.make_async_copy(q_ref.at[rank], out_ref.at[rank], recv_q.at[0])
    own_q.start()
    for o in range(1, TEAM):
        other = mate(rank, o)
        copy = remote(kv_ref.at[other], place(rank), send_kv.at[o], recv_kv.at[o],
                      {"ctx": base + other})
        copy.start()
        kv_copies.append(copy)
    for o in range(1, TEAM):
        other = mate(rank, o)
        copy = remote(q_ref.at[other], out_ref.at[rank], send_q.at[o], recv_q.at[o],
                      {"ctx": base + other})
        copy.start()
        q_copies.append(copy)

    def onward(o):
        r = mate(rank, o)
        to_right = remote(
            place(r), win_ref.at[pl.ds(pl.multiple_of((r + TEAM - 1) % TEAM * block, 16), block), :],
            send_r.at[o], recv_r.at[o], {"ctx": right},
        )
        to_left = remote(
            place(r),
            win_ref.at[pl.ds(pl.multiple_of(halo + TEAM * block + lax.rem(r, TEAM - 1) * block, 16), block), :],
            send_l.at[o], recv_l.at[o], {"ctx": left},
        )
        return r, to_right, to_left

    for o in range(TEAM):
        if o == 0:
            own_kv.wait()
        else:
            kv_copies[o - 1].wait_recv()
        r, to_right, to_left = onward(o)
        pl.when((r >= 1) & (team < teams - 1))(to_right.start)
        pl.when((r <= TEAM - 2) & (team > 0))(to_left.start)
    own_q.wait()
    for copy in kv_copies:
        copy.wait_send()
    for copy in q_copies:
        copy.wait()
    for o in range(TEAM):
        r, to_right, to_left = onward(o)
        pl.when((r >= 1) & (team < teams - 1))(to_right.wait_send)
        pl.when((r <= TEAM - 2) & (team > 0))(to_left.wait_send)
        pl.when((r >= 1) & (team > 0))(to_right.wait_recv)
        pl.when((r <= TEAM - 2) & (team < teams - 1))(to_left.wait_recv)


def spread(kv_parts, q_parts):
    team, block, width = kv_parts.shape
    return pl.pallas_call(
        spread_kernel,
        out_shape=[
            jax.ShapeDtypeStruct(((3 * team - 2) * block, width), kv_parts.dtype),
            jax.ShapeDtypeStruct(q_parts.shape, q_parts.dtype),
        ],
        in_specs=[pl.BlockSpec(memory_space=pl.ANY)] * 2,
        out_specs=[pl.BlockSpec(memory_space=pl.ANY)] * 2,
        scratch_shapes=[pltpu.SemaphoreType.DMA((team,))] * 8,
        compiler_params=pltpu.CompilerParams(collective_id=1, has_side_effects=True),
        name="spread",
    )(kv_parts, q_parts)


def swap_kernel(src_ref, out_ref, send, recv):
    me = lax.axis_index("ctx")
    rank = lax.rem(me, TEAM)
    base = me - rank
    greet([{"ctx": base + mate(rank, o)} for o in range(1, TEAM)])
    copies = [pltpu.make_async_copy(src_ref.at[rank], out_ref.at[rank], recv.at[0])]
    for o in range(1, TEAM):
        other = mate(rank, o)
        copies.append(
            remote(src_ref.at[other], out_ref.at[rank], send.at[o], recv.at[o],
                   {"ctx": base + other})
        )
    for copy in copies:
        copy.start()
    for copy in copies:
        copy.wait()


def swap(parts, ident):
    return pl.pallas_call(
        swap_kernel,
        out_shape=jax.ShapeDtypeStruct(parts.shape, parts.dtype),
        in_specs=[pl.BlockSpec(memory_space=pl.ANY)],
        out_specs=pl.BlockSpec(memory_space=pl.ANY),
        scratch_shapes=[pltpu.SemaphoreType.DMA((TEAM,))] * 2,
        compiler_params=pltpu.CompilerParams(collective_id=ident, has_side_effects=True),
        name="swap",
    )(parts)


def collect_kernel(win_ref, dq_ref, kv_out, q_out, from_right, from_left, mine, total,
                   send_q, recv_q, send_z, recv_z, load, send_kv, recv_kv):
    me = lax.axis_index("ctx")
    count = lax.axis_size("ctx")
    rank = lax.rem(me, TEAM)
    base = me - rank
    team = lax.div(me, TEAM)
    teams = count // TEAM
    block = dq_ref.shape[1]
    halo = (TEAM - 1) * block
    right, left = lax.rem(me + TEAM, count), lax.rem(me + count - TEAM, count)
    greet([{"ctx": base + mate(rank, o)} for o in range(1, TEAM)] + [{"ctx": right}, {"ctx": left}])
    to_left = remote(win_ref.at[pl.ds(0, halo), :], from_right, send_z.at[0], recv_z.at[0],
                     {"ctx": left})
    to_right = remote(win_ref.at[pl.ds(halo + TEAM * block, halo), :], from_left, send_z.at[1],
                      recv_z.at[1], {"ctx": right})
    pl.when(team > 0)(to_left.start)
    pl.when(team < teams - 1)(to_right.start)
    center = pltpu.make_async_copy(win_ref.at[pl.ds(halo, TEAM * block), :], mine, load.at[0])
    center.start()
    own_q = pltpu.make_async_copy(dq_ref.at[rank], q_out.at[rank], recv_q.at[0])
    own_q.start()
    q_copies = []
    for o in range(1, TEAM):
        other = mate(rank, o)
        copy = remote(dq_ref.at[other], q_out.at[rank], send_q.at[o], recv_q.at[o],
                      {"ctx": base + other})
        copy.start()
        q_copies.append(copy)

    @pl.when(team == 0)
    def _():
        from_left[...] = jnp.zeros_like(from_left)

    @pl.when(team == teams - 1)
    def _():
        from_right[...] = jnp.zeros_like(from_right)

    center.wait()
    pl.when(team < teams - 1)(to_left.wait_recv)
    pl.when(team > 0)(to_right.wait_recv)
    for r in range(TEAM):
        rows = pl.ds(r * block, block)
        value = mine[rows, :].astype(jnp.float32)
        if r < TEAM - 1:
            value += from_left[rows, :].astype(jnp.float32)
        if r > 0:
            value += from_right[pl.ds((r - 1) * block, block), :].astype(jnp.float32)
        total[r] = value.astype(total.dtype)
    kv_copies = [pltpu.make_async_copy(total.at[rank], kv_out.at[rank], recv_kv.at[0])]
    for o in range(1, TEAM):
        other = mate(rank, o)
        kv_copies.append(
            remote(total.at[other], kv_out.at[rank], send_kv.at[o], recv_kv.at[o],
                   {"ctx": base + other})
        )
    for copy in kv_copies:
        copy.start()
    own_q.wait()
    for copy in q_copies + kv_copies:
        copy.wait()
    pl.when(team > 0)(to_left.wait_send)
    pl.when(team < teams - 1)(to_right.wait_send)


def collect(window, dq_parts):
    team, block, _ = dq_parts.shape
    width = window.shape[1]
    halo = (team - 1) * block
    return pl.pallas_call(
        collect_kernel,
        out_shape=[
            jax.ShapeDtypeStruct((team, block, width), window.dtype),
            jax.ShapeDtypeStruct(dq_parts.shape, dq_parts.dtype),
        ],
        in_specs=[pl.BlockSpec(memory_space=pl.ANY)] * 2,
        out_specs=[pl.BlockSpec(memory_space=pl.ANY)] * 2,
        scratch_shapes=[
            pltpu.VMEM((halo, width), window.dtype),
            pltpu.VMEM((halo, width), window.dtype),
            pltpu.VMEM((team * block, width), window.dtype),
            pltpu.VMEM((team, block, width), window.dtype),
            pltpu.SemaphoreType.DMA((team,)),
            pltpu.SemaphoreType.DMA((team,)),
            pltpu.SemaphoreType.DMA((2,)),
            pltpu.SemaphoreType.DMA((2,)),
            pltpu.SemaphoreType.DMA((1,)),
            pltpu.SemaphoreType.DMA((team,)),
            pltpu.SemaphoreType.DMA((team,)),
        ],
        compiler_params=pltpu.CompilerParams(
            collective_id=4, has_side_effects=True, vmem_limit_bytes=32 * 2**20
        ),
        name="collect",
    )(window, dq_parts)


def reduce_kernel(levels, g_ref, out_ref, acc, mine, came, *rest):
    steps = len(levels)
    sends, recvs = rest[:steps], rest[steps : 2 * steps]
    load, send_sem, recv_sem, send_back, recv_back = rest[2 * steps :]
    me, side = lax.axis_index("ctx"), lax.axis_index("wsh")
    core = lax.rem(me, 2)
    twin, across = {"ctx": flip(me, 1)}, {"wsh": 1 - side}
    peers = [twin, across] + [{"ctx": flip(me, step)} for step in levels[1:]]
    greet(peers)
    rows = g_ref.shape[1]
    half = rows // 2

    def add(n, write):
        chunk = max(c for c in range(16, 385, 16) if n % c == 0)

        def body(i, carry):
            write(pl.ds(pl.multiple_of(i * chunk, 16), chunk))
            return carry

        lax.fori_loop(0, n // chunk, body, 0)

    first = remote(
        g_ref.at[:, pl.ds(pl.multiple_of((1 - core) * half, 16), half), :], came,
        send_sem.at[0], recv_sem.at[0], twin,
    )
    first.start()
    own = pltpu.make_async_copy(
        g_ref.at[:, pl.ds(pl.multiple_of(core * half, 16), half), :], mine, load.at[0]
    )
    own.start()
    own.wait()
    first.wait()

    def level0(view):
        sends[0][view, :] = (
            mine[1 - side, view, :].astype(jnp.float32) + came[1 - side, view, :].astype(jnp.float32)
        ).astype(jnp.bfloat16)
        acc[view, :] = mine[side, view, :].astype(jnp.float32) + came[side, view, :].astype(
            jnp.float32
        )

    add(half, level0)
    copy = remote(sends[0], recvs[0], send_sem.at[1], recv_sem.at[1], across)
    copy.start()
    copy.wait()
    start = jnp.int32(0)
    size = half
    arrived = recvs[0]
    for i, step in enumerate(levels[1:]):
        bit = lax.rem(lax.div(me, step), 2)
        size = size // 2
        keep = start + bit * size
        give = start + (1 - bit) * size
        shift_keep, shift_give = bit * size, (1 - bit) * size

        def both(view, arrived=arrived, keep=keep, give=give, sk=shift_keep, sg=shift_give, i=i):
            lo = view.start
            n = view.size
            g_rows = pl.ds(pl.multiple_of(give + lo, 16), n)
            k_rows = pl.ds(pl.multiple_of(keep + lo, 16), n)
            sends[i + 1][view, :] = (
                acc[g_rows, :]
                + arrived[pl.ds(pl.multiple_of(sg + lo, 16), n), :].astype(jnp.float32)
            ).astype(jnp.bfloat16)
            acc[k_rows, :] = acc[k_rows, :] + arrived[
                pl.ds(pl.multiple_of(sk + lo, 16), n), :
            ].astype(jnp.float32)

        add(size, both)
        copy = remote(
            sends[i + 1], recvs[i + 1], send_sem.at[i + 2], recv_sem.at[i + 2],
            {"ctx": flip(me, step)},
        )
        copy.start()
        copy.wait()
        arrived = recvs[i + 1]
        start = keep
    final = mine.at[0]

    def last(view):
        rows_ = pl.ds(pl.multiple_of(start + view.start, 16), view.size)
        mine[0, rows_, :] = (acc[rows_, :] + arrived[view, :].astype(jnp.float32)).astype(
            jnp.bfloat16
        )

    add(size, last)
    for i, step in reversed(list(enumerate(levels[1:]))):
        view = mine.at[0, pl.ds(pl.multiple_of(start, 16), size), :]
        copy = remote(view, view, send_back.at[i + 1], recv_back.at[i + 1], {"ctx": flip(me, step)})
        copy.start()
        copy.wait()
        start = start - lax.rem(lax.div(me, step), 2) * size
        size = size * 2
    here = out_ref.at[pl.ds(pl.multiple_of(core * half, 16), half), :]
    own = pltpu.make_async_copy(final, here, load.at[0])
    own.start()
    copy = remote(final, here, send_back.at[0], recv_back.at[0], twin)
    copy.start()
    own.wait()
    copy.wait()


def reduce_grads(packed):
    _, rows, width = packed.shape
    half = rows // 2
    levels, step = [1], 2
    while step < lax.axis_size("ctx"):
        levels.append(step)
        step *= 2
    sizes = [half >> i for i in range(len(levels))]
    return pl.pallas_call(
        functools.partial(reduce_kernel, tuple(levels)),
        out_shape=jax.ShapeDtypeStruct((rows, width), packed.dtype),
        in_specs=[pl.BlockSpec(memory_space=pl.ANY)],
        out_specs=pl.BlockSpec(memory_space=pl.ANY),
        scratch_shapes=[
            pltpu.VMEM((half, width), jnp.float32),
            pltpu.VMEM((2, half, width), jnp.bfloat16),
            pltpu.VMEM((2, half, width), jnp.bfloat16),
        ]
        + [pltpu.VMEM((n, width), jnp.bfloat16) for n in sizes] * 2
        + [
            pltpu.SemaphoreType.DMA((1,)),
            pltpu.SemaphoreType.DMA((len(levels) + 1,)),
            pltpu.SemaphoreType.DMA((len(levels) + 1,)),
            pltpu.SemaphoreType.DMA((len(levels),)),
            pltpu.SemaphoreType.DMA((len(levels),)),
        ],
        compiler_params=pltpu.CompilerParams(
            collective_id=5, has_side_effects=True, vmem_limit_bytes=56 * 2**20
        ),
        name="reduce_grads",
    )(packed)


def small_rows(vectors, depth, kernel_w, count):
    flat = jnp.concatenate([v.reshape(-1) for v in vectors])
    flat = jnp.pad(flat, (0, -flat.shape[0] % 384))
    rows = jnp.concatenate([depth, flat.reshape(-1, 384), kernel_w.T.reshape(-1, 384)])
    return jnp.pad(rows, ((0, count - rows.shape[0]), (0, 0)))


def on_device(
    hidden_in,
    segment_ids,
    out_grad,
    query_w,
    query_b,
    key_w,
    value_w,
    value_b,
    depth_kernel,
    point_w,
    point_b,
    kernel_w,
    kernel_b,
    conv_w,
    conv_b,
    output_w,
    output_b,
    norm1_gain,
    norm1_bias,
    inner_w,
    inner_b,
    outer_w,
    outer_b,
    norm2_gain,
    norm2_bias,
):
    vectors = [query_b, value_b, point_b, conv_b, output_b, norm1_gain, norm1_bias, inner_b,
               outer_b, norm2_gain, norm2_bias, kernel_b]
    small = small_rows(vectors, depth_kernel, kernel_w, 64)
    (key_mat, value_mat, query_mat, point_mat, conv_mat, small_full, output_mat, inner_mat,
     outer_mat) = gather_weights(
        [key_w, value_w, query_w, point_w, conv_w, small, output_w, inner_w, outer_w]
    )
    small_full = small_full.reshape(2, 64, 384)
    depth_taps = small_full[:, :KERNEL].transpose(1, 0, 2).reshape(KERNEL, -1)
    sizes = [v.shape[0] for v in vectors]
    total = sum(sizes)
    flat_rows_ = (total + 383) // 384
    flat = small_full[:, KERNEL : KERNEL + flat_rows_].reshape(2, -1)
    offsets = [sum(sizes[:i]) for i in range(len(sizes) + 1)]
    (query_vec, value_vec, point_vec, conv_vec, output_vec, gain_one, shift_one, inner_vec,
     outer_vec, gain_two, shift_two, kernel_vec) = [
        flat[:, offsets[i] : offsets[i + 1]].reshape(-1) for i in range(len(sizes))
    ]
    kernel_rows = kernel_w.shape[0] * kernel_w.shape[1] // 384
    kernel_mat = (
        small_full[:, KERNEL + flat_rows_ : KERNEL + flat_rows_ + kernel_rows]
        .reshape(2, kernel_w.shape[1], kernel_w.shape[0])
        .transpose(0, 2, 1)
        .reshape(-1, kernel_w.shape[1])
    )
    micro_count, seq_local, block_len, model_width = hidden_in.shape
    seq_count = micro_count * seq_local
    row_count = seq_count * block_len
    att_width = query_mat.shape[1]
    half_taps = KERNEL // 2
    flat_rows = hidden_in.reshape(row_count, model_width)
    position = lax.axis_index("ctx")
    seg_rows = segment_ids.reshape(seq_count, segment_ids.shape[2])
    pad_rows = (TEAM - 1) * block_len
    seg_pad = jnp.pad(seg_rows, ((0, 0), (pad_rows, pad_rows)), constant_values=-1)
    own_seg = lax.dynamic_slice_in_dim(seg_pad, position * block_len + pad_rows, block_len, 1)
    rank = lax.rem(position, TEAM)
    team_seg = lax.dynamic_slice(
        jnp.concatenate(
            [seg_pad[:, : pad_rows + seg_rows.shape[1]],
             jnp.full((seq_count, pad_rows), 2**24, seg_pad.dtype)], axis=1
        ),
        (lax.div(rank, 2), (position - rank) * block_len),
        (1, (3 * TEAM - 2) * block_len),
    )
    query_seg = team_seg[:, pad_rows : pad_rows + TEAM * block_len]
    lows = query_seg[0, ::TILE]
    highs = query_seg[0, TILE - 1 :: TILE]
    before = jnp.sum(team_seg < lows[:, None], axis=1, dtype=jnp.int32)
    through = jnp.sum(team_seg <= highs[:, None], axis=1, dtype=jnp.int32)
    bounds = jnp.stack([before // TILE, (through + TILE - 1) // TILE])
    seg_keys = jnp.broadcast_to(team_seg.astype(jnp.float32), (8, team_seg.shape[1]))
    seg_queries = jnp.broadcast_to(query_seg.astype(jnp.float32), (8, query_seg.shape[1]))
    rim_seg = lax.dynamic_slice_in_dim(
        seg_pad, position * block_len + pad_rows - half_taps, block_len + 2 * half_taps, 1
    )
    tap_mask = jnp.stack(
        [rim_seg[:, offset : offset + block_len] == own_seg for offset in range(KERNEL)], axis=2
    ).astype(jnp.float32)
    rimmed = with_halo(
        hidden_in.reshape(seq_count, block_len, model_width), (("ctx", 1),), half_taps
    )
    queries = (product(flat_rows, query_mat) + query_vec).astype(jnp.bfloat16)
    query_blocks = queries.reshape(seq_count, block_len, att_width)
    keys = product(flat_rows, key_mat).astype(jnp.bfloat16)
    values = (product(flat_rows, value_mat) + value_vec).astype(jnp.bfloat16)
    window, query_team = spread(
        parts_of_keys(
            keys.reshape(seq_count, block_len, att_width),
            values.reshape(seq_count, block_len, att_width),
        ),
        parts_of_queries(query_blocks, False),
    )
    query_team = query_team.reshape(TEAM * block_len, 2 * LANES)
    depth_sum = sum(
        (
            depth_taps[offset].astype(jnp.float32)
            * rimmed[:, offset : offset + block_len]
            * tap_mask[:, :, offset : offset + 1]
            for offset in range(KERNEL)
        )
    )
    depth_low = depth_sum.astype(jnp.bfloat16).reshape(row_count, model_width)
    span_keys = product(depth_low, point_mat) + point_vec
    mixed_low = (span_keys * queries).astype(jnp.bfloat16)
    logits = (product(mixed_low, kernel_mat) + kernel_vec).reshape(
        seq_count, block_len, HEADS, KERNEL
    )
    kernels, kern_pull = jax.vjp(kernel_softmax, logits)
    conv_ext = (product(rimmed.reshape(-1, model_width), conv_mat) + conv_vec).reshape(
        seq_count, block_len + 2 * half_taps, HEADS, HEAD_DIM
    )
    convolved = sum(
        (
            (kernels[..., offset] * tap_mask[:, :, offset : offset + 1])[..., None]
            * conv_ext[:, offset : offset + block_len]
            for offset in range(KERNEL)
        )
    )
    attended_team, attended_t, log_sums = attend(
        bounds, query_team, window, seg_keys, seg_queries
    )
    attended = natural_rows(swap(attended_team.reshape(TEAM, block_len, -1), 2))
    joined = jnp.concatenate(
        [
            attended.reshape(row_count, att_width),
            convolved.reshape(row_count, att_width).astype(jnp.bfloat16),
        ],
        axis=1,
    )
    branch = product(joined, output_mat) + output_vec
    normed, norm1_pull = jax.vjp(
        layer_norm, branch + flat_rows, gain_one.astype(jnp.float32), shift_one.astype(jnp.float32)
    )
    normed_low = normed.astype(jnp.bfloat16).reshape(row_count, GROUPS, -1)
    inner_pre = jnp.einsum(
        "ngd,gdf->ngf", normed_low, inner_mat, preferred_element_type=jnp.float32
    ) + inner_vec.reshape(GROUPS, -1)
    active, gelu_pull = jax.vjp(gelu_exact, inner_pre)
    active_low = active.astype(jnp.bfloat16)
    outer_out = (
        jnp.einsum("ngf,gfd->ngd", active_low, outer_mat, preferred_element_type=jnp.float32)
        + outer_vec.reshape(GROUPS, -1)
    ).reshape(row_count, model_width)
    final_out, norm2_pull = jax.vjp(
        layer_norm, outer_out + normed, gain_two.astype(jnp.float32), shift_two.astype(jnp.float32)
    )
    output = final_out.astype(jnp.bfloat16).reshape(hidden_in.shape)
    grad_sum2, grad_gain2, grad_shift2 = norm2_pull(
        out_grad.reshape(row_count, model_width).astype(jnp.float32)
    )
    grad_outer = grad_sum2.astype(jnp.bfloat16).reshape(row_count, GROUPS, -1)
    grad_outer_w = jnp.einsum(
        "ngf,ngd->gfd", active_low, grad_outer, preferred_element_type=jnp.float32
    )
    grad_outer_b = column_sum(grad_outer).reshape(-1)
    (grad_inner,) = gelu_pull(
        jnp.einsum("ngd,gfd->ngf", grad_outer, outer_mat, preferred_element_type=jnp.float32)
    )
    grad_inner = grad_inner.astype(jnp.bfloat16)
    grad_inner_w = jnp.einsum(
        "ngd,ngf->gdf", normed_low, grad_inner, preferred_element_type=jnp.float32
    )
    grad_inner_b = column_sum(grad_inner).reshape(-1)
    grad_normed = grad_sum2 + jnp.einsum(
        "ngf,gdf->ngd", grad_inner, inner_mat, preferred_element_type=jnp.float32
    ).reshape(row_count, model_width)
    grad_sum1, grad_gain1, grad_shift1 = norm1_pull(grad_normed)
    grad_branch = grad_sum1.astype(jnp.bfloat16)
    grad_output_w = product_tn(joined, grad_branch)
    grad_output_b = column_sum(grad_branch)
    grad_joined = product_nt(grad_branch, output_mat).astype(jnp.bfloat16)
    grad_attended = grad_joined[:, :att_width].reshape(seq_count, block_len, att_width)
    grad_conv = (
        grad_joined[:, att_width:]
        .astype(jnp.float32)
        .reshape(seq_count, block_len, HEADS, HEAD_DIM)
    )
    grad_kern_list = []
    ext_terms = []
    for offset in range(KERNEL):
        tap_weight = tap_mask[:, :, offset : offset + 1]
        grad_kern_list.append(
            jnp.sum(grad_conv * conv_ext[:, offset : offset + block_len], axis=-1) * tap_weight
        )
        ext_terms.append(
            placed_rows(
                (kernels[..., offset] * tap_weight)[..., None] * grad_conv,
                offset,
                2 * half_taps - offset,
            )
        )
    grad_ext = sum(ext_terms)
    (grad_logits,) = kern_pull(jnp.stack(grad_kern_list, axis=-1))
    grad_logits = grad_logits.reshape(row_count, HEADS * KERNEL).astype(jnp.bfloat16)
    grad_kernel_w = product_tn(mixed_low, grad_logits)
    grad_kernel_b = column_sum(grad_logits)
    grad_mixed = product_nt(grad_logits, kernel_mat)
    grad_spans = (grad_mixed * queries).astype(jnp.bfloat16)
    grad_query_conv = grad_mixed * span_keys
    grad_point_w = product_tn(depth_low, grad_spans)
    grad_point_b = column_sum(grad_spans)
    grad_depth = product_nt(grad_spans, point_mat).reshape(seq_count, block_len, model_width)
    grad_taps = []
    rim_terms = []
    for offset in range(KERNEL):
        masked_grad = grad_depth * tap_mask[:, :, offset : offset + 1]
        grad_taps.append(jnp.sum(masked_grad * rimmed[:, offset : offset + block_len], axis=(0, 1)))
        rim_terms.append(
            placed_rows(
                masked_grad * depth_taps[offset].astype(jnp.float32), offset, 2 * half_taps - offset
            )
        )
    grad_rim = sum(rim_terms)
    grad_depth_taps = jnp.stack(grad_taps, axis=0)
    rim_parts = jnp.concatenate([grad_ext.reshape(seq_count, -1, att_width), grad_rim], axis=2)
    edges = jnp.concatenate(
        [rim_parts[:, :half_taps], rim_parts[:, block_len + half_taps :]], axis=1
    )
    arrived = with_halo(edges.astype(jnp.bfloat16), (("ctx", 1),), half_taps).astype(edges.dtype)
    own_parts = (
        rim_parts[:, half_taps : half_taps + block_len]
        + placed_rows(arrived[:, :half_taps], 0, block_len - half_taps)
        + placed_rows(arrived[:, 3 * half_taps :], block_len - half_taps, 0)
    )
    grad_conv_vals = own_parts[..., :att_width].reshape(row_count, att_width).astype(jnp.bfloat16)
    grad_conv_w = product_tn(flat_rows, grad_conv_vals)
    grad_conv_b = column_sum(grad_conv_vals)
    grad_team = swap(parts_of_queries(grad_attended, True), 3).reshape(TEAM * block_len, 2 * LANES)
    grad_query_team, grad_window = attend_back(
        bounds, query_team, window, seg_keys, seg_queries, grad_team, attended_t, log_sums
    )
    kv_parts, dq_parts = collect(grad_window, grad_query_team.reshape(TEAM, block_len, -1))
    grad_query_att = natural_rows(dq_parts).astype(jnp.float32)
    grad_keys, grad_values = [
        part.reshape(row_count, att_width) for part in natural_keys(kv_parts)
    ]
    grad_queries = (grad_query_att.reshape(row_count, att_width) + grad_query_conv).astype(
        jnp.bfloat16
    )
    grad_query_w = product_tn(flat_rows, grad_queries)
    grad_query_b = column_sum(grad_queries)
    grad_key_w = product_tn(flat_rows, grad_keys)
    grad_value_w = product_tn(flat_rows, grad_values)
    grad_value_b = column_sum(grad_values)
    grad_input = (
        grad_sum1
        + product_nt(grad_queries, query_mat)
        + product_nt(grad_keys, key_mat)
        + product_nt(grad_values, value_mat)
        + product_nt(grad_conv_vals, conv_mat)
        + own_parts[..., att_width:].reshape(row_count, model_width)
    ).reshape(hidden_in.shape)
    low = lambda part: part.astype(jnp.bfloat16)
    halves = []
    for w in range(2):
        def cut(part, axis=0):
            size = part.shape[axis] // 2
            return lax.slice_in_dim(part, w * size, (w + 1) * size, axis=axis)

        grads = [cut(v) for v in (
            grad_query_b, grad_value_b, grad_point_b, grad_conv_b, grad_output_b, grad_gain1,
            grad_shift1, grad_inner_b, grad_outer_b, grad_gain2, grad_shift2, grad_kernel_b)]
        pieces = [cut(m) for m in (grad_key_w, grad_value_w, grad_query_w, grad_point_w, grad_conv_w)]
        pieces.append(small_rows(grads, cut(grad_depth_taps, 1), cut(grad_kernel_w), 64))
        pieces.append(cut(grad_output_w).reshape(-1, 384))
        pieces.append(cut(grad_inner_w, 1).reshape(-1, 384))
        pieces.append(cut(grad_outer_w, 1).reshape(-1, 384))
        halves.append(jnp.concatenate([low(p) for p in pieces]))
    packed = jnp.stack(halves)
    unit = 16 * lax.axis_size("ctx")
    packed = jnp.pad(packed, ((0, 0), (0, -packed.shape[1] % unit), (0, 0)))
    shared = reduce_grads(packed).astype(jnp.float32)
    taken = [0]

    def take(shape):
        rows = 1
        for n in shape:
            rows *= n
        rows //= 384
        taken[0] += rows
        return shared[taken[0] - rows : taken[0]].reshape(shape)

    o_key, o_value, o_query, o_point, o_conv = [take(key_w.shape) for _ in range(5)]
    o_small = take((64, 384))
    o_output = take(output_w.shape)
    o_inner = take(inner_w.shape)
    o_outer = take(outer_w.shape)
    flat = o_small[KERNEL : KERNEL + flat_rows_].reshape(-1)
    (o_query_b, o_value_b, o_point_b, o_conv_b, o_output_b, o_gain1, o_shift1, o_inner_b,
     o_outer_b, o_gain2, o_shift2, o_kernel_b) = [
        flat[offsets[i] : offsets[i + 1]] for i in range(len(sizes))
    ]
    o_kernel = (
        o_small[KERNEL + flat_rows_ : KERNEL + flat_rows_ + kernel_rows]
        .reshape(kernel_w.shape[1], kernel_w.shape[0])
        .T
    )
    shares = (
        o_query, o_query_b, o_key, o_value, o_value_b, o_small[:KERNEL], o_point, o_point_b,
        o_kernel, o_kernel_b, o_conv, o_conv_b, o_output, o_output_b, o_gain1, o_shift1,
        o_inner, o_inner_b, o_outer, o_outer_b, o_gain2, o_shift2,
    )
    return (output, grad_input) + shares


def solution(mesh):
    in_specs = (
        P(None, "wsh", "ctx", None),
        P(None, "wsh", None),
        P(None, "wsh", "ctx", None),
        P("wsh", None),
        P("wsh"),
        P("wsh", None),
        P("wsh", None),
        P("wsh"),
        P(None, "wsh"),
        P("wsh", None),
        P("wsh"),
        P("wsh", None),
        P("wsh"),
        P("wsh", None),
        P("wsh"),
        P("wsh", None),
        P("wsh"),
        P("wsh"),
        P("wsh"),
        P(None, "wsh", None),
        P("wsh"),
        P(None, "wsh", None),
        P("wsh"),
        P("wsh"),
        P("wsh"),
    )
    out_specs = (
        P(None, "wsh", "ctx", None),
        P(None, "wsh", "ctx", None),
        P("wsh", None),
        P("wsh"),
        P("wsh", None),
        P("wsh", None),
        P("wsh"),
        P(None, "wsh"),
        P("wsh", None),
        P("wsh"),
        P("wsh", None),
        P("wsh"),
        P("wsh", None),
        P("wsh"),
        P("wsh", None),
        P("wsh"),
        P("wsh"),
        P("wsh"),
        P(None, "wsh", None),
        P("wsh"),
        P(None, "wsh", None),
        P("wsh"),
        P("wsh"),
        P("wsh"),
    )
    return jax.shard_map(
        on_device, mesh=mesh, in_specs=in_specs, out_specs=out_specs, check_vma=False
    )
```

```python
import functools
import types

import jax
import jax.numpy as jnp
from jax import lax
from jax.experimental import pallas as pl
from jax.experimental.pallas import tpu as pltpu
from jax.sharding import PartitionSpec as P

HEADS = 6
HEAD_DIM = 64
KERNEL = 9
GROUPS = 2


TILE = 256
NEG = -1000000000.0
LANES = 128
HEADS_HERE = HEADS // 2


def rows_nt(left, right):
    return lax.dot_general(
        left, right, (((1,), (1,)), ((), ())), preferred_element_type=jnp.float32
    )


def lane_half(block, upper):
    lane = lax.broadcasted_iota(jnp.int32, block.shape, 1)
    keep = lane >= HEAD_DIM if upper else lane < HEAD_DIM
    return jnp.where(keep, block, jnp.zeros_like(block))


def same_document(segk_ref, segq_ref, j):
    cols = pl.ds(pl.multiple_of(j * TILE, TILE), TILE)
    row = segk_ref[0:1, cols]
    column = jnp.broadcast_to(row, (LANES, TILE)).T
    wide = jnp.concatenate([column] * (TILE // LANES), axis=1)
    return wide == segq_ref[0:1, :]


def load_queries(q_ref, qm_ref):
    scale = jnp.asarray(HEAD_DIM ** (-0.5), q_ref.dtype)
    first = q_ref[:, 0:LANES] * scale
    qm_ref[0] = lane_half(first, False)
    qm_ref[1] = lane_half(first, True)
    qm_ref[2] = lane_half(q_ref[:, LANES : 2 * LANES] * scale, False)


KEY_GROUP = (0, 0, 1)
VALUE_GROUP = (2, 2, 1)


def lane_group(group):
    return slice(group * LANES, (group + 1) * LANES)


def attend_kernel(bounds, q_ref, kv_ref, segk_ref, segq_ref, out_ref, outt_ref, lse_ref,
                  qm_ref, m_ref, l_ref, acc_ref):
    tile = pl.program_id(0)
    load_queries(q_ref, qm_ref)
    m_ref[...] = jnp.full_like(m_ref, -jnp.inf)
    l_ref[...] = jnp.zeros_like(l_ref)
    acc_ref[...] = jnp.zeros_like(acc_ref)

    def step(j, carry):
        rows = pl.ds(pl.multiple_of(j * TILE, TILE), TILE)
        same = same_document(segk_ref, segq_ref, j)
        values_t = kv_ref[rows, LANES : 3 * LANES].T
        value_rows = (2 * HEAD_DIM, 3 * HEAD_DIM, HEAD_DIM)
        raw = [
            rows_nt(kv_ref[rows, lane_group(KEY_GROUP[head])], qm_ref[head])
            for head in range(HEADS_HERE)
        ]
        highs, alphas = [], []
        for head in range(HEADS_HERE):
            scores = jnp.where(same, raw[head], NEG)
            old = m_ref[head : head + 1, :]
            top = jnp.maximum(old, jnp.max(scores, axis=0, keepdims=True))
            expo = jnp.exp(scores - top)
            alpha = jnp.exp(old - top)
            m_ref[head : head + 1, :] = top
            l_ref[head : head + 1, :] = l_ref[head : head + 1, :] * alpha + jnp.sum(
                expo, axis=0, keepdims=True
            )
            high = expo.astype(jnp.bfloat16)
            highs.append(high)
            alphas.append(alpha)
        for head in range(HEADS_HERE):
            span = slice(head * HEAD_DIM, (head + 1) * HEAD_DIM)
            vals = values_t[value_rows[head] : value_rows[head] + HEAD_DIM, :]
            acc_ref[span, :] = acc_ref[span, :] * alphas[head] + jnp.dot(
                vals, highs[head], preferred_element_type=jnp.float32
            )
        return carry

    lax.fori_loop(bounds[0, tile], bounds[1, tile], step, 0)
    lse_ref[...] = m_ref[...] + jnp.log(l_ref[...])
    used = HEADS_HERE * HEAD_DIM
    for head in range(HEADS_HERE):
        span = slice(head * HEAD_DIM, (head + 1) * HEAD_DIM)
        inv = 1.0 / l_ref[head : head + 1, :]
        acc_ref[span, :] = acc_ref[span, :] * inv
    outt_ref[...] = acc_ref[...]
    out_ref[...] = acc_ref[...].T.astype(jnp.bfloat16)


def attend(bounds, queries, window, seg_keys, seg_queries):
    rows, wide = queries.shape
    span, width = window.shape
    return pl.pallas_call(
        attend_kernel,
        grid_spec=pltpu.PrefetchScalarGridSpec(
            num_scalar_prefetch=1,
            grid=(rows // TILE,),
            in_specs=[
                pl.BlockSpec((TILE, wide), lambda i, b: (i, 0)),
                pl.BlockSpec((span, width), lambda i, b: (0, 0)),
                pl.BlockSpec((8, span), lambda i, b: (0, 0)),
                pl.BlockSpec((8, TILE), lambda i, b: (0, i)),
            ],
            out_specs=[
                pl.BlockSpec((TILE, wide), lambda i, b: (i, 0)),
                pl.BlockSpec((wide, TILE), lambda i, b: (0, i)),
                pl.BlockSpec((8, TILE), lambda i, b: (0, i)),
            ],
            scratch_shapes=[
                pltpu.VMEM((HEADS_HERE, TILE, LANES), jnp.bfloat16),
                pltpu.VMEM((8, TILE), jnp.float32),
                pltpu.VMEM((8, TILE), jnp.float32),
                pltpu.VMEM((wide, TILE), jnp.float32),
            ],
        ),
        out_shape=[
            jax.ShapeDtypeStruct((rows, wide), jnp.bfloat16),
            jax.ShapeDtypeStruct((wide, rows), jnp.float32),
            jax.ShapeDtypeStruct((8, rows), jnp.float32),
        ],
        compiler_params=pltpu.CompilerParams(vmem_limit_bytes=40 * 2**20),
        name="attend",
    )(bounds, queries, window, seg_keys, seg_queries)


def attend_back_kernel(bounds, q_ref, kv_ref, segk_ref, segq_ref, grad_ref, outt_ref, lse_ref,
                       dq_ref, dkv_ref, qm_ref, gm_ref, delta_ref, dq_acc, dkv_acc):
    tile = pl.program_id(0)

    @pl.when(tile == 0)
    def _():
        dkv_acc[...] = jnp.zeros_like(dkv_acc)

    load_queries(q_ref, qm_ref)
    gm_ref[0] = lane_half(grad_ref[:, 0:LANES], False)
    gm_ref[1] = lane_half(grad_ref[:, 0:LANES], True)
    gm_ref[2] = lane_half(grad_ref[:, LANES : 2 * LANES], True)
    grads_t = grad_ref[...].astype(jnp.float32).T
    grad_rows = (0, HEAD_DIM, 3 * HEAD_DIM)
    for head in range(HEADS_HERE):
        span = slice(head * HEAD_DIM, (head + 1) * HEAD_DIM)
        delta_ref[head : head + 1, :] = jnp.sum(
            grads_t[grad_rows[head] : grad_rows[head] + HEAD_DIM, :] * outt_ref[span, :],
            axis=0, keepdims=True,
        )
    dq_acc[...] = jnp.zeros_like(dq_acc)

    def step(j, carry):
        rows = pl.ds(pl.multiple_of(j * TILE, TILE), TILE)
        same = same_document(segk_ref, segq_ref, j)
        keys_t = kv_ref[rows, 0 : 2 * LANES].T
        sums = [dkv_acc[rows, lane_group(g)] for g in range(3)]
        raw = [
            rows_nt(kv_ref[rows, lane_group(KEY_GROUP[head])], qm_ref[head])
            for head in range(HEADS_HERE)
        ]
        draw = [
            rows_nt(kv_ref[rows, lane_group(VALUE_GROUP[head])], gm_ref[head])
            for head in range(HEADS_HERE)
        ]
        ps, dss = [], []
        for head in range(HEADS_HERE):
            probs = jnp.where(same, jnp.exp(raw[head] - lse_ref[head : head + 1, :]), 0.0)
            dss.append((probs * (draw[head] - delta_ref[head : head + 1, :])).astype(jnp.bfloat16))
            ps.append(probs.astype(jnp.bfloat16))
        for head in range(HEADS_HERE):
            span = slice(head * HEAD_DIM, (head + 1) * HEAD_DIM)
            dq_acc[span, :] += jnp.dot(
                keys_t[span, :], dss[head], preferred_element_type=jnp.float32
            )
            sums[KEY_GROUP[head]] += jnp.dot(
                dss[head], qm_ref[head], preferred_element_type=jnp.float32
            )
            sums[VALUE_GROUP[head]] += jnp.dot(
                ps[head], gm_ref[head], preferred_element_type=jnp.float32
            )
        for g in range(3):
            dkv_acc[rows, lane_group(g)] = sums[g]
        return carry

    lax.fori_loop(bounds[0, tile], bounds[1, tile], step, 0)
    dq_ref[...] = (dq_acc[...].T * HEAD_DIM ** (-0.5)).astype(dq_ref.dtype)

    @pl.when(tile == pl.num_programs(0) - 1)
    def _():
        dkv_ref[...] = dkv_acc[...].astype(dkv_ref.dtype)


def attend_back(bounds, queries, window, seg_keys, seg_queries, grads, outt, lse):
    rows, wide = queries.shape
    span, width = window.shape
    return pl.pallas_call(
        attend_back_kernel,
        grid_spec=pltpu.PrefetchScalarGridSpec(
            num_scalar_prefetch=1,
            grid=(rows // TILE,),
            in_specs=[
                pl.BlockSpec((TILE, wide), lambda i, b: (i, 0)),
                pl.BlockSpec((span, width), lambda i, b: (0, 0)),
                pl.BlockSpec((8, span), lambda i, b: (0, 0)),
                pl.BlockSpec((8, TILE), lambda i, b: (0, i)),
                pl.BlockSpec((TILE, wide), lambda i, b: (i, 0)),
                pl.BlockSpec((wide, TILE), lambda i, b: (0, i)),
                pl.BlockSpec((8, TILE), lambda i, b: (0, i)),
            ],
            out_specs=[
                pl.BlockSpec((TILE, wide), lambda i, b: (i, 0)),
                pl.BlockSpec((span, width), lambda i, b: (0, 0)),
            ],
            scratch_shapes=[
                pltpu.VMEM((HEADS_HERE, TILE, LANES), jnp.bfloat16),
                pltpu.VMEM((HEADS_HERE, TILE, LANES), jnp.bfloat16),
                pltpu.VMEM((8, TILE), jnp.float32),
                pltpu.VMEM((wide, TILE), jnp.float32),
                pltpu.VMEM((span, width), jnp.float32),
            ],
        ),
        out_shape=[
            jax.ShapeDtypeStruct((rows, wide), jnp.bfloat16),
            jax.ShapeDtypeStruct((span, width), jnp.bfloat16),
        ],
        compiler_params=pltpu.CompilerParams(vmem_limit_bytes=48 * 2**20),
        name="attend_back",
    )(bounds, queries, window, seg_keys, seg_queries, grads, outt, lse)


def rolled(part):
    return jnp.concatenate([part[..., HEAD_DIM:], part[..., :HEAD_DIM]], axis=-1)


def joined_halves(lower, upper):
    return jnp.concatenate([lower[..., :HEAD_DIM], upper[..., HEAD_DIM:]], axis=-1)


def lanes_of(values):
    return [values[..., lane_group(g)] for g in range(3)]


def parts_of_queries(queries, upper):
    one, two, three = lanes_of(queries)
    swapped = rolled(two)
    first, second = (swapped, two) if upper else (two, swapped)
    return jnp.stack(
        [jnp.concatenate([one, first], axis=-1), jnp.concatenate([three, second], axis=-1)], axis=1
    ).reshape(TEAM, queries.shape[1], 2 * LANES)


def parts_of_keys(keys, values):
    k = lanes_of(keys)
    v = lanes_of(values)
    low = jnp.concatenate([k[0], joined_halves(k[1], rolled(v[1])), v[0]], axis=-1)
    high = jnp.concatenate([k[2], joined_halves(rolled(k[1]), v[1]), v[2]], axis=-1)
    return jnp.stack([low, high], axis=1).reshape(TEAM, keys.shape[1], 3 * LANES)


def natural_rows(parts):
    pairs = parts.reshape(TEAM // 2, 2, parts.shape[1], 2 * LANES)
    low, high = pairs[:, 0], pairs[:, 1]
    middle = joined_halves(low[..., LANES:], rolled(high[..., LANES:]))
    return jnp.concatenate([low[..., :LANES], middle, high[..., :LANES]], axis=-1)


def natural_keys(parts):
    pairs = parts.reshape(TEAM // 2, 2, parts.shape[1], 3 * LANES)
    low, high = lanes_of(pairs[:, 0]), lanes_of(pairs[:, 1])
    keys = jnp.concatenate([low[0], joined_halves(low[1], rolled(high[1])), high[0]], axis=-1)
    values = jnp.concatenate([low[2], joined_halves(rolled(low[1]), high[1]), high[2]], axis=-1)
    return keys, values


TEAM = 4


def flip(index, step):
    return index + step * (1 - 2 * lax.rem(lax.div(index, step), 2))


def mate(rank, offset):
    if offset % 2:
        rank = flip(rank, 1)
    if offset // 2:
        rank = flip(rank, 2)
    return rank


def greet(peers):
    barrier = pltpu.get_barrier_semaphore()
    for peer in peers:
        pl.semaphore_signal(
            barrier, inc=1, device_id=peer, device_id_type=pl.DeviceIdType.MESH
        )
    pl.semaphore_wait(barrier, len(peers))


def remote(src, dst, send, recv, peer):
    return pltpu.make_async_remote_copy(
        src_ref=src,
        dst_ref=dst,
        send_sem=send,
        recv_sem=recv,
        device_id=peer,
        device_id_type=pl.DeviceIdType.MESH,
    )


RIM = 16
SMALL_ROWS = 128
ROW_OUTPUT_B, ROW_GAIN1, ROW_SHIFT1, ROW_OUTER_B, ROW_GAIN2, ROW_SHIFT2 = range(9, 15)
ROW_INNER_B = 15
ROW_QUERY_B, ROW_VALUE_B, ROW_POINT_B, ROW_CONV_B = range(19, 23)
ROW_KERNEL_B = 24
ROW_KERNEL_W = 48
TAP_ROWS = 8 * KERNEL


def dot(left, right):
    return jnp.dot(left, right, preferred_element_type=jnp.float32)


def dot_tn(left, right):
    return lax.dot_general(
        left, right, (((0,), (0,)), ((), ())), preferred_element_type=jnp.float32
    )


def half_turn(block):
    return pltpu.roll(block, HEAD_DIM, axis=1)


def mixed_lanes(lower, upper):
    lane = lax.broadcasted_iota(jnp.int32, lower.shape, 1)
    return jnp.where(lane < HEAD_DIM, lower, upper)


def small_row(small_ref, row):
    return small_ref[0, row : row + 1, :].astype(jnp.float32), small_ref[
        1, row : row + 1, :
    ].astype(jnp.float32)


def row_sum(small_ref, row):
    one, two = small_row(small_ref, row)
    return one + two


def row_join(small_ref, row):
    return jnp.concatenate(small_row(small_ref, row), axis=1)


def rows_of(ref, base, count):
    view = pl.ds(pl.multiple_of(base, 16), count)
    return ref.at[:, view, :] if len(ref.shape) == 3 else ref.at[view, :]


def front_kernel(count, *refs):
    x_ref, seg_ref, mask_ref = refs[:3]
    shards = refs[3 : 3 + count]
    rest = refs[3 + count :]
    fulls = rest[:count]
    (win_ref, qteam_ref, queries_ref, xrim_ref, depth_ref, spans_ref, mixed_ref, kern_ref,
     ext_ref, conv_ref) = rest[count : count + 10]
    (kv_part, q_part, seg_col, halo_low, halo_high, spread_ref, taps_ref, wide_ref,
     send_y, recv_y, send_c, recv_c, local, send_h, recv_h, send_kv, recv_kv, send_q, recv_q,
     send_l, recv_l, send_r, recv_r) = rest[count + 10 :]
    key_ref, value_ref, query_ref, small2d, point_ref, convw_ref = fulls[:6]
    me, side = lax.axis_index("ctx"), lax.axis_index("wsh")
    size = lax.axis_size("ctx")
    core = lax.rem(me, 2)
    rank = lax.rem(me, TEAM)
    base = me - rank
    team = lax.div(me, TEAM)
    teams = size // TEAM
    right, left = lax.rem(me + TEAM, size), lax.rem(me + size - TEAM, size)
    after, prior = lax.rem(me + 1, size), lax.rem(me + size - 1, size)
    twin, across = {"ctx": flip(me, 1)}, {"wsh": 1 - side}
    seqs, block, model = x_ref.shape
    halo = (TEAM - 1) * block
    width = HEADS * HEAD_DIM
    greet(
        [{"ctx": base + mate(rank, o)} for o in range(1, TEAM)]
        + [across, {"ctx": right}, {"ctx": left}, {"ctx": after}, {"ctx": prior}]
    )

    to_y, passed, own = [], [], []
    for i in range(count):
        rows = shards[i].shape[-2]
        to_y.append(
            remote(
                rows_of(shards[i], core * (rows // 2), rows // 2),
                rows_of(fulls[i], side * rows + core * (rows // 2), rows // 2),
                send_y.at[i], recv_y.at[i], across,
            )
        )
        came = rows_of(fulls[i], (1 - side) * rows + core * (rows // 2), rows // 2)
        passed.append(remote(came, came, send_c.at[i], recv_c.at[i], twin))
        own.append(
            pltpu.make_async_copy(shards[i], rows_of(fulls[i], side * rows, rows), local.at[i])
        )
    urgent = 4
    for i in range(urgent):
        to_y[i].start()
    for i in range(urgent):
        own[i].start()
    to_after = remote(x_ref.at[:, pl.ds(block - RIM, RIM), :], halo_low, send_h.at[0],
                      recv_h.at[0], {"ctx": after})
    to_prior = remote(x_ref.at[:, pl.ds(0, RIM), :], halo_high, send_h.at[1], recv_h.at[1],
                      {"ctx": prior})
    pl.when(me < size - 1)(to_after.start)
    pl.when(me > 0)(to_prior.start)
    for i in range(urgent, count):
        to_y[i].start()
        own[i].start()

    @pl.when(me == 0)
    def _():
        halo_low[...] = jnp.zeros_like(halo_low)

    @pl.when(me == size - 1)
    def _():
        halo_high[...] = jnp.zeros_like(halo_high)

    for s in range(seqs):
        seg_col[s] = jnp.broadcast_to(seg_ref[s, 0:1, :], (LANES, seg_ref.shape[2])).T
        for g in range(model // LANES):
            xrim_ref[s, g, pl.ds(RIM, block), :] = x_ref[s, :, lane_group(g)].astype(jnp.float32)
    for j in range(KERNEL):
        row = lax.broadcasted_iota(jnp.int32, (2 * LANES, width), 0)
        col = lax.broadcasted_iota(jnp.int32, (2 * LANES, width), 1)
        row = jnp.where(row >= LANES, row - LANES, row)
        spread_ref[j] = jnp.where(row == 8 * j + col // HEAD_DIM, 1.0, 0.0).astype(jnp.bfloat16)

    def arrive(i):
        to_y[i].wait_recv()
        passed[i].start()

    def settle(i):
        own[i].wait()
        passed[i].wait_recv()

    for i in range(urgent):
        arrive(i)
    for i in range(urgent):
        settle(i)
    small_ref = taps_ref
    for w in range(2):
        small_ref[w] = small2d[pl.ds(w * SMALL_ROWS, SMALL_ROWS), :].astype(jnp.float32)
    value_bias = row_sum(small_ref, ROW_VALUE_B)
    query_bias = row_sum(small_ref, ROW_QUERY_B)

    def place(r):
        return win_ref.at[pl.ds(pl.multiple_of(halo + r * block, 16), block), :]

    def kv_copy(r):
        return (
            pltpu.make_async_copy(kv_part.at[r], place(rank), recv_kv.at[rank]),
            remote(kv_part.at[r], place(rank), send_kv.at[r], recv_kv.at[rank], {"ctx": base + r}),
        )

    def q_copy(r):
        return (
            pltpu.make_async_copy(q_part.at[r], qteam_ref.at[rank], recv_q.at[rank]),
            remote(q_part.at[r], qteam_ref.at[rank], send_q.at[r], recv_q.at[rank],
                   {"ctx": base + r}),
        )

    def begin(pair, r):
        pl.when(rank == r)(pair[0].start)
        pl.when(rank != r)(pair[1].start)

    for s in range(seqs):
        rows = x_ref[s]
        keys = dot(rows, key_ref[...])
        values = dot(rows, value_ref[...]) + value_bias
        k = [keys[:, lane_group(g)] for g in range(3)]
        v = [values[:, lane_group(g)] for g in range(3)]
        for half, groups in enumerate((
            (k[0], mixed_lanes(k[1], half_turn(v[1])), v[0]),
            (k[2], mixed_lanes(half_turn(k[1]), v[1]), v[2]),
        )):
            for g in range(3):
                kv_part[2 * s + half, :, lane_group(g)] = groups[g].astype(jnp.bfloat16)
        for half in range(2):
            begin(kv_copy(2 * s + half), 2 * s + half)
    for s in range(seqs):
        queries = dot(x_ref[s], query_ref[...]) + query_bias
        queries_ref[s] = queries.astype(jnp.bfloat16)
        q = [queries[:, lane_group(g)] for g in range(3)]
        for half, groups in enumerate(((q[0], q[1]), (q[2], half_turn(q[1])))):
            for g in range(2):
                q_part[2 * s + half, :, lane_group(g)] = groups[g].astype(jnp.bfloat16)
        for half in range(2):
            begin(q_copy(2 * s + half), 2 * s + half)

    def onward(r):
        to_right = remote(
            place(r),
            win_ref.at[pl.ds(pl.multiple_of(lax.rem(r + TEAM - 1, TEAM) * block, 16), block), :],
            send_r.at[r], recv_r.at[r], {"ctx": right},
        )
        to_left = remote(
            place(r),
            win_ref.at[
                pl.ds(pl.multiple_of(halo + TEAM * block + lax.rem(r, TEAM - 1) * block, 16), block), :
            ],
            send_l.at[r], recv_l.at[r], {"ctx": left},
        )
        return to_right, to_left

    def arrived(ref, sem, shape_ref):
        return pltpu.make_async_copy(shape_ref, ref, sem)

    def relay(o):
        r = mate(rank, o)
        if o == 0:
            pltpu.make_async_copy(kv_part.at[r], place(r), recv_kv.at[r]).wait()
        else:
            remote(kv_part.at[r], place(r), send_kv.at[r], recv_kv.at[r],
                   {"ctx": base + r}).wait_recv()
        to_right, to_left = onward(r)
        pl.when((r >= 1) & (team < teams - 1))(to_right.start)
        pl.when((r <= TEAM - 2) & (team > 0))(to_left.start)

    relay(0)
    relay(1)

    pl.when(me > 0)(to_after.wait_recv)
    pl.when(me < size - 1)(to_prior.wait_recv)
    for s in range(seqs):
        for g in range(model // LANES):
            xrim_ref[s, g, pl.ds(0, RIM), :] = halo_low[s, :, lane_group(g)].astype(jnp.float32)
            xrim_ref[s, g, pl.ds(RIM + block, RIM), :] = halo_high[s, :, lane_group(g)].astype(
                jnp.float32
            )
    strip = 32
    lead = RIM - KERNEL // 2

    def taps_row(j, g):
        return small_ref[g // 3, j : j + 1, lane_group(g % 3)]

    def depth_strip(c, s):
        start = c * strip
        here = seg_col[s, pl.ds(RIM + start, strip), :]
        sums = [jnp.zeros((strip, LANES), jnp.float32) for _ in range(model // LANES)]
        for j in range(KERNEL):
            same = seg_col[s, pl.ds(lead + j + start, strip), :] == here
            for g in range(model // LANES):
                near = xrim_ref[s, g, pl.ds(lead + j + start, strip), :]
                sums[g] = sums[g] + jnp.where(same, near, 0.0) * taps_row(j, g)
        for g in range(model // LANES):
            depth_ref[s, pl.ds(pl.multiple_of(start, strip), strip), lane_group(g)] = sums[
                g
            ].astype(jnp.bfloat16)
        return s

    for s in range(seqs):
        lax.fori_loop(0, block // strip, depth_strip, s)
    relay(2)
    relay(3)
    for i in range(urgent, 6):
        arrive(i)
    for i in range(urgent, 6):
        settle(i)
    point_bias = row_sum(small_ref, ROW_POINT_B)
    conv_bias = row_sum(small_ref, ROW_CONV_B)
    kernel_w = (
        small_ref[0, ROW_KERNEL_W : ROW_KERNEL_W + TAP_ROWS, :]
        + small_ref[1, ROW_KERNEL_W : ROW_KERNEL_W + TAP_ROWS, :]
    ).astype(jnp.bfloat16)
    both_b = (
        small_ref[0, ROW_KERNEL_B : ROW_KERNEL_B + 24, :]
        + small_ref[1, ROW_KERNEL_B : ROW_KERNEL_B + 24, :]
    )
    kernel_b = jnp.concatenate([both_b[:, lane_group(g)] for g in range(3)], axis=0)
    kernel_b = jnp.concatenate([kernel_b] * (block // LANES), axis=1)
    for s in range(seqs):
        spans = dot(depth_ref[s], point_ref[...]) + point_bias
        spans_ref[s] = spans
        mixed = (spans * queries_ref[s].astype(jnp.float32)).astype(jnp.bfloat16)
        mixed_ref[s] = mixed
        logits = rows_nt(kernel_w, mixed) + kernel_b
        cut = [logits[8 * j : 8 * j + 8, :] for j in range(KERNEL)]
        top = functools.reduce(jnp.maximum, cut)
        expo = [jnp.exp(part - top) for part in cut]
        inverse = 1.0 / sum(expo)
        for j in range(KERNEL):
            kern = expo[j] * inverse
            kern_ref[s, 8 * j : 8 * j + 8, :] = kern
            wide_ref[8 * j : 8 * j + 8, :] = kern * mask_ref[s, j : j + 1, :]
        wide_ref[TAP_ROWS:, :] = jnp.zeros((LANES - TAP_ROWS, block), jnp.float32)
        tall = wide_ref[...].T
        high = tall.astype(jnp.bfloat16)
        low = (tall - high.astype(jnp.float32)).astype(jnp.bfloat16)
        both = jnp.concatenate([high, low], axis=1)
        for g in range(3):
            row_ext = [xrim_ref[s, k] for k in range(model // LANES)]
        ext = dot(
            jnp.concatenate([part.astype(jnp.bfloat16) for part in row_ext], axis=1),
            convw_ref[...],
        ) + conv_bias
        for g in range(3):
            ext_ref[s, g] = ext[:, lane_group(g)]
        chunk = 128
        for c in range(block // chunk):
            sums = [jnp.zeros((chunk, LANES), jnp.float32) for _ in range(3)]
            for j in range(KERNEL):
                weight = dot(both[c * chunk : (c + 1) * chunk, :], spread_ref[j])
                for g in range(3):
                    near = ext_ref[s, g, pl.ds(lead + j + c * chunk, chunk), :]
                    sums[g] = sums[g] + weight[:, lane_group(g)] * near
            for g in range(3):
                conv_ref[s, pl.ds(c * chunk, chunk), lane_group(g)] = sums[g].astype(jnp.bfloat16)

    for i in range(6, count):
        arrive(i)
    for i in range(6, count):
        settle(i)
    for r in range(TEAM):
        pl.when(rank != r)(kv_copy(r)[1].wait_send)
        pl.when(rank != r)(q_copy(r)[1].wait_send)
    for o in range(TEAM):
        r = mate(rank, o)
        if o == 0:
            pltpu.make_async_copy(q_part.at[r], qteam_ref.at[r], recv_q.at[r]).wait()
        else:
            remote(q_part.at[r], qteam_ref.at[r], send_q.at[r], recv_q.at[r],
                   {"ctx": base + r}).wait_recv()
    for r in range(TEAM):
        to_right, to_left = onward(jnp.int32(r))
        if r >= 1:
            pl.when(team < teams - 1)(to_right.wait_send)
            pl.when(team > 0)(to_right.wait_recv)
        if r <= TEAM - 2:
            pl.when(team > 0)(to_left.wait_send)
            pl.when(team < teams - 1)(to_left.wait_recv)
    for i in range(count):
        to_y[i].wait_send()
        passed[i].wait_send()
    pl.when(me < size - 1)(to_after.wait_send)
    pl.when(me > 0)(to_prior.wait_send)


def front(hidden, seg_rim, tap_mask, shards):
    seqs, block, model = hidden.shape
    count = len(shards)
    width = HEADS * HEAD_DIM
    wide = block + 2 * RIM
    fulls = [
        jax.ShapeDtypeStruct(s.shape[:-2] + (2 * s.shape[-2], s.shape[-1]), s.dtype) for s in shards
    ]
    vmem = pl.BlockSpec(memory_space=pltpu.VMEM)
    anywhere = pl.BlockSpec(memory_space=pl.ANY)
    low, full = jnp.bfloat16, jnp.float32
    outs = [
        jax.ShapeDtypeStruct(((3 * TEAM - 2) * block, width), low),
        jax.ShapeDtypeStruct((TEAM, block, 2 * LANES), low),
        jax.ShapeDtypeStruct((seqs, block, width), low),
        jax.ShapeDtypeStruct((seqs, model // LANES, wide, LANES), full),
        jax.ShapeDtypeStruct((seqs, block, model), low),
        jax.ShapeDtypeStruct((seqs, block, width), full),
        jax.ShapeDtypeStruct((seqs, block, width), low),
        jax.ShapeDtypeStruct((seqs, TAP_ROWS, block), full),
        jax.ShapeDtypeStruct((seqs, 3, wide, LANES), full),
        jax.ShapeDtypeStruct((seqs, block, width), low),
    ]
    dma = pltpu.SemaphoreType.DMA
    return pl.pallas_call(
        functools.partial(front_kernel, count),
        out_shape=fulls + outs,
        in_specs=[vmem] * 3 + [anywhere] * count,
        out_specs=[vmem] * count + [anywhere] * 2 + [vmem] * 8,
        scratch_shapes=[
            pltpu.VMEM((TEAM, block, width), low),
            pltpu.VMEM((TEAM, block, 2 * LANES), low),
            pltpu.VMEM((seqs, seg_rim.shape[2], LANES), full),
            pltpu.VMEM((seqs, RIM, model), low),
            pltpu.VMEM((seqs, RIM, model), low),
            pltpu.VMEM((KERNEL, 2 * LANES, width), low),
            pltpu.VMEM((2, SMALL_ROWS, 384), full),
            pltpu.VMEM((LANES, block), full),
            dma((count,)), dma((count,)), dma((count,)), dma((count,)), dma((count,)),
            dma((2,)), dma((2,)),
            dma((TEAM,)), dma((TEAM,)), dma((TEAM,)), dma((TEAM,)),
            dma((TEAM,)), dma((TEAM,)), dma((TEAM,)), dma((TEAM,)),
        ],
        compiler_params=pltpu.CompilerParams(
            collective_id=0, has_side_effects=True, vmem_limit_bytes=56 * 2**20
        ),
        name="front",
    )(hidden, seg_rim, tap_mask, *shards)


PACK_A = 768
PACK_B = 1280
SMALL_AT = 1152


def chips_of(me, size):
    core = lax.rem(me, 2)
    count = size // 2
    index = lax.div(me, 2)
    return index, count, lambda other: other * 2 + core


def pair_of(me, size):
    index = lax.rem(lax.div(me, 2), 2)
    return index, 2, lambda other: flip(me, 2)


def column_of(me, size):
    index = lax.div(me, TEAM)
    rest = lax.rem(me, TEAM)
    return index, size // TEAM, lambda other: other * TEAM + rest


def part_rows(base, count):
    return pl.ds(pl.multiple_of(base, 16), count)


def others(index, count):
    return [lax.rem(index + o, count) for o in range(1, count)]


def scatter_copies(stage, me, size, staged, came, send, recv):
    index, count, device = stage(me, size)
    piece = staged.shape[0] // count
    return [
        remote(staged.at[part_rows(other * piece, piece), :], came.at[index], send.at[other],
               recv.at[index], {"ctx": device(other)})
        for other in others(index, count)
    ]


def scatter_wait(stage, me, size, staged, came, send, recv):
    index, count, device = stage(me, size)
    piece = staged.shape[0] // count
    for other in others(index, count):
        remote(staged.at[part_rows(index * piece, piece), :], came.at[other], send.at[index],
               recv.at[other], {"ctx": device(other)}).wait_recv()


def share_copies(stage, me, size, fin, base, piece, send, recv):
    index, count, device = stage(me, size)
    view = fin.at[part_rows(base + index * piece, piece), :]
    return [
        remote(view, view, send.at[other], recv.at[index], {"ctx": device(other)})
        for other in others(index, count)
    ]


def share_wait(stage, me, size, fin, base, piece, send, recv):
    index, count, device = stage(me, size)
    for other in others(index, count):
        view = fin.at[part_rows(base + other * piece, piece), :]
        remote(view, view, send.at[index], recv.at[other], {"ctx": device(other)}).wait_recv()


def in_chunks(rows, body):
    chunk = max(c for c in range(16, 241, 16) if rows % c == 0)

    def step(i, carry):
        body(pl.multiple_of(i * chunk, 16), chunk)
        return carry

    lax.fori_loop(0, rows // chunk, step, 0)


def wide(value):
    return value.astype(jnp.float32)


def back_kernel(names, a_names, b_names, loaded, *refs):
    count_a, count_b = len(a_names), len(b_names)
    r = types.SimpleNamespace(**dict(zip(names, refs)))
    late = refs[len(names) :]
    block_a = types.SimpleNamespace(**dict(zip(a_names, late[:count_a])))
    block_b = types.SimpleNamespace(**dict(zip(b_names, late[count_a : count_a + count_b])))
    fetch_refs = late[count_a + count_b :]
    v = types.SimpleNamespace(**dict(zip(loaded, fetch_refs[len(loaded) :])))
    me, side = lax.axis_index("ctx"), lax.axis_index("wsh")
    size = lax.axis_size("ctx")
    core = lax.rem(me, 2)
    rank = lax.rem(me, TEAM)
    chip = lax.div(rank, 2)
    base = me - rank
    team = lax.div(me, TEAM)
    teams = size // TEAM
    twin, across = {"ctx": flip(me, 1)}, {"wsh": 1 - side}
    right, left = lax.rem(me + TEAM, size), lax.rem(me + size - TEAM, size)
    after, prior = lax.rem(me + 1, size), lax.rem(me + size - 1, size)
    seqs, block, model = v.x.shape
    width = HEADS * HEAD_DIM
    halo = (TEAM - 1) * block
    groups = model // LANES
    low = jnp.bfloat16
    index, count, device = chips_of(me, size)
    greet(
        [twin, across, {"ctx": base + mate(rank, 3)}, {"ctx": after}, {"ctx": prior}]
        + [{"ctx": device(other)} for other in others(index, count)]
    )

    def block_of(k):
        return pl.ds(pl.multiple_of(k * block, 16), block)

    def halo_left(c):
        return remote(r.window.at[block_of(2 * TEAM - 1 + c), :], r.from_left.at[block_of(c), :],
                      r.send_l.at[c], r.recv_l.at[c], {"ctx": right})

    def halo_right(c):
        return remote(r.window.at[block_of(c), :], r.from_right.at[block_of(c + 1), :],
                      r.send_r.at[c], r.recv_r.at[c], {"ctx": left})

    for k in range(TEAM - 1):
        to_right = halo_left(chip * k + (1 - chip) * (TEAM - 2 - k))
        to_left = halo_right(chip * k + (1 - chip) * ((k + 1) % (TEAM - 1)))
        pl.when(team < teams - 1)(to_right.start)
        pl.when(team > 0)(to_left.start)

    fetched = types.SimpleNamespace()
    for k, name in enumerate(loaded):
        copy = pltpu.make_async_copy(fetch_refs[k], fetch_refs[len(loaded) + k], r.load.at[k])
        setattr(fetched, name, copy)
    center = pltpu.make_async_copy(r.window.at[pl.ds(halo, TEAM * block), :], r.mine,
                                   r.load.at[len(loaded)])
    fetched.keep.start()
    fetched.came.start()
    center.start()

    def q_copy(o):
        other = mate(rank, o)
        return remote(r.dq.at[other], r.q_parts.at[rank], r.send_q.at[o], r.recv_q.at[o],
                      {"ctx": base + other})

    own_q = pltpu.make_async_copy(r.dq.at[rank], r.q_parts.at[rank], r.recv_q.at[0])
    for o in (3, 2, 1):
        q_copy(o).start()
    own_q.start()
    for name in loaded[2:]:
        getattr(fetched, name).start()

    def have(*copies):
        for copy in copies:
            copy.wait()

    half_ff = v.keep.shape[1]
    pair_index, _, _ = pair_of(me, size)
    have(fetched.keep, fetched.came)

    def stage_across(at, n):
        rows = part_rows(at, n)
        r.ff_send[rows, :] = (v.keep[1 - side, rows, :] + wide(v.came[1 - side, rows, :])).astype(low)
        v.keep[side, rows, :] = v.keep[side, rows, :] + wide(v.came[side, rows, :])

    in_chunks(half_ff, stage_across)
    ff_across = remote(r.ff_send, r.ff_came, r.send_p.at[0], r.recv_p.at[0], across)
    ff_across.start()

    small = r.sums
    small[...] = jnp.zeros_like(small)
    for j in range(KERNEL):
        row = lax.broadcasted_iota(jnp.int32, (2 * LANES, width), 0)
        col = lax.broadcasted_iota(jnp.int32, (2 * LANES, width), 1)
        row = jnp.where(row >= LANES, row - LANES, row)
        r.spread[j] = jnp.where(row == 8 * j + col // HEAD_DIM, 1.0, 0.0).astype(low)

    zero_block = jnp.zeros((block, width), low)
    r.from_left[pl.ds((TEAM - 1) * block, block), :] = zero_block
    r.from_right[0:block, :] = zero_block

    @pl.when(team == 0)
    def _():
        for k in range(TEAM - 1):
            r.from_left[pl.ds(k * block, block), :] = zero_block

    @pl.when(team == teams - 1)
    def _():
        for k in range(1, TEAM):
            r.from_right[pl.ds(k * block, block), :] = zero_block

    @pl.when(me == 0)
    def _():
        r.dd_low[...] = jnp.zeros_like(r.dd_low)
        r.rim_low[...] = jnp.zeros_like(r.rim_low)

    @pl.when(me == size - 1)
    def _():
        r.dd_high[...] = jnp.zeros_like(r.dd_high)
        r.rim_high[...] = jnp.zeros_like(r.rim_high)

    small_ref = r.small
    kernel_w = (
        wide(small_ref[ROW_KERNEL_W : ROW_KERNEL_W + TAP_ROWS, :])
        + wide(small_ref[SMALL_ROWS + ROW_KERNEL_W : SMALL_ROWS + ROW_KERNEL_W + TAP_ROWS, :])
    )
    kernel_w = jnp.concatenate(
        [kernel_w, jnp.zeros((LANES - TAP_ROWS, width), jnp.float32)], axis=0
    ).astype(low)
    lead = RIM - KERNEL // 2
    chunk = 128
    r.d_ext[...] = jnp.zeros_like(r.d_ext)
    have(fetched.dconv, fetched.ext, fetched.kern, fetched.point, fetched.queries, fetched.spans)
    wide_ref, tall_ref = r.wide, r.tall

    def conv_back(s):
        r.seg_col[s] = jnp.broadcast_to(r.seg[s, 0:1, :], (LANES, r.seg.shape[2])).T
        for j in range(KERNEL):
            wide_ref[8 * j : 8 * j + 8, :] = (
                v.kern[s, 8 * j : 8 * j + 8, :] * r.mask[s, j : j + 1, :]
            )
        wide_ref[TAP_ROWS:, :] = jnp.zeros((LANES - TAP_ROWS, block), jnp.float32)
        tall = wide_ref[...].T
        high = tall.astype(low)
        both = jnp.concatenate([high, (tall - wide(high)).astype(low)], axis=1)
        for c in range(block // chunk):
            rows = slice(c * chunk, (c + 1) * chunk)
            grad = wide(v.dconv[s, rows, :])
            taps = jnp.zeros((chunk, LANES), jnp.float32)
            for j in range(KERNEL):
                near = jnp.concatenate(
                    [v.ext[s, g, pl.ds(lead + j + c * chunk, chunk), :] for g in range(3)],
                    axis=1,
                )
                term = near * grad
                first = term.astype(low)
                second = (term - wide(first)).astype(low)
                taps = taps + rows_nt(first, r.spread[j, 0:LANES, :])
                taps = taps + rows_nt(second, r.spread[j, 0:LANES, :])
                weight = dot(both[rows, :], r.spread[j]) * grad
                for g in range(3):
                    r.d_ext[s, g, pl.ds(lead + j + c * chunk, chunk), :] += weight[
                        :, lane_group(g)
                    ]
            tall_ref[rows, :] = taps
        back = tall_ref[...].T
        inner = jnp.zeros((8, block), jnp.float32)
        for j in range(KERNEL):
            inner = inner + v.kern[s, 8 * j : 8 * j + 8, :] * (
                back[8 * j : 8 * j + 8, :] * r.mask[s, j : j + 1, :]
            )
        for j in range(KERNEL):
            wide_ref[8 * j : 8 * j + 8, :] = v.kern[s, 8 * j : 8 * j + 8, :] * (
                back[8 * j : 8 * j + 8, :] * r.mask[s, j : j + 1, :] - inner
            )
        d_logits = wide_ref[0:TAP_ROWS, :].astype(low)
        mixed = (v.spans[s] * wide(v.queries[s])).astype(low)
        kernel_grad = dot(d_logits, mixed)
        kernel_bias = dot(d_logits, jnp.ones((block, LANES), low))
        for w in range(2):
            small[w, ROW_KERNEL_W : ROW_KERNEL_W + TAP_ROWS, :] += kernel_grad
            for g in range(3):
                small[w, ROW_KERNEL_B : ROW_KERNEL_B + 24, lane_group(g)] += kernel_bias[
                    24 * g : 24 * g + 24, :
                ]
        d_mixed = dot(wide_ref[...].T.astype(low), kernel_w)
        d_spans = (d_mixed * wide(v.queries[s])).astype(low)
        v.spans[s] = d_mixed * v.spans[s]
        v.dconv[s] = d_spans
        bias = jnp.sum(wide(d_spans), axis=0, keepdims=True)
        for w in range(2):
            small[w, ROW_POINT_B : ROW_POINT_B + 1, :] += bias
        d_depth = rows_nt(d_spans, v.point[...])
        for g in range(groups):
            r.dd[s, g, pl.ds(RIM, block), :] = d_depth[:, lane_group(g)]
        r.dd_first[s] = d_depth[0:RIM, :].astype(low)
        r.dd_last[s] = d_depth[block - RIM : block, :].astype(low)
        for g in range(3):
            r.rim_first[s, :, lane_group(g)] = r.d_ext[s, g, 0:RIM, :].astype(low)
            r.rim_last[s, :, lane_group(g)] = r.d_ext[
                s, g, RIM + block : 2 * RIM + block, :
            ].astype(low)


    def kv_copy(k):
        return (
            pltpu.make_async_copy(r.mine.at[block_of(k), :], r.kv_parts.at[rank], r.recv_kv.at[rank]),
            remote(r.mine.at[block_of(k), :], r.kv_parts.at[rank], r.send_kv.at[k],
                   r.recv_kv.at[rank], {"ctx": base + k}),
        )

    def return_block(k):
        pl.when((k <= TEAM - 2) & (team > 0))(lambda: halo_left(lax.rem(k, TEAM - 1)).wait_recv())
        pl.when((k >= 1) & (team < teams - 1))(
            lambda: halo_right(lax.rem(k + TEAM - 2, TEAM - 1)).wait_recv()
        )
        rows = block_of(k)
        r.mine[rows, :] = (
            wide(r.mine[rows, :]) + wide(r.from_left[rows, :]) + wide(r.from_right[rows, :])
        ).astype(low)
        pair = kv_copy(k)
        pl.when(k == rank)(pair[0].start)
        pl.when(k != rank)(pair[1].start)


    ff_base = core * (2 * half_ff) + pair_index * half_ff
    column_index, column_count, _ = column_of(me, size)
    column_piece = half_ff // column_count
    column_args = (column_of, me, size, r.ff_send, r.ff_column, r.send_c, r.recv_c)
    column_share = (column_of, me, size, r.fin_ff, ff_base, column_piece, r.send_cg, r.recv_cg)
    pair_share = (pair_of, me, size, r.fin_ff, core * (2 * half_ff), half_ff, r.send_pg, r.recv_pg)

    def ff_to_column():
        ff_across.wait()

        def body(at, n):
            rows = part_rows(at, n)
            value = v.keep[side, rows, :] + wide(r.ff_came[rows, :])
            v.keep[side, rows, :] = value
            r.ff_send[rows, :] = value.astype(low)

        in_chunks(half_ff, body)
        for copy in scatter_copies(*column_args):
            copy.start()

    def ff_to_share():
        scatter_wait(*column_args)
        rows = part_rows(column_index * column_piece, column_piece)
        total = v.keep[side, rows, :]
        for other in others(column_index, column_count):
            total = total + wide(r.ff_column[other])
        r.ff_send[rows, :] = total.astype(low)
        own = pltpu.make_async_copy(
            r.ff_send.at[rows, :],
            r.fin_ff.at[part_rows(ff_base + column_index * column_piece, column_piece), :],
            r.load.at[0],
        )
        own.start()
        own.wait()
        for copy in share_copies(*column_share):
            copy.start()

    def ff_to_pair():
        share_wait(*column_share)
        for copy in share_copies(*pair_share):
            copy.start()

    def ff_twin():
        view = r.fin_ff.at[part_rows(core * (2 * half_ff), 2 * half_ff), :]
        return remote(view, view, r.send_pg.at[2], r.recv_pg.at[2], twin)

    def ff_to_twin():
        share_wait(*pair_share)
        ff_twin().start()


    conv_back(0)
    center.wait()
    there = (1 - chip) * (TEAM // 2)
    here = chip * (TEAM // 2)
    return_block(there)
    conv_back(1)
    rims = [
        (remote(r.dd_last, r.dd_low, r.send_h.at[0], r.recv_h.at[0], {"ctx": after}), 1),
        (remote(r.rim_last, r.rim_low, r.send_h.at[1], r.recv_h.at[1], {"ctx": after}), 1),
        (remote(r.dd_first, r.dd_high, r.send_h.at[2], r.recv_h.at[2], {"ctx": prior}), 0),
        (remote(r.rim_first, r.rim_high, r.send_h.at[3], r.recv_h.at[3], {"ctx": prior}), 0),
    ]
    for copy, forward in rims:
        pl.when(me < size - 1 if forward else me > 0)(copy.start)

    return_block(there + 1)
    ff_to_column()
    have(fetched.depth, fetched.xrim)
    strip = 32

    def flat_rows(ref):
        return ref[...].reshape(seqs * block, ref.shape[2])

    point_grad = dot_tn(flat_rows(v.depth), flat_rows(v.dconv)).astype(low)
    for w in range(2):
        block_a.pack[w, 0:width, :] = point_grad[w * width : (w + 1) * width, :]
    for g in range(groups):
        def tap_step(c, sums, g=g):
            out = list(sums)
            for s in range(seqs):
                start = c * strip
                here = r.seg_col[s, pl.ds(RIM + start, strip), :]
                grad = r.dd[s, g, pl.ds(RIM + start, strip), :]
                for j in range(KERNEL):
                    same = r.seg_col[s, pl.ds(lead + j + start, strip), :] == here
                    near = v.xrim[s, g, pl.ds(lead + j + start, strip), :]
                    out[j] = out[j] + fold_rows(jnp.where(same, near, 0.0) * grad)
            return tuple(out)

        sums = lax.fori_loop(
            0, block // strip, tap_step,
            tuple(jnp.zeros((8, LANES), jnp.float32) for _ in range(KERNEL)),
        )
        for j in range(KERNEL):
            small[g // 3, j : j + 1, lane_group(g % 3)] = jnp.sum(sums[j], axis=0, keepdims=True)

    return_block(here + 1 - chip)
    return_block(here + chip)
    have(fetched.convw, fetched.x)
    for copy, forward in rims:
        pl.when(me > 0 if forward else me < size - 1)(copy.wait_recv)
    near_taps = KERNEL // 2
    for s in range(seqs):
        for g in range(3):
            head = pl.ds(RIM, RIM)
            tail = pl.ds(block, RIM)
            r.d_ext[s, g, head, :] += wide(r.rim_low[s, :, lane_group(g)])
            r.d_ext[s, g, tail, :] += wide(r.rim_high[s, :, lane_group(g)])
            v.queries[s, :, lane_group(g)] = r.d_ext[s, g, pl.ds(RIM, block), :].astype(low)
        for g in range(groups):
            r.dd[s, g, 0:RIM, :] = wide(r.dd_low[s, :, lane_group(g)])
            r.dd[s, g, pl.ds(RIM + block, RIM), :] = wide(r.dd_high[s, :, lane_group(g)])
        bias = jnp.sum(wide(v.queries[s]), axis=0, keepdims=True)
        for w in range(2):
            small[w, ROW_CONV_B : ROW_CONV_B + 1, :] += bias
    conv_grad = dot_tn(flat_rows(v.x), flat_rows(v.queries)).astype(low)
    for w in range(2):
        block_a.pack[w, width : 2 * width, :] = conv_grad[w * width : (w + 1) * width, :]

    def core_copy(blk):
        pack = blk.pack
        half = pack.shape[1] // 2
        return remote(pack.at[:, part_rows((1 - core) * half, half), :], blk.twin,
                      blk.send_core.at[0], blk.recv_core.at[0], twin)

    def y_copy(blk):
        return remote(blk.ysend, blk.ycame, blk.send_core.at[1],
                      blk.recv_core.at[1], across)

    def core_done(blk):
        core_copy(blk).wait()
        pack, came = blk.pack, blk.twin
        half = pack.shape[1] // 2

        def body(at, n):
            rows, there = part_rows(at, n), part_rows(core * half + at, n)
            blk.ysend[rows, :] = (
                wide(pack[1 - side, there, :]) + wide(came[1 - side, rows, :])
            ).astype(low)
            blk.acc[rows, :] = wide(pack[side, there, :]) + wide(came[side, rows, :])

        in_chunks(half, body)
        y_copy(blk).start()

    def chips_args(blk):
        return (chips_of, me, size, blk.ysend, blk.chips,
                blk.send_s, blk.recv_s)

    def y_done(blk):
        y_copy(blk).wait()

        def body(at, n):
            rows = part_rows(at, n)
            value = blk.acc[rows, :] + wide(blk.ycame[rows, :])
            blk.acc[rows, :] = value
            blk.ysend[rows, :] = value.astype(low)

        in_chunks(blk.ysend.shape[0], body)
        for copy in scatter_copies(*chips_args(blk)):
            copy.start()

    def share_args(blk):
        half = blk.ysend.shape[0]
        return (chips_of, me, size, blk.fin, core * half, half // count,
                blk.send_g, blk.recv_g)

    def chips_done(blk):
        scatter_wait(*chips_args(blk))
        half = blk.ysend.shape[0]
        piece = half // count
        value = blk.acc[part_rows(index * piece, piece), :]
        for other in others(index, count):
            value = value + wide(blk.chips[other])
        blk.fin[part_rows(core * half + index * piece, piece), :] = value.astype(low)
        for copy in share_copies(*share_args(blk)):
            copy.start()

    def twin_copy(blk):
        fin = blk.fin
        half = fin.shape[0] // 2
        view = fin.at[part_rows(core * half, half), :]
        return remote(view, view, blk.send_core.at[2], blk.recv_core.at[2], twin)

    def share_done(blk):
        share_wait(*share_args(blk))
        twin_copy(blk).start()

    def finish(blk):
        for copy in scatter_copies(*chips_args(blk)):
            copy.wait_send()
        for copy in share_copies(*share_args(blk)):
            copy.wait_send()
        twin_copy(blk).wait()

    core_copy(block_a).start()
    for k, row in enumerate((ROW_GAIN2, ROW_SHIFT2, ROW_OUTER_B, ROW_GAIN1, ROW_SHIFT1, ROW_OUTPUT_B)):
        for w in range(2):
            small[w, row : row + 1, :] = r.vec[k : k + 1, w * 384 : (w + 1) * 384]
    for w in range(2):
        for k in range(4):
            at = (4 * w + k) * 384
            small[w, ROW_INNER_B + k : ROW_INNER_B + k + 1, :] = r.bias[0:1, at : at + 384]

    own_q.wait()
    for o in range(1, TEAM):
        q_copy(o).wait_send()
        remote(r.dq.at[rank], r.q_parts.at[mate(rank, o)], r.send_q.at[o], r.recv_q.at[o],
               {"ctx": base + mate(rank, o)}).wait_recv()
    for s in range(seqs):
        one, two = r.q_parts.at[2 * s], r.q_parts.at[2 * s + 1]
        queries = (
            one[:, lane_group(0)],
            mixed_lanes(wide(one[:, lane_group(1)]), half_turn(wide(two[:, lane_group(1)]))),
            two[:, lane_group(0)],
        )
        for g in range(3):
            r.d_cat[s, :, lane_group(6 + g)] = (
                wide(queries[g]) + v.spans[s, :, lane_group(g)]
            ).astype(low)
    for k in range(TEAM):
        pl.when(k == rank)(kv_copy(k)[0].wait)
        pl.when(k != rank)(kv_copy(k)[1].wait_send)
    for o in range(1, TEAM):
        other = mate(rank, o)
        remote(r.mine.at[block_of(rank), :], r.kv_parts.at[other], r.send_kv.at[rank],
               r.recv_kv.at[other], {"ctx": base + other}).wait_recv()
    for s in range(seqs):
        one, two = r.kv_parts.at[2 * s], r.kv_parts.at[2 * s + 1]
        mid_one, mid_two = wide(one[:, lane_group(1)]), wide(two[:, lane_group(1)])
        r.d_cat[s, :, lane_group(0)] = one[:, lane_group(0)]
        r.d_cat[s, :, lane_group(1)] = mixed_lanes(mid_one, half_turn(mid_two)).astype(low)
        r.d_cat[s, :, lane_group(2)] = two[:, lane_group(0)]
        r.d_cat[s, :, lane_group(3)] = one[:, lane_group(2)]
        r.d_cat[s, :, lane_group(4)] = mixed_lanes(half_turn(mid_one), mid_two).astype(low)
        r.d_cat[s, :, lane_group(5)] = two[:, lane_group(2)]
        for k, row in ((1, ROW_VALUE_B), (2, ROW_QUERY_B)):
            bias = jnp.sum(wide(r.d_cat[s, :, k * width : (k + 1) * width]), axis=0, keepdims=True)
            for w in range(2):
                small[w, row : row + 1, :] += bias
    grads = flat_rows(r.d_cat)
    for w in range(2):
        piece = dot_tn(
            v.x[:, :, w * width : (w + 1) * width].reshape(seqs * block, width), grads
        ).astype(low)
        for k in range(3):
            block_b.pack[w, k * width : (k + 1) * width, :] = piece[:, k * width : (k + 1) * width]
        block_b.pack[w, SMALL_AT : SMALL_AT + SMALL_ROWS, :] = small[w].astype(low)
    core_copy(block_b).start()
    core_done(block_a)
    core_done(block_b)
    have(fetched.ds, fetched.key, fetched.value, fetched.query)
    def taps_row(j, g):
        return wide(small_ref[(g // 3) * SMALL_ROWS + j : (g // 3) * SMALL_ROWS + j + 1,
                              lane_group(g % 3)])

    def depth_strip(c, s):
        start = c * strip
        here = r.seg_col[s, pl.ds(RIM + start, strip), :]
        rows = pl.ds(pl.multiple_of(start, strip), strip)
        sums = [v.ds[s, rows, lane_group(g)] for g in range(groups)]
        for j in range(KERNEL):
            same = r.seg_col[s, pl.ds(RIM + near_taps - j + start, strip), :] == here
            for g in range(groups):
                near = r.dd[s, g, pl.ds(RIM + near_taps - j + start, strip), :]
                sums[g] = sums[g] + jnp.where(same, near, 0.0) * taps_row(j, g)
        for g in range(groups):
            v.ds[s, rows, lane_group(g)] = sums[g]
        return s

    for s in range(seqs):
        lax.fori_loop(0, block // strip, depth_strip, s)
    ff_to_share()
    y_done(block_a)
    y_done(block_b)
    for s in range(seqs):
        v.ds[s] += (
            rows_nt(v.queries[s], v.convw[...])
            + rows_nt(r.d_cat[s, :, 0:width], v.key[...])
            + rows_nt(r.d_cat[s, :, width : 2 * width], v.value[...])
            + rows_nt(r.d_cat[s, :, 2 * width :], v.query[...])
        )
    out_copy = pltpu.make_async_copy(v.ds, r.input_grad, r.load.at[1])
    out_copy.start()
    chips_done(block_a)
    ff_to_pair()
    chips_done(block_b)
    share_done(block_a)
    share_done(block_b)
    ff_to_twin()
    finish(block_a)
    finish(block_b)
    ff_twin().wait()
    for copy in scatter_copies(*column_args):
        copy.wait_send()
    for copy in share_copies(*column_share) + share_copies(*pair_share):
        copy.wait_send()
    for copy, forward in rims:
        pl.when(me < size - 1 if forward else me > 0)(copy.wait_send)
    for k in range(TEAM - 1):
        pl.when(team < teams - 1)(halo_left(k).wait_send)
        pl.when(team > 0)(halo_right(k).wait_send)
    out_copy.wait()


def padded(rows, unit):
    return -(-rows // unit) * unit


def back(held, window, dq_parts, loaded):
    size = lax.axis_size("ctx")
    unit = 16 * size
    seqs, block, model = loaded["x"].shape
    width = HEADS * HEAD_DIM
    halo = (TEAM - 1) * block
    span = block + 2 * RIM
    chips, column = size // 2, size // TEAM
    low, full = jnp.bfloat16, jnp.float32
    dma = pltpu.SemaphoreType.DMA
    half_ff = loaded["keep"].shape[1]
    outs = dict(
        input_grad=jax.ShapeDtypeStruct((seqs, block, model), full),
        fin_ff=jax.ShapeDtypeStruct((4 * half_ff, width), low),
    )
    scratch = dict(
        mine=pltpu.VMEM((TEAM * block, width), low),
        from_right=pltpu.VMEM((TEAM * block, width), low),
        from_left=pltpu.VMEM((TEAM * block, width), low),
        kv_parts=pltpu.VMEM((TEAM, block, width), low),
        q_parts=pltpu.VMEM((TEAM, block, 2 * LANES), low),
        ff_send=pltpu.VMEM((half_ff, width), low),
        ff_came=pltpu.VMEM((half_ff, width), low),
        ff_column=pltpu.VMEM((column, half_ff // column, width), low),
        spread=pltpu.VMEM((KERNEL, 2 * LANES, width), low),
        sums=pltpu.VMEM((2, SMALL_ROWS, width), full),
        wide=pltpu.VMEM((LANES, block), full),
        tall=pltpu.VMEM((block, LANES), full),
        seg_col=pltpu.VMEM((seqs, held["seg"].shape[2], LANES), full),
        d_ext=pltpu.VMEM((seqs, 3, span, LANES), full),
        dd=pltpu.VMEM((seqs, model // LANES, span, LANES), full),
        d_cat=pltpu.VMEM((seqs, block, 3 * width), low),
        dd_first=pltpu.VMEM((seqs, RIM, model), low),
        dd_last=pltpu.VMEM((seqs, RIM, model), low),
        dd_low=pltpu.VMEM((seqs, RIM, model), low),
        dd_high=pltpu.VMEM((seqs, RIM, model), low),
        rim_first=pltpu.VMEM((seqs, RIM, width), low),
        rim_last=pltpu.VMEM((seqs, RIM, width), low),
        rim_low=pltpu.VMEM((seqs, RIM, width), low),
        rim_high=pltpu.VMEM((seqs, RIM, width), low),
        send_l=dma((TEAM,)), recv_l=dma((TEAM,)), send_r=dma((TEAM,)), recv_r=dma((TEAM,)),
        send_q=dma((TEAM,)), recv_q=dma((TEAM,)), send_kv=dma((TEAM,)), recv_kv=dma((TEAM,)),
        send_h=dma((4,)), recv_h=dma((4,)), send_p=dma((1,)), recv_p=dma((1,)),
        send_c=dma((column,)), recv_c=dma((column,)), send_cg=dma((column,)),
        recv_cg=dma((column,)), send_pg=dma((3,)), recv_pg=dma((3,)),
        load=dma((len(loaded) + 1,)),
    )

    def block_scratch(rows):
        rows = padded(rows, unit)
        return dict(
            pack=pltpu.VMEM((2, rows, width), low),
            twin=pltpu.VMEM((2, rows // 2, width), low),
            ysend=pltpu.VMEM((rows // 2, width), low),
            ycame=pltpu.VMEM((rows // 2, width), low),
            acc=pltpu.VMEM((rows // 2, width), full),
            chips=pltpu.VMEM((chips, rows // 2 // chips, width), low),
            fin=pltpu.VMEM((rows, width), low),
            send_s=dma((chips,)), recv_s=dma((chips,)), send_g=dma((chips,)),
            recv_g=dma((chips,)), send_core=dma((3,)), recv_core=dma((3,)),
        )

    a_scratch, b_scratch = block_scratch(PACK_A), block_scratch(PACK_B)
    del a_scratch["fin"], b_scratch["fin"]
    fin_shapes = [jax.ShapeDtypeStruct((padded(n, unit), width), low) for n in (PACK_A, PACK_B)]
    vmem = pl.BlockSpec(memory_space=pltpu.VMEM)
    anywhere = pl.BlockSpec(memory_space=pl.ANY)
    names = tuple(held) + ("window", "dq") + tuple(outs) + tuple(scratch)
    total_in = len(held) + 2
    fetch_count = len(loaded)

    def kernel(*refs):
        ins, loads = refs[:total_in], refs[total_in : total_in + fetch_count]
        at = total_in + fetch_count
        results = refs[at : at + len(outs)]
        fin_a, fin_b = refs[at + len(outs) : at + len(outs) + 2]
        late = refs[at + len(outs) + 2 :]
        first, late = late[: len(scratch)], late[len(scratch) :]
        a_refs, late = late[: len(a_scratch)], late[len(a_scratch) :]
        b_refs, holds = late[: len(b_scratch)], late[len(b_scratch) :]
        back_kernel(
            names, tuple(a_scratch) + ("fin",), tuple(b_scratch) + ("fin",), tuple(loaded),
            *ins, *results, *first, *a_refs, fin_a, *b_refs, fin_b, *loads, *holds,
        )

    holds = [pltpu.VMEM(a.shape, a.dtype) for a in loaded.values()]
    return pl.pallas_call(
        kernel,
        out_shape=list(outs.values()) + fin_shapes,
        in_specs=[vmem] * len(held) + [anywhere] * (2 + len(loaded)),
        out_specs=[anywhere] * 2 + [vmem] * 2,
        scratch_shapes=list(scratch.values()) + list(a_scratch.values())
        + list(b_scratch.values()) + holds,
        compiler_params=pltpu.CompilerParams(
            collective_id=5, has_side_effects=True, vmem_limit_bytes=65400 * 2**10
        ),
        name="back",
    )(*held.values(), window, dq_parts, *loaded.values())


STEP = 256
FF_CHUNK = 512
PACK_FF = 3840


def gelu_pair(value):
    size = jnp.abs(value) * 0.7071067811865476
    denominator = 1.0 + 0.3275911 * size
    t = pl.reciprocal(denominator, approx=True)
    t = t * (2.0 - denominator * t)
    bell = jnp.exp(-0.5 * value * value)
    tail = t * (0.127414796 + t * (-0.142248368 + t * (0.7107068705 + t * (
        -0.7265760135 + t * 0.5307027145))))
    tail = tail * bell
    share = jnp.where(value >= 0, 1.0 - tail, tail)
    return value * share, share + value * bell * 0.3989422804014327


def fold_rows(block):
    return jnp.sum(block.reshape(block.shape[0] // 8, 8, block.shape[1]), axis=0)


def norm_parts(value):
    center = value - jnp.mean(value, axis=-1, keepdims=True)
    spread = jnp.mean(center * center, axis=-1, keepdims=True)
    scale = lax.rsqrt(spread + 1e-05)
    return center * scale, scale


def norm_back(grad, unit, scale):
    return scale * (
        grad
        - jnp.mean(grad, axis=-1, keepdims=True)
        - unit * jnp.mean(grad * unit, axis=-1, keepdims=True)
    )


def middle_kernel(att_ref, conv_ref, x_ref, og_ref, ow_ref, iw_ref, uw_ref, small_ref,
                  out_ref, ds_ref, dc_ref, team_ref, keep_ref, xsend_ref, vec_ref, bias_ref,
                  pack_ref, twin_ref, pieces, parts, joined_ref, low_ref, act_ref, slope_ref, do_ref, di_ref, db_ref,
                  sums_ref, wide_sums, send_a, recv_a, send_g, recv_g, send_t, recv_t):
    me = lax.axis_index("ctx")
    rank = lax.rem(me, TEAM)
    base = me - rank
    seqs, block, model = x_ref.shape
    width = HEADS * HEAD_DIM
    greet([{"ctx": base + mate(rank, o)} for o in range(1, TEAM)])

    def piece_copy(r):
        return (
            pltpu.make_async_copy(att_ref.at[r], pieces.at[rank], recv_a.at[rank]),
            remote(att_ref.at[r], pieces.at[rank], send_a.at[r], recv_a.at[rank],
                   {"ctx": base + r}),
        )

    def team_copy(r):
        return (
            pltpu.make_async_copy(parts.at[r], team_ref.at[rank], recv_g.at[rank]),
            remote(parts.at[r], team_ref.at[rank], send_g.at[r], recv_g.at[rank],
                   {"ctx": base + r}),
        )

    for o in (3, 2, 1):
        piece_copy(mate(rank, o))[1].start()
    piece_copy(rank)[0].start()
    sums_ref[...] = jnp.zeros_like(sums_ref)
    wide_sums[...] = jnp.zeros_like(wide_sums)
    own = lax.div(rank, 2)
    steps = block // STEP

    def row(index):
        return jnp.concatenate(
            [small_ref[index : index + 1, :], small_ref[SMALL_ROWS + index : SMALL_ROWS + index + 1, :]],
            axis=1,
        ).astype(jnp.float32)

    def body(i, carry):
        s = lax.rem(own + lax.div(i, steps), seqs)
        start = pl.multiple_of(lax.rem(i, steps) * STEP, STEP)
        rows = pl.ds(start, STEP)
        flat = pl.ds(pl.multiple_of(s * block + start, STEP), STEP)

        @pl.when(i == 0)
        def _():
            piece_copy(rank)[0].wait()
            remote(att_ref.at[rank], pieces.at[mate(rank, 1)], send_a.at[rank],
                   recv_a.at[mate(rank, 1)], {"ctx": base + mate(rank, 1)}).wait_recv()

        @pl.when(i == steps)
        def _():
            for o in (2, 3):
                remote(att_ref.at[rank], pieces.at[mate(rank, o)], send_a.at[rank],
                       recv_a.at[mate(rank, o)], {"ctx": base + mate(rank, o)}).wait_recv()

        first, second = pieces.at[2 * s], pieces.at[2 * s + 1]
        joined_ref[flat, lane_group(0)] = first[rows, lane_group(0)]
        joined_ref[flat, lane_group(1)] = mixed_lanes(
            first[rows, lane_group(1)].astype(jnp.float32),
            half_turn(second[rows, lane_group(1)].astype(jnp.float32)),
        ).astype(jnp.bfloat16)
        joined_ref[flat, lane_group(2)] = second[rows, lane_group(0)]
        joined_ref[flat, width:] = conv_ref[s, rows, :]
        branch = dot(joined_ref[flat, :], ow_ref[...]) + row(ROW_OUTPUT_B)
        unit1, scale1 = norm_parts(branch + x_ref[s, rows, :].astype(jnp.float32))
        gain1 = row(ROW_GAIN1)
        normed = unit1 * gain1 + row(ROW_SHIFT1)
        low_ref[flat, :] = normed.astype(jnp.bfloat16)
        outer = []
        part = model // GROUPS
        hidden = iw_ref.shape[2]
        for g in range(GROUPS):
            cols = slice(g * part, (g + 1) * part)
            for c in range(hidden // FF_CHUNK):
                span = slice(g * hidden + c * FF_CHUNK, g * hidden + (c + 1) * FF_CHUNK)
                near = slice(c * FF_CHUNK, (c + 1) * FF_CHUNK)
                bias = jnp.concatenate(
                    [
                        small_ref[
                            g * SMALL_ROWS + ROW_INNER_B + k // 3 : g * SMALL_ROWS + ROW_INNER_B + k // 3 + 1,
                            lane_group(k % 3),
                        ]
                        for k in range(c * FF_CHUNK // LANES, (c + 1) * FF_CHUNK // LANES)
                    ],
                    axis=1,
                ).astype(jnp.float32)
                inner = dot(low_ref[flat, cols], iw_ref[g, :, near]) + bias
                active, slope = gelu_pair(inner)
                act_ref[flat, span] = active.astype(jnp.bfloat16)
                slope_ref[:, span] = slope
            outer.append(dot(act_ref[flat, g * hidden : (g + 1) * hidden], uw_ref[g]))
        summed = jnp.concatenate(outer, axis=1) + row(ROW_OUTER_B) + normed
        unit2, scale2 = norm_parts(summed)
        gain2 = row(ROW_GAIN2)
        out_ref[s, rows, :] = (unit2 * gain2 + row(ROW_SHIFT2)).astype(jnp.bfloat16)
        grad = og_ref[s, rows, :].astype(jnp.float32)
        sums_ref[0] += fold_rows(grad * unit2)
        sums_ref[1] += fold_rows(grad)
        d_sum2 = norm_back(grad * gain2, unit2, scale2)
        d_outer = d_sum2.astype(jnp.bfloat16)
        do_ref[flat, :] = d_outer
        sums_ref[2] += fold_rows(d_outer.astype(jnp.float32))
        back = []
        for g in range(GROUPS):
            cols = slice(g * part, (g + 1) * part)
            for c in range(hidden // FF_CHUNK):
                span = slice(g * hidden + c * FF_CHUNK, g * hidden + (c + 1) * FF_CHUNK)
                near = slice(c * FF_CHUNK, (c + 1) * FF_CHUNK)
                d_inner = (
                    rows_nt(do_ref[flat, cols], uw_ref[g, near, :]) * slope_ref[:, span]
                ).astype(jnp.bfloat16)
                di_ref[flat, span] = d_inner
                wide_sums[:, span] += fold_rows(d_inner.astype(jnp.float32))
            back.append(rows_nt(di_ref[flat, g * hidden : (g + 1) * hidden], iw_ref[g]))
        d_normed = d_sum2 + jnp.concatenate(back, axis=1)
        sums_ref[3] += fold_rows(d_normed * unit1)
        sums_ref[4] += fold_rows(d_normed)
        d_sum1 = norm_back(d_normed * gain1, unit1, scale1)
        ds_ref[s, rows, :] = d_sum1
        d_branch = d_sum1.astype(jnp.bfloat16)
        db_ref[flat, :] = d_branch
        sums_ref[5] += fold_rows(d_branch.astype(jnp.float32))
        d_joined = rows_nt(d_branch, ow_ref[...])
        dc_ref[s, rows, :] = d_joined[:, width:].astype(jnp.bfloat16)
        parts[2 * s, rows, lane_group(0)] = d_joined[:, lane_group(0)].astype(jnp.bfloat16)
        parts[2 * s, rows, lane_group(1)] = half_turn(d_joined[:, lane_group(1)]).astype(
            jnp.bfloat16
        )
        parts[2 * s + 1, rows, lane_group(0)] = d_joined[:, lane_group(2)].astype(jnp.bfloat16)
        parts[2 * s + 1, rows, lane_group(1)] = d_joined[:, lane_group(1)].astype(jnp.bfloat16)

        @pl.when(i == steps - 1)
        def _():
            team_copy(rank)[0].start()
            team_copy(mate(rank, 1))[1].start()

        @pl.when(i == 2 * steps - 1)
        def _():
            team_copy(mate(rank, 2))[1].start()
            team_copy(mate(rank, 3))[1].start()

        return carry

    lax.fori_loop(0, seqs * steps, body, 0)

    half = width
    for w in range(2):
        for k in range(2):
            pack_ref[w, pl.ds(k * half, half), :] = dot_tn(
                joined_ref[:, w * half : (w + 1) * half], db_ref[:, k * half : (k + 1) * half]
            ).astype(jnp.bfloat16)
    part = model // GROUPS
    hidden = iw_ref.shape[2]
    for g in range(GROUPS):
        for k in range(hidden // half):
            grads = dot_tn(
                low_ref[:, g * part : (g + 1) * part],
                di_ref[:, g * hidden + k * half : g * hidden + (k + 1) * half],
            ).astype(jnp.bfloat16)
            for w in range(2):
                pack_ref[w, pl.ds(2 * half + (g * 4 + k) * (part // 2), part // 2), :] = grads[
                    w * (part // 2) : (w + 1) * (part // 2), :
                ]
        for k in range(hidden // half):
            w, lower = k // 2, k % 2
            grads = dot_tn(
                act_ref[:, g * hidden + k * half : g * hidden + (k + 1) * half],
                do_ref[:, g * part : (g + 1) * part],
            ).astype(jnp.bfloat16)
            pack_ref[w, pl.ds(6 * half + g * 2 * half + lower * half, half), :] = grads
    for k in range(6):
        vec_ref[k : k + 1, :] = jnp.sum(sums_ref[k], axis=0, keepdims=True)
    vec_ref[6:, :] = jnp.zeros((2, model), jnp.float32)
    bias_ref[...] = jnp.broadcast_to(jnp.sum(wide_sums[...], axis=0, keepdims=True), bias_ref.shape)

    core = lax.rem(me, 2)
    half_ff = pack_ref.shape[1] // 2
    exchange = remote(pack_ref.at[:, part_rows((1 - core) * half_ff, half_ff), :], twin_ref,
                      send_t.at[0], recv_t.at[0], {"ctx": flip(me, 1)})
    exchange.start()
    exchange.wait()

    pair_index, _, _ = pair_of(me, lax.axis_size("ctx"))
    quarter = half_ff // 2

    def add(at, n):
        here = part_rows(at, n)
        keep, give = pair_index * quarter, (1 - pair_index) * quarter
        for w in range(2):
            xsend_ref[w, here, :] = (
                wide(pack_ref[w, part_rows(core * half_ff + give + at, n), :])
                + wide(twin_ref[w, part_rows(give + at, n), :])
            ).astype(jnp.bfloat16)
            keep_ref[w, here, :] = wide(
                pack_ref[w, part_rows(core * half_ff + keep + at, n), :]
            ) + wide(twin_ref[w, part_rows(keep + at, n), :])

    in_chunks(quarter, add)
    team_copy(rank)[0].wait()
    for o in range(1, TEAM):
        other = mate(rank, o)
        piece_copy(other)[1].wait_send()
        team_copy(other)[1].wait_send()
        remote(parts.at[rank], team_ref.at[other], send_g.at[rank], recv_g.at[other],
               {"ctx": base + other}).wait_recv()


def middle(attended, convolved, hidden, out_grad, output_w, inner_w, outer_w, small):
    seqs, block, model = hidden.shape
    rows = seqs * block
    width = convolved.shape[2]
    inner = GROUPS * inner_w.shape[2]
    pack_rows = padded(PACK_FF, 16 * lax.axis_size("ctx"))
    vmem = pl.BlockSpec(memory_space=pltpu.VMEM)
    anywhere = pl.BlockSpec(memory_space=pl.ANY)
    low, full = jnp.bfloat16, jnp.float32
    dma = pltpu.SemaphoreType.DMA
    return pl.pallas_call(
        middle_kernel,
        out_shape=[
            jax.ShapeDtypeStruct((seqs, block, model), low),
            jax.ShapeDtypeStruct((seqs, block, model), full),
            jax.ShapeDtypeStruct((seqs, block, width), low),
            jax.ShapeDtypeStruct((TEAM, block, 2 * LANES), low),
            jax.ShapeDtypeStruct((2, pack_rows // 4, width), full),
            jax.ShapeDtypeStruct((2, pack_rows // 4, width), low),
            jax.ShapeDtypeStruct((8, model), full),
            jax.ShapeDtypeStruct((8, inner), full),
        ],
        in_specs=[anywhere] + [vmem] * 7,
        out_specs=[vmem] * 3 + [anywhere] + [vmem] * 4,
        scratch_shapes=[
            pltpu.VMEM((2, pack_rows, width), low),
            pltpu.VMEM((2, pack_rows // 2, width), low),
            pltpu.VMEM((TEAM, block, 2 * LANES), low),
            pltpu.VMEM((TEAM, block, 2 * LANES), low),
            pltpu.VMEM((rows, model), low),
            pltpu.VMEM((rows, model), low),
            pltpu.VMEM((rows, inner), low),
            pltpu.VMEM((STEP, inner), full),
            pltpu.VMEM((rows, model), low),
            pltpu.VMEM((rows, inner), low),
            pltpu.VMEM((rows, model), low),
            pltpu.VMEM((6, 8, model), full),
            pltpu.VMEM((8, inner), full),
            dma((TEAM,)), dma((TEAM,)), dma((TEAM,)), dma((TEAM,)), dma((1,)), dma((1,)),
        ],
        compiler_params=pltpu.CompilerParams(
            collective_id=2, has_side_effects=True, vmem_limit_bytes=63 * 2**20
        ),
        name="middle",
    )(attended, convolved, hidden, out_grad, output_w, inner_w, outer_w, small)


def small_block(side, vectors, depth, query_b, value_b, point_b, conv_b, kernel_b, kernel_w):
    def spread_out(part, axis=-1):
        none = jnp.zeros_like(part)
        return jnp.where(
            side == 0,
            jnp.concatenate([part, none], axis=axis),
            jnp.concatenate([none, part], axis=axis),
        )

    def by_tap(part):
        return jnp.pad(part, ((0, 0), (0, 8 - HEADS), (0, 0))).reshape(TAP_ROWS, -1)

    bias = by_tap(spread_out(kernel_b).reshape(HEADS, KERNEL).T[:, :, None])
    bias = jnp.broadcast_to(bias, (TAP_ROWS, LANES)).reshape(3, 24, LANES)
    taps = by_tap(kernel_w.reshape(-1, HEADS, KERNEL).transpose(2, 1, 0))
    rows = [depth] + [v.reshape(-1, 384) for v in vectors]
    rows += [spread_out(v).reshape(1, 384) for v in (query_b, value_b, point_b, conv_b)]
    rows += [jnp.zeros((1, 384), depth.dtype)]
    rows += [bias.transpose(1, 0, 2).reshape(24, 384), spread_out(taps)]
    rows = jnp.concatenate(rows)
    return jnp.pad(rows, ((0, SMALL_ROWS - rows.shape[0]), (0, 0)))


def on_device(
    hidden_in,
    segment_ids,
    out_grad,
    query_w,
    query_b,
    key_w,
    value_w,
    value_b,
    depth_kernel,
    point_w,
    point_b,
    kernel_w,
    kernel_b,
    conv_w,
    conv_b,
    output_w,
    output_b,
    norm1_gain,
    norm1_bias,
    inner_w,
    inner_b,
    outer_w,
    outer_b,
    norm2_gain,
    norm2_bias,
):
    micro_count, seq_local, block_len, model_width = hidden_in.shape
    seq_count = micro_count * seq_local
    att_width = HEADS * HEAD_DIM
    half_taps = KERNEL // 2
    position = lax.axis_index("ctx")
    seg_rows = segment_ids.reshape(seq_count, segment_ids.shape[2])
    pad_rows = (TEAM - 1) * block_len
    seg_pad = jnp.pad(seg_rows, ((0, 0), (pad_rows, pad_rows)), constant_values=-1)
    own_seg = lax.dynamic_slice_in_dim(seg_pad, position * block_len + pad_rows, block_len, 1)
    rank = lax.rem(position, TEAM)
    team_seg = lax.dynamic_slice(
        jnp.concatenate(
            [seg_pad[:, : pad_rows + seg_rows.shape[1]],
             jnp.full((seq_count, pad_rows), 2**24, seg_pad.dtype)], axis=1
        ),
        (lax.div(rank, 2), (position - rank) * block_len),
        (1, (3 * TEAM - 2) * block_len),
    )
    query_seg = team_seg[:, pad_rows : pad_rows + TEAM * block_len]
    lows = query_seg[0, ::TILE]
    highs = query_seg[0, TILE - 1 :: TILE]
    before = jnp.sum(team_seg < lows[:, None], axis=1, dtype=jnp.int32)
    through = jnp.sum(team_seg <= highs[:, None], axis=1, dtype=jnp.int32)
    bounds = jnp.stack([before // TILE, (through + TILE - 1) // TILE])
    seg_keys = jnp.broadcast_to(team_seg.astype(jnp.float32), (8, team_seg.shape[1]))
    seg_queries = jnp.broadcast_to(query_seg.astype(jnp.float32), (8, query_seg.shape[1]))
    rim_seg = lax.dynamic_slice_in_dim(
        seg_pad, position * block_len + pad_rows - RIM, block_len + 2 * RIM, 1
    )
    tap_mask = jnp.stack(
        [
            rim_seg[:, RIM - half_taps + j : RIM - half_taps + j + block_len] == own_seg
            for j in range(KERNEL)
        ],
        axis=1,
    ).astype(jnp.float32)
    seg_rim = jnp.pad(
        rim_seg.astype(jnp.float32), ((0, 0), (0, -rim_seg.shape[1] % LANES)), constant_values=-1
    )
    seg_rim = jnp.broadcast_to(seg_rim[:, None], (seq_count, 8, seg_rim.shape[1]))
    side = lax.axis_index("wsh")
    small = small_block(
        side,
        [output_b, norm1_gain, norm1_bias, outer_b, norm2_gain, norm2_bias, inner_b],
        depth_kernel, query_b, value_b, point_b, conv_b, kernel_b, kernel_w,
    )
    tap_rows = jnp.pad(tap_mask, ((0, 0), (0, 16 - KERNEL), (0, 0)))
    (key_mat, value_mat, query_mat, small_full, point_mat, conv_mat, output_mat, inner_mat,
     outer_mat, window, query_team, queries, xrim, depth_low, span_keys, mixed_low, kern,
     ext, convolved) = front(
        hidden_in.reshape(seq_count, block_len, model_width), seg_rim,
        tap_rows,
        [key_w, value_w, query_w, small, point_w, conv_w, output_w, inner_w, outer_w],
    )

    query_team = query_team.reshape(TEAM * block_len, 2 * LANES)
    attended_team, attended_t, log_sums = attend(
        bounds, query_team, window, seg_keys, seg_queries
    )
    hidden = hidden_in.reshape(seq_count, block_len, model_width)
    (output, grad_sum1, grad_conv, grad_team, keep, xsend, vec_grads, bias_grads) = middle(
        attended_team.reshape(TEAM, block_len, -1), convolved, hidden,
        out_grad.reshape(seq_count, block_len, model_width),
        output_mat, inner_mat, outer_mat, small_full,
    )
    came = lax.ppermute(xsend, "ctx", [(i, i ^ 2) for i in range(lax.axis_size("ctx"))])
    grad_query_team, grad_window = attend_back(
        bounds, query_team, window, seg_keys, seg_queries,
        grad_team.reshape(TEAM * block_len, 2 * LANES), attended_t, log_sums,
    )
    grad_input, fin_ff, fin_a, fin_b = back(
        dict(seg=seg_rim, mask=tap_rows, small=small_full, vec=vec_grads, bias=bias_grads),
        grad_window, grad_query_team.reshape(TEAM, block_len, -1),
        dict(keep=keep, came=came, dconv=grad_conv, ext=ext, kern=kern, point=point_mat,
             queries=queries, spans=span_keys, depth=depth_low, xrim=xrim, x=hidden,
             convw=conv_mat, ds=grad_sum1, key=key_mat, value=value_mat, query=query_mat),
    )
    grad_key, grad_value, grad_query = [
        fin_b[k * att_width : (k + 1) * att_width].astype(jnp.float32) for k in range(3)
    ]
    own = fin_b[SMALL_AT : SMALL_AT + SMALL_ROWS].astype(jnp.float32)
    grad_point, grad_conv = [
        fin_a[k * att_width : (k + 1) * att_width].astype(jnp.float32) for k in range(2)
    ]
    half = att_width // 2
    mine = lax.dynamic_slice_in_dim(own, side * half, half, 1)
    by_tap = mine[ROW_KERNEL_W : ROW_KERNEL_W + TAP_ROWS].reshape(KERNEL, 8, half)[:, :HEADS]
    grad_kernel = by_tap.transpose(2, 1, 0).reshape(half, HEADS * KERNEL)
    bias_rows = own[ROW_KERNEL_B : ROW_KERNEL_B + 24].reshape(24, 3, LANES)[:, :, 0].T
    bias_taps = bias_rows.reshape(KERNEL, 8)[:, :HEADS].T.reshape(-1)
    count = HEADS * KERNEL // 2
    grad_kernel_bias = lax.dynamic_slice_in_dim(bias_taps, side * count, count)
    ff = fin_ff.astype(jnp.float32)
    hidden_units = inner_w.shape[2]
    grad_output = ff[: 2 * att_width].reshape(2, att_width, att_width).transpose(1, 0, 2)
    rows = inner_w.shape[1]
    grad_inner = (
        ff[2 * att_width : 6 * att_width]
        .reshape(GROUPS, hidden_units // att_width, rows, att_width)
        .transpose(0, 2, 1, 3)
        .reshape(inner_w.shape)
    )
    grad_outer = ff[6 * att_width : 10 * att_width].reshape(outer_w.shape)
    return (
        output.reshape(hidden_in.shape), grad_input.reshape(hidden_in.shape),
        grad_query, mine[ROW_QUERY_B], grad_key, grad_value, mine[ROW_VALUE_B], own[:KERNEL],
        grad_point, mine[ROW_POINT_B], grad_kernel, grad_kernel_bias, grad_conv,
        mine[ROW_CONV_B], grad_output.reshape(output_w.shape), own[ROW_OUTPUT_B],
        own[ROW_GAIN1], own[ROW_SHIFT1], grad_inner,
        own[ROW_INNER_B : ROW_INNER_B + 4].reshape(-1), grad_outer, own[ROW_OUTER_B],
        own[ROW_GAIN2], own[ROW_SHIFT2],
    )


def solution(mesh):
    in_specs = (
        P(None, "wsh", "ctx", None),
        P(None, "wsh", None),
        P(None, "wsh", "ctx", None),
        P("wsh", None),
        P("wsh"),
        P("wsh", None),
        P("wsh", None),
        P("wsh"),
        P(None, "wsh"),
        P("wsh", None),
        P("wsh"),
        P("wsh", None),
        P("wsh"),
        P("wsh", None),
        P("wsh"),
        P("wsh", None),
        P("wsh"),
        P("wsh"),
        P("wsh"),
        P(None, "wsh", None),
        P("wsh"),
        P(None, "wsh", None),
        P("wsh"),
        P("wsh"),
        P("wsh"),
    )
    out_specs = (
        P(None, "wsh", "ctx", None),
        P(None, "wsh", "ctx", None),
        P("wsh", None),
        P("wsh"),
        P("wsh", None),
        P("wsh", None),
        P("wsh"),
        P(None, "wsh"),
        P("wsh", None),
        P("wsh"),
        P("wsh", None),
        P("wsh"),
        P("wsh", None),
        P("wsh"),
        P("wsh", None),
        P("wsh"),
        P("wsh"),
        P("wsh"),
        P(None, "wsh", None),
        P("wsh"),
        P(None, "wsh", None),
        P("wsh"),
        P("wsh"),
        P("wsh"),
    )
    return jax.shard_map(
        on_device, mesh=mesh, in_specs=in_specs, out_specs=out_specs, check_vma=False
    )
```

```python
import functools
import types

import jax
import jax.numpy as jnp
from jax import lax
from jax.experimental import pallas as pl
from jax.experimental.pallas import tpu as pltpu
from jax.sharding import PartitionSpec as P

HEADS = 6
HEAD_DIM = 64
KERNEL = 9
GROUPS = 2


TILE = 256
NEG = -1000000000.0
LANES = 128
HEADS_HERE = HEADS // 2


def rows_nt(left, right):
    return lax.dot_general(
        left, right, (((1,), (1,)), ((), ())), preferred_element_type=jnp.float32
    )


def lane_half(block, upper):
    lane = lax.broadcasted_iota(jnp.int32, block.shape, 1)
    keep = lane >= HEAD_DIM if upper else lane < HEAD_DIM
    return jnp.where(keep, block, jnp.zeros_like(block))


def same_document(segk_ref, segq_ref, j):
    cols = pl.ds(pl.multiple_of(j * TILE, TILE), TILE)
    row = segk_ref[0:1, cols]
    column = jnp.broadcast_to(row, (LANES, TILE)).T
    wide = jnp.concatenate([column] * (TILE // LANES), axis=1)
    return wide == segq_ref[0:1, :]


def load_queries(q_ref, qm_ref):
    scale = jnp.asarray(HEAD_DIM ** (-0.5), q_ref.dtype)
    first = q_ref[:, 0:LANES] * scale
    qm_ref[0] = lane_half(first, False)
    qm_ref[1] = lane_half(first, True)
    qm_ref[2] = lane_half(q_ref[:, LANES : 2 * LANES] * scale, False)


KEY_GROUP = (0, 0, 1)
VALUE_GROUP = (2, 2, 1)


def lane_group(group):
    return slice(group * LANES, (group + 1) * LANES)


def attend_kernel(bounds, q_ref, kv_ref, segk_ref, segq_ref, out_ref, outt_ref, lse_ref,
                  qm_ref, m_ref, l_ref, acc_ref):
    tile = pl.program_id(0)
    load_queries(q_ref, qm_ref)
    m_ref[...] = jnp.full_like(m_ref, -jnp.inf)
    l_ref[...] = jnp.zeros_like(l_ref)
    acc_ref[...] = jnp.zeros_like(acc_ref)

    def step(j, carry):
        rows = pl.ds(pl.multiple_of(j * TILE, TILE), TILE)
        same = same_document(segk_ref, segq_ref, j)
        values_t = kv_ref[rows, LANES : 3 * LANES].T
        value_rows = (2 * HEAD_DIM, 3 * HEAD_DIM, HEAD_DIM)
        raw = [
            rows_nt(kv_ref[rows, lane_group(KEY_GROUP[head])], qm_ref[head])
            for head in range(HEADS_HERE)
        ]
        highs, alphas = [], []
        for head in range(HEADS_HERE):
            scores = jnp.where(same, raw[head], NEG)
            old = m_ref[head : head + 1, :]
            top = jnp.maximum(old, jnp.max(scores, axis=0, keepdims=True))
            expo = jnp.exp(scores - top)
            alpha = jnp.exp(old - top)
            m_ref[head : head + 1, :] = top
            l_ref[head : head + 1, :] = l_ref[head : head + 1, :] * alpha + jnp.sum(
                expo, axis=0, keepdims=True
            )
            high = expo.astype(jnp.bfloat16)
            highs.append(high)
            alphas.append(alpha)
        for head in range(HEADS_HERE):
            span = slice(head * HEAD_DIM, (head + 1) * HEAD_DIM)
            vals = values_t[value_rows[head] : value_rows[head] + HEAD_DIM, :]
            acc_ref[span, :] = acc_ref[span, :] * alphas[head] + jnp.dot(
                vals, highs[head], preferred_element_type=jnp.float32
            )
        return carry

    lax.fori_loop(bounds[0, tile], bounds[1, tile], step, 0)
    lse_ref[...] = m_ref[...] + jnp.log(l_ref[...])
    used = HEADS_HERE * HEAD_DIM
    for head in range(HEADS_HERE):
        span = slice(head * HEAD_DIM, (head + 1) * HEAD_DIM)
        inv = 1.0 / l_ref[head : head + 1, :]
        acc_ref[span, :] = acc_ref[span, :] * inv
    outt_ref[...] = acc_ref[...]
    out_ref[...] = acc_ref[...].T.astype(jnp.bfloat16)


def attend(bounds, queries, window, seg_keys, seg_queries):
    rows, wide = queries.shape
    span, width = window.shape
    return pl.pallas_call(
        attend_kernel,
        grid_spec=pltpu.PrefetchScalarGridSpec(
            num_scalar_prefetch=1,
            grid=(rows // TILE,),
            in_specs=[
                pl.BlockSpec((TILE, wide), lambda i, b: (i, 0)),
                pl.BlockSpec((span, width), lambda i, b: (0, 0)),
                pl.BlockSpec((1, span), lambda i, b: (0, 0)),
                pl.BlockSpec((1, TILE), lambda i, b: (0, i)),
            ],
            out_specs=[
                pl.BlockSpec((TILE, wide), lambda i, b: (i, 0)),
                pl.BlockSpec((wide, TILE), lambda i, b: (0, i)),
                pl.BlockSpec((8, TILE), lambda i, b: (0, i)),
            ],
            scratch_shapes=[
                pltpu.VMEM((HEADS_HERE, TILE, LANES), jnp.bfloat16),
                pltpu.VMEM((8, TILE), jnp.float32),
                pltpu.VMEM((8, TILE), jnp.float32),
                pltpu.VMEM((wide, TILE), jnp.float32),
            ],
        ),
        out_shape=[
            jax.ShapeDtypeStruct((rows, wide), jnp.bfloat16),
            jax.ShapeDtypeStruct((wide, rows), jnp.float32),
            jax.ShapeDtypeStruct((8, rows), jnp.float32),
        ],
        compiler_params=pltpu.CompilerParams(vmem_limit_bytes=63 * 2**20),
        name="attend",
    )(bounds, queries, window, seg_keys, seg_queries)


def attend_back_kernel(bounds, q_ref, kv_ref, segk_ref, segq_ref, grad_ref, outt_ref, lse_ref,
                       dq_ref, dkv_ref, qm_ref, gm_ref, delta_ref, dq_acc, dkv_acc):
    tile = pl.program_id(0)

    @pl.when(tile == 0)
    def _():
        dkv_acc[...] = jnp.zeros_like(dkv_acc)

    load_queries(q_ref, qm_ref)
    gm_ref[0] = lane_half(grad_ref[:, 0:LANES], False)
    gm_ref[1] = lane_half(grad_ref[:, 0:LANES], True)
    gm_ref[2] = lane_half(grad_ref[:, LANES : 2 * LANES], True)
    grads_t = grad_ref[...].astype(jnp.float32).T
    grad_rows = (0, HEAD_DIM, 3 * HEAD_DIM)
    for head in range(HEADS_HERE):
        span = slice(head * HEAD_DIM, (head + 1) * HEAD_DIM)
        delta_ref[head : head + 1, :] = jnp.sum(
            grads_t[grad_rows[head] : grad_rows[head] + HEAD_DIM, :] * outt_ref[span, :],
            axis=0, keepdims=True,
        )
    dq_acc[...] = jnp.zeros_like(dq_acc)

    def step(j, carry):
        rows = pl.ds(pl.multiple_of(j * TILE, TILE), TILE)
        same = same_document(segk_ref, segq_ref, j)
        keys_t = kv_ref[rows, 0 : 2 * LANES].T
        sums = [dkv_acc[rows, lane_group(g)] for g in range(3)]
        raw = [
            rows_nt(kv_ref[rows, lane_group(KEY_GROUP[head])], qm_ref[head])
            for head in range(HEADS_HERE)
        ]
        draw = [
            rows_nt(kv_ref[rows, lane_group(VALUE_GROUP[head])], gm_ref[head])
            for head in range(HEADS_HERE)
        ]
        ps, dss = [], []
        for head in range(HEADS_HERE):
            probs = jnp.where(same, jnp.exp(raw[head] - lse_ref[head : head + 1, :]), 0.0)
            dss.append((probs * (draw[head] - delta_ref[head : head + 1, :])).astype(jnp.bfloat16))
            ps.append(probs.astype(jnp.bfloat16))
        for head in range(HEADS_HERE):
            span = slice(head * HEAD_DIM, (head + 1) * HEAD_DIM)
            dq_acc[span, :] += jnp.dot(
                keys_t[span, :], dss[head], preferred_element_type=jnp.float32
            )
            sums[KEY_GROUP[head]] += jnp.dot(
                dss[head], qm_ref[head], preferred_element_type=jnp.float32
            )
            sums[VALUE_GROUP[head]] += jnp.dot(
                ps[head], gm_ref[head], preferred_element_type=jnp.float32
            )
        for g in range(3):
            dkv_acc[rows, lane_group(g)] = sums[g]
        return carry

    lax.fori_loop(bounds[0, tile], bounds[1, tile], step, 0)
    dq_ref[...] = (dq_acc[...].T * HEAD_DIM ** (-0.5)).astype(dq_ref.dtype)

    @pl.when(tile == pl.num_programs(0) - 1)
    def _():
        dkv_ref[...] = dkv_acc[...].astype(dkv_ref.dtype)


def attend_back(bounds, queries, window, seg_keys, seg_queries, grads, outt, lse):
    rows, wide = queries.shape
    span, width = window.shape
    return pl.pallas_call(
        attend_back_kernel,
        grid_spec=pltpu.PrefetchScalarGridSpec(
            num_scalar_prefetch=1,
            grid=(rows // TILE,),
            in_specs=[
                pl.BlockSpec((TILE, wide), lambda i, b: (i, 0)),
                pl.BlockSpec((span, width), lambda i, b: (0, 0)),
                pl.BlockSpec((1, span), lambda i, b: (0, 0)),
                pl.BlockSpec((1, TILE), lambda i, b: (0, i)),
                pl.BlockSpec((TILE, wide), lambda i, b: (i, 0)),
                pl.BlockSpec((wide, TILE), lambda i, b: (0, i)),
                pl.BlockSpec((8, TILE), lambda i, b: (0, i)),
            ],
            out_specs=[
                pl.BlockSpec((TILE, wide), lambda i, b: (i, 0)),
                pl.BlockSpec((span, width), lambda i, b: (0, 0)),
            ],
            scratch_shapes=[
                pltpu.VMEM((HEADS_HERE, TILE, LANES), jnp.bfloat16),
                pltpu.VMEM((HEADS_HERE, TILE, LANES), jnp.bfloat16),
                pltpu.VMEM((8, TILE), jnp.float32),
                pltpu.VMEM((wide, TILE), jnp.float32),
                pltpu.VMEM((span, width), jnp.float32),
            ],
        ),
        out_shape=[
            jax.ShapeDtypeStruct((rows, wide), jnp.bfloat16),
            jax.ShapeDtypeStruct((span, width), jnp.bfloat16),
        ],
        compiler_params=pltpu.CompilerParams(vmem_limit_bytes=63 * 2**20),
        name="attend_back",
    )(bounds, queries, window, seg_keys, seg_queries, grads, outt, lse)


def rolled(part):
    return jnp.concatenate([part[..., HEAD_DIM:], part[..., :HEAD_DIM]], axis=-1)


def joined_halves(lower, upper):
    return jnp.concatenate([lower[..., :HEAD_DIM], upper[..., HEAD_DIM:]], axis=-1)


def lanes_of(values):
    return [values[..., lane_group(g)] for g in range(3)]


def parts_of_queries(queries, upper):
    one, two, three = lanes_of(queries)
    swapped = rolled(two)
    first, second = (swapped, two) if upper else (two, swapped)
    return jnp.stack(
        [jnp.concatenate([one, first], axis=-1), jnp.concatenate([three, second], axis=-1)], axis=1
    ).reshape(TEAM, queries.shape[1], 2 * LANES)


def parts_of_keys(keys, values):
    k = lanes_of(keys)
    v = lanes_of(values)
    low = jnp.concatenate([k[0], joined_halves(k[1], rolled(v[1])), v[0]], axis=-1)
    high = jnp.concatenate([k[2], joined_halves(rolled(k[1]), v[1]), v[2]], axis=-1)
    return jnp.stack([low, high], axis=1).reshape(TEAM, keys.shape[1], 3 * LANES)


def natural_rows(parts):
    pairs = parts.reshape(TEAM // 2, 2, parts.shape[1], 2 * LANES)
    low, high = pairs[:, 0], pairs[:, 1]
    middle = joined_halves(low[..., LANES:], rolled(high[..., LANES:]))
    return jnp.concatenate([low[..., :LANES], middle, high[..., :LANES]], axis=-1)


def natural_keys(parts):
    pairs = parts.reshape(TEAM // 2, 2, parts.shape[1], 3 * LANES)
    low, high = lanes_of(pairs[:, 0]), lanes_of(pairs[:, 1])
    keys = jnp.concatenate([low[0], joined_halves(low[1], rolled(high[1])), high[0]], axis=-1)
    values = jnp.concatenate([low[2], joined_halves(rolled(low[1]), high[1]), high[2]], axis=-1)
    return keys, values


TEAM = 4


def flip(index, step):
    return index + step * (1 - 2 * lax.rem(lax.div(index, step), 2))


def mate(rank, offset):
    if offset % 2:
        rank = flip(rank, 1)
    if offset // 2:
        rank = flip(rank, 2)
    return rank


def greet(peers):
    barrier = pltpu.get_barrier_semaphore()
    for peer in peers:
        pl.semaphore_signal(
            barrier, inc=1, device_id=peer, device_id_type=pl.DeviceIdType.MESH
        )
    pl.semaphore_wait(barrier, len(peers))


def remote(src, dst, send, recv, peer):
    return pltpu.make_async_remote_copy(
        src_ref=src,
        dst_ref=dst,
        send_sem=send,
        recv_sem=recv,
        device_id=peer,
        device_id_type=pl.DeviceIdType.MESH,
    )


RIM = 16
SMALL_ROWS = 128
SMALL_IN = 128
ROW_IN_KERNEL_W = 32
ROW_PAIR_QV, ROW_PAIR_PC, ROW_IN_KERNEL_B = 19, 20, 21
ROW_OUTPUT_B, ROW_GAIN1, ROW_SHIFT1, ROW_OUTER_B, ROW_GAIN2, ROW_SHIFT2 = range(9, 15)
ROW_INNER_B = 15
ROW_QUERY_B, ROW_VALUE_B, ROW_POINT_B, ROW_CONV_B = range(19, 23)
ROW_KERNEL_B = 24
ROW_KERNEL_W = 48
TAP_ROWS = 8 * KERNEL


def dot(left, right):
    return jnp.dot(left, right, preferred_element_type=jnp.float32)


def dot_tn(left, right):
    return lax.dot_general(
        left, right, (((0,), (0,)), ((), ())), preferred_element_type=jnp.float32
    )


def half_turn(block):
    return pltpu.roll(block, HEAD_DIM, axis=1)


def mixed_lanes(lower, upper):
    lane = lax.broadcasted_iota(jnp.int32, lower.shape, 1)
    return jnp.where(lane < HEAD_DIM, lower, upper)


def pair_row(small_ref, row, second):
    first = jnp.broadcast_to(small_ref[0, row : row + 1, :], (8, 384))
    other = jnp.broadcast_to(small_ref[1, row : row + 1, :], (8, 384))
    lane = lax.broadcasted_iota(jnp.int32, first.shape, 1)
    if second:
        first = pltpu.roll(first, 192, axis=1)
    else:
        other = pltpu.roll(other, 192, axis=1)
    return jnp.where(lane < 192, first, other)[0:1, :]


def tap_major(shape, offset):
    row = lax.broadcasted_iota(jnp.int32, shape, 0)
    column = lax.broadcasted_iota(jnp.int32, shape, 1) + offset
    head = lax.rem(row, 8)
    wanted = (head * KERNEL + lax.div(row, 8) == column) & (head < HEADS)
    return wanted & (row < TAP_ROWS)


def kernel_rows(first, other):
    lane = lax.broadcasted_iota(jnp.int32, first.shape, 1)
    rows = jnp.where(lane < 192, first, pltpu.roll(other, 192, axis=1))
    return jnp.concatenate(
        [rows, jnp.zeros((LANES - TAP_ROWS, rows.shape[1]), jnp.float32)], axis=0
    ).astype(jnp.bfloat16)


def kernel_bias(small_ref):
    half = HEADS * KERNEL // 2
    total = jnp.zeros((LANES, 1), jnp.float32)
    for w in range(2):
        row = small_ref[w, ROW_IN_KERNEL_B : ROW_IN_KERNEL_B + 1, 0:LANES]
        lane = lax.broadcasted_iota(jnp.int32, (LANES, LANES), 1)
        wanted = tap_major((LANES, LANES), w * half) & (lane < half)
        total = total + jnp.sum(jnp.where(wanted, row, 0.0), axis=1, keepdims=True)
    return total


def rows_of(ref, base, count):
    view = pl.ds(pl.multiple_of(base, 16), count)
    return ref.at[:, view, :] if len(ref.shape) == 3 else ref.at[view, :]


CHUNKS = 4


def front_kernel(count, *refs):
    x_ref, seg_ref, mask_ref, depth_in, kernel_in, kernel_b_in = refs[:6]
    vectors, pairs = refs[6:13], refs[13:17]
    shards = list(refs[17 : 16 + count])
    outer_any = refs[16 + count]
    rest = refs[17 + count :]
    outs = rest[: count + 9]
    half_any = rest[count + 9]
    win_ref, qteam_ref = outs[count : count + 2]
    holds = rest[count + 10 : 2 * count + 17]
    fulls = holds[:count]
    queries_ref, xrim_ref, depth_ref, spans_ref, kern_ref, ext_ref, conv_ref = holds[count:]
    (kv_part, q_part, seg_col, halo_low, halo_high, spread_ref, taps_ref, wide_ref,
     send_y, recv_y, send_c, recv_c, local, send_h, recv_h, send_kv, recv_kv, send_q, recv_q,
     send_l, recv_l, send_r, recv_r, emit_sem, small_f32, small_own, outer_half, half_sem) = rest[
        2 * count + 17 :
    ]
    shards.insert(2, small_own)
    key_ref, value_ref, small2d, query_ref, point_ref, convw_ref = fulls[:6]
    me, side = lax.axis_index("ctx"), lax.axis_index("wsh")
    size = lax.axis_size("ctx")
    core = lax.rem(me, 2)
    rank = lax.rem(me, TEAM)
    chip = lax.div(rank, 2)
    base = me - rank
    team = lax.div(me, TEAM)
    teams = size // TEAM
    right, left = lax.rem(me + TEAM, size), lax.rem(me + size - TEAM, size)
    after, prior = lax.rem(me + 1, size), lax.rem(me + size - 1, size)
    twin, across = {"ctx": flip(me, 1)}, {"wsh": 1 - side}
    seqs, block, model = x_ref.shape
    halo = (TEAM - 1) * block
    width = HEADS * HEAD_DIM
    chunk_rows = block // CHUNKS
    greet(
        [{"ctx": base + mate(rank, o)} for o in range(1, TEAM)]
        + [across, {"ctx": right}, {"ctx": left}, {"ctx": after}, {"ctx": prior}]
    )

    to_y, passed, own, emitted = [], [], [], []
    for i in range(count):
        rows = shards[i].shape[-2]
        to_y.append(
            remote(
                rows_of(shards[i], core * (rows // 2), rows // 2),
                rows_of(fulls[i], side * rows + core * (rows // 2), rows // 2),
                send_y.at[i], recv_y.at[i], across,
            )
        )
        came = rows_of(fulls[i], (1 - side) * rows + core * (rows // 2), rows // 2)
        passed.append(remote(came, came, send_c.at[i], recv_c.at[i], twin))
        own.append(
            pltpu.make_async_copy(shards[i], rows_of(fulls[i], side * rows, rows), local.at[i])
        )

    def emit(hold, out):
        copy = pltpu.make_async_copy(hold, out, emit_sem.at[len(emitted)])
        copy.start()
        emitted.append(copy)

    def emit_named(k):
        emit(holds[count + k], outs[count + 2 + k])

    urgent = 3
    for i in range(2):
        to_y[i].start()
    for i in range(2):
        own[i].start()
    half_rows = outer_half.shape[1]
    load_half = pltpu.make_async_copy(
        outer_any.at[:, part_rows(core * half_rows, half_rows), :], outer_half, half_sem.at[0]
    )
    load_half.start()
    small_f32[...] = jnp.zeros_like(small_f32)
    small_f32[0:KERNEL, :] = depth_in[...].astype(jnp.float32)

    def as_row(ref):
        return ref[...].astype(jnp.float32).reshape(1, ref.shape[0])

    at = KERNEL
    for ref in vectors:
        row = as_row(ref)
        for k in range(ref.shape[0] // 384):
            small_f32[at : at + 1, :] = row[:, k * 384 : (k + 1) * 384]
            at += 1
    for k in range(2):
        small_f32[at : at + 1, 0:192] = as_row(pairs[2 * k])
        small_f32[at : at + 1, 192:384] = as_row(pairs[2 * k + 1])
        at += 1
    small_f32[at : at + 1, 0 : kernel_b_in.shape[0]] = as_row(kernel_b_in)
    pick = jnp.where(tap_major((LANES, HEADS * KERNEL), 0), 1.0, 0.0).astype(jnp.bfloat16)
    small_f32[ROW_IN_KERNEL_W : ROW_IN_KERNEL_W + TAP_ROWS, 0:192] = dot(pick, kernel_in[...])[
        0:TAP_ROWS, :
    ]
    small_own[...] = small_f32[...].astype(jnp.bfloat16)
    to_y[2].start()
    own[2].start()
    to_after = remote(x_ref.at[:, pl.ds(block - RIM, RIM), :], halo_low, send_h.at[0],
                      recv_h.at[0], {"ctx": after})
    to_prior = remote(x_ref.at[:, pl.ds(0, RIM), :], halo_high, send_h.at[1], recv_h.at[1],
                      {"ctx": prior})
    pl.when(me < size - 1)(to_after.start)
    pl.when(me > 0)(to_prior.start)
    to_y[urgent].start()
    own[urgent].start()

    @pl.when(me == 0)
    def _():
        halo_low[...] = jnp.zeros_like(halo_low)

    @pl.when(me == size - 1)
    def _():
        halo_high[...] = jnp.zeros_like(halo_high)

    for s in range(seqs):
        seg_col[s] = jnp.broadcast_to(seg_ref[s : s + 1, :], (LANES, seg_ref.shape[1])).T
        for g in range(model // LANES):
            xrim_ref[s, g, pl.ds(RIM, block), :] = x_ref[s, :, lane_group(g)].astype(jnp.float32)

    def arrive(i):
        to_y[i].wait_recv()
        passed[i].start()

    def settle(i):
        own[i].wait()
        passed[i].wait_recv()
        emit(fulls[i], outs[i])

    for i in range(urgent):
        arrive(i)
    for i in (4, 5, 6, 7):
        to_y[i].start()
        own[i].start()
    for i in range(urgent):
        settle(i)
    small_ref = taps_ref
    for w in range(2):
        small_ref[w] = small2d[pl.ds(w * SMALL_IN, SMALL_IN), :].astype(jnp.float32)
    value_bias = pair_row(small_ref, ROW_PAIR_QV, True)
    query_bias = pair_row(small_ref, ROW_PAIR_QV, False)

    def piece(r, c):
        return win_ref.at[
            pl.ds(pl.multiple_of(halo + r * block + c * chunk_rows, 16), chunk_rows), :
        ]

    def part(r, c):
        return kv_part.at[r, pl.ds(c * chunk_rows, chunk_rows), :]

    def kv_copy(r, c):
        return (
            pltpu.make_async_copy(part(r, c), piece(rank, c), recv_kv.at[rank * CHUNKS + c]),
            remote(part(r, c), piece(rank, c), send_kv.at[r * CHUNKS + c],
                   recv_kv.at[rank * CHUNKS + c], {"ctx": base + r}),
        )

    def q_copy(r):
        return (
            pltpu.make_async_copy(q_part.at[r], qteam_ref.at[rank], recv_q.at[rank]),
            remote(q_part.at[r], qteam_ref.at[rank], send_q.at[r], recv_q.at[rank],
                   {"ctx": base + r}),
        )

    def begin(pair, r):
        pl.when(rank == r)(pair[0].start)
        pl.when(rank != r)(pair[1].start)

    for s in (1 - chip, chip):
        rows = x_ref[s]
        keys = dot(rows, key_ref[...])
        values = dot(rows, value_ref[...]) + value_bias
        k = [keys[:, lane_group(g)] for g in range(3)]
        v = [values[:, lane_group(g)] for g in range(3)]
        for half, groups in enumerate((
            (k[0], mixed_lanes(k[1], half_turn(v[1])), v[0]),
            (k[2], mixed_lanes(half_turn(k[1]), v[1]), v[2]),
        )):
            for g in range(3):
                kv_part[2 * s + half, :, lane_group(g)] = groups[g].astype(jnp.bfloat16)
        for c in range(CHUNKS):
            for half in range(2):
                begin(kv_copy(2 * s + half, c), 2 * s + half)

    def onward(r, c):
        to_right = remote(
            piece(r, c),
            win_ref.at[
                pl.ds(pl.multiple_of(lax.rem(r + TEAM - 1, TEAM) * block + c * chunk_rows, 16),
                      chunk_rows), :
            ],
            send_r.at[r * CHUNKS + c], recv_r.at[r * CHUNKS + c], {"ctx": right},
        )
        to_left = remote(
            piece(r, c),
            win_ref.at[
                pl.ds(
                    pl.multiple_of(
                        halo + TEAM * block + lax.rem(r, TEAM - 1) * block + c * chunk_rows, 16
                    ),
                    chunk_rows,
                ), :
            ],
            send_l.at[r * CHUNKS + c], recv_l.at[r * CHUNKS + c], {"ctx": left},
        )
        return to_right, to_left

    def relay(o, c):
        r = mate(rank, o)
        if o == 0:
            kv_copy(r, c)[0].wait()
        else:
            remote(part(rank, c), piece(r, c), send_kv.at[rank * CHUNKS + c],
                   recv_kv.at[r * CHUNKS + c], {"ctx": base + r}).wait_recv()
        to_right, to_left = onward(r, c)
        pl.when((r >= 1) & (team < teams - 1))(to_right.start)
        pl.when((r <= TEAM - 2) & (team > 0))(to_left.start)

    for c in range(CHUNKS):
        relay(0, c)
        relay(1, c)
    arrive(urgent)
    settle(urgent)
    for s in range(seqs):
        queries = dot(x_ref[s], query_ref[...]) + query_bias
        queries_ref[s] = queries.astype(jnp.bfloat16)
        q = [queries[:, lane_group(g)] for g in range(3)]
        for half, groups in enumerate(((q[0], q[1]), (q[2], half_turn(q[1])))):
            for g in range(2):
                q_part[2 * s + half, :, lane_group(g)] = groups[g].astype(jnp.bfloat16)
        for half in range(2):
            begin(q_copy(2 * s + half), 2 * s + half)
    emit_named(0)

    pl.when(me > 0)(to_after.wait_recv)
    pl.when(me < size - 1)(to_prior.wait_recv)
    for s in range(seqs):
        for g in range(model // LANES):
            xrim_ref[s, g, pl.ds(0, RIM), :] = halo_low[s, :, lane_group(g)].astype(jnp.float32)
            xrim_ref[s, g, pl.ds(RIM + block, RIM), :] = halo_high[s, :, lane_group(g)].astype(
                jnp.float32
            )
    emit_named(1)
    strip = 32
    lead = RIM - KERNEL // 2

    def taps_row(j, g):
        return small_ref[g // 3, j : j + 1, lane_group(g % 3)]

    def depth_strip(c, s):
        start = c * strip
        here = seg_col[s, pl.ds(RIM + start, strip), :]
        sums = [jnp.zeros((strip, LANES), jnp.float32) for _ in range(model // LANES)]
        for j in range(KERNEL):
            same = seg_col[s, pl.ds(lead + j + start, strip), :] == here
            for g in range(model // LANES):
                near = xrim_ref[s, g, pl.ds(lead + j + start, strip), :]
                sums[g] = sums[g] + jnp.where(same, near, 0.0) * taps_row(j, g)
        for g in range(model // LANES):
            depth_ref[s, pl.ds(pl.multiple_of(start, strip), strip), lane_group(g)] = sums[
                g
            ].astype(jnp.bfloat16)
        return s

    relay(2, 0)
    relay(3, 0)
    lax.fori_loop(0, block // strip, depth_strip, 0)
    relay(2, 1)
    relay(3, 1)
    lax.fori_loop(0, block // strip, depth_strip, 1)
    emit_named(2)
    for c in range(2, CHUNKS):
        relay(2, c)
        relay(3, c)
    for j in range(KERNEL):
        row = lax.broadcasted_iota(jnp.int32, (2 * LANES, width), 0)
        col = lax.broadcasted_iota(jnp.int32, (2 * LANES, width), 1)
        row = jnp.where(row >= LANES, row - LANES, row)
        spread_ref[j] = jnp.where(row == 8 * j + col // HEAD_DIM, 1.0, 0.0).astype(jnp.bfloat16)
    for i in (4, 5):
        arrive(i)
    for i in (4, 5):
        settle(i)
    load_half.wait()
    emit(outer_half, half_any)
    point_bias = pair_row(small_ref, ROW_PAIR_PC, False)
    conv_bias = pair_row(small_ref, ROW_PAIR_PC, True)
    tap_view = slice(ROW_IN_KERNEL_W, ROW_IN_KERNEL_W + TAP_ROWS)
    kernel_w = kernel_rows(small_ref[0, tap_view, :], small_ref[1, tap_view, :])
    kernel_b = kernel_bias(small_ref)
    for s in range(seqs):
        spans = dot(depth_ref[s], point_ref[...]) + point_bias
        spans_ref[s] = spans
        mixed = (spans * queries_ref[s].astype(jnp.float32)).astype(jnp.bfloat16)
        logits = rows_nt(kernel_w, mixed) + kernel_b
        cut = [logits[8 * j : 8 * j + 8, :] for j in range(KERNEL)]
        top = functools.reduce(jnp.maximum, cut)
        expo = [jnp.exp(part - top) for part in cut]
        inverse = 1.0 / sum(expo)
        for j in range(KERNEL):
            kern = expo[j] * inverse
            kern_ref[s, 8 * j : 8 * j + 8, :] = kern
            wide_ref[8 * j : 8 * j + 8, :] = kern * mask_ref[s, j : j + 1, :]
        wide_ref[TAP_ROWS:, :] = jnp.zeros((LANES - TAP_ROWS, block), jnp.float32)
        tall = wide_ref[...].T
        high = tall.astype(jnp.bfloat16)
        low = (tall - high.astype(jnp.float32)).astype(jnp.bfloat16)
        both = jnp.concatenate([high, low], axis=1)
        for g in range(3):
            row_ext = [xrim_ref[s, k] for k in range(model // LANES)]
        ext = dot(
            jnp.concatenate([part.astype(jnp.bfloat16) for part in row_ext], axis=1),
            convw_ref[...],
        ) + conv_bias
        for g in range(3):
            ext_ref[s, g] = ext[:, lane_group(g)]
        chunk = 128
        for c in range(block // chunk):
            sums = [jnp.zeros((chunk, LANES), jnp.float32) for _ in range(3)]
            for j in range(KERNEL):
                weight = dot(both[c * chunk : (c + 1) * chunk, :], spread_ref[j])
                for g in range(3):
                    near = ext_ref[s, g, pl.ds(lead + j + c * chunk, chunk), :]
                    sums[g] = sums[g] + weight[:, lane_group(g)] * near
            for g in range(3):
                conv_ref[s, pl.ds(c * chunk, chunk), lane_group(g)] = sums[g].astype(jnp.bfloat16)

    for k in range(3, 7):
        emit_named(k)
    for i in (6, 7):
        arrive(i)
    for i in (6, 7):
        settle(i)
    for r in range(TEAM):
        for c in range(CHUNKS):
            pl.when(rank != r)(kv_copy(r, c)[1].wait_send)
        pl.when(rank != r)(q_copy(r)[1].wait_send)
    for o in range(TEAM):
        r = mate(rank, o)
        if o == 0:
            q_copy(r)[0].wait()
        else:
            remote(q_part.at[rank], qteam_ref.at[r], send_q.at[rank], recv_q.at[r],
                   {"ctx": base + r}).wait_recv()
    for r in range(TEAM):
        for c in range(CHUNKS):
            to_right, to_left = onward(jnp.int32(r), c)
            if r >= 1:
                pl.when(team < teams - 1)(to_right.wait_send)
                pl.when(team > 0)(to_right.wait_recv)
            if r <= TEAM - 2:
                pl.when(team > 0)(to_left.wait_send)
                pl.when(team < teams - 1)(to_left.wait_recv)
    for i in range(count):
        to_y[i].wait_send()
        passed[i].wait_send()
    pl.when(me < size - 1)(to_after.wait_send)
    pl.when(me > 0)(to_prior.wait_send)
    for copy in emitted:
        copy.wait()


def front(hidden, seg_rim, tap_mask, depth, kernel, kernel_b, vectors, pairs, shards, outer):
    seqs, block, model = hidden.shape
    small = jax.ShapeDtypeStruct((SMALL_IN, 384), hidden.dtype)
    gathered = list(shards[:2]) + [small] + list(shards[2:])
    count = len(gathered)
    half = jax.ShapeDtypeStruct((outer.shape[0], outer.shape[1] // 2, outer.shape[2]), outer.dtype)
    width = HEADS * HEAD_DIM
    wide = block + 2 * RIM
    fulls = [
        jax.ShapeDtypeStruct(s.shape[:-2] + (2 * s.shape[-2], s.shape[-1]), s.dtype) for s in gathered
    ]
    vmem = pl.BlockSpec(memory_space=pltpu.VMEM)
    anywhere = pl.BlockSpec(memory_space=pl.ANY)
    low, full = jnp.bfloat16, jnp.float32
    outs = [
        jax.ShapeDtypeStruct(((3 * TEAM - 2) * block, width), low),
        jax.ShapeDtypeStruct((TEAM, block, 2 * LANES), low),
        jax.ShapeDtypeStruct((seqs, block, width), low),
        jax.ShapeDtypeStruct((seqs, model // LANES, wide, LANES), full),
        jax.ShapeDtypeStruct((seqs, block, model), low),
        jax.ShapeDtypeStruct((seqs, block, width), full),
        jax.ShapeDtypeStruct((seqs, TAP_ROWS, block), full),
        jax.ShapeDtypeStruct((seqs, 3, wide, LANES), full),
        jax.ShapeDtypeStruct((seqs, block, width), low),
    ]
    dma = pltpu.SemaphoreType.DMA
    return pl.pallas_call(
        functools.partial(front_kernel, count),
        out_shape=fulls + outs + [half],
        in_specs=[vmem] * 17 + [anywhere] * count,
        out_specs=[anywhere] * (count + 10),
        scratch_shapes=[pltpu.VMEM(s.shape, s.dtype) for s in fulls + outs[2:]] + [
            pltpu.VMEM((TEAM, block, width), low),
            pltpu.VMEM((TEAM, block, 2 * LANES), low),
            pltpu.VMEM((seqs, seg_rim.shape[1], LANES), full),
            pltpu.VMEM((seqs, RIM, model), low),
            pltpu.VMEM((seqs, RIM, model), low),
            pltpu.VMEM((KERNEL, 2 * LANES, width), low),
            pltpu.VMEM((2, SMALL_IN, 384), full),
            pltpu.VMEM((LANES, block), full),
            dma((count,)), dma((count,)), dma((count,)), dma((count,)), dma((count,)),
            dma((2,)), dma((2,)),
            dma((TEAM * CHUNKS,)), dma((TEAM * CHUNKS,)), dma((TEAM,)), dma((TEAM,)),
            dma((TEAM * CHUNKS,)), dma((TEAM * CHUNKS,)), dma((TEAM * CHUNKS,)),
            dma((TEAM * CHUNKS,)), dma((count + 8,)),
            pltpu.VMEM((SMALL_IN, 384), full), pltpu.VMEM((SMALL_IN, 384), low),
            pltpu.VMEM(half.shape, low), dma((1,)),
        ],
        compiler_params=pltpu.CompilerParams(
            collective_id=0, has_side_effects=True, vmem_limit_bytes=56 * 2**20
        ),
        name="front",
    )(hidden, seg_rim, tap_mask, depth, kernel, kernel_b, *vectors, *pairs, *shards, outer)
PACK_A = 768
PACK_B = 1280
SMALL_AT = 1152


def chips_of(me, size):
    core = lax.rem(me, 2)
    count = size // 2
    index = lax.div(me, 2)
    return index, count, lambda other: other * 2 + core


def pair_of(me, size):
    index = lax.rem(lax.div(me, 2), 2)
    return index, 2, lambda other: flip(me, 2)


def column_of(me, size):
    index = lax.div(me, TEAM)
    rest = lax.rem(me, TEAM)
    return index, size // TEAM, lambda other: other * TEAM + rest


def part_rows(base, count):
    return pl.ds(pl.multiple_of(base, 16), count)


def others(index, count):
    return [lax.rem(index + o, count) for o in range(1, count)]


def scatter_copies(stage, me, size, staged, came, send, recv):
    index, count, device = stage(me, size)
    piece = staged.shape[0] // count
    return [
        remote(staged.at[part_rows(other * piece, piece), :], came.at[index], send.at[other],
               recv.at[index], {"ctx": device(other)})
        for other in others(index, count)
    ]


def scatter_wait(stage, me, size, staged, came, send, recv):
    index, count, device = stage(me, size)
    piece = staged.shape[0] // count
    for other in others(index, count):
        remote(staged.at[part_rows(index * piece, piece), :], came.at[other], send.at[index],
               recv.at[other], {"ctx": device(other)}).wait_recv()


def share_copies(stage, me, size, fin, base, piece, send, recv):
    index, count, device = stage(me, size)
    view = fin.at[part_rows(base + index * piece, piece), :]
    return [
        remote(view, view, send.at[other], recv.at[index], {"ctx": device(other)})
        for other in others(index, count)
    ]


def share_wait(stage, me, size, fin, base, piece, send, recv):
    index, count, device = stage(me, size)
    for other in others(index, count):
        view = fin.at[part_rows(base + other * piece, piece), :]
        remote(view, view, send.at[index], recv.at[other], {"ctx": device(other)}).wait_recv()


def in_chunks(rows, body):
    chunk = max(c for c in range(16, 241, 16) if rows % c == 0)

    def step(i, carry):
        body(pl.multiple_of(i * chunk, 16), chunk)
        return carry

    lax.fori_loop(0, rows // chunk, step, 0)


def wide(value):
    return value.astype(jnp.float32)


def back_kernel(names, a_names, b_names, loaded, *refs):
    count_a, count_b = len(a_names), len(b_names)
    r = types.SimpleNamespace(**dict(zip(names, refs)))
    late = refs[len(names) :]
    block_a = types.SimpleNamespace(**dict(zip(a_names, late[:count_a])))
    block_b = types.SimpleNamespace(**dict(zip(b_names, late[count_a : count_a + count_b])))
    fetch_refs = late[count_a + count_b :]
    v = types.SimpleNamespace(**dict(zip(loaded, fetch_refs[len(loaded) :])))
    me, side = lax.axis_index("ctx"), lax.axis_index("wsh")
    size = lax.axis_size("ctx")
    core = lax.rem(me, 2)
    rank = lax.rem(me, TEAM)
    chip = lax.div(rank, 2)
    base = me - rank
    team = lax.div(me, TEAM)
    teams = size // TEAM
    twin, across = {"ctx": flip(me, 1)}, {"wsh": 1 - side}
    right, left = lax.rem(me + TEAM, size), lax.rem(me + size - TEAM, size)
    after, prior = lax.rem(me + 1, size), lax.rem(me + size - 1, size)
    seqs, block, model = v.x.shape
    width = HEADS * HEAD_DIM
    halo = (TEAM - 1) * block
    groups = model // LANES
    low = jnp.bfloat16
    index, count, device = chips_of(me, size)
    greet(
        [twin, across, {"ctx": base + mate(rank, 3)}, {"ctx": after}, {"ctx": prior}]
        + [{"ctx": device(other)} for other in others(index, count)]
    )

    def block_of(k):
        return pl.ds(pl.multiple_of(k * block, 16), block)

    def halo_left(c):
        return remote(r.window.at[block_of(2 * TEAM - 1 + c), :], r.from_left.at[block_of(c), :],
                      r.send_l.at[c], r.recv_l.at[c], {"ctx": right})

    def halo_right(c):
        return remote(r.window.at[block_of(c), :], r.from_right.at[block_of(c + 1), :],
                      r.send_r.at[c], r.recv_r.at[c], {"ctx": left})

    for k in range(TEAM - 1):
        to_right = halo_left(chip * k + (1 - chip) * (TEAM - 2 - k))
        to_left = halo_right(chip * k + (1 - chip) * ((k + 1) % (TEAM - 1)))
        pl.when(team < teams - 1)(to_right.start)
        pl.when(team > 0)(to_left.start)

    fetched = types.SimpleNamespace()
    for k, name in enumerate(loaded):
        copy = pltpu.make_async_copy(fetch_refs[k], fetch_refs[len(loaded) + k], r.load.at[k])
        setattr(fetched, name, copy)
    center = pltpu.make_async_copy(r.window.at[pl.ds(halo, TEAM * block), :], r.mine,
                                   r.load.at[len(loaded)])
    fetched.keep.start()
    fetched.came.start()
    center.start()

    def q_copy(o):
        other = mate(rank, o)
        return remote(r.dq.at[other], r.q_parts.at[rank], r.send_q.at[o], r.recv_q.at[o],
                      {"ctx": base + other})

    own_q = pltpu.make_async_copy(r.dq.at[rank], r.q_parts.at[rank], r.recv_q.at[0])
    for o in (3, 2, 1):
        q_copy(o).start()
    own_q.start()
    for name in loaded[2:]:
        getattr(fetched, name).start()

    def have(*copies):
        for copy in copies:
            copy.wait()

    half_ff = v.keep.shape[1]
    pair_index, _, _ = pair_of(me, size)
    have(fetched.keep, fetched.came)

    def stage_across(at, n):
        rows = part_rows(at, n)
        r.ff_send[rows, :] = (v.keep[1 - side, rows, :] + wide(v.came[1 - side, rows, :])).astype(low)
        v.keep[side, rows, :] = v.keep[side, rows, :] + wide(v.came[side, rows, :])

    in_chunks(half_ff, stage_across)
    ff_across = remote(r.ff_send, r.ff_came, r.send_p.at[0], r.recv_p.at[0], across)
    ff_across.start()

    small = r.sums
    small[...] = jnp.zeros_like(small)
    for j in range(KERNEL):
        row = lax.broadcasted_iota(jnp.int32, (2 * LANES, width), 0)
        col = lax.broadcasted_iota(jnp.int32, (2 * LANES, width), 1)
        row = jnp.where(row >= LANES, row - LANES, row)
        r.spread[j] = jnp.where(row == 8 * j + col // HEAD_DIM, 1.0, 0.0).astype(low)

    zero_block = jnp.zeros((block, width), low)
    r.from_left[pl.ds((TEAM - 1) * block, block), :] = zero_block
    r.from_right[0:block, :] = zero_block

    @pl.when(team == 0)
    def _():
        for k in range(TEAM - 1):
            r.from_left[pl.ds(k * block, block), :] = zero_block

    @pl.when(team == teams - 1)
    def _():
        for k in range(1, TEAM):
            r.from_right[pl.ds(k * block, block), :] = zero_block

    @pl.when(me == 0)
    def _():
        r.dd_low[...] = jnp.zeros_like(r.dd_low)
        r.rim_low[...] = jnp.zeros_like(r.rim_low)

    @pl.when(me == size - 1)
    def _():
        r.dd_high[...] = jnp.zeros_like(r.dd_high)
        r.rim_high[...] = jnp.zeros_like(r.rim_high)

    small_ref = r.small
    kernel_w = kernel_rows(
        wide(small_ref[ROW_IN_KERNEL_W : ROW_IN_KERNEL_W + TAP_ROWS, :]),
        wide(small_ref[SMALL_IN + ROW_IN_KERNEL_W : SMALL_IN + ROW_IN_KERNEL_W + TAP_ROWS, :]),
    )
    lead = RIM - KERNEL // 2
    chunk = 128
    r.d_ext[...] = jnp.zeros_like(r.d_ext)
    have(fetched.dconv, fetched.ext, fetched.kern, fetched.point, fetched.queries, fetched.spans)
    wide_ref, tall_ref = r.wide, r.tall

    def conv_back(s):
        r.seg_col[s] = jnp.broadcast_to(r.seg[s : s + 1, :], (LANES, r.seg.shape[1])).T
        for j in range(KERNEL):
            wide_ref[8 * j : 8 * j + 8, :] = (
                v.kern[s, 8 * j : 8 * j + 8, :] * r.mask[s, j : j + 1, :]
            )
        wide_ref[TAP_ROWS:, :] = jnp.zeros((LANES - TAP_ROWS, block), jnp.float32)
        tall = wide_ref[...].T
        high = tall.astype(low)
        both = jnp.concatenate([high, (tall - wide(high)).astype(low)], axis=1)
        for c in range(block // chunk):
            rows = slice(c * chunk, (c + 1) * chunk)
            grad = wide(v.dconv[s, rows, :])
            taps = jnp.zeros((chunk, LANES), jnp.float32)
            for j in range(KERNEL):
                near = jnp.concatenate(
                    [v.ext[s, g, pl.ds(lead + j + c * chunk, chunk), :] for g in range(3)],
                    axis=1,
                )
                term = near * grad
                first = term.astype(low)
                second = (term - wide(first)).astype(low)
                taps = taps + rows_nt(first, r.spread[j, 0:LANES, :])
                taps = taps + rows_nt(second, r.spread[j, 0:LANES, :])
                weight = dot(both[rows, :], r.spread[j]) * grad
                for g in range(3):
                    r.d_ext[s, g, pl.ds(lead + j + c * chunk, chunk), :] += weight[
                        :, lane_group(g)
                    ]
            tall_ref[rows, :] = taps
        back = tall_ref[...].T
        inner = jnp.zeros((8, block), jnp.float32)
        for j in range(KERNEL):
            inner = inner + v.kern[s, 8 * j : 8 * j + 8, :] * (
                back[8 * j : 8 * j + 8, :] * r.mask[s, j : j + 1, :]
            )
        for j in range(KERNEL):
            wide_ref[8 * j : 8 * j + 8, :] = v.kern[s, 8 * j : 8 * j + 8, :] * (
                back[8 * j : 8 * j + 8, :] * r.mask[s, j : j + 1, :] - inner
            )
        d_logits = wide_ref[0:TAP_ROWS, :].astype(low)
        mixed = (v.spans[s] * wide(v.queries[s])).astype(low)
        kernel_grad = dot(d_logits, mixed)
        kernel_bias = dot(d_logits, jnp.ones((block, LANES), low))
        for w in range(2):
            small[w, ROW_KERNEL_W : ROW_KERNEL_W + TAP_ROWS, :] += kernel_grad
            for g in range(3):
                small[w, ROW_KERNEL_B : ROW_KERNEL_B + 24, lane_group(g)] += kernel_bias[
                    24 * g : 24 * g + 24, :
                ]
        d_mixed = dot(wide_ref[...].T.astype(low), kernel_w)
        d_spans = (d_mixed * wide(v.queries[s])).astype(low)
        v.spans[s] = d_mixed * v.spans[s]
        v.dconv[s] = d_spans
        bias = jnp.sum(wide(d_spans), axis=0, keepdims=True)
        for w in range(2):
            small[w, ROW_POINT_B : ROW_POINT_B + 1, :] += bias
        d_depth = rows_nt(d_spans, v.point[...])
        for g in range(groups):
            r.dd[s, g, pl.ds(RIM, block), :] = d_depth[:, lane_group(g)]
        r.dd_first[s] = d_depth[0:RIM, :].astype(low)
        r.dd_last[s] = d_depth[block - RIM : block, :].astype(low)
        for g in range(3):
            r.rim_first[s, :, lane_group(g)] = r.d_ext[s, g, 0:RIM, :].astype(low)
            r.rim_last[s, :, lane_group(g)] = r.d_ext[
                s, g, RIM + block : 2 * RIM + block, :
            ].astype(low)


    def kv_copy(k):
        return (
            pltpu.make_async_copy(r.mine.at[block_of(k), :], r.kv_parts.at[rank], r.recv_kv.at[rank]),
            remote(r.mine.at[block_of(k), :], r.kv_parts.at[rank], r.send_kv.at[k],
                   r.recv_kv.at[rank], {"ctx": base + k}),
        )

    def return_block(k):
        pl.when((k <= TEAM - 2) & (team > 0))(lambda: halo_left(lax.rem(k, TEAM - 1)).wait_recv())
        pl.when((k >= 1) & (team < teams - 1))(
            lambda: halo_right(lax.rem(k + TEAM - 2, TEAM - 1)).wait_recv()
        )
        rows = block_of(k)
        r.mine[rows, :] = (
            wide(r.mine[rows, :]) + wide(r.from_left[rows, :]) + wide(r.from_right[rows, :])
        ).astype(low)
        pair = kv_copy(k)
        pl.when(k == rank)(pair[0].start)
        pl.when(k != rank)(pair[1].start)


    ff_base = core * (2 * half_ff) + pair_index * half_ff
    column_index, column_count, _ = column_of(me, size)
    column_piece = half_ff // column_count
    column_args = (column_of, me, size, r.ff_send, r.ff_column, r.send_c, r.recv_c)
    column_share = (column_of, me, size, r.fin_ff, ff_base, column_piece, r.send_cg, r.recv_cg)
    pair_share = (pair_of, me, size, r.fin_ff, core * (2 * half_ff), half_ff, r.send_pg, r.recv_pg)

    def ff_to_column():
        ff_across.wait()

        def body(at, n):
            rows = part_rows(at, n)
            value = v.keep[side, rows, :] + wide(r.ff_came[rows, :])
            v.keep[side, rows, :] = value
            r.ff_send[rows, :] = value.astype(low)

        in_chunks(half_ff, body)
        for copy in scatter_copies(*column_args):
            copy.start()

    def ff_to_share():
        scatter_wait(*column_args)
        rows = part_rows(column_index * column_piece, column_piece)
        total = v.keep[side, rows, :]
        for other in others(column_index, column_count):
            total = total + wide(r.ff_column[other])
        r.ff_send[rows, :] = total.astype(low)
        own = pltpu.make_async_copy(
            r.ff_send.at[rows, :],
            r.fin_ff.at[part_rows(ff_base + column_index * column_piece, column_piece), :],
            r.load.at[0],
        )
        own.start()
        own.wait()
        for copy in share_copies(*column_share):
            copy.start()

    def ff_to_pair():
        share_wait(*column_share)
        for copy in share_copies(*pair_share):
            copy.start()

    def ff_twin():
        view = r.fin_ff.at[part_rows(core * (2 * half_ff), 2 * half_ff), :]
        return remote(view, view, r.send_pg.at[2], r.recv_pg.at[2], twin)

    def ff_to_twin():
        share_wait(*pair_share)
        ff_twin().start()


    conv_back(0)
    center.wait()
    there = (1 - chip) * (TEAM // 2)
    here = chip * (TEAM // 2)
    return_block(there)
    conv_back(1)
    rims = [
        (remote(r.dd_last, r.dd_low, r.send_h.at[0], r.recv_h.at[0], {"ctx": after}), 1),
        (remote(r.rim_last, r.rim_low, r.send_h.at[1], r.recv_h.at[1], {"ctx": after}), 1),
        (remote(r.dd_first, r.dd_high, r.send_h.at[2], r.recv_h.at[2], {"ctx": prior}), 0),
        (remote(r.rim_first, r.rim_high, r.send_h.at[3], r.recv_h.at[3], {"ctx": prior}), 0),
    ]
    for copy, forward in rims:
        pl.when(me < size - 1 if forward else me > 0)(copy.start)

    return_block(there + 1)
    ff_to_column()
    have(fetched.depth, fetched.xrim)
    strip = 32

    def flat_rows(ref):
        return ref[...].reshape(seqs * block, ref.shape[2])

    point_grad = dot_tn(flat_rows(v.depth), flat_rows(v.dconv)).astype(low)
    for w in range(2):
        block_a.pack[w, 0:width, :] = point_grad[w * width : (w + 1) * width, :]
    for g in range(groups):
        def tap_step(c, sums, g=g):
            out = list(sums)
            for s in range(seqs):
                start = c * strip
                here = r.seg_col[s, pl.ds(RIM + start, strip), :]
                grad = r.dd[s, g, pl.ds(RIM + start, strip), :]
                for j in range(KERNEL):
                    same = r.seg_col[s, pl.ds(lead + j + start, strip), :] == here
                    near = v.xrim[s, g, pl.ds(lead + j + start, strip), :]
                    out[j] = out[j] + fold_rows(jnp.where(same, near, 0.0) * grad)
            return tuple(out)

        sums = lax.fori_loop(
            0, block // strip, tap_step,
            tuple(jnp.zeros((8, LANES), jnp.float32) for _ in range(KERNEL)),
        )
        for j in range(KERNEL):
            small[g // 3, j : j + 1, lane_group(g % 3)] = jnp.sum(sums[j], axis=0, keepdims=True)

    return_block(here + 1 - chip)
    return_block(here + chip)
    have(fetched.convw, fetched.x)
    for copy, forward in rims:
        pl.when(me > 0 if forward else me < size - 1)(copy.wait_recv)
    near_taps = KERNEL // 2
    for s in range(seqs):
        for g in range(3):
            head = pl.ds(RIM, RIM)
            tail = pl.ds(block, RIM)
            r.d_ext[s, g, head, :] += wide(r.rim_low[s, :, lane_group(g)])
            r.d_ext[s, g, tail, :] += wide(r.rim_high[s, :, lane_group(g)])
            v.queries[s, :, lane_group(g)] = r.d_ext[s, g, pl.ds(RIM, block), :].astype(low)
        for g in range(groups):
            r.dd[s, g, 0:RIM, :] = wide(r.dd_low[s, :, lane_group(g)])
            r.dd[s, g, pl.ds(RIM + block, RIM), :] = wide(r.dd_high[s, :, lane_group(g)])
        bias = jnp.sum(wide(v.queries[s]), axis=0, keepdims=True)
        for w in range(2):
            small[w, ROW_CONV_B : ROW_CONV_B + 1, :] += bias
    conv_grad = dot_tn(flat_rows(v.x), flat_rows(v.queries)).astype(low)
    for w in range(2):
        block_a.pack[w, width : 2 * width, :] = conv_grad[w * width : (w + 1) * width, :]

    def core_copy(blk):
        pack = blk.pack
        half = pack.shape[1] // 2
        return remote(pack.at[:, part_rows((1 - core) * half, half), :], blk.twin,
                      blk.send_core.at[0], blk.recv_core.at[0], twin)

    def y_copy(blk):
        return remote(blk.ysend, blk.ycame, blk.send_core.at[1],
                      blk.recv_core.at[1], across)

    def core_done(blk):
        core_copy(blk).wait()
        pack, came = blk.pack, blk.twin
        half = pack.shape[1] // 2

        def body(at, n):
            rows, there = part_rows(at, n), part_rows(core * half + at, n)
            blk.ysend[rows, :] = (
                wide(pack[1 - side, there, :]) + wide(came[1 - side, rows, :])
            ).astype(low)
            blk.acc[rows, :] = wide(pack[side, there, :]) + wide(came[side, rows, :])

        in_chunks(half, body)
        y_copy(blk).start()

    def chips_args(blk):
        return (chips_of, me, size, blk.ysend, blk.chips,
                blk.send_s, blk.recv_s)

    def y_done(blk):
        y_copy(blk).wait()

        def body(at, n):
            rows = part_rows(at, n)
            value = blk.acc[rows, :] + wide(blk.ycame[rows, :])
            blk.acc[rows, :] = value
            blk.ysend[rows, :] = value.astype(low)

        in_chunks(blk.ysend.shape[0], body)
        for copy in scatter_copies(*chips_args(blk)):
            copy.start()

    def share_args(blk):
        half = blk.ysend.shape[0]
        return (chips_of, me, size, blk.fin, core * half, half // count,
                blk.send_g, blk.recv_g)

    def chips_done(blk):
        scatter_wait(*chips_args(blk))
        half = blk.ysend.shape[0]
        piece = half // count
        value = blk.acc[part_rows(index * piece, piece), :]
        for other in others(index, count):
            value = value + wide(blk.chips[other])
        blk.fin[part_rows(core * half + index * piece, piece), :] = value.astype(low)
        for copy in share_copies(*share_args(blk)):
            copy.start()

    def twin_copy(blk):
        fin = blk.fin
        half = fin.shape[0] // 2
        view = fin.at[part_rows(core * half, half), :]
        return remote(view, view, blk.send_core.at[2], blk.recv_core.at[2], twin)

    def share_done(blk):
        share_wait(*share_args(blk))
        twin_copy(blk).start()

    def finish(blk):
        for copy in scatter_copies(*chips_args(blk)):
            copy.wait_send()
        for copy in share_copies(*share_args(blk)):
            copy.wait_send()
        twin_copy(blk).wait()

    core_copy(block_a).start()
    for k, row in enumerate((ROW_GAIN2, ROW_SHIFT2, ROW_OUTER_B, ROW_GAIN1, ROW_SHIFT1, ROW_OUTPUT_B)):
        for w in range(2):
            small[w, row : row + 1, :] = r.vec[k : k + 1, w * 384 : (w + 1) * 384]
    for w in range(2):
        for k in range(4):
            at = (4 * w + k) * 384
            small[w, ROW_INNER_B + k : ROW_INNER_B + k + 1, :] = r.bias[0:1, at : at + 384]

    own_q.wait()
    for o in range(1, TEAM):
        q_copy(o).wait_send()
        remote(r.dq.at[rank], r.q_parts.at[mate(rank, o)], r.send_q.at[o], r.recv_q.at[o],
               {"ctx": base + mate(rank, o)}).wait_recv()
    for s in range(seqs):
        one, two = r.q_parts.at[2 * s], r.q_parts.at[2 * s + 1]
        queries = (
            one[:, lane_group(0)],
            mixed_lanes(wide(one[:, lane_group(1)]), half_turn(wide(two[:, lane_group(1)]))),
            two[:, lane_group(0)],
        )
        for g in range(3):
            r.d_cat[s, :, lane_group(6 + g)] = (
                wide(queries[g]) + v.spans[s, :, lane_group(g)]
            ).astype(low)
    for k in range(TEAM):
        pl.when(k == rank)(kv_copy(k)[0].wait)
        pl.when(k != rank)(kv_copy(k)[1].wait_send)
    for o in range(1, TEAM):
        other = mate(rank, o)
        remote(r.mine.at[block_of(rank), :], r.kv_parts.at[other], r.send_kv.at[rank],
               r.recv_kv.at[other], {"ctx": base + other}).wait_recv()
    for s in range(seqs):
        one, two = r.kv_parts.at[2 * s], r.kv_parts.at[2 * s + 1]
        mid_one, mid_two = wide(one[:, lane_group(1)]), wide(two[:, lane_group(1)])
        r.d_cat[s, :, lane_group(0)] = one[:, lane_group(0)]
        r.d_cat[s, :, lane_group(1)] = mixed_lanes(mid_one, half_turn(mid_two)).astype(low)
        r.d_cat[s, :, lane_group(2)] = two[:, lane_group(0)]
        r.d_cat[s, :, lane_group(3)] = one[:, lane_group(2)]
        r.d_cat[s, :, lane_group(4)] = mixed_lanes(half_turn(mid_one), mid_two).astype(low)
        r.d_cat[s, :, lane_group(5)] = two[:, lane_group(2)]
        for k, row in ((1, ROW_VALUE_B), (2, ROW_QUERY_B)):
            bias = jnp.sum(wide(r.d_cat[s, :, k * width : (k + 1) * width]), axis=0, keepdims=True)
            for w in range(2):
                small[w, row : row + 1, :] += bias
    grads = flat_rows(r.d_cat)
    for w in range(2):
        piece = dot_tn(
            v.x[:, :, w * width : (w + 1) * width].reshape(seqs * block, width), grads
        ).astype(low)
        for k in range(3):
            block_b.pack[w, k * width : (k + 1) * width, :] = piece[:, k * width : (k + 1) * width]
        block_b.pack[w, SMALL_AT : SMALL_AT + SMALL_ROWS, :] = small[w].astype(low)
    core_copy(block_b).start()
    core_done(block_a)
    core_done(block_b)
    have(fetched.ds, fetched.key, fetched.value, fetched.query)
    def taps_row(j, g):
        return wide(small_ref[(g // 3) * SMALL_IN + j : (g // 3) * SMALL_IN + j + 1,
                              lane_group(g % 3)])

    def depth_strip(c, s):
        start = c * strip
        here = r.seg_col[s, pl.ds(RIM + start, strip), :]
        rows = pl.ds(pl.multiple_of(start, strip), strip)
        sums = [v.ds[s, rows, lane_group(g)] for g in range(groups)]
        for j in range(KERNEL):
            same = r.seg_col[s, pl.ds(RIM + near_taps - j + start, strip), :] == here
            for g in range(groups):
                near = r.dd[s, g, pl.ds(RIM + near_taps - j + start, strip), :]
                sums[g] = sums[g] + jnp.where(same, near, 0.0) * taps_row(j, g)
        for g in range(groups):
            v.ds[s, rows, lane_group(g)] = sums[g]
        return s

    for s in range(seqs):
        lax.fori_loop(0, block // strip, depth_strip, s)
    ff_to_share()
    y_done(block_a)
    y_done(block_b)
    for s in range(seqs):
        v.ds[s] += (
            rows_nt(v.queries[s], v.convw[...])
            + rows_nt(r.d_cat[s, :, 0:width], v.key[...])
            + rows_nt(r.d_cat[s, :, width : 2 * width], v.value[...])
            + rows_nt(r.d_cat[s, :, 2 * width :], v.query[...])
        )
    out_copy = pltpu.make_async_copy(v.ds, r.input_grad, r.load.at[1])
    out_copy.start()
    chips_done(block_a)
    ff_to_pair()
    chips_done(block_b)
    share_done(block_a)
    share_done(block_b)
    ff_to_twin()
    finish(block_a)
    finish(block_b)
    ff_twin().wait()
    for copy in scatter_copies(*column_args):
        copy.wait_send()
    for copy in share_copies(*column_share) + share_copies(*pair_share):
        copy.wait_send()
    for copy, forward in rims:
        pl.when(me < size - 1 if forward else me > 0)(copy.wait_send)
    for k in range(TEAM - 1):
        pl.when(team < teams - 1)(halo_left(k).wait_send)
        pl.when(team > 0)(halo_right(k).wait_send)
    out_copy.wait()


def padded(rows, unit):
    return -(-rows // unit) * unit


def back(held, window, dq_parts, loaded):
    size = lax.axis_size("ctx")
    unit = 16 * size
    seqs, block, model = loaded["x"].shape
    width = HEADS * HEAD_DIM
    halo = (TEAM - 1) * block
    span = block + 2 * RIM
    chips, column = size // 2, size // TEAM
    low, full = jnp.bfloat16, jnp.float32
    dma = pltpu.SemaphoreType.DMA
    half_ff = loaded["keep"].shape[1]
    outs = dict(
        input_grad=jax.ShapeDtypeStruct((seqs, block, model), full),
        fin_ff=jax.ShapeDtypeStruct((4 * half_ff, width), low),
    )
    scratch = dict(
        mine=pltpu.VMEM((TEAM * block, width), low),
        from_right=pltpu.VMEM((TEAM * block, width), low),
        from_left=pltpu.VMEM((TEAM * block, width), low),
        kv_parts=pltpu.VMEM((TEAM, block, width), low),
        q_parts=pltpu.VMEM((TEAM, block, 2 * LANES), low),
        ff_send=pltpu.VMEM((half_ff, width), low),
        ff_came=pltpu.VMEM((half_ff, width), low),
        ff_column=pltpu.VMEM((column, half_ff // column, width), low),
        spread=pltpu.VMEM((KERNEL, 2 * LANES, width), low),
        sums=pltpu.VMEM((2, SMALL_ROWS, width), full),
        wide=pltpu.VMEM((LANES, block), full),
        tall=pltpu.VMEM((block, LANES), full),
        seg_col=pltpu.VMEM((seqs, held["seg"].shape[1], LANES), full),
        d_ext=pltpu.VMEM((seqs, 3, span, LANES), full),
        dd=pltpu.VMEM((seqs, model // LANES, span, LANES), full),
        d_cat=pltpu.VMEM((seqs, block, 3 * width), low),
        dd_first=pltpu.VMEM((seqs, RIM, model), low),
        dd_last=pltpu.VMEM((seqs, RIM, model), low),
        dd_low=pltpu.VMEM((seqs, RIM, model), low),
        dd_high=pltpu.VMEM((seqs, RIM, model), low),
        rim_first=pltpu.VMEM((seqs, RIM, width), low),
        rim_last=pltpu.VMEM((seqs, RIM, width), low),
        rim_low=pltpu.VMEM((seqs, RIM, width), low),
        rim_high=pltpu.VMEM((seqs, RIM, width), low),
        send_l=dma((TEAM,)), recv_l=dma((TEAM,)), send_r=dma((TEAM,)), recv_r=dma((TEAM,)),
        send_q=dma((TEAM,)), recv_q=dma((TEAM,)), send_kv=dma((TEAM,)), recv_kv=dma((TEAM,)),
        send_h=dma((4,)), recv_h=dma((4,)), send_p=dma((1,)), recv_p=dma((1,)),
        send_c=dma((column,)), recv_c=dma((column,)), send_cg=dma((column,)),
        recv_cg=dma((column,)), send_pg=dma((3,)), recv_pg=dma((3,)),
        load=dma((len(loaded) + 1,)),
    )

    def block_scratch(rows):
        rows = padded(rows, unit)
        return dict(
            pack=pltpu.VMEM((2, rows, width), low),
            twin=pltpu.VMEM((2, rows // 2, width), low),
            ysend=pltpu.VMEM((rows // 2, width), low),
            ycame=pltpu.VMEM((rows // 2, width), low),
            acc=pltpu.VMEM((rows // 2, width), full),
            chips=pltpu.VMEM((chips, rows // 2 // chips, width), low),
            fin=pltpu.VMEM((rows, width), low),
            send_s=dma((chips,)), recv_s=dma((chips,)), send_g=dma((chips,)),
            recv_g=dma((chips,)), send_core=dma((3,)), recv_core=dma((3,)),
        )

    a_scratch, b_scratch = block_scratch(PACK_A), block_scratch(PACK_B)
    del a_scratch["fin"], b_scratch["fin"]
    fin_shapes = [jax.ShapeDtypeStruct((padded(n, unit), width), low) for n in (PACK_A, PACK_B)]
    vmem = pl.BlockSpec(memory_space=pltpu.VMEM)
    anywhere = pl.BlockSpec(memory_space=pl.ANY)
    names = tuple(held) + ("window", "dq") + tuple(outs) + tuple(scratch)
    total_in = len(held) + 2
    fetch_count = len(loaded)

    def kernel(*refs):
        ins, loads = refs[:total_in], refs[total_in : total_in + fetch_count]
        at = total_in + fetch_count
        results = refs[at : at + len(outs)]
        fin_a, fin_b = refs[at + len(outs) : at + len(outs) + 2]
        late = refs[at + len(outs) + 2 :]
        first, late = late[: len(scratch)], late[len(scratch) :]
        a_refs, late = late[: len(a_scratch)], late[len(a_scratch) :]
        b_refs, holds = late[: len(b_scratch)], late[len(b_scratch) :]
        back_kernel(
            names, tuple(a_scratch) + ("fin",), tuple(b_scratch) + ("fin",), tuple(loaded),
            *ins, *results, *first, *a_refs, fin_a, *b_refs, fin_b, *loads, *holds,
        )

    holds = [pltpu.VMEM(a.shape, a.dtype) for a in loaded.values()]
    return pl.pallas_call(
        kernel,
        out_shape=list(outs.values()) + fin_shapes,
        in_specs=[vmem] * len(held) + [anywhere] * (2 + len(loaded)),
        out_specs=[anywhere] * 2 + [vmem] * 2,
        scratch_shapes=list(scratch.values()) + list(a_scratch.values())
        + list(b_scratch.values()) + holds,
        compiler_params=pltpu.CompilerParams(
            collective_id=5, has_side_effects=True, vmem_limit_bytes=65400 * 2**10
        ),
        name="back",
    )(*held.values(), window, dq_parts, *loaded.values())


STEP = 256
FF_CHUNK = 512
PACK_FF = 3840


def gelu_pair(value):
    size = jnp.abs(value) * 0.7071067811865476
    denominator = 1.0 + 0.3275911 * size
    t = pl.reciprocal(denominator, approx=True)
    t = t * (2.0 - denominator * t)
    bell = jnp.exp(-0.5 * value * value)
    tail = t * (0.127414796 + t * (-0.142248368 + t * (0.7107068705 + t * (
        -0.7265760135 + t * 0.5307027145))))
    tail = tail * bell
    share = jnp.where(value >= 0, 1.0 - tail, tail)
    return value * share, share + value * bell * 0.3989422804014327


def fold_rows(block):
    return jnp.sum(block.reshape(block.shape[0] // 8, 8, block.shape[1]), axis=0)


def norm_parts(value):
    center = value - jnp.mean(value, axis=-1, keepdims=True)
    spread = jnp.mean(center * center, axis=-1, keepdims=True)
    scale = lax.rsqrt(spread + 1e-05)
    return center * scale, scale


def norm_back(grad, unit, scale):
    return scale * (
        grad
        - jnp.mean(grad, axis=-1, keepdims=True)
        - unit * jnp.mean(grad * unit, axis=-1, keepdims=True)
    )


def middle_kernel(att_ref, conv_ref, x_ref, small_ref, og_any, ow_any, iw_any, uw_any, uw_came,
                  out_any, ds_any, dc_any, team_ref, keep_ref, xsend_ref, vec_ref, bias_ref,
                  og_ref, ow_ref, iw_ref, uw_ref, out_ref, ds_ref, dc_ref,
                  pack_ref, twin_ref, pieces, parts, joined_ref, low_ref, act_ref, slope_ref, do_ref, di_ref, db_ref,
                  sums_ref, wide_sums, send_a, recv_a, send_g, recv_g, send_t, recv_t, load, store):
    me = lax.axis_index("ctx")
    rank = lax.rem(me, TEAM)
    base = me - rank
    seqs, block, model = x_ref.shape
    width = HEADS * HEAD_DIM
    greet([{"ctx": base + mate(rank, o)} for o in range(1, TEAM)])

    def piece_copy(r):
        return (
            pltpu.make_async_copy(att_ref.at[r], pieces.at[rank], recv_a.at[rank]),
            remote(att_ref.at[r], pieces.at[rank], send_a.at[r], recv_a.at[rank],
                   {"ctx": base + r}),
        )

    def team_copy(r):
        return (
            pltpu.make_async_copy(parts.at[r], team_ref.at[rank], recv_g.at[rank]),
            remote(parts.at[r], team_ref.at[rank], send_g.at[r], recv_g.at[rank],
                   {"ctx": base + r}),
        )

    core, side = lax.rem(me, 2), lax.axis_index("wsh")
    for o in (1, 3, 2):
        piece_copy(mate(rank, o))[1].start()
    piece_copy(rank)[0].start()
    rows_in = uw_came.shape[1]
    came_at = part_rows((1 - side) * (2 * rows_in) + core * rows_in, rows_in)
    loads = [
        pltpu.make_async_copy(ow_any, ow_ref, load.at[0]),
        pltpu.make_async_copy(iw_any, iw_ref, load.at[1]),
        pltpu.make_async_copy(
            uw_any, uw_ref.at[:, part_rows(side * (2 * rows_in), 2 * rows_in), :], load.at[2]
        ),
        pltpu.make_async_copy(uw_came, uw_ref.at[:, came_at, :], load.at[3]),
        pltpu.make_async_copy(og_any, og_ref, load.at[4]),
    ]
    for copy in loads:
        copy.start()
    outer_twin = remote(uw_came, uw_ref.at[:, came_at, :], send_t.at[1], recv_t.at[1],
                        {"ctx": flip(me, 1)})
    outer_twin.start()
    sums_ref[...] = jnp.zeros_like(sums_ref)
    wide_sums[...] = jnp.zeros_like(wide_sums)
    own = lax.div(rank, 2)
    steps = block // STEP

    def row(index):
        return jnp.concatenate(
            [small_ref[index : index + 1, :], small_ref[SMALL_IN + index : SMALL_IN + index + 1, :]],
            axis=1,
        ).astype(jnp.float32)

    def body(i, carry):
        s = lax.rem(own + lax.div(i, steps), seqs)
        start = pl.multiple_of(lax.rem(i, steps) * STEP, STEP)
        rows = pl.ds(start, STEP)
        flat = pl.ds(pl.multiple_of(s * block + start, STEP), STEP)

        @pl.when(i == 0)
        def _():
            piece_copy(rank)[0].wait()
            remote(att_ref.at[rank], pieces.at[mate(rank, 1)], send_a.at[rank],
                   recv_a.at[mate(rank, 1)], {"ctx": base + mate(rank, 1)}).wait_recv()
            for copy in loads:
                copy.wait()
            outer_twin.wait()

        @pl.when(i == steps)
        def _():
            for o in (2, 3):
                remote(att_ref.at[rank], pieces.at[mate(rank, o)], send_a.at[rank],
                       recv_a.at[mate(rank, o)], {"ctx": base + mate(rank, o)}).wait_recv()

        first, second = pieces.at[2 * s], pieces.at[2 * s + 1]
        joined_ref[flat, lane_group(0)] = first[rows, lane_group(0)]
        joined_ref[flat, lane_group(1)] = mixed_lanes(
            first[rows, lane_group(1)].astype(jnp.float32),
            half_turn(second[rows, lane_group(1)].astype(jnp.float32)),
        ).astype(jnp.bfloat16)
        joined_ref[flat, lane_group(2)] = second[rows, lane_group(0)]
        joined_ref[flat, width:] = conv_ref[s, rows, :]
        branch = dot(joined_ref[flat, :], ow_ref[...]) + row(ROW_OUTPUT_B)
        unit1, scale1 = norm_parts(branch + x_ref[s, rows, :].astype(jnp.float32))
        gain1 = row(ROW_GAIN1)
        normed = unit1 * gain1 + row(ROW_SHIFT1)
        low_ref[flat, :] = normed.astype(jnp.bfloat16)
        outer = []
        part = model // GROUPS
        hidden = iw_ref.shape[2]
        for g in range(GROUPS):
            cols = slice(g * part, (g + 1) * part)
            for c in range(hidden // FF_CHUNK):
                span = slice(g * hidden + c * FF_CHUNK, g * hidden + (c + 1) * FF_CHUNK)
                near = slice(c * FF_CHUNK, (c + 1) * FF_CHUNK)
                bias = jnp.concatenate(
                    [
                        small_ref[
                            g * SMALL_IN + ROW_INNER_B + k // 3 : g * SMALL_IN + ROW_INNER_B + k // 3 + 1,
                            lane_group(k % 3),
                        ]
                        for k in range(c * FF_CHUNK // LANES, (c + 1) * FF_CHUNK // LANES)
                    ],
                    axis=1,
                ).astype(jnp.float32)
                inner = dot(low_ref[flat, cols], iw_ref[g, :, near]) + bias
                active, slope = gelu_pair(inner)
                act_ref[flat, span] = active.astype(jnp.bfloat16)
                slope_ref[:, span] = slope
            outer.append(dot(act_ref[flat, g * hidden : (g + 1) * hidden], uw_ref[g]))
        summed = jnp.concatenate(outer, axis=1) + row(ROW_OUTER_B) + normed
        unit2, scale2 = norm_parts(summed)
        gain2 = row(ROW_GAIN2)
        out_ref[s, rows, :] = (unit2 * gain2 + row(ROW_SHIFT2)).astype(jnp.bfloat16)
        grad = og_ref[s, rows, :].astype(jnp.float32)
        sums_ref[0] += fold_rows(grad * unit2)
        sums_ref[1] += fold_rows(grad)
        d_sum2 = norm_back(grad * gain2, unit2, scale2)
        d_outer = d_sum2.astype(jnp.bfloat16)
        do_ref[flat, :] = d_outer
        sums_ref[2] += fold_rows(d_outer.astype(jnp.float32))
        back = []
        for g in range(GROUPS):
            cols = slice(g * part, (g + 1) * part)
            for c in range(hidden // FF_CHUNK):
                span = slice(g * hidden + c * FF_CHUNK, g * hidden + (c + 1) * FF_CHUNK)
                near = slice(c * FF_CHUNK, (c + 1) * FF_CHUNK)
                d_inner = (
                    rows_nt(do_ref[flat, cols], uw_ref[g, near, :]) * slope_ref[:, span]
                ).astype(jnp.bfloat16)
                di_ref[flat, span] = d_inner
                wide_sums[:, span] += fold_rows(d_inner.astype(jnp.float32))
            back.append(rows_nt(di_ref[flat, g * hidden : (g + 1) * hidden], iw_ref[g]))
        d_normed = d_sum2 + jnp.concatenate(back, axis=1)
        sums_ref[3] += fold_rows(d_normed * unit1)
        sums_ref[4] += fold_rows(d_normed)
        d_sum1 = norm_back(d_normed * gain1, unit1, scale1)
        ds_ref[s, rows, :] = d_sum1
        d_branch = d_sum1.astype(jnp.bfloat16)
        db_ref[flat, :] = d_branch
        sums_ref[5] += fold_rows(d_branch.astype(jnp.float32))
        d_joined = rows_nt(d_branch, ow_ref[...])
        dc_ref[s, rows, :] = d_joined[:, width:].astype(jnp.bfloat16)
        parts[2 * s, rows, lane_group(0)] = d_joined[:, lane_group(0)].astype(jnp.bfloat16)
        parts[2 * s, rows, lane_group(1)] = half_turn(d_joined[:, lane_group(1)]).astype(
            jnp.bfloat16
        )
        parts[2 * s + 1, rows, lane_group(0)] = d_joined[:, lane_group(2)].astype(jnp.bfloat16)
        parts[2 * s + 1, rows, lane_group(1)] = d_joined[:, lane_group(1)].astype(jnp.bfloat16)

        @pl.when(i == steps - 1)
        def _():
            team_copy(rank)[0].start()
            team_copy(mate(rank, 1))[1].start()

        @pl.when(i == 2 * steps - 1)
        def _():
            team_copy(mate(rank, 2))[1].start()
            team_copy(mate(rank, 3))[1].start()

        return carry

    lax.fori_loop(0, seqs * steps, body, 0)
    stores = [
        pltpu.make_async_copy(out_ref, out_any, store.at[0]),
        pltpu.make_async_copy(ds_ref, ds_any, store.at[1]),
        pltpu.make_async_copy(dc_ref, dc_any, store.at[2]),
    ]
    for copy in stores:
        copy.start()

    half = width
    for w in range(2):
        for k in range(2):
            pack_ref[w, pl.ds(k * half, half), :] = dot_tn(
                joined_ref[:, w * half : (w + 1) * half], db_ref[:, k * half : (k + 1) * half]
            ).astype(jnp.bfloat16)
    part = model // GROUPS
    hidden = iw_ref.shape[2]
    for g in range(GROUPS):
        for k in range(hidden // half):
            grads = dot_tn(
                low_ref[:, g * part : (g + 1) * part],
                di_ref[:, g * hidden + k * half : g * hidden + (k + 1) * half],
            ).astype(jnp.bfloat16)
            for w in range(2):
                pack_ref[w, pl.ds(2 * half + (g * 4 + k) * (part // 2), part // 2), :] = grads[
                    w * (part // 2) : (w + 1) * (part // 2), :
                ]
        for k in range(hidden // half):
            w, lower = k // 2, k % 2
            grads = dot_tn(
                act_ref[:, g * hidden + k * half : g * hidden + (k + 1) * half],
                do_ref[:, g * part : (g + 1) * part],
            ).astype(jnp.bfloat16)
            pack_ref[w, pl.ds(6 * half + g * 2 * half + lower * half, half), :] = grads
    for k in range(6):
        vec_ref[k : k + 1, :] = jnp.sum(sums_ref[k], axis=0, keepdims=True)
    vec_ref[6:, :] = jnp.zeros((2, model), jnp.float32)
    bias_ref[...] = jnp.broadcast_to(jnp.sum(wide_sums[...], axis=0, keepdims=True), bias_ref.shape)

    half_ff = pack_ref.shape[1] // 2
    exchange = remote(pack_ref.at[:, part_rows((1 - core) * half_ff, half_ff), :], twin_ref,
                      send_t.at[0], recv_t.at[0], {"ctx": flip(me, 1)})
    exchange.start()
    exchange.wait()

    pair_index, _, _ = pair_of(me, lax.axis_size("ctx"))
    quarter = half_ff // 2

    def add(at, n):
        here = part_rows(at, n)
        keep, give = pair_index * quarter, (1 - pair_index) * quarter
        for w in range(2):
            xsend_ref[w, here, :] = (
                wide(pack_ref[w, part_rows(core * half_ff + give + at, n), :])
                + wide(twin_ref[w, part_rows(give + at, n), :])
            ).astype(jnp.bfloat16)
            keep_ref[w, here, :] = wide(
                pack_ref[w, part_rows(core * half_ff + keep + at, n), :]
            ) + wide(twin_ref[w, part_rows(keep + at, n), :])

    in_chunks(quarter, add)
    team_copy(rank)[0].wait()
    for o in range(1, TEAM):
        other = mate(rank, o)
        piece_copy(other)[1].wait_send()
        team_copy(other)[1].wait_send()
        remote(parts.at[rank], team_ref.at[other], send_g.at[rank], recv_g.at[other],
               {"ctx": base + other}).wait_recv()
    for copy in stores:
        copy.wait()


def middle(attended, convolved, hidden, small, out_grad, output_w, inner_w, outer_w, outer_came):
    seqs, block, model = hidden.shape
    rows = seqs * block
    width = convolved.shape[2]
    inner = GROUPS * inner_w.shape[2]
    pack_rows = padded(PACK_FF, 16 * lax.axis_size("ctx"))
    vmem = pl.BlockSpec(memory_space=pltpu.VMEM)
    anywhere = pl.BlockSpec(memory_space=pl.ANY)
    low, full = jnp.bfloat16, jnp.float32
    dma = pltpu.SemaphoreType.DMA
    return pl.pallas_call(
        middle_kernel,
        out_shape=[
            jax.ShapeDtypeStruct((seqs, block, model), low),
            jax.ShapeDtypeStruct((seqs, block, model), full),
            jax.ShapeDtypeStruct((seqs, block, width), low),
            jax.ShapeDtypeStruct((TEAM, block, 2 * LANES), low),
            jax.ShapeDtypeStruct((2, pack_rows // 4, width), full),
            jax.ShapeDtypeStruct((2, pack_rows // 4, width), low),
            jax.ShapeDtypeStruct((8, model), full),
            jax.ShapeDtypeStruct((8, inner), full),
        ],
        in_specs=[anywhere] + [vmem] * 3 + [anywhere] * 5,
        out_specs=[anywhere] * 4 + [vmem] * 4,
        scratch_shapes=[
            pltpu.VMEM((seqs, block, model), low),
            pltpu.VMEM(output_w.shape, low),
            pltpu.VMEM(inner_w.shape, low),
            pltpu.VMEM((GROUPS, 2 * outer_w.shape[1], outer_w.shape[2]), low),
            pltpu.VMEM((seqs, block, model), low),
            pltpu.VMEM((seqs, block, model), full),
            pltpu.VMEM((seqs, block, width), low),
            pltpu.VMEM((2, pack_rows, width), low),
            pltpu.VMEM((2, pack_rows // 2, width), low),
            pltpu.VMEM((TEAM, block, 2 * LANES), low),
            pltpu.VMEM((TEAM, block, 2 * LANES), low),
            pltpu.VMEM((rows, model), low),
            pltpu.VMEM((rows, model), low),
            pltpu.VMEM((rows, inner), low),
            pltpu.VMEM((STEP, inner), full),
            pltpu.VMEM((rows, model), low),
            pltpu.VMEM((rows, inner), low),
            pltpu.VMEM((rows, model), low),
            pltpu.VMEM((6, 8, model), full),
            pltpu.VMEM((8, inner), full),
            dma((TEAM,)), dma((TEAM,)), dma((TEAM,)), dma((TEAM,)), dma((2,)), dma((2,)),
            dma((5,)), dma((3,)),
        ],
        compiler_params=pltpu.CompilerParams(
            collective_id=2, has_side_effects=True, vmem_limit_bytes=63 * 2**20
        ),
        name="middle",
    )(attended, convolved, hidden, small, out_grad, output_w, inner_w, outer_w, outer_came)


def finish_kernel(side_ref, ff_any, a_any, b_any, grad_any, out_any,
                  grad_out, out_out, query_out, key_out, value_out, point_out, conv_out,
                  output_out, inner_out, outer_out, depth_out, kernel_out, query_b, value_b, point_b, conv_b,
                  output_b, gain1, shift1, outer_b, gain2, shift2, inner_b, kernel_b,
                  ff, a, b, grad, out, wide_a, wide_b, wide_output, wide_inner, wide_outer,
                  load, store):
    width = HEADS * HEAD_DIM
    loads = [
        pltpu.make_async_copy(b_any.at[pl.ds(0, b.shape[0]), :], b, load.at[0]),
        pltpu.make_async_copy(a_any.at[pl.ds(0, a.shape[0]), :], a, load.at[1]),
        pltpu.make_async_copy(ff_any.at[pl.ds(0, ff.shape[0]), :], ff, load.at[2]),
        pltpu.make_async_copy(grad_any, grad, load.at[3]),
        pltpu.make_async_copy(out_any, out, load.at[4]),
    ]
    for copy in loads:
        copy.start()
    stores = []

    def put(src, dst):
        copy = pltpu.make_async_copy(src, dst, store.at[len(stores)])
        copy.start()
        stores.append(copy)

    loads[0].wait()
    for k, place in enumerate((key_out, value_out, query_out)):
        rows = pl.ds(k * width, width)
        wide_b[rows, :] = b[rows, :].astype(jnp.float32)
        put(wide_b.at[rows, :], place)
    small = b[pl.ds(SMALL_AT, SMALL_ROWS), :].astype(jnp.float32)
    depth_out[...] = small[0:KERNEL, :]
    first = side_ref[0] == 0
    for ref, row in ((output_b, ROW_OUTPUT_B), (gain1, ROW_GAIN1), (shift1, ROW_SHIFT1),
                     (outer_b, ROW_OUTER_B), (gain2, ROW_GAIN2), (shift2, ROW_SHIFT2)):
        ref[...] = small[row : row + 1, :].reshape(width)
    inner_b[...] = jnp.concatenate(
        [small[ROW_INNER_B + k : ROW_INNER_B + k + 1, :] for k in range(4)], axis=1
    ).reshape(4 * width)
    block = small[16:24, :]
    turned = jnp.where(first, block, pltpu.roll(block, 192, axis=1))
    for ref, row in ((query_b, ROW_QUERY_B), (value_b, ROW_VALUE_B), (point_b, ROW_POINT_B),
                     (conv_b, ROW_CONV_B)):
        ref[...] = turned[row - 16 : row - 15, 0:192].reshape(192)
    taps = small[ROW_KERNEL_W : ROW_KERNEL_W + TAP_ROWS, :]
    half = jnp.where(first, taps, pltpu.roll(taps, 192, axis=1))[:, 0:192]
    pick = jnp.where(tap_major((TAP_ROWS, HEADS * KERNEL), 0), 1.0, 0.0)
    kernel_out[...] = dot_tn(pick.astype(jnp.bfloat16), half.astype(jnp.bfloat16))
    lanes = small[ROW_KERNEL_B : ROW_KERNEL_B + 24, :]
    column = jnp.concatenate([lanes[:, lane_group(g)] for g in range(3)], axis=0)
    wide_pick = jnp.where(
        first,
        jnp.where(tap_major((TAP_ROWS, LANES), 0), 1.0, 0.0),
        jnp.where(tap_major((TAP_ROWS, LANES), HEADS * KERNEL // 2), 1.0, 0.0),
    )
    count = HEADS * KERNEL // 2
    kernel_b[...] = jnp.sum(column * wide_pick, axis=0, keepdims=True)[:, 0:count].reshape(count)
    loads[1].wait()
    for k, place in enumerate((point_out, conv_out)):
        rows = pl.ds(k * width, width)
        wide_a[rows, :] = a[rows, :].astype(jnp.float32)
        put(wide_a.at[rows, :], place)
    loads[2].wait()
    for k in range(2):
        wide_output[:, k * width : (k + 1) * width] = ff[pl.ds(k * width, width), :].astype(
            jnp.float32
        )
    put(wide_output, output_out)
    count = inner_out.shape[1]
    for g in range(GROUPS):
        for k in range(inner_out.shape[2] // width):
            at = 2 * width + (g * (inner_out.shape[2] // width) + k) * count
            wide_inner[g, :, k * width : (k + 1) * width] = ff[pl.ds(at, count), :].astype(
                jnp.float32
            )
    put(wide_inner, inner_out)
    rows = outer_out.shape[1]
    for g in range(GROUPS):
        wide_outer[g] = ff[pl.ds(6 * width + g * rows, rows), :].astype(jnp.float32)
    put(wide_outer, outer_out)
    loads[3].wait()
    put(grad, grad_out)
    loads[4].wait()
    put(out, out_out)
    for copy in stores:
        copy.wait()


def finish(side, fin_ff, fin_a, fin_b, grad_input, output, inner_shape, outer_shape):
    width = HEADS * HEAD_DIM
    full, low = jnp.float32, jnp.bfloat16
    anywhere = pl.BlockSpec(memory_space=pl.ANY)
    vmem = pl.BlockSpec(memory_space=pltpu.VMEM)
    square = jax.ShapeDtypeStruct((width, width), full)
    lengths = [width // 2] * 4 + [width] * 6 + [4 * width, HEADS * KERNEL // 2]
    return pl.pallas_call(
        finish_kernel,
        out_shape=[
            jax.ShapeDtypeStruct(grad_input.shape, full),
            jax.ShapeDtypeStruct(output.shape, low),
            square, square, square, square, square,
            jax.ShapeDtypeStruct((width, 2 * width), full),
            jax.ShapeDtypeStruct(inner_shape, full),
            jax.ShapeDtypeStruct(outer_shape, full),
            jax.ShapeDtypeStruct((KERNEL, width), full),
            jax.ShapeDtypeStruct((HEADS * KERNEL, width // 2), full),
        ] + [jax.ShapeDtypeStruct((n,), full) for n in lengths],
        in_specs=[pl.BlockSpec(memory_space=pltpu.SMEM)] + [anywhere] * 5,
        out_specs=[anywhere] * 10 + [vmem] * 14,
        scratch_shapes=[
            pltpu.VMEM((PACK_FF, width), low),
            pltpu.VMEM((PACK_A, width), low),
            pltpu.VMEM((PACK_B, width), low),
            pltpu.VMEM(grad_input.shape, full),
            pltpu.VMEM(output.shape, low),
            pltpu.VMEM((PACK_A, width), full),
            pltpu.VMEM((SMALL_AT, width), full),
            pltpu.VMEM((width, 2 * width), full),
            pltpu.VMEM(inner_shape, full),
            pltpu.VMEM(outer_shape, full),
            pltpu.SemaphoreType.DMA((5,)),
            pltpu.SemaphoreType.DMA((10,)),
        ],
        compiler_params=pltpu.CompilerParams(vmem_limit_bytes=60 * 2**20),
        name="finish",
    )(side, fin_ff, fin_a, fin_b, grad_input, output)


def on_device(
    hidden_in,
    segment_ids,
    out_grad,
    query_w,
    query_b,
    key_w,
    value_w,
    value_b,
    depth_kernel,
    point_w,
    point_b,
    kernel_w,
    kernel_b,
    conv_w,
    conv_b,
    output_w,
    output_b,
    norm1_gain,
    norm1_bias,
    inner_w,
    inner_b,
    outer_w,
    outer_b,
    norm2_gain,
    norm2_bias,
):
    micro_count, seq_local, block_len, model_width = hidden_in.shape
    seq_count = micro_count * seq_local
    att_width = HEADS * HEAD_DIM
    half_taps = KERNEL // 2
    position = lax.axis_index("ctx")
    seg_rows = segment_ids.reshape(seq_count, segment_ids.shape[2])
    pad_rows = (TEAM - 1) * block_len
    seg_pad = jnp.pad(seg_rows, ((0, 0), (pad_rows, pad_rows)), constant_values=-1)
    own_seg = lax.dynamic_slice_in_dim(seg_pad, position * block_len + pad_rows, block_len, 1)
    rank = lax.rem(position, TEAM)
    team_seg = lax.dynamic_slice(
        jnp.concatenate(
            [seg_pad[:, : pad_rows + seg_rows.shape[1]],
             jnp.full((seq_count, pad_rows), 2**24, seg_pad.dtype)], axis=1
        ),
        (lax.div(rank, 2), (position - rank) * block_len),
        (1, (3 * TEAM - 2) * block_len),
    )
    query_seg = team_seg[:, pad_rows : pad_rows + TEAM * block_len]
    lows = query_seg[0, ::TILE]
    highs = query_seg[0, TILE - 1 :: TILE]
    before = jnp.sum(team_seg < lows[:, None], axis=1, dtype=jnp.int32)
    through = jnp.sum(team_seg <= highs[:, None], axis=1, dtype=jnp.int32)
    bounds = jnp.stack([before // TILE, (through + TILE - 1) // TILE])
    seg_keys = team_seg.astype(jnp.float32)
    seg_queries = query_seg.astype(jnp.float32)
    rim_seg = lax.dynamic_slice_in_dim(
        seg_pad, position * block_len + pad_rows - RIM, block_len + 2 * RIM, 1
    )
    tap_mask = jnp.stack(
        [
            rim_seg[:, RIM - half_taps + j : RIM - half_taps + j + block_len] == own_seg
            for j in range(KERNEL)
        ],
        axis=1,
    ).astype(jnp.float32)
    seg_rim = jnp.pad(
        rim_seg.astype(jnp.float32), ((0, 0), (0, -rim_seg.shape[1] % LANES)), constant_values=-1
    )
    side = lax.axis_index("wsh")
    tap_rows = jnp.pad(tap_mask, ((0, 0), (0, 16 - KERNEL), (0, 0)))
    hidden = hidden_in.reshape(seq_count, block_len, model_width)
    (key_mat, value_mat, small_full, query_mat, point_mat, conv_mat, output_mat, inner_mat,
     window, query_team, queries, xrim, depth_low, span_keys, kern, ext, convolved,
     outer_half) = front(
        hidden, seg_rim, tap_rows, depth_kernel, kernel_w.T, kernel_b,
        [output_b, norm1_gain, norm1_bias, outer_b, norm2_gain, norm2_bias, inner_b],
        [query_b, value_b, point_b, conv_b],
        [key_w, value_w, query_w, point_w, conv_w, output_w, inner_w], outer_w,
    )
    outer_came = lax.ppermute(outer_half, "wsh", [(0, 1), (1, 0)])
    query_team = query_team.reshape(TEAM * block_len, 2 * LANES)
    attended_team, attended_t, log_sums = attend(
        bounds, query_team, window, seg_keys, seg_queries
    )
    (output, grad_sum1, grad_conv, grad_team, keep, xsend, vec_grads, bias_grads) = middle(
        attended_team.reshape(TEAM, block_len, -1), convolved, hidden, small_full,
        out_grad.reshape(seq_count, block_len, model_width),
        output_mat, inner_mat, outer_w, outer_came,
    )
    came = lax.ppermute(xsend, "ctx", [(i, i ^ 2) for i in range(lax.axis_size("ctx"))])
    grad_query_team, grad_window = attend_back(
        bounds, query_team, window, seg_keys, seg_queries,
        grad_team.reshape(TEAM * block_len, 2 * LANES), attended_t, log_sums,
    )
    grad_input, fin_ff, fin_a, fin_b = back(
        dict(seg=seg_rim, mask=tap_rows, small=small_full, vec=vec_grads, bias=bias_grads),
        grad_window, grad_query_team.reshape(TEAM, block_len, -1),
        dict(keep=keep, came=came, dconv=grad_conv, ext=ext, kern=kern, point=point_mat,
             queries=queries, spans=span_keys, depth=depth_low, xrim=xrim, x=hidden,
             convw=conv_mat, ds=grad_sum1, key=key_mat, value=value_mat, query=query_mat),
    )
    (grad_input, output, grad_query, grad_key, grad_value, grad_point, grad_conv, grad_output,
     grad_inner, grad_outer, grad_depth, grad_kernel, g_query_b, g_value_b, g_point_b, g_conv_b,
     g_output_b, gain1, shift1, g_outer_b, gain2, shift2, g_inner_b, g_kernel_b) = finish(
        side.astype(jnp.int32).reshape(1), fin_ff, fin_a, fin_b, grad_input, output,
        inner_w.shape, outer_w.shape,
    )
    return (
        output.reshape(hidden_in.shape), grad_input.reshape(hidden_in.shape),
        grad_query, g_query_b, grad_key, grad_value, g_value_b, grad_depth, grad_point,
        g_point_b, grad_kernel.T, g_kernel_b, grad_conv, g_conv_b, grad_output, g_output_b,
        gain1, shift1, grad_inner, g_inner_b, grad_outer, g_outer_b, gain2, shift2,
    )


def solution(mesh):
    in_specs = (
        P(None, "wsh", "ctx", None),
        P(None, "wsh", None),
        P(None, "wsh", "ctx", None),
        P("wsh", None),
        P("wsh"),
        P("wsh", None),
        P("wsh", None),
        P("wsh"),
        P(None, "wsh"),
        P("wsh", None),
        P("wsh"),
        P("wsh", None),
        P("wsh"),
        P("wsh", None),
        P("wsh"),
        P("wsh", None),
        P("wsh"),
        P("wsh"),
        P("wsh"),
        P(None, "wsh", None),
        P("wsh"),
        P(None, "wsh", None),
        P("wsh"),
        P("wsh"),
        P("wsh"),
    )
    out_specs = (
        P(None, "wsh", "ctx", None),
        P(None, "wsh", "ctx", None),
        P("wsh", None),
        P("wsh"),
        P("wsh", None),
        P("wsh", None),
        P("wsh"),
        P(None, "wsh"),
        P("wsh", None),
        P("wsh"),
        P("wsh", None),
        P("wsh"),
        P("wsh", None),
        P("wsh"),
        P("wsh", None),
        P("wsh"),
        P("wsh"),
        P("wsh"),
        P(None, "wsh", None),
        P("wsh"),
        P(None, "wsh", None),
        P("wsh"),
        P("wsh"),
        P("wsh"),
    )
    return jax.shard_map(
        on_device, mesh=mesh, in_specs=in_specs, out_specs=out_specs, check_vma=False
    )
```

```python
import functools
import types

import jax
import jax.numpy as jnp
from jax import lax
from jax.experimental import pallas as pl
from jax.experimental.pallas import tpu as pltpu
from jax.sharding import PartitionSpec as P

HEADS = 6
HEAD_DIM = 64
KERNEL = 9
GROUPS = 2


TILE = 256
NEG = -1000000000.0
LANES = 128
HEADS_HERE = HEADS // 2


def rows_nt(left, right):
    return lax.dot_general(
        left, right, (((1,), (1,)), ((), ())), preferred_element_type=jnp.float32
    )


def lane_half(block, upper):
    lane = lax.broadcasted_iota(jnp.int32, block.shape, 1)
    keep = lane >= HEAD_DIM if upper else lane < HEAD_DIM
    return jnp.where(keep, block, jnp.zeros_like(block))


def same_document(segk_ref, segq_ref, j):
    cols = pl.ds(pl.multiple_of(j * TILE, TILE), TILE)
    row = segk_ref[0:1, cols]
    column = jnp.broadcast_to(row, (LANES, TILE)).T
    wide = jnp.concatenate([column] * (TILE // LANES), axis=1)
    return wide == segq_ref[0:1, :]


def load_queries(q_ref, qm_ref):
    scale = jnp.asarray(HEAD_DIM ** (-0.5), q_ref.dtype)
    first = q_ref[:, 0:LANES] * scale
    qm_ref[0] = lane_half(first, False)
    qm_ref[1] = lane_half(first, True)
    qm_ref[2] = lane_half(q_ref[:, LANES : 2 * LANES] * scale, False)


KEY_GROUP = (0, 0, 1)
VALUE_GROUP = (2, 2, 1)


def lane_group(group):
    return slice(group * LANES, (group + 1) * LANES)


def attend_kernel(bounds, q_ref, kv_ref, segk_ref, segq_ref, out_ref, outt_ref, lse_ref,
                  qm_ref, m_ref, l_ref, acc_ref):
    tile = pl.program_id(0)
    load_queries(q_ref, qm_ref)
    m_ref[...] = jnp.full_like(m_ref, -jnp.inf)
    l_ref[...] = jnp.zeros_like(l_ref)
    acc_ref[...] = jnp.zeros_like(acc_ref)

    def step(j, carry):
        rows = pl.ds(pl.multiple_of(j * TILE, TILE), TILE)
        same = same_document(segk_ref, segq_ref, j)
        values_t = kv_ref[rows, LANES : 3 * LANES].T
        value_rows = (2 * HEAD_DIM, 3 * HEAD_DIM, HEAD_DIM)
        raw = [
            rows_nt(kv_ref[rows, lane_group(KEY_GROUP[head])], qm_ref[head])
            for head in range(HEADS_HERE)
        ]
        highs, alphas = [], []
        for head in range(HEADS_HERE):
            scores = jnp.where(same, raw[head], NEG)
            old = m_ref[head : head + 1, :]
            top = jnp.maximum(old, jnp.max(scores, axis=0, keepdims=True))
            expo = jnp.exp(scores - top)
            alpha = jnp.exp(old - top)
            m_ref[head : head + 1, :] = top
            l_ref[head : head + 1, :] = l_ref[head : head + 1, :] * alpha + jnp.sum(
                expo, axis=0, keepdims=True
            )
            high = expo.astype(jnp.bfloat16)
            highs.append(high)
            alphas.append(alpha)
        for head in range(HEADS_HERE):
            span = slice(head * HEAD_DIM, (head + 1) * HEAD_DIM)
            vals = values_t[value_rows[head] : value_rows[head] + HEAD_DIM, :]
            acc_ref[span, :] = acc_ref[span, :] * alphas[head] + jnp.dot(
                vals, highs[head], preferred_element_type=jnp.float32
            )
        return carry

    lax.fori_loop(bounds[0, tile], bounds[1, tile], step, 0)
    lse_ref[...] = m_ref[...] + jnp.log(l_ref[...])
    used = HEADS_HERE * HEAD_DIM
    for head in range(HEADS_HERE):
        span = slice(head * HEAD_DIM, (head + 1) * HEAD_DIM)
        inv = 1.0 / l_ref[head : head + 1, :]
        acc_ref[span, :] = acc_ref[span, :] * inv
    outt_ref[...] = acc_ref[...]
    out_ref[...] = acc_ref[...].T.astype(jnp.bfloat16)


def attend(bounds, queries, window, seg_keys, seg_queries):
    rows, wide = queries.shape
    span, width = window.shape
    return pl.pallas_call(
        attend_kernel,
        grid_spec=pltpu.PrefetchScalarGridSpec(
            num_scalar_prefetch=1,
            grid=(rows // TILE,),
            in_specs=[
                pl.BlockSpec((TILE, wide), lambda i, b: (i, 0)),
                pl.BlockSpec((span, width), lambda i, b: (0, 0)),
                pl.BlockSpec((1, span), lambda i, b: (0, 0)),
                pl.BlockSpec((1, TILE), lambda i, b: (0, i)),
            ],
            out_specs=[
                pl.BlockSpec((TILE, wide), lambda i, b: (i, 0)),
                pl.BlockSpec((wide, TILE), lambda i, b: (0, i)),
                pl.BlockSpec((8, TILE), lambda i, b: (0, i)),
            ],
            scratch_shapes=[
                pltpu.VMEM((HEADS_HERE, TILE, LANES), jnp.bfloat16),
                pltpu.VMEM((8, TILE), jnp.float32),
                pltpu.VMEM((8, TILE), jnp.float32),
                pltpu.VMEM((wide, TILE), jnp.float32),
            ],
        ),
        out_shape=[
            jax.ShapeDtypeStruct((rows, wide), jnp.bfloat16),
            jax.ShapeDtypeStruct((wide, rows), jnp.float32),
            jax.ShapeDtypeStruct((8, rows), jnp.float32),
        ],
        compiler_params=pltpu.CompilerParams(vmem_limit_bytes=63 * 2**20),
        name="attend",
    )(bounds, queries, window, seg_keys, seg_queries)


def attend_back_kernel(bounds, q_ref, kv_ref, segk_ref, segq_ref, grad_ref, outt_ref, lse_ref,
                       dq_ref, dkv_ref, qm_ref, gm_ref, delta_ref, dq_acc, dkv_acc):
    tile = pl.program_id(0)

    @pl.when(tile == 0)
    def _():
        dkv_acc[...] = jnp.zeros_like(dkv_acc)

    load_queries(q_ref, qm_ref)
    gm_ref[0] = lane_half(grad_ref[:, 0:LANES], False)
    gm_ref[1] = lane_half(grad_ref[:, 0:LANES], True)
    gm_ref[2] = lane_half(grad_ref[:, LANES : 2 * LANES], True)
    grads_t = grad_ref[...].astype(jnp.float32).T
    grad_rows = (0, HEAD_DIM, 3 * HEAD_DIM)
    for head in range(HEADS_HERE):
        span = slice(head * HEAD_DIM, (head + 1) * HEAD_DIM)
        delta_ref[head : head + 1, :] = jnp.sum(
            grads_t[grad_rows[head] : grad_rows[head] + HEAD_DIM, :] * outt_ref[span, :],
            axis=0, keepdims=True,
        )
    dq_acc[...] = jnp.zeros_like(dq_acc)

    def step(j, carry):
        rows = pl.ds(pl.multiple_of(j * TILE, TILE), TILE)
        same = same_document(segk_ref, segq_ref, j)
        keys_t = kv_ref[rows, 0 : 2 * LANES].T
        sums = [dkv_acc[rows, lane_group(g)] for g in range(3)]
        raw = [
            rows_nt(kv_ref[rows, lane_group(KEY_GROUP[head])], qm_ref[head])
            for head in range(HEADS_HERE)
        ]
        draw = [
            rows_nt(kv_ref[rows, lane_group(VALUE_GROUP[head])], gm_ref[head])
            for head in range(HEADS_HERE)
        ]
        ps, dss = [], []
        for head in range(HEADS_HERE):
            probs = jnp.where(same, jnp.exp(raw[head] - lse_ref[head : head + 1, :]), 0.0)
            dss.append((probs * (draw[head] - delta_ref[head : head + 1, :])).astype(jnp.bfloat16))
            ps.append(probs.astype(jnp.bfloat16))
        for head in range(HEADS_HERE):
            span = slice(head * HEAD_DIM, (head + 1) * HEAD_DIM)
            dq_acc[span, :] += jnp.dot(
                keys_t[span, :], dss[head], preferred_element_type=jnp.float32
            )
            sums[KEY_GROUP[head]] += jnp.dot(
                dss[head], qm_ref[head], preferred_element_type=jnp.float32
            )
            sums[VALUE_GROUP[head]] += jnp.dot(
                ps[head], gm_ref[head], preferred_element_type=jnp.float32
            )
        for g in range(3):
            dkv_acc[rows, lane_group(g)] = sums[g]
        return carry

    lax.fori_loop(bounds[0, tile], bounds[1, tile], step, 0)
    dq_ref[...] = (dq_acc[...].T * HEAD_DIM ** (-0.5)).astype(dq_ref.dtype)

    @pl.when(tile == pl.num_programs(0) - 1)
    def _():
        dkv_ref[...] = dkv_acc[...].astype(dkv_ref.dtype)


def attend_back(bounds, queries, window, seg_keys, seg_queries, grads, outt, lse):
    rows, wide = queries.shape
    span, width = window.shape
    return pl.pallas_call(
        attend_back_kernel,
        grid_spec=pltpu.PrefetchScalarGridSpec(
            num_scalar_prefetch=1,
            grid=(rows // TILE,),
            in_specs=[
                pl.BlockSpec((TILE, wide), lambda i, b: (i, 0)),
                pl.BlockSpec((span, width), lambda i, b: (0, 0)),
                pl.BlockSpec((1, span), lambda i, b: (0, 0)),
                pl.BlockSpec((1, TILE), lambda i, b: (0, i)),
                pl.BlockSpec((TILE, wide), lambda i, b: (i, 0)),
                pl.BlockSpec((wide, TILE), lambda i, b: (0, i)),
                pl.BlockSpec((8, TILE), lambda i, b: (0, i)),
            ],
            out_specs=[
                pl.BlockSpec((TILE, wide), lambda i, b: (i, 0)),
                pl.BlockSpec((span, width), lambda i, b: (0, 0)),
            ],
            scratch_shapes=[
                pltpu.VMEM((HEADS_HERE, TILE, LANES), jnp.bfloat16),
                pltpu.VMEM((HEADS_HERE, TILE, LANES), jnp.bfloat16),
                pltpu.VMEM((8, TILE), jnp.float32),
                pltpu.VMEM((wide, TILE), jnp.float32),
                pltpu.VMEM((span, width), jnp.float32),
            ],
        ),
        out_shape=[
            jax.ShapeDtypeStruct((rows, wide), jnp.bfloat16),
            jax.ShapeDtypeStruct((span, width), jnp.bfloat16),
        ],
        compiler_params=pltpu.CompilerParams(vmem_limit_bytes=63 * 2**20),
        name="attend_back",
    )(bounds, queries, window, seg_keys, seg_queries, grads, outt, lse)


def rolled(part):
    return jnp.concatenate([part[..., HEAD_DIM:], part[..., :HEAD_DIM]], axis=-1)


def joined_halves(lower, upper):
    return jnp.concatenate([lower[..., :HEAD_DIM], upper[..., HEAD_DIM:]], axis=-1)


def lanes_of(values):
    return [values[..., lane_group(g)] for g in range(3)]


def parts_of_queries(queries, upper):
    one, two, three = lanes_of(queries)
    swapped = rolled(two)
    first, second = (swapped, two) if upper else (two, swapped)
    return jnp.stack(
        [jnp.concatenate([one, first], axis=-1), jnp.concatenate([three, second], axis=-1)], axis=1
    ).reshape(TEAM, queries.shape[1], 2 * LANES)


def parts_of_keys(keys, values):
    k = lanes_of(keys)
    v = lanes_of(values)
    low = jnp.concatenate([k[0], joined_halves(k[1], rolled(v[1])), v[0]], axis=-1)
    high = jnp.concatenate([k[2], joined_halves(rolled(k[1]), v[1]), v[2]], axis=-1)
    return jnp.stack([low, high], axis=1).reshape(TEAM, keys.shape[1], 3 * LANES)


def natural_rows(parts):
    pairs = parts.reshape(TEAM // 2, 2, parts.shape[1], 2 * LANES)
    low, high = pairs[:, 0], pairs[:, 1]
    middle = joined_halves(low[..., LANES:], rolled(high[..., LANES:]))
    return jnp.concatenate([low[..., :LANES], middle, high[..., :LANES]], axis=-1)


def natural_keys(parts):
    pairs = parts.reshape(TEAM // 2, 2, parts.shape[1], 3 * LANES)
    low, high = lanes_of(pairs[:, 0]), lanes_of(pairs[:, 1])
    keys = jnp.concatenate([low[0], joined_halves(low[1], rolled(high[1])), high[0]], axis=-1)
    values = jnp.concatenate([low[2], joined_halves(rolled(low[1]), high[1]), high[2]], axis=-1)
    return keys, values


TEAM = 4


def flip(index, step):
    return index + step * (1 - 2 * lax.rem(lax.div(index, step), 2))


def mate(rank, offset):
    if offset % 2:
        rank = flip(rank, 1)
    if offset // 2:
        rank = flip(rank, 2)
    return rank


def greet(peers):
    barrier = pltpu.get_barrier_semaphore()
    for peer in peers:
        pl.semaphore_signal(
            barrier, inc=1, device_id=peer, device_id_type=pl.DeviceIdType.MESH
        )
    pl.semaphore_wait(barrier, len(peers))


def remote(src, dst, send, recv, peer):
    return pltpu.make_async_remote_copy(
        src_ref=src,
        dst_ref=dst,
        send_sem=send,
        recv_sem=recv,
        device_id=peer,
        device_id_type=pl.DeviceIdType.MESH,
    )


RIM = 16
SMALL_ROWS = 128
SMALL_IN = 128
ROW_IN_KERNEL_W = 32
ROW_PAIR_QV, ROW_PAIR_PC, ROW_IN_KERNEL_B = 19, 20, 21
ROW_OUTPUT_B, ROW_GAIN1, ROW_SHIFT1, ROW_OUTER_B, ROW_GAIN2, ROW_SHIFT2 = range(9, 15)
ROW_INNER_B = 15
ROW_QUERY_B, ROW_VALUE_B, ROW_POINT_B, ROW_CONV_B = range(19, 23)
ROW_KERNEL_B = 24
ROW_KERNEL_W = 48
TAP_ROWS = 8 * KERNEL


def dot(left, right):
    return jnp.dot(left, right, preferred_element_type=jnp.float32)


def dot_tn(left, right):
    return lax.dot_general(
        left, right, (((0,), (0,)), ((), ())), preferred_element_type=jnp.float32
    )


def half_turn(block):
    return pltpu.roll(block, HEAD_DIM, axis=1)


def mixed_lanes(lower, upper):
    lane = lax.broadcasted_iota(jnp.int32, lower.shape, 1)
    return jnp.where(lane < HEAD_DIM, lower, upper)


def pair_row(small_ref, row, second):
    first = jnp.broadcast_to(small_ref[0, row : row + 1, :], (8, 384))
    other = jnp.broadcast_to(small_ref[1, row : row + 1, :], (8, 384))
    lane = lax.broadcasted_iota(jnp.int32, first.shape, 1)
    if second:
        first = pltpu.roll(first, 192, axis=1)
    else:
        other = pltpu.roll(other, 192, axis=1)
    return jnp.where(lane < 192, first, other)[0:1, :]


def tap_major(shape, offset):
    row = lax.broadcasted_iota(jnp.int32, shape, 0)
    column = lax.broadcasted_iota(jnp.int32, shape, 1) + offset
    head = lax.rem(row, 8)
    wanted = (head * KERNEL + lax.div(row, 8) == column) & (head < HEADS)
    return wanted & (row < TAP_ROWS)


def kernel_rows(first, other):
    lane = lax.broadcasted_iota(jnp.int32, first.shape, 1)
    rows = jnp.where(lane < 192, first, pltpu.roll(other, 192, axis=1))
    return jnp.concatenate(
        [rows, jnp.zeros((LANES - TAP_ROWS, rows.shape[1]), jnp.float32)], axis=0
    ).astype(jnp.bfloat16)


def kernel_bias(small_ref):
    half = HEADS * KERNEL // 2
    total = jnp.zeros((LANES, 1), jnp.float32)
    for w in range(2):
        row = small_ref[w, ROW_IN_KERNEL_B : ROW_IN_KERNEL_B + 1, 0:LANES]
        lane = lax.broadcasted_iota(jnp.int32, (LANES, LANES), 1)
        wanted = tap_major((LANES, LANES), w * half) & (lane < half)
        total = total + jnp.sum(jnp.where(wanted, row, 0.0), axis=1, keepdims=True)
    return total


def rows_of(ref, base, count):
    view = pl.ds(pl.multiple_of(base, 16), count)
    return ref.at[:, view, :] if len(ref.shape) == 3 else ref.at[view, :]


CHUNKS = 4


def front_kernel(count, *refs):
    x_ref, seg_ref, mask_ref, depth_in, kernel_in, kernel_b_in = refs[:6]
    vectors, pairs = refs[6:13], refs[13:17]
    shards = list(refs[17 : 16 + count])
    outer_any = refs[16 + count]
    rest = refs[17 + count :]
    outs = rest[: count + 9]
    half_any = rest[count + 9]
    win_ref, qteam_ref = outs[count : count + 2]
    holds = rest[count + 10 : 2 * count + 17]
    fulls = holds[:count]
    queries_ref, xrim_ref, depth_ref, spans_ref, kern_ref, ext_ref, conv_ref = holds[count:]
    (kv_part, q_part, seg_col, halo_low, halo_high, spread_ref, taps_ref, wide_ref,
     send_y, recv_y, send_c, recv_c, local, send_h, recv_h, send_kv, recv_kv, send_q, recv_q,
     send_l, recv_l, send_r, recv_r, emit_sem, small_f32, small_own, outer_half, half_sem) = rest[
        2 * count + 17 :
    ]
    shards.insert(2, small_own)
    key_ref, value_ref, small2d, query_ref, point_ref, convw_ref = fulls[:6]
    me, side = lax.axis_index("ctx"), lax.axis_index("wsh")
    size = lax.axis_size("ctx")
    core = lax.rem(me, 2)
    rank = lax.rem(me, TEAM)
    chip = lax.div(rank, 2)
    base = me - rank
    team = lax.div(me, TEAM)
    teams = size // TEAM
    right, left = lax.rem(me + TEAM, size), lax.rem(me + size - TEAM, size)
    after, prior = lax.rem(me + 1, size), lax.rem(me + size - 1, size)
    twin, across = {"ctx": flip(me, 1)}, {"wsh": 1 - side}
    seqs, block, model = x_ref.shape
    halo = (TEAM - 1) * block
    width = HEADS * HEAD_DIM
    chunk_rows = block // CHUNKS
    greet(
        [{"ctx": base + mate(rank, o)} for o in range(1, TEAM)]
        + [across, {"ctx": right}, {"ctx": left}, {"ctx": after}, {"ctx": prior}]
    )

    to_y, passed, own, emitted = [], [], [], []
    for i in range(count):
        rows = shards[i].shape[-2]
        to_y.append(
            remote(
                rows_of(shards[i], core * (rows // 2), rows // 2),
                rows_of(fulls[i], side * rows + core * (rows // 2), rows // 2),
                send_y.at[i], recv_y.at[i], across,
            )
        )
        came = rows_of(fulls[i], (1 - side) * rows + core * (rows // 2), rows // 2)
        passed.append(remote(came, came, send_c.at[i], recv_c.at[i], twin))
        own.append(
            pltpu.make_async_copy(shards[i], rows_of(fulls[i], side * rows, rows), local.at[i])
        )

    def emit(hold, out):
        copy = pltpu.make_async_copy(hold, out, emit_sem.at[len(emitted)])
        copy.start()
        emitted.append(copy)

    def emit_named(k):
        emit(holds[count + k], outs[count + 2 + k])

    urgent = 3
    for i in range(2):
        to_y[i].start()
    for i in range(2):
        own[i].start()
    half_rows = outer_half.shape[1]
    load_half = pltpu.make_async_copy(
        outer_any.at[:, part_rows(core * half_rows, half_rows), :], outer_half, half_sem.at[0]
    )
    load_half.start()
    small_f32[...] = jnp.zeros_like(small_f32)
    small_f32[0:KERNEL, :] = depth_in[...].astype(jnp.float32)

    def as_row(ref):
        return ref[...].astype(jnp.float32).reshape(1, ref.shape[0])

    at = KERNEL
    for ref in vectors:
        row = as_row(ref)
        for k in range(ref.shape[0] // 384):
            small_f32[at : at + 1, :] = row[:, k * 384 : (k + 1) * 384]
            at += 1
    for k in range(2):
        small_f32[at : at + 1, 0:192] = as_row(pairs[2 * k])
        small_f32[at : at + 1, 192:384] = as_row(pairs[2 * k + 1])
        at += 1
    small_f32[at : at + 1, 0 : kernel_b_in.shape[0]] = as_row(kernel_b_in)
    pick = jnp.where(tap_major((LANES, HEADS * KERNEL), 0), 1.0, 0.0).astype(jnp.bfloat16)
    small_f32[ROW_IN_KERNEL_W : ROW_IN_KERNEL_W + TAP_ROWS, 0:192] = dot(pick, kernel_in[...])[
        0:TAP_ROWS, :
    ]
    small_own[...] = small_f32[...].astype(jnp.bfloat16)
    to_y[2].start()
    own[2].start()
    to_after = remote(x_ref.at[:, pl.ds(block - RIM, RIM), :], halo_low, send_h.at[0],
                      recv_h.at[0], {"ctx": after})
    to_prior = remote(x_ref.at[:, pl.ds(0, RIM), :], halo_high, send_h.at[1], recv_h.at[1],
                      {"ctx": prior})
    pl.when(me < size - 1)(to_after.start)
    pl.when(me > 0)(to_prior.start)
    to_y[urgent].start()
    own[urgent].start()

    @pl.when(me == 0)
    def _():
        halo_low[...] = jnp.zeros_like(halo_low)

    @pl.when(me == size - 1)
    def _():
        halo_high[...] = jnp.zeros_like(halo_high)

    for s in range(seqs):
        seg_col[s] = jnp.broadcast_to(seg_ref[s : s + 1, :], (LANES, seg_ref.shape[1])).T
        for g in range(model // LANES):
            xrim_ref[s, g, pl.ds(RIM, block), :] = x_ref[s, :, lane_group(g)].astype(jnp.float32)

    def arrive(i):
        to_y[i].wait_recv()
        passed[i].start()

    def settle(i):
        own[i].wait()
        passed[i].wait_recv()
        emit(fulls[i], outs[i])

    for i in range(urgent):
        arrive(i)
    for i in (4, 5, 6, 7):
        to_y[i].start()
        own[i].start()
    for i in range(urgent):
        settle(i)
    small_ref = taps_ref
    for w in range(2):
        small_ref[w] = small2d[pl.ds(w * SMALL_IN, SMALL_IN), :].astype(jnp.float32)
    value_bias = pair_row(small_ref, ROW_PAIR_QV, True)
    query_bias = pair_row(small_ref, ROW_PAIR_QV, False)

    def piece(r, c):
        return win_ref.at[
            pl.ds(pl.multiple_of(halo + r * block + c * chunk_rows, 16), chunk_rows), :
        ]

    def part(r, c):
        return kv_part.at[r, pl.ds(c * chunk_rows, chunk_rows), :]

    def kv_copy(r, c):
        return (
            pltpu.make_async_copy(part(r, c), piece(rank, c), recv_kv.at[rank * CHUNKS + c]),
            remote(part(r, c), piece(rank, c), send_kv.at[r * CHUNKS + c],
                   recv_kv.at[rank * CHUNKS + c], {"ctx": base + r}),
        )

    def q_copy(r):
        return (
            pltpu.make_async_copy(q_part.at[r], qteam_ref.at[rank], recv_q.at[rank]),
            remote(q_part.at[r], qteam_ref.at[rank], send_q.at[r], recv_q.at[rank],
                   {"ctx": base + r}),
        )

    def begin(pair, r):
        pl.when(rank == r)(pair[0].start)
        pl.when(rank != r)(pair[1].start)

    for s in (1 - chip, chip):
        rows = x_ref[s]
        keys = dot(rows, key_ref[...])
        values = dot(rows, value_ref[...]) + value_bias
        k = [keys[:, lane_group(g)] for g in range(3)]
        v = [values[:, lane_group(g)] for g in range(3)]
        for half, groups in enumerate((
            (k[0], mixed_lanes(k[1], half_turn(v[1])), v[0]),
            (k[2], mixed_lanes(half_turn(k[1]), v[1]), v[2]),
        )):
            for g in range(3):
                kv_part[2 * s + half, :, lane_group(g)] = groups[g].astype(jnp.bfloat16)
        for c in range(CHUNKS):
            for half in range(2):
                begin(kv_copy(2 * s + half, c), 2 * s + half)

    def onward(r, c):
        to_right = remote(
            piece(r, c),
            win_ref.at[
                pl.ds(pl.multiple_of(lax.rem(r + TEAM - 1, TEAM) * block + c * chunk_rows, 16),
                      chunk_rows), :
            ],
            send_r.at[r * CHUNKS + c], recv_r.at[r * CHUNKS + c], {"ctx": right},
        )
        to_left = remote(
            piece(r, c),
            win_ref.at[
                pl.ds(
                    pl.multiple_of(
                        halo + TEAM * block + lax.rem(r, TEAM - 1) * block + c * chunk_rows, 16
                    ),
                    chunk_rows,
                ), :
            ],
            send_l.at[r * CHUNKS + c], recv_l.at[r * CHUNKS + c], {"ctx": left},
        )
        return to_right, to_left

    def relay(o, c):
        r = mate(rank, o)
        if o == 0:
            kv_copy(r, c)[0].wait()
        else:
            remote(part(rank, c), piece(r, c), send_kv.at[rank * CHUNKS + c],
                   recv_kv.at[r * CHUNKS + c], {"ctx": base + r}).wait_recv()
        to_right, to_left = onward(r, c)
        pl.when((r >= 1) & (team < teams - 1))(to_right.start)
        pl.when((r <= TEAM - 2) & (team > 0))(to_left.start)

    for c in range(CHUNKS):
        relay(0, c)
        relay(1, c)
    arrive(urgent)
    settle(urgent)
    for s in range(seqs):
        queries = dot(x_ref[s], query_ref[...]) + query_bias
        queries_ref[s] = queries.astype(jnp.bfloat16)
        q = [queries[:, lane_group(g)] for g in range(3)]
        for half, groups in enumerate(((q[0], q[1]), (q[2], half_turn(q[1])))):
            for g in range(2):
                q_part[2 * s + half, :, lane_group(g)] = groups[g].astype(jnp.bfloat16)
        for half in range(2):
            begin(q_copy(2 * s + half), 2 * s + half)
    emit_named(0)

    pl.when(me > 0)(to_after.wait_recv)
    pl.when(me < size - 1)(to_prior.wait_recv)
    for s in range(seqs):
        for g in range(model // LANES):
            xrim_ref[s, g, pl.ds(0, RIM), :] = halo_low[s, :, lane_group(g)].astype(jnp.float32)
            xrim_ref[s, g, pl.ds(RIM + block, RIM), :] = halo_high[s, :, lane_group(g)].astype(
                jnp.float32
            )
    emit_named(1)
    strip = 32
    lead = RIM - KERNEL // 2

    def taps_row(j, g):
        return small_ref[g // 3, j : j + 1, lane_group(g % 3)]

    def depth_strip(c, s):
        start = c * strip
        here = seg_col[s, pl.ds(RIM + start, strip), :]
        sums = [jnp.zeros((strip, LANES), jnp.float32) for _ in range(model // LANES)]
        for j in range(KERNEL):
            same = seg_col[s, pl.ds(lead + j + start, strip), :] == here
            for g in range(model // LANES):
                near = xrim_ref[s, g, pl.ds(lead + j + start, strip), :]
                sums[g] = sums[g] + jnp.where(same, near, 0.0) * taps_row(j, g)
        for g in range(model // LANES):
            depth_ref[s, pl.ds(pl.multiple_of(start, strip), strip), lane_group(g)] = sums[
                g
            ].astype(jnp.bfloat16)
        return s

    relay(2, 0)
    relay(3, 0)
    lax.fori_loop(0, block // strip, depth_strip, 0)
    relay(2, 1)
    relay(3, 1)
    lax.fori_loop(0, block // strip, depth_strip, 1)
    emit_named(2)
    for c in range(2, CHUNKS):
        relay(2, c)
        relay(3, c)
    for j in range(KERNEL):
        row = lax.broadcasted_iota(jnp.int32, (2 * LANES, width), 0)
        col = lax.broadcasted_iota(jnp.int32, (2 * LANES, width), 1)
        row = jnp.where(row >= LANES, row - LANES, row)
        spread_ref[j] = jnp.where(row == 8 * j + col // HEAD_DIM, 1.0, 0.0).astype(jnp.bfloat16)
    for i in (4, 5):
        arrive(i)
    for i in (4, 5):
        settle(i)
    load_half.wait()
    emit(outer_half, half_any)
    point_bias = pair_row(small_ref, ROW_PAIR_PC, False)
    conv_bias = pair_row(small_ref, ROW_PAIR_PC, True)
    tap_view = slice(ROW_IN_KERNEL_W, ROW_IN_KERNEL_W + TAP_ROWS)
    kernel_w = kernel_rows(small_ref[0, tap_view, :], small_ref[1, tap_view, :])
    kernel_b = kernel_bias(small_ref)
    for s in range(seqs):
        spans = dot(depth_ref[s], point_ref[...]) + point_bias
        spans_ref[s] = spans
        mixed = (spans * queries_ref[s].astype(jnp.float32)).astype(jnp.bfloat16)
        logits = rows_nt(kernel_w, mixed) + kernel_b
        cut = [logits[8 * j : 8 * j + 8, :] for j in range(KERNEL)]
        top = functools.reduce(jnp.maximum, cut)
        expo = [jnp.exp(part - top) for part in cut]
        inverse = 1.0 / sum(expo)
        for j in range(KERNEL):
            kern = expo[j] * inverse
            kern_ref[s, 8 * j : 8 * j + 8, :] = kern
            wide_ref[8 * j : 8 * j + 8, :] = kern * mask_ref[s, j : j + 1, :]
        wide_ref[TAP_ROWS:, :] = jnp.zeros((LANES - TAP_ROWS, block), jnp.float32)
        tall = wide_ref[...].T
        high = tall.astype(jnp.bfloat16)
        low = (tall - high.astype(jnp.float32)).astype(jnp.bfloat16)
        both = jnp.concatenate([high, low], axis=1)
        for g in range(3):
            row_ext = [xrim_ref[s, k] for k in range(model // LANES)]
        ext = dot(
            jnp.concatenate([part.astype(jnp.bfloat16) for part in row_ext], axis=1),
            convw_ref[...],
        ) + conv_bias
        for g in range(3):
            ext_ref[s, g] = ext[:, lane_group(g)]
        chunk = 128
        for c in range(block // chunk):
            sums = [jnp.zeros((chunk, LANES), jnp.float32) for _ in range(3)]
            for j in range(KERNEL):
                weight = dot(both[c * chunk : (c + 1) * chunk, :], spread_ref[j])
                for g in range(3):
                    near = ext_ref[s, g, pl.ds(lead + j + c * chunk, chunk), :]
                    sums[g] = sums[g] + weight[:, lane_group(g)] * near
            for g in range(3):
                conv_ref[s, pl.ds(c * chunk, chunk), lane_group(g)] = sums[g].astype(jnp.bfloat16)

    for k in range(3, 7):
        emit_named(k)
    for i in (6, 7):
        arrive(i)
    for i in (6, 7):
        settle(i)
    for r in range(TEAM):
        for c in range(CHUNKS):
            pl.when(rank != r)(kv_copy(r, c)[1].wait_send)
        pl.when(rank != r)(q_copy(r)[1].wait_send)
    for o in range(TEAM):
        r = mate(rank, o)
        if o == 0:
            q_copy(r)[0].wait()
        else:
            remote(q_part.at[rank], qteam_ref.at[r], send_q.at[rank], recv_q.at[r],
                   {"ctx": base + r}).wait_recv()
    for r in range(TEAM):
        for c in range(CHUNKS):
            to_right, to_left = onward(jnp.int32(r), c)
            if r >= 1:
                pl.when(team < teams - 1)(to_right.wait_send)
                pl.when(team > 0)(to_right.wait_recv)
            if r <= TEAM - 2:
                pl.when(team > 0)(to_left.wait_send)
                pl.when(team < teams - 1)(to_left.wait_recv)
    for i in range(count):
        to_y[i].wait_send()
        passed[i].wait_send()
    pl.when(me < size - 1)(to_after.wait_send)
    pl.when(me > 0)(to_prior.wait_send)
    for copy in emitted:
        copy.wait()


def front(hidden, seg_rim, tap_mask, depth, kernel, kernel_b, vectors, pairs, shards, outer):
    seqs, block, model = hidden.shape
    small = jax.ShapeDtypeStruct((SMALL_IN, 384), hidden.dtype)
    gathered = list(shards[:2]) + [small] + list(shards[2:])
    count = len(gathered)
    half = jax.ShapeDtypeStruct((outer.shape[0], outer.shape[1] // 2, outer.shape[2]), outer.dtype)
    width = HEADS * HEAD_DIM
    wide = block + 2 * RIM
    fulls = [
        jax.ShapeDtypeStruct(s.shape[:-2] + (2 * s.shape[-2], s.shape[-1]), s.dtype) for s in gathered
    ]
    vmem = pl.BlockSpec(memory_space=pltpu.VMEM)
    anywhere = pl.BlockSpec(memory_space=pl.ANY)
    low, full = jnp.bfloat16, jnp.float32
    outs = [
        jax.ShapeDtypeStruct(((3 * TEAM - 2) * block, width), low),
        jax.ShapeDtypeStruct((TEAM, block, 2 * LANES), low),
        jax.ShapeDtypeStruct((seqs, block, width), low),
        jax.ShapeDtypeStruct((seqs, model // LANES, wide, LANES), full),
        jax.ShapeDtypeStruct((seqs, block, model), low),
        jax.ShapeDtypeStruct((seqs, block, width), full),
        jax.ShapeDtypeStruct((seqs, TAP_ROWS, block), full),
        jax.ShapeDtypeStruct((seqs, 3, wide, LANES), full),
        jax.ShapeDtypeStruct((seqs, block, width), low),
    ]
    dma = pltpu.SemaphoreType.DMA
    return pl.pallas_call(
        functools.partial(front_kernel, count),
        out_shape=fulls + outs + [half],
        in_specs=[vmem] * 17 + [anywhere] * count,
        out_specs=[anywhere] * (count + 10),
        scratch_shapes=[pltpu.VMEM(s.shape, s.dtype) for s in fulls + outs[2:]] + [
            pltpu.VMEM((TEAM, block, width), low),
            pltpu.VMEM((TEAM, block, 2 * LANES), low),
            pltpu.VMEM((seqs, seg_rim.shape[1], LANES), full),
            pltpu.VMEM((seqs, RIM, model), low),
            pltpu.VMEM((seqs, RIM, model), low),
            pltpu.VMEM((KERNEL, 2 * LANES, width), low),
            pltpu.VMEM((2, SMALL_IN, 384), full),
            pltpu.VMEM((LANES, block), full),
            dma((count,)), dma((count,)), dma((count,)), dma((count,)), dma((count,)),
            dma((2,)), dma((2,)),
            dma((TEAM * CHUNKS,)), dma((TEAM * CHUNKS,)), dma((TEAM,)), dma((TEAM,)),
            dma((TEAM * CHUNKS,)), dma((TEAM * CHUNKS,)), dma((TEAM * CHUNKS,)),
            dma((TEAM * CHUNKS,)), dma((count + 8,)),
            pltpu.VMEM((SMALL_IN, 384), full), pltpu.VMEM((SMALL_IN, 384), low),
            pltpu.VMEM(half.shape, low), dma((1,)),
        ],
        compiler_params=pltpu.CompilerParams(
            collective_id=0, has_side_effects=True, vmem_limit_bytes=56 * 2**20
        ),
        name="front",
    )(hidden, seg_rim, tap_mask, depth, kernel, kernel_b, *vectors, *pairs, *shards, outer)
PACK_A = 1280
PACK_B = 768
SMALL_AT = 1152


def chips_of(me, size):
    core = lax.rem(me, 2)
    count = size // 2
    index = lax.div(me, 2)
    return index, count, lambda other: other * 2 + core


def pair_of(me, size):
    index = lax.rem(lax.div(me, 2), 2)
    return index, 2, lambda other: flip(me, 2)


def column_of(me, size):
    index = lax.div(me, TEAM)
    rest = lax.rem(me, TEAM)
    return index, size // TEAM, lambda other: other * TEAM + rest


def part_rows(base, count):
    return pl.ds(pl.multiple_of(base, 16), count)


def others(index, count):
    return [lax.rem(index + o, count) for o in range(1, count)]


def scatter_copies(stage, me, size, staged, came, send, recv):
    index, count, device = stage(me, size)
    piece = staged.shape[0] // count
    return [
        remote(staged.at[part_rows(other * piece, piece), :], came.at[index], send.at[other],
               recv.at[index], {"ctx": device(other)})
        for other in others(index, count)
    ]


def scatter_wait(stage, me, size, staged, came, send, recv):
    index, count, device = stage(me, size)
    piece = staged.shape[0] // count
    for other in others(index, count):
        remote(staged.at[part_rows(index * piece, piece), :], came.at[other], send.at[index],
               recv.at[other], {"ctx": device(other)}).wait_recv()


def share_copies(stage, me, size, fin, base, piece, send, recv):
    index, count, device = stage(me, size)
    view = fin.at[part_rows(base + index * piece, piece), :]
    return [
        remote(view, view, send.at[other], recv.at[index], {"ctx": device(other)})
        for other in others(index, count)
    ]


def share_wait(stage, me, size, fin, base, piece, send, recv):
    index, count, device = stage(me, size)
    for other in others(index, count):
        view = fin.at[part_rows(base + other * piece, piece), :]
        remote(view, view, send.at[index], recv.at[other], {"ctx": device(other)}).wait_recv()


def in_chunks(rows, body):
    chunk = max(c for c in range(16, 241, 16) if rows % c == 0)

    def step(i, carry):
        body(pl.multiple_of(i * chunk, 16), chunk)
        return carry

    lax.fori_loop(0, rows // chunk, step, 0)


def wide(value):
    return value.astype(jnp.float32)


def back_kernel(names, a_names, b_names, loaded, *refs):
    count_a, count_b = len(a_names), len(b_names)
    r = types.SimpleNamespace(**dict(zip(names, refs)))
    late = refs[len(names) :]
    block_a = types.SimpleNamespace(**dict(zip(a_names, late[:count_a])))
    block_b = types.SimpleNamespace(**dict(zip(b_names, late[count_a : count_a + count_b])))
    fetch_refs = late[count_a + count_b :]
    v = types.SimpleNamespace(**dict(zip(loaded, fetch_refs[len(loaded) :])))
    me, side = lax.axis_index("ctx"), lax.axis_index("wsh")
    size = lax.axis_size("ctx")
    core = lax.rem(me, 2)
    rank = lax.rem(me, TEAM)
    chip = lax.div(rank, 2)
    base = me - rank
    team = lax.div(me, TEAM)
    teams = size // TEAM
    twin, across = {"ctx": flip(me, 1)}, {"wsh": 1 - side}
    right, left = lax.rem(me + TEAM, size), lax.rem(me + size - TEAM, size)
    after, prior = lax.rem(me + 1, size), lax.rem(me + size - 1, size)
    seqs, block, model = v.x.shape
    width = HEADS * HEAD_DIM
    halo = (TEAM - 1) * block
    groups = model // LANES
    low = jnp.bfloat16
    index, count, device = chips_of(me, size)
    greet(
        [twin, across, {"ctx": base + mate(rank, 3)}, {"ctx": after}, {"ctx": prior}]
        + [{"ctx": device(other)} for other in others(index, count)]
    )

    def block_of(k):
        return pl.ds(pl.multiple_of(k * block, 16), block)

    def halo_left(c):
        return remote(r.window.at[block_of(2 * TEAM - 1 + c), :], r.from_left.at[block_of(c), :],
                      r.send_l.at[c], r.recv_l.at[c], {"ctx": right})

    def halo_right(c):
        return remote(r.window.at[block_of(c), :], r.from_right.at[block_of(c + 1), :],
                      r.send_r.at[c], r.recv_r.at[c], {"ctx": left})

    for k in range(TEAM - 1):
        to_right = halo_left(chip * k + (1 - chip) * (TEAM - 2 - k))
        to_left = halo_right(chip * k + (1 - chip) * ((k + 1) % (TEAM - 1)))
        pl.when(team < teams - 1)(to_right.start)
        pl.when(team > 0)(to_left.start)

    fetched = types.SimpleNamespace()
    for k, name in enumerate(loaded):
        copy = pltpu.make_async_copy(fetch_refs[k], fetch_refs[len(loaded) + k], r.load.at[k])
        setattr(fetched, name, copy)
    center = pltpu.make_async_copy(r.window.at[pl.ds(halo, TEAM * block), :], r.mine,
                                   r.load.at[len(loaded)])
    fetched.keep.start()
    fetched.came.start()
    center.start()

    def q_copy(o):
        other = mate(rank, o)
        return remote(r.dq.at[other], r.q_parts.at[rank], r.send_q.at[o], r.recv_q.at[o],
                      {"ctx": base + other})

    own_q = pltpu.make_async_copy(r.dq.at[rank], r.q_parts.at[rank], r.recv_q.at[0])
    for o in (3, 2, 1):
        q_copy(o).start()
    own_q.start()
    for name in loaded[2:]:
        getattr(fetched, name).start()

    def have(*copies):
        for copy in copies:
            copy.wait()

    half_ff = v.keep.shape[1]
    pair_index, _, _ = pair_of(me, size)
    have(fetched.keep, fetched.came)

    def stage_across(at, n):
        rows = part_rows(at, n)
        r.ff_send[rows, :] = (v.keep[1 - side, rows, :] + wide(v.came[1 - side, rows, :])).astype(low)
        v.keep[side, rows, :] = v.keep[side, rows, :] + wide(v.came[side, rows, :])

    in_chunks(half_ff, stage_across)
    ff_across = remote(r.ff_send, r.ff_came, r.send_p.at[0], r.recv_p.at[0], across)
    ff_across.start()

    small = r.sums
    small[...] = jnp.zeros_like(small)
    for j in range(KERNEL):
        row = lax.broadcasted_iota(jnp.int32, (2 * LANES, width), 0)
        col = lax.broadcasted_iota(jnp.int32, (2 * LANES, width), 1)
        row = jnp.where(row >= LANES, row - LANES, row)
        r.spread[j] = jnp.where(row == 8 * j + col // HEAD_DIM, 1.0, 0.0).astype(low)

    zero_block = jnp.zeros((block, width), low)
    r.from_left[pl.ds((TEAM - 1) * block, block), :] = zero_block
    r.from_right[0:block, :] = zero_block

    @pl.when(team == 0)
    def _():
        for k in range(TEAM - 1):
            r.from_left[pl.ds(k * block, block), :] = zero_block

    @pl.when(team == teams - 1)
    def _():
        for k in range(1, TEAM):
            r.from_right[pl.ds(k * block, block), :] = zero_block

    @pl.when(me == 0)
    def _():
        r.dd_low[...] = jnp.zeros_like(r.dd_low)
        r.rim_low[...] = jnp.zeros_like(r.rim_low)

    @pl.when(me == size - 1)
    def _():
        r.dd_high[...] = jnp.zeros_like(r.dd_high)
        r.rim_high[...] = jnp.zeros_like(r.rim_high)

    small_ref = r.small
    kernel_w = kernel_rows(
        wide(small_ref[ROW_IN_KERNEL_W : ROW_IN_KERNEL_W + TAP_ROWS, :]),
        wide(small_ref[SMALL_IN + ROW_IN_KERNEL_W : SMALL_IN + ROW_IN_KERNEL_W + TAP_ROWS, :]),
    )
    lead = RIM - KERNEL // 2
    chunk = 128
    r.d_ext[...] = jnp.zeros_like(r.d_ext)
    have(fetched.dconv, fetched.ext, fetched.kern, fetched.point, fetched.queries, fetched.spans)
    wide_ref, tall_ref = r.wide, r.tall

    def conv_back(s):
        r.seg_col[s] = jnp.broadcast_to(r.seg[s : s + 1, :], (LANES, r.seg.shape[1])).T
        for j in range(KERNEL):
            wide_ref[8 * j : 8 * j + 8, :] = (
                v.kern[s, 8 * j : 8 * j + 8, :] * r.mask[s, j : j + 1, :]
            )
        wide_ref[TAP_ROWS:, :] = jnp.zeros((LANES - TAP_ROWS, block), jnp.float32)
        tall = wide_ref[...].T
        high = tall.astype(low)
        both = jnp.concatenate([high, (tall - wide(high)).astype(low)], axis=1)
        for c in range(block // chunk):
            rows = slice(c * chunk, (c + 1) * chunk)
            grad = wide(v.dconv[s, rows, :])
            taps = jnp.zeros((chunk, LANES), jnp.float32)
            for j in range(KERNEL):
                near = jnp.concatenate(
                    [v.ext[s, g, pl.ds(lead + j + c * chunk, chunk), :] for g in range(3)],
                    axis=1,
                )
                term = near * grad
                first = term.astype(low)
                second = (term - wide(first)).astype(low)
                taps = taps + rows_nt(first, r.spread[j, 0:LANES, :])
                taps = taps + rows_nt(second, r.spread[j, 0:LANES, :])
                weight = dot(both[rows, :], r.spread[j]) * grad
                for g in range(3):
                    r.d_ext[s, g, pl.ds(lead + j + c * chunk, chunk), :] += weight[
                        :, lane_group(g)
                    ]
            tall_ref[rows, :] = taps
        back = tall_ref[...].T
        inner = jnp.zeros((8, block), jnp.float32)
        for j in range(KERNEL):
            inner = inner + v.kern[s, 8 * j : 8 * j + 8, :] * (
                back[8 * j : 8 * j + 8, :] * r.mask[s, j : j + 1, :]
            )
        for j in range(KERNEL):
            wide_ref[8 * j : 8 * j + 8, :] = v.kern[s, 8 * j : 8 * j + 8, :] * (
                back[8 * j : 8 * j + 8, :] * r.mask[s, j : j + 1, :] - inner
            )
        d_logits = wide_ref[0:TAP_ROWS, :].astype(low)
        mixed = (v.spans[s] * wide(v.queries[s])).astype(low)
        kernel_grad = dot(d_logits, mixed)
        kernel_bias = dot(d_logits, jnp.ones((block, LANES), low))
        for w in range(2):
            small[w, ROW_KERNEL_W : ROW_KERNEL_W + TAP_ROWS, :] += kernel_grad
            for g in range(3):
                small[w, ROW_KERNEL_B : ROW_KERNEL_B + 24, lane_group(g)] += kernel_bias[
                    24 * g : 24 * g + 24, :
                ]
        d_mixed = dot(wide_ref[...].T.astype(low), kernel_w)
        d_spans = (d_mixed * wide(v.queries[s])).astype(low)
        v.spans[s] = d_mixed * v.spans[s]
        v.dconv[s] = d_spans
        bias = jnp.sum(wide(d_spans), axis=0, keepdims=True)
        for w in range(2):
            small[w, ROW_POINT_B : ROW_POINT_B + 1, :] += bias
        d_depth = rows_nt(d_spans, v.point[...])
        for g in range(groups):
            r.dd[s, g, pl.ds(RIM, block), :] = d_depth[:, lane_group(g)]
        r.dd_first[s] = d_depth[0:RIM, :].astype(low)
        r.dd_last[s] = d_depth[block - RIM : block, :].astype(low)
        for g in range(3):
            r.rim_first[s, :, lane_group(g)] = r.d_ext[s, g, 0:RIM, :].astype(low)
            r.rim_last[s, :, lane_group(g)] = r.d_ext[
                s, g, RIM + block : 2 * RIM + block, :
            ].astype(low)


    def kv_copy(k):
        return (
            pltpu.make_async_copy(r.mine.at[block_of(k), :], r.kv_parts.at[rank], r.recv_kv.at[rank]),
            remote(r.mine.at[block_of(k), :], r.kv_parts.at[rank], r.send_kv.at[k],
                   r.recv_kv.at[rank], {"ctx": base + k}),
        )

    def return_block(k):
        pl.when((k <= TEAM - 2) & (team > 0))(lambda: halo_left(lax.rem(k, TEAM - 1)).wait_recv())
        pl.when((k >= 1) & (team < teams - 1))(
            lambda: halo_right(lax.rem(k + TEAM - 2, TEAM - 1)).wait_recv()
        )
        rows = block_of(k)
        r.mine[rows, :] = (
            wide(r.mine[rows, :]) + wide(r.from_left[rows, :]) + wide(r.from_right[rows, :])
        ).astype(low)
        pair = kv_copy(k)
        pl.when(k == rank)(pair[0].start)
        pl.when(k != rank)(pair[1].start)


    ff_base = core * (2 * half_ff) + pair_index * half_ff
    column_index, column_count, _ = column_of(me, size)
    column_piece = half_ff // column_count
    column_args = (column_of, me, size, r.ff_send, r.ff_column, r.send_c, r.recv_c)
    column_share = (column_of, me, size, r.fin_ff, ff_base, column_piece, r.send_cg, r.recv_cg)

    def piece_copy(fin, start, pair_rows, rows, k, mine, send, recv):
        side_of_pair = pair_index if mine else 1 - pair_index
        view = fin.at[part_rows(start + side_of_pair * pair_rows + k * rows, rows), :]
        return remote(view, view, send.at[k], recv.at[k], {"ctx": flip(me, 2)})

    def ff_piece(k, mine):
        return piece_copy(r.fin_ff, core * (2 * half_ff), half_ff, column_piece, k, mine,
                          r.send_pg, r.recv_pg)

    def wait_piece(spec, other):
        stage, _, _, fin, start, rows, send, recv = spec
        place, _, device_of = stage(me, size)
        view = fin.at[part_rows(start + other * rows, rows), :]
        remote(view, view, send.at[place], recv.at[other], {"ctx": device_of(other)}).wait_recv()

    def ff_to_column():
        ff_across.wait()

        def body(at, n):
            rows = part_rows(at, n)
            value = v.keep[side, rows, :] + wide(r.ff_came[rows, :])
            v.keep[side, rows, :] = value
            r.ff_send[rows, :] = value.astype(low)

        in_chunks(half_ff, body)
        for copy in scatter_copies(*column_args):
            copy.start()

    def ff_to_share():
        scatter_wait(*column_args)
        rows = part_rows(column_index * column_piece, column_piece)
        total = v.keep[side, rows, :]
        for other in others(column_index, column_count):
            total = total + wide(r.ff_column[other])
        r.ff_send[rows, :] = total.astype(low)
        own = pltpu.make_async_copy(
            r.ff_send.at[rows, :],
            r.fin_ff.at[part_rows(ff_base + column_index * column_piece, column_piece), :],
            r.load.at[0],
        )
        own.start()
        own.wait()
        for copy in share_copies(*column_share):
            copy.start()
        ff_piece(column_index, True).start()

    def ff_to_pair():
        for other in others(column_index, column_count):
            wait_piece(column_share, other)
            ff_piece(other, True).start()

    def ff_twin():
        view = r.fin_ff.at[part_rows(core * (2 * half_ff), 2 * half_ff), :]
        return remote(view, view, r.send_pg.at[column_count], r.recv_pg.at[column_count], twin)

    def ff_to_twin():
        for k in range(column_count):
            ff_piece(k, False).wait_recv()
        ff_twin().start()


    conv_back(0)
    center.wait()
    there = (1 - chip) * (TEAM // 2)
    here = chip * (TEAM // 2)
    return_block(there)
    conv_back(1)
    rims = [
        (remote(r.dd_last, r.dd_low, r.send_h.at[0], r.recv_h.at[0], {"ctx": after}), 1),
        (remote(r.rim_last, r.rim_low, r.send_h.at[1], r.recv_h.at[1], {"ctx": after}), 1),
        (remote(r.dd_first, r.dd_high, r.send_h.at[2], r.recv_h.at[2], {"ctx": prior}), 0),
        (remote(r.rim_first, r.rim_high, r.send_h.at[3], r.recv_h.at[3], {"ctx": prior}), 0),
    ]
    for copy, forward in rims:
        pl.when(me < size - 1 if forward else me > 0)(copy.start)

    return_block(there + 1)
    ff_to_column()
    have(fetched.depth, fetched.xrim)
    strip = 32

    def flat_rows(ref):
        return ref[...].reshape(seqs * block, ref.shape[2])

    point_grad = dot_tn(flat_rows(v.depth), flat_rows(v.dconv)).astype(low)
    for w in range(2):
        block_a.pack[w, 0:width, :] = point_grad[w * width : (w + 1) * width, :]
    for g in range(groups):
        def tap_step(c, sums, g=g):
            out = list(sums)
            for s in range(seqs):
                start = c * strip
                here = r.seg_col[s, pl.ds(RIM + start, strip), :]
                grad = r.dd[s, g, pl.ds(RIM + start, strip), :]
                for j in range(KERNEL):
                    same = r.seg_col[s, pl.ds(lead + j + start, strip), :] == here
                    near = v.xrim[s, g, pl.ds(lead + j + start, strip), :]
                    out[j] = out[j] + fold_rows(jnp.where(same, near, 0.0) * grad)
            return tuple(out)

        sums = lax.fori_loop(
            0, block // strip, tap_step,
            tuple(jnp.zeros((8, LANES), jnp.float32) for _ in range(KERNEL)),
        )
        for j in range(KERNEL):
            small[g // 3, j : j + 1, lane_group(g % 3)] = jnp.sum(sums[j], axis=0, keepdims=True)

    return_block(here + 1 - chip)
    return_block(here + chip)
    have(fetched.convw, fetched.x)
    for copy, forward in rims:
        pl.when(me > 0 if forward else me < size - 1)(copy.wait_recv)
    near_taps = KERNEL // 2
    for s in range(seqs):
        for g in range(3):
            head = pl.ds(RIM, RIM)
            tail = pl.ds(block, RIM)
            r.d_ext[s, g, head, :] += wide(r.rim_low[s, :, lane_group(g)])
            r.d_ext[s, g, tail, :] += wide(r.rim_high[s, :, lane_group(g)])
            v.queries[s, :, lane_group(g)] = r.d_ext[s, g, pl.ds(RIM, block), :].astype(low)
        for g in range(groups):
            r.dd[s, g, 0:RIM, :] = wide(r.dd_low[s, :, lane_group(g)])
            r.dd[s, g, pl.ds(RIM + block, RIM), :] = wide(r.dd_high[s, :, lane_group(g)])
        bias = jnp.sum(wide(v.queries[s]), axis=0, keepdims=True)
        for w in range(2):
            small[w, ROW_CONV_B : ROW_CONV_B + 1, :] += bias
    conv_grad = dot_tn(flat_rows(v.x), flat_rows(v.queries)).astype(low)
    for w in range(2):
        block_a.pack[w, width : 2 * width, :] = conv_grad[w * width : (w + 1) * width, :]

    def core_copy(blk):
        pack = blk.pack
        half = pack.shape[1] // 2
        return remote(pack.at[:, part_rows((1 - core) * half, half), :], blk.twin,
                      blk.send_core.at[0], blk.recv_core.at[0], twin)

    def y_copy(blk):
        return remote(blk.ysend, blk.ycame, blk.send_core.at[1],
                      blk.recv_core.at[1], across)

    def core_done(blk):
        core_copy(blk).wait()
        pack, came = blk.pack, blk.twin
        half = pack.shape[1] // 2

        def body(at, n):
            rows, there = part_rows(at, n), part_rows(core * half + at, n)
            blk.ysend[rows, :] = (
                wide(pack[1 - side, there, :]) + wide(came[1 - side, rows, :])
            ).astype(low)
            blk.acc[rows, :] = wide(pack[side, there, :]) + wide(came[side, rows, :])

        in_chunks(half, body)
        y_copy(blk).start()

    def chips_args(blk):
        return (chips_of, me, size, blk.ysend, blk.chips,
                blk.send_s, blk.recv_s)

    def y_done(blk):
        y_copy(blk).wait()

        def body(at, n):
            rows = part_rows(at, n)
            value = blk.acc[rows, :] + wide(blk.ycame[rows, :])
            blk.acc[rows, :] = value
            blk.ysend[rows, :] = value.astype(low)

        in_chunks(blk.ysend.shape[0], body)
        for copy in scatter_copies(*chips_args(blk)):
            copy.start()

    def pair_copy_a():
        rows = block_a.ysend.shape[0] // 2
        return remote(block_a.ysend.at[part_rows((1 - pair_index) * rows, rows), :], block_a.pair,
                      block_a.send_core.at[3], block_a.recv_core.at[3], {"ctx": flip(me, 2)})

    def y_done_a():
        y_copy(block_a).wait()

        def body(at, n):
            rows = part_rows(at, n)
            value = block_a.acc[rows, :] + wide(block_a.ycame[rows, :])
            block_a.acc[rows, :] = value
            block_a.ysend[rows, :] = value.astype(low)

        in_chunks(block_a.ysend.shape[0], body)
        pair_copy_a().start()

    def column_args_a():
        rows = block_a.ysend.shape[0] // 2
        return (column_of, me, size, block_a.ysend.at[pl.ds(0, rows), :], block_a.column,
                block_a.send_s, block_a.recv_s)

    def pair_done_a():
        pair_copy_a().wait()
        half = block_a.ysend.shape[0] // 2

        def body(at, n):
            rows = part_rows(at, n)
            value = block_a.acc[part_rows(pair_index * half + at, n), :] + wide(
                block_a.pair[rows, :]
            )
            block_a.acc[rows, :] = value
            block_a.ysend[rows, :] = value.astype(low)

        in_chunks(half, body)
        for copy in scatter_copies(*column_args_a()):
            copy.start()

    def column_share_a():
        half = block_a.ysend.shape[0]
        return (column_of, me, size, block_a.fin, core * half + pair_index * (half // 2),
                half // 2 // (size // TEAM), block_a.send_g, block_a.recv_g)

    def piece_a(k, mine):
        half = block_a.ysend.shape[0]
        return piece_copy(block_a.fin, core * half, half // 2, half // 2 // column_count, k, mine,
                          block_a.send_p, block_a.recv_p)

    def column_done_a():
        scatter_wait(*column_args_a())
        place, number, _ = column_of(me, size)
        half = block_a.ysend.shape[0]
        piece_rows = half // 2 // number
        value = block_a.acc[part_rows(place * piece_rows, piece_rows), :]
        for other in others(place, number):
            value = value + wide(block_a.column[other])
        at = core * half + pair_index * (half // 2) + place * piece_rows
        block_a.fin[part_rows(at, piece_rows), :] = value.astype(low)
        for copy in share_copies(*column_share_a()):
            copy.start()
        piece_a(column_index, True).start()

    def share_done_a():
        for other in others(column_index, column_count):
            wait_piece(column_share_a(), other)
            piece_a(other, True).start()

    def last_done_a():
        for k in range(column_count):
            piece_a(k, False).wait_recv()
        twin_copy(block_a).start()

    def finish_a():
        for copy in scatter_copies(*column_args_a()):
            copy.wait_send()
        for copy in share_copies(*column_share_a()):
            copy.wait_send()
        for k in range(column_count):
            piece_a(k, True).wait_send()
        twin_copy(block_a).wait()

    def share_args(blk):
        half = blk.ysend.shape[0]
        return (chips_of, me, size, blk.fin, core * half, half // count,
                blk.send_g, blk.recv_g)

    def chips_done(blk):
        scatter_wait(*chips_args(blk))
        half = blk.ysend.shape[0]
        piece = half // count
        value = blk.acc[part_rows(index * piece, piece), :]
        for other in others(index, count):
            value = value + wide(blk.chips[other])
        blk.fin[part_rows(core * half + index * piece, piece), :] = value.astype(low)
        for copy in share_copies(*share_args(blk)):
            copy.start()

    def twin_copy(blk):
        fin = blk.fin
        half = fin.shape[0] // 2
        view = fin.at[part_rows(core * half, half), :]
        return remote(view, view, blk.send_core.at[2], blk.recv_core.at[2], twin)

    def share_done(blk):
        share_wait(*share_args(blk))
        twin_copy(blk).start()

    def finish(blk):
        for copy in scatter_copies(*chips_args(blk)):
            copy.wait_send()
        for copy in share_copies(*share_args(blk)):
            copy.wait_send()
        twin_copy(blk).wait()

    own_q.wait()
    for o in range(1, TEAM):
        q_copy(o).wait_send()
        remote(r.dq.at[rank], r.q_parts.at[mate(rank, o)], r.send_q.at[o], r.recv_q.at[o],
               {"ctx": base + mate(rank, o)}).wait_recv()
    for s in range(seqs):
        one, two = r.q_parts.at[2 * s], r.q_parts.at[2 * s + 1]
        queries = (
            one[:, lane_group(0)],
            mixed_lanes(wide(one[:, lane_group(1)]), half_turn(wide(two[:, lane_group(1)]))),
            two[:, lane_group(0)],
        )
        for g in range(3):
            r.d_cat[s, :, lane_group(6 + g)] = (
                wide(queries[g]) + v.spans[s, :, lane_group(g)]
            ).astype(low)
    for s in range(seqs):
        bias = jnp.sum(wide(r.d_cat[s, :, 2 * width :]), axis=0, keepdims=True)
        for w in range(2):
            small[w, ROW_QUERY_B : ROW_QUERY_B + 1, :] += bias
    query_grad = dot_tn(
        flat_rows(v.x), r.d_cat[:, :, 2 * width :].reshape(seqs * block, width)
    ).astype(low)
    for w in range(2):
        block_a.pack[w, 2 * width : 3 * width, :] = query_grad[w * width : (w + 1) * width, :]
    for k, row in enumerate((ROW_GAIN2, ROW_SHIFT2, ROW_OUTER_B, ROW_GAIN1, ROW_SHIFT1, ROW_OUTPUT_B)):
        for w in range(2):
            small[w, row : row + 1, :] = r.vec[k : k + 1, w * 384 : (w + 1) * 384]
    for w in range(2):
        for k in range(4):
            at = (4 * w + k) * 384
            small[w, ROW_INNER_B + k : ROW_INNER_B + k + 1, :] = r.bias[0:1, at : at + 384]

    upper = lax.rem(rank, 2) == 1
    heads = jnp.sum(wide(r.mine[...]), axis=0, keepdims=True)
    heads = jnp.broadcast_to(heads, (8, width))
    middle, outer_pair = heads[:, lane_group(1)], heads[:, lane_group(2)]
    none = jnp.zeros_like(middle)
    bias = (
        jnp.where(upper, none, outer_pair),
        jnp.where(upper, mixed_lanes(none, middle), mixed_lanes(half_turn(middle), none)),
        jnp.where(upper, outer_pair, none),
    )
    for w in range(2):
        for g in range(3):
            small[w, ROW_VALUE_B : ROW_VALUE_B + 1, lane_group(g)] = bias[g][0:1, :]
    for w in range(2):
        block_a.pack[w, SMALL_AT : SMALL_AT + SMALL_ROWS, :] = small[w].astype(low)
    core_copy(block_a).start()
    core_done(block_a)
    ff_to_share()
    for k in range(TEAM):
        pl.when(k == rank)(kv_copy(k)[0].wait)
        pl.when(k != rank)(kv_copy(k)[1].wait_send)
    for o in range(1, TEAM):
        other = mate(rank, o)
        remote(r.mine.at[block_of(rank), :], r.kv_parts.at[other], r.send_kv.at[rank],
               r.recv_kv.at[other], {"ctx": base + other}).wait_recv()
    for s in range(seqs):
        one, two = r.kv_parts.at[2 * s], r.kv_parts.at[2 * s + 1]
        mid_one, mid_two = wide(one[:, lane_group(1)]), wide(two[:, lane_group(1)])
        r.d_cat[s, :, lane_group(0)] = one[:, lane_group(0)]
        r.d_cat[s, :, lane_group(1)] = mixed_lanes(mid_one, half_turn(mid_two)).astype(low)
        r.d_cat[s, :, lane_group(2)] = two[:, lane_group(0)]
        r.d_cat[s, :, lane_group(3)] = one[:, lane_group(2)]
        r.d_cat[s, :, lane_group(4)] = mixed_lanes(half_turn(mid_one), mid_two).astype(low)
        r.d_cat[s, :, lane_group(5)] = two[:, lane_group(2)]
    grads = r.d_cat[:, :, 0 : 2 * width].reshape(seqs * block, 2 * width)
    for w in range(2):
        piece = dot_tn(
            v.x[:, :, w * width : (w + 1) * width].reshape(seqs * block, width), grads
        ).astype(low)
        for k in range(2):
            block_b.pack[w, k * width : (k + 1) * width, :] = piece[:, k * width : (k + 1) * width]
    core_copy(block_b).start()
    core_done(block_b)
    y_done_a()
    have(fetched.ds, fetched.key, fetched.value, fetched.query)
    def taps_row(j, g):
        return wide(small_ref[(g // 3) * SMALL_IN + j : (g // 3) * SMALL_IN + j + 1,
                              lane_group(g % 3)])

    def depth_strip(c, s):
        start = c * strip
        here = r.seg_col[s, pl.ds(RIM + start, strip), :]
        rows = pl.ds(pl.multiple_of(start, strip), strip)
        sums = [v.ds[s, rows, lane_group(g)] for g in range(groups)]
        for j in range(KERNEL):
            same = r.seg_col[s, pl.ds(RIM + near_taps - j + start, strip), :] == here
            for g in range(groups):
                near = r.dd[s, g, pl.ds(RIM + near_taps - j + start, strip), :]
                sums[g] = sums[g] + jnp.where(same, near, 0.0) * taps_row(j, g)
        for g in range(groups):
            v.ds[s, rows, lane_group(g)] = sums[g]
        return s

    for s in range(seqs):
        lax.fori_loop(0, block // strip, depth_strip, s)
    pair_done_a()
    y_done(block_b)
    ff_to_pair()
    column_done_a()
    for s in range(seqs):
        v.ds[s] += (
            rows_nt(v.queries[s], v.convw[...])
            + rows_nt(r.d_cat[s, :, 0:width], v.key[...])
            + rows_nt(r.d_cat[s, :, width : 2 * width], v.value[...])
            + rows_nt(r.d_cat[s, :, 2 * width :], v.query[...])
        )
    out_copy = pltpu.make_async_copy(v.ds, r.input_grad, r.load.at[1])
    out_copy.start()
    ff_to_twin()
    chips_done(block_b)
    share_done_a()
    last_done_a()
    share_done(block_b)
    finish_a()
    finish(block_b)
    ff_twin().wait()
    for copy in scatter_copies(*column_args):
        copy.wait_send()
    for copy in share_copies(*column_share):
        copy.wait_send()
    for k in range(column_count):
        ff_piece(k, True).wait_send()
    for copy, forward in rims:
        pl.when(me < size - 1 if forward else me > 0)(copy.wait_send)
    for k in range(TEAM - 1):
        pl.when(team < teams - 1)(halo_left(k).wait_send)
        pl.when(team > 0)(halo_right(k).wait_send)
    out_copy.wait()


def padded(rows, unit):
    return -(-rows // unit) * unit


def back(held, window, dq_parts, loaded):
    size = lax.axis_size("ctx")
    unit = 16 * size
    seqs, block, model = loaded["x"].shape
    width = HEADS * HEAD_DIM
    halo = (TEAM - 1) * block
    span = block + 2 * RIM
    chips, column = size // 2, size // TEAM
    low, full = jnp.bfloat16, jnp.float32
    dma = pltpu.SemaphoreType.DMA
    half_ff = loaded["keep"].shape[1]
    outs = dict(
        input_grad=jax.ShapeDtypeStruct((seqs, block, model), full),
        fin_ff=jax.ShapeDtypeStruct((4 * half_ff, width), low),
    )
    scratch = dict(
        mine=pltpu.VMEM((TEAM * block, width), low),
        from_right=pltpu.VMEM((TEAM * block, width), low),
        from_left=pltpu.VMEM((TEAM * block, width), low),
        kv_parts=pltpu.VMEM((TEAM, block, width), low),
        q_parts=pltpu.VMEM((TEAM, block, 2 * LANES), low),
        ff_send=pltpu.VMEM((half_ff, width), low),
        ff_came=pltpu.VMEM((half_ff, width), low),
        ff_column=pltpu.VMEM((column, half_ff // column, width), low),
        spread=pltpu.VMEM((KERNEL, 2 * LANES, width), low),
        sums=pltpu.VMEM((2, SMALL_ROWS, width), full),
        wide=pltpu.VMEM((LANES, block), full),
        tall=pltpu.VMEM((block, LANES), full),
        seg_col=pltpu.VMEM((seqs, held["seg"].shape[1], LANES), full),
        d_ext=pltpu.VMEM((seqs, 3, span, LANES), full),
        dd=pltpu.VMEM((seqs, model // LANES, span, LANES), full),
        d_cat=pltpu.VMEM((seqs, block, 3 * width), low),
        dd_first=pltpu.VMEM((seqs, RIM, model), low),
        dd_last=pltpu.VMEM((seqs, RIM, model), low),
        dd_low=pltpu.VMEM((seqs, RIM, model), low),
        dd_high=pltpu.VMEM((seqs, RIM, model), low),
        rim_first=pltpu.VMEM((seqs, RIM, width), low),
        rim_last=pltpu.VMEM((seqs, RIM, width), low),
        rim_low=pltpu.VMEM((seqs, RIM, width), low),
        rim_high=pltpu.VMEM((seqs, RIM, width), low),
        send_l=dma((TEAM,)), recv_l=dma((TEAM,)), send_r=dma((TEAM,)), recv_r=dma((TEAM,)),
        send_q=dma((TEAM,)), recv_q=dma((TEAM,)), send_kv=dma((TEAM,)), recv_kv=dma((TEAM,)),
        send_h=dma((4,)), recv_h=dma((4,)), send_p=dma((1,)), recv_p=dma((1,)),
        send_c=dma((column,)), recv_c=dma((column,)), send_cg=dma((column,)),
        recv_cg=dma((column,)), send_pg=dma((column + 1,)),
        recv_pg=dma((column + 1,)),
        load=dma((len(loaded) + 1,)),
    )

    def block_scratch(rows):
        rows = padded(rows, unit)
        return dict(
            pack=pltpu.VMEM((2, rows, width), low),
            twin=pltpu.VMEM((2, rows // 2, width), low),
            ysend=pltpu.VMEM((rows // 2, width), low),
            ycame=pltpu.VMEM((rows // 2, width), low),
            acc=pltpu.VMEM((rows // 2, width), full),
            chips=pltpu.VMEM((chips, rows // 2 // chips, width), low),
            fin=pltpu.VMEM((rows, width), low),
            send_s=dma((chips,)), recv_s=dma((chips,)), send_g=dma((chips,)),
            recv_g=dma((chips,)), send_core=dma((4,)), recv_core=dma((4,)),
        )

    a_scratch, b_scratch = block_scratch(PACK_A), block_scratch(PACK_B)
    quarter = padded(PACK_A, unit) // 4
    del a_scratch["chips"]
    a_scratch.update(
        pair=pltpu.VMEM((quarter, width), low),
        column=pltpu.VMEM((column, quarter // column, width), low),
        send_p=dma((column,)), recv_p=dma((column,)),
    )
    del a_scratch["fin"], b_scratch["fin"]
    fin_shapes = [jax.ShapeDtypeStruct((padded(n, unit), width), low) for n in (PACK_A, PACK_B)]
    vmem = pl.BlockSpec(memory_space=pltpu.VMEM)
    anywhere = pl.BlockSpec(memory_space=pl.ANY)
    names = tuple(held) + ("window", "dq") + tuple(outs) + tuple(scratch)
    total_in = len(held) + 2
    fetch_count = len(loaded)

    def kernel(*refs):
        ins, loads = refs[:total_in], refs[total_in : total_in + fetch_count]
        at = total_in + fetch_count
        results = refs[at : at + len(outs)]
        fin_a, fin_b = refs[at + len(outs) : at + len(outs) + 2]
        late = refs[at + len(outs) + 2 :]
        first, late = late[: len(scratch)], late[len(scratch) :]
        a_refs, late = late[: len(a_scratch)], late[len(a_scratch) :]
        b_refs, holds = late[: len(b_scratch)], late[len(b_scratch) :]
        back_kernel(
            names, tuple(a_scratch) + ("fin",), tuple(b_scratch) + ("fin",), tuple(loaded),
            *ins, *results, *first, *a_refs, fin_a, *b_refs, fin_b, *loads, *holds,
        )

    holds = [pltpu.VMEM(a.shape, a.dtype) for a in loaded.values()]
    return pl.pallas_call(
        kernel,
        out_shape=list(outs.values()) + fin_shapes,
        in_specs=[vmem] * len(held) + [anywhere] * (2 + len(loaded)),
        out_specs=[anywhere] * 2 + [vmem] * 2,
        scratch_shapes=list(scratch.values()) + list(a_scratch.values())
        + list(b_scratch.values()) + holds,
        compiler_params=pltpu.CompilerParams(
            collective_id=5, has_side_effects=True, vmem_limit_bytes=65400 * 2**10
        ),
        name="back",
    )(*held.values(), window, dq_parts, *loaded.values())


STEP = 256
FF_CHUNK = 512
PACK_FF = 3840


def gelu_pair(value):
    share = 0.5 + 0.5 * lax.erf(value * 0.7071067811865476)
    bell = jnp.exp(-0.5 * value * value)
    return value * share, share + value * bell * 0.3989422804014327


def fold_rows(block):
    return jnp.sum(block.reshape(block.shape[0] // 8, 8, block.shape[1]), axis=0)


def norm_parts(value):
    center = value - jnp.mean(value, axis=-1, keepdims=True)
    spread = jnp.mean(center * center, axis=-1, keepdims=True)
    scale = lax.rsqrt(spread + 1e-05)
    return center * scale, scale


def norm_back(grad, unit, scale):
    return scale * (
        grad
        - jnp.mean(grad, axis=-1, keepdims=True)
        - unit * jnp.mean(grad * unit, axis=-1, keepdims=True)
    )


def middle_kernel(att_ref, conv_ref, x_ref, small_ref, og_any, ow_any, iw_any, uw_any, uw_came,
                  out_any, ds_any, dc_any, team_ref, keep_ref, xsend_ref, vec_ref, bias_ref,
                  og_ref, ow_ref, iw_ref, uw_ref, out_ref, ds_ref, dc_ref,
                  pack_ref, twin_ref, pieces, parts, joined_ref, low_ref, act_ref, slope_ref, do_ref, di_ref, db_ref,
                  sums_ref, wide_sums, send_a, recv_a, send_g, recv_g, send_t, recv_t, load, store):
    me = lax.axis_index("ctx")
    rank = lax.rem(me, TEAM)
    base = me - rank
    seqs, block, model = x_ref.shape
    width = HEADS * HEAD_DIM
    greet([{"ctx": base + mate(rank, o)} for o in range(1, TEAM)])

    def piece_copy(r):
        return (
            pltpu.make_async_copy(att_ref.at[r], pieces.at[rank], recv_a.at[rank]),
            remote(att_ref.at[r], pieces.at[rank], send_a.at[r], recv_a.at[rank],
                   {"ctx": base + r}),
        )

    def team_copy(r):
        return (
            pltpu.make_async_copy(parts.at[r], team_ref.at[rank], recv_g.at[rank]),
            remote(parts.at[r], team_ref.at[rank], send_g.at[r], recv_g.at[rank],
                   {"ctx": base + r}),
        )

    core, side = lax.rem(me, 2), lax.axis_index("wsh")
    for o in (1, 3, 2):
        piece_copy(mate(rank, o))[1].start()
    piece_copy(rank)[0].start()
    rows_in = uw_came.shape[1]
    came_at = part_rows((1 - side) * (2 * rows_in) + core * rows_in, rows_in)
    loads = [
        pltpu.make_async_copy(ow_any, ow_ref, load.at[0]),
        pltpu.make_async_copy(iw_any, iw_ref, load.at[1]),
        pltpu.make_async_copy(
            uw_any, uw_ref.at[:, part_rows(side * (2 * rows_in), 2 * rows_in), :], load.at[2]
        ),
        pltpu.make_async_copy(uw_came, uw_ref.at[:, came_at, :], load.at[3]),
        pltpu.make_async_copy(og_any, og_ref, load.at[4]),
    ]
    for copy in loads:
        copy.start()
    outer_twin = remote(uw_came, uw_ref.at[:, came_at, :], send_t.at[1], recv_t.at[1],
                        {"ctx": flip(me, 1)})
    outer_twin.start()
    sums_ref[...] = jnp.zeros_like(sums_ref)
    wide_sums[...] = jnp.zeros_like(wide_sums)
    own = lax.div(rank, 2)
    steps = block // STEP

    def row(index):
        return jnp.concatenate(
            [small_ref[index : index + 1, :], small_ref[SMALL_IN + index : SMALL_IN + index + 1, :]],
            axis=1,
        ).astype(jnp.float32)

    def body(i, carry):
        s = lax.rem(own + lax.div(i, steps), seqs)
        start = pl.multiple_of(lax.rem(i, steps) * STEP, STEP)
        rows = pl.ds(start, STEP)
        flat = pl.ds(pl.multiple_of(s * block + start, STEP), STEP)

        @pl.when(i == 0)
        def _():
            piece_copy(rank)[0].wait()
            remote(att_ref.at[rank], pieces.at[mate(rank, 1)], send_a.at[rank],
                   recv_a.at[mate(rank, 1)], {"ctx": base + mate(rank, 1)}).wait_recv()
            for copy in loads:
                copy.wait()
            outer_twin.wait()

        @pl.when(i == steps)
        def _():
            for o in (2, 3):
                remote(att_ref.at[rank], pieces.at[mate(rank, o)], send_a.at[rank],
                       recv_a.at[mate(rank, o)], {"ctx": base + mate(rank, o)}).wait_recv()

        first, second = pieces.at[2 * s], pieces.at[2 * s + 1]
        joined_ref[flat, lane_group(0)] = first[rows, lane_group(0)]
        joined_ref[flat, lane_group(1)] = mixed_lanes(
            first[rows, lane_group(1)].astype(jnp.float32),
            half_turn(second[rows, lane_group(1)].astype(jnp.float32)),
        ).astype(jnp.bfloat16)
        joined_ref[flat, lane_group(2)] = second[rows, lane_group(0)]
        joined_ref[flat, width:] = conv_ref[s, rows, :]
        branch = dot(joined_ref[flat, :], ow_ref[...]) + row(ROW_OUTPUT_B)
        unit1, scale1 = norm_parts(branch + x_ref[s, rows, :].astype(jnp.float32))
        gain1 = row(ROW_GAIN1)
        normed = unit1 * gain1 + row(ROW_SHIFT1)
        low_ref[flat, :] = normed.astype(jnp.bfloat16)
        outer = []
        part = model // GROUPS
        hidden = iw_ref.shape[2]
        for g in range(GROUPS):
            cols = slice(g * part, (g + 1) * part)
            for c in range(hidden // FF_CHUNK):
                span = slice(g * hidden + c * FF_CHUNK, g * hidden + (c + 1) * FF_CHUNK)
                near = slice(c * FF_CHUNK, (c + 1) * FF_CHUNK)
                bias = jnp.concatenate(
                    [
                        small_ref[
                            g * SMALL_IN + ROW_INNER_B + k // 3 : g * SMALL_IN + ROW_INNER_B + k // 3 + 1,
                            lane_group(k % 3),
                        ]
                        for k in range(c * FF_CHUNK // LANES, (c + 1) * FF_CHUNK // LANES)
                    ],
                    axis=1,
                ).astype(jnp.float32)
                inner = dot(low_ref[flat, cols], iw_ref[g, :, near]) + bias
                active, slope = gelu_pair(inner)
                act_ref[flat, span] = active.astype(jnp.bfloat16)
                slope_ref[:, span] = slope
            outer.append(dot(act_ref[flat, g * hidden : (g + 1) * hidden], uw_ref[g]))
        summed = jnp.concatenate(outer, axis=1) + row(ROW_OUTER_B) + normed
        unit2, scale2 = norm_parts(summed)
        gain2 = row(ROW_GAIN2)
        out_ref[s, rows, :] = (unit2 * gain2 + row(ROW_SHIFT2)).astype(jnp.bfloat16)
        grad = og_ref[s, rows, :].astype(jnp.float32)
        sums_ref[0] += fold_rows(grad * unit2)
        sums_ref[1] += fold_rows(grad)
        d_sum2 = norm_back(grad * gain2, unit2, scale2)
        d_outer = d_sum2.astype(jnp.bfloat16)
        do_ref[flat, :] = d_outer
        sums_ref[2] += fold_rows(d_outer.astype(jnp.float32))
        back = []
        for g in range(GROUPS):
            cols = slice(g * part, (g + 1) * part)
            for c in range(hidden // FF_CHUNK):
                span = slice(g * hidden + c * FF_CHUNK, g * hidden + (c + 1) * FF_CHUNK)
                near = slice(c * FF_CHUNK, (c + 1) * FF_CHUNK)
                d_inner = (
                    rows_nt(do_ref[flat, cols], uw_ref[g, near, :]) * slope_ref[:, span]
                ).astype(jnp.bfloat16)
                di_ref[flat, span] = d_inner
                wide_sums[:, span] += fold_rows(d_inner.astype(jnp.float32))
            back.append(rows_nt(di_ref[flat, g * hidden : (g + 1) * hidden], iw_ref[g]))
        d_normed = d_sum2 + jnp.concatenate(back, axis=1)
        sums_ref[3] += fold_rows(d_normed * unit1)
        sums_ref[4] += fold_rows(d_normed)
        d_sum1 = norm_back(d_normed * gain1, unit1, scale1)
        ds_ref[s, rows, :] = d_sum1
        d_branch = d_sum1.astype(jnp.bfloat16)
        db_ref[flat, :] = d_branch
        sums_ref[5] += fold_rows(d_branch.astype(jnp.float32))
        d_joined = rows_nt(d_branch, ow_ref[...])
        dc_ref[s, rows, :] = d_joined[:, width:].astype(jnp.bfloat16)
        parts[2 * s, rows, lane_group(0)] = d_joined[:, lane_group(0)].astype(jnp.bfloat16)
        parts[2 * s, rows, lane_group(1)] = half_turn(d_joined[:, lane_group(1)]).astype(
            jnp.bfloat16
        )
        parts[2 * s + 1, rows, lane_group(0)] = d_joined[:, lane_group(2)].astype(jnp.bfloat16)
        parts[2 * s + 1, rows, lane_group(1)] = d_joined[:, lane_group(1)].astype(jnp.bfloat16)

        @pl.when(i == steps - 1)
        def _():
            team_copy(rank)[0].start()
            team_copy(mate(rank, 1))[1].start()

        @pl.when(i == 2 * steps - 1)
        def _():
            team_copy(mate(rank, 2))[1].start()
            team_copy(mate(rank, 3))[1].start()

        return carry

    lax.fori_loop(0, seqs * steps, body, 0)
    stores = [
        pltpu.make_async_copy(out_ref, out_any, store.at[0]),
        pltpu.make_async_copy(ds_ref, ds_any, store.at[1]),
        pltpu.make_async_copy(dc_ref, dc_any, store.at[2]),
    ]
    for copy in stores:
        copy.start()

    half = width
    part = model // GROUPS
    hidden = iw_ref.shape[2]
    half_ff = pack_ref.shape[1] // 2
    early = half + part // 2 * (hidden // half)

    def exchange(at, rows, sem):
        return remote(
            pack_ref.at[:, part_rows((1 - core) * half_ff + at, rows), :],
            twin_ref.at[:, pl.ds(at, rows), :], send_t.at[sem], recv_t.at[sem],
            {"ctx": flip(me, 1)},
        )

    for w in range(2):
        for k in range(2):
            pack_ref[w, pl.ds(k * half_ff, half), :] = dot_tn(
                joined_ref[:, w * half : (w + 1) * half], db_ref[:, k * half : (k + 1) * half]
            ).astype(jnp.bfloat16)
    for g in range(GROUPS):
        for k in range(hidden // half):
            grads = dot_tn(
                low_ref[:, g * part : (g + 1) * part],
                di_ref[:, g * hidden + k * half : g * hidden + (k + 1) * half],
            ).astype(jnp.bfloat16)
            for w in range(2):
                pack_ref[w, pl.ds(g * half_ff + half + k * (part // 2), part // 2), :] = grads[
                    w * (part // 2) : (w + 1) * (part // 2), :
                ]
    exchange(0, early, 0).start()
    for g in range(GROUPS):
        for k in range(hidden // half):
            w, lower = k // 2, k % 2
            grads = dot_tn(
                act_ref[:, g * hidden + k * half : g * hidden + (k + 1) * half],
                do_ref[:, g * part : (g + 1) * part],
            ).astype(jnp.bfloat16)
            pack_ref[w, pl.ds(g * half_ff + early + lower * half, half), :] = grads
    exchange(early, half_ff - early, 2).start()
    for k in range(6):
        vec_ref[k : k + 1, :] = jnp.sum(sums_ref[k], axis=0, keepdims=True)
    vec_ref[6:, :] = jnp.zeros((2, model), jnp.float32)
    bias_ref[...] = jnp.broadcast_to(jnp.sum(wide_sums[...], axis=0, keepdims=True), bias_ref.shape)

    exchange(0, early, 0).wait()
    exchange(early, half_ff - early, 2).wait()
    pair_index, _, _ = pair_of(me, lax.axis_size("ctx"))
    quarter = half_ff // 2

    def add(at, n):
        here = part_rows(at, n)
        keep, give = pair_index * quarter, (1 - pair_index) * quarter
        for w in range(2):
            xsend_ref[w, here, :] = (
                wide(pack_ref[w, part_rows(core * half_ff + give + at, n), :])
                + wide(twin_ref[w, part_rows(give + at, n), :])
            ).astype(jnp.bfloat16)
            keep_ref[w, here, :] = wide(
                pack_ref[w, part_rows(core * half_ff + keep + at, n), :]
            ) + wide(twin_ref[w, part_rows(keep + at, n), :])

    in_chunks(quarter, add)
    team_copy(rank)[0].wait()
    for o in range(1, TEAM):
        other = mate(rank, o)
        piece_copy(other)[1].wait_send()
        team_copy(other)[1].wait_send()
        remote(parts.at[rank], team_ref.at[other], send_g.at[rank], recv_g.at[other],
               {"ctx": base + other}).wait_recv()
    for copy in stores:
        copy.wait()


def middle(attended, convolved, hidden, small, out_grad, output_w, inner_w, outer_w, outer_came):
    seqs, block, model = hidden.shape
    rows = seqs * block
    width = convolved.shape[2]
    inner = GROUPS * inner_w.shape[2]
    pack_rows = padded(PACK_FF, 16 * lax.axis_size("ctx"))
    vmem = pl.BlockSpec(memory_space=pltpu.VMEM)
    anywhere = pl.BlockSpec(memory_space=pl.ANY)
    low, full = jnp.bfloat16, jnp.float32
    dma = pltpu.SemaphoreType.DMA
    return pl.pallas_call(
        middle_kernel,
        out_shape=[
            jax.ShapeDtypeStruct((seqs, block, model), low),
            jax.ShapeDtypeStruct((seqs, block, model), full),
            jax.ShapeDtypeStruct((seqs, block, width), low),
            jax.ShapeDtypeStruct((TEAM, block, 2 * LANES), low),
            jax.ShapeDtypeStruct((2, pack_rows // 4, width), full),
            jax.ShapeDtypeStruct((2, pack_rows // 4, width), low),
            jax.ShapeDtypeStruct((8, model), full),
            jax.ShapeDtypeStruct((8, inner), full),
        ],
        in_specs=[anywhere] + [vmem] * 3 + [anywhere] * 5,
        out_specs=[anywhere] * 4 + [vmem] * 4,
        scratch_shapes=[
            pltpu.VMEM((seqs, block, model), low),
            pltpu.VMEM(output_w.shape, low),
            pltpu.VMEM(inner_w.shape, low),
            pltpu.VMEM((GROUPS, 2 * outer_w.shape[1], outer_w.shape[2]), low),
            pltpu.VMEM((seqs, block, model), low),
            pltpu.VMEM((seqs, block, model), full),
            pltpu.VMEM((seqs, block, width), low),
            pltpu.VMEM((2, pack_rows, width), low),
            pltpu.VMEM((2, pack_rows // 2, width), low),
            pltpu.VMEM((TEAM, block, 2 * LANES), low),
            pltpu.VMEM((TEAM, block, 2 * LANES), low),
            pltpu.VMEM((rows, model), low),
            pltpu.VMEM((rows, model), low),
            pltpu.VMEM((rows, inner), low),
            pltpu.VMEM((STEP, inner), full),
            pltpu.VMEM((rows, model), low),
            pltpu.VMEM((rows, inner), low),
            pltpu.VMEM((rows, model), low),
            pltpu.VMEM((6, 8, model), full),
            pltpu.VMEM((8, inner), full),
            dma((TEAM,)), dma((TEAM,)), dma((TEAM,)), dma((TEAM,)), dma((3,)), dma((3,)),
            dma((5,)), dma((3,)),
        ],
        compiler_params=pltpu.CompilerParams(
            collective_id=2, has_side_effects=True, vmem_limit_bytes=63 * 2**20
        ),
        name="middle",
    )(attended, convolved, hidden, small, out_grad, output_w, inner_w, outer_w, outer_came)


def finish_kernel(side_ref, ff_any, a_any, b_any, grad_any, out_any,
                  grad_out, out_out, query_out, key_out, value_out, point_out, conv_out,
                  output_out, inner_out, outer_out, depth_out, kernel_out, query_b, value_b, point_b, conv_b,
                  output_b, gain1, shift1, outer_b, gain2, shift2, inner_b, kernel_b,
                  ff, a, b, grad, out, wide_a, wide_b, wide_output, wide_inner, wide_outer,
                  load, store):
    width = HEADS * HEAD_DIM
    loads = [
        pltpu.make_async_copy(a_any.at[pl.ds(0, a.shape[0]), :], a, load.at[0]),
        pltpu.make_async_copy(b_any.at[pl.ds(0, b.shape[0]), :], b, load.at[1]),
        pltpu.make_async_copy(ff_any.at[pl.ds(0, ff.shape[0]), :], ff, load.at[2]),
        pltpu.make_async_copy(grad_any, grad, load.at[3]),
        pltpu.make_async_copy(out_any, out, load.at[4]),
    ]
    for copy in loads:
        copy.start()
    stores = []

    def put(src, dst):
        copy = pltpu.make_async_copy(src, dst, store.at[len(stores)])
        copy.start()
        stores.append(copy)

    loads[0].wait()
    for k, place in enumerate((point_out, conv_out, query_out)):
        rows = pl.ds(k * width, width)
        wide_a[rows, :] = a[rows, :].astype(jnp.float32)
        put(wide_a.at[rows, :], place)
    small = a[pl.ds(SMALL_AT, SMALL_ROWS), :].astype(jnp.float32)
    depth_out[...] = small[0:KERNEL, :]
    first = side_ref[0] == 0
    for ref, row in ((output_b, ROW_OUTPUT_B), (gain1, ROW_GAIN1), (shift1, ROW_SHIFT1),
                     (outer_b, ROW_OUTER_B), (gain2, ROW_GAIN2), (shift2, ROW_SHIFT2)):
        ref[...] = small[row : row + 1, :].reshape(width)
    inner_b[...] = jnp.concatenate(
        [small[ROW_INNER_B + k : ROW_INNER_B + k + 1, :] for k in range(4)], axis=1
    ).reshape(4 * width)
    block = small[16:24, :]
    turned = jnp.where(first, block, pltpu.roll(block, 192, axis=1))
    for ref, row in ((query_b, ROW_QUERY_B), (value_b, ROW_VALUE_B), (point_b, ROW_POINT_B),
                     (conv_b, ROW_CONV_B)):
        ref[...] = turned[row - 16 : row - 15, 0:192].reshape(192)
    taps = small[ROW_KERNEL_W : ROW_KERNEL_W + TAP_ROWS, :]
    half = jnp.where(first, taps, pltpu.roll(taps, 192, axis=1))[:, 0:192]
    pick = jnp.where(tap_major((TAP_ROWS, HEADS * KERNEL), 0), 1.0, 0.0)
    kernel_out[...] = dot_tn(pick.astype(jnp.bfloat16), half.astype(jnp.bfloat16))
    lanes = small[ROW_KERNEL_B : ROW_KERNEL_B + 24, :]
    column = jnp.concatenate([lanes[:, lane_group(g)] for g in range(3)], axis=0)
    wide_pick = jnp.where(
        first,
        jnp.where(tap_major((TAP_ROWS, LANES), 0), 1.0, 0.0),
        jnp.where(tap_major((TAP_ROWS, LANES), HEADS * KERNEL // 2), 1.0, 0.0),
    )
    count = HEADS * KERNEL // 2
    kernel_b[...] = jnp.sum(column * wide_pick, axis=0, keepdims=True)[:, 0:count].reshape(count)
    loads[1].wait()
    for k, place in enumerate((key_out, value_out)):
        rows = pl.ds(k * width, width)
        wide_b[rows, :] = b[rows, :].astype(jnp.float32)
        put(wide_b.at[rows, :], place)
    loads[2].wait()
    half_ff = ff.shape[0] // 2
    count = inner_out.shape[1]
    blocks = inner_out.shape[2] // width
    rows = outer_out.shape[1]
    for g in range(GROUPS):
        cols = slice(g * width, (g + 1) * width)
        wide_output[:, cols] = ff[pl.ds(g * half_ff, width), :].astype(jnp.float32)
        for k in range(blocks):
            at = g * half_ff + width + k * count
            wide_inner[g, :, k * width : (k + 1) * width] = ff[pl.ds(at, count), :].astype(
                jnp.float32
            )
        wide_outer[g] = ff[pl.ds(g * half_ff + width + blocks * count, rows), :].astype(
            jnp.float32
        )
    put(wide_output, output_out)
    put(wide_inner, inner_out)
    put(wide_outer, outer_out)
    loads[3].wait()
    put(grad, grad_out)
    loads[4].wait()
    put(out, out_out)
    for copy in stores:
        copy.wait()


def finish(side, fin_ff, fin_a, fin_b, grad_input, output, inner_shape, outer_shape):
    width = HEADS * HEAD_DIM
    full, low = jnp.float32, jnp.bfloat16
    anywhere = pl.BlockSpec(memory_space=pl.ANY)
    vmem = pl.BlockSpec(memory_space=pltpu.VMEM)
    square = jax.ShapeDtypeStruct((width, width), full)
    lengths = [width // 2] * 4 + [width] * 6 + [4 * width, HEADS * KERNEL // 2]
    return pl.pallas_call(
        finish_kernel,
        out_shape=[
            jax.ShapeDtypeStruct(grad_input.shape, full),
            jax.ShapeDtypeStruct(output.shape, low),
            square, square, square, square, square,
            jax.ShapeDtypeStruct((width, 2 * width), full),
            jax.ShapeDtypeStruct(inner_shape, full),
            jax.ShapeDtypeStruct(outer_shape, full),
            jax.ShapeDtypeStruct((KERNEL, width), full),
            jax.ShapeDtypeStruct((HEADS * KERNEL, width // 2), full),
        ] + [jax.ShapeDtypeStruct((n,), full) for n in lengths],
        in_specs=[pl.BlockSpec(memory_space=pltpu.SMEM)] + [anywhere] * 5,
        out_specs=[anywhere] * 10 + [vmem] * 14,
        scratch_shapes=[
            pltpu.VMEM(fin_ff.shape, low),
            pltpu.VMEM((PACK_A, width), low),
            pltpu.VMEM((PACK_B, width), low),
            pltpu.VMEM(grad_input.shape, full),
            pltpu.VMEM(output.shape, low),
            pltpu.VMEM((SMALL_AT, width), full),
            pltpu.VMEM((PACK_B, width), full),
            pltpu.VMEM((width, 2 * width), full),
            pltpu.VMEM(inner_shape, full),
            pltpu.VMEM(outer_shape, full),
            pltpu.SemaphoreType.DMA((5,)),
            pltpu.SemaphoreType.DMA((10,)),
        ],
        compiler_params=pltpu.CompilerParams(vmem_limit_bytes=60 * 2**20),
        name="finish",
    )(side, fin_ff, fin_a, fin_b, grad_input, output)


def on_device(
    hidden_in,
    segment_ids,
    out_grad,
    query_w,
    query_b,
    key_w,
    value_w,
    value_b,
    depth_kernel,
    point_w,
    point_b,
    kernel_w,
    kernel_b,
    conv_w,
    conv_b,
    output_w,
    output_b,
    norm1_gain,
    norm1_bias,
    inner_w,
    inner_b,
    outer_w,
    outer_b,
    norm2_gain,
    norm2_bias,
):
    micro_count, seq_local, block_len, model_width = hidden_in.shape
    seq_count = micro_count * seq_local
    att_width = HEADS * HEAD_DIM
    half_taps = KERNEL // 2
    position = lax.axis_index("ctx")
    seg_rows = segment_ids.reshape(seq_count, segment_ids.shape[2])
    pad_rows = (TEAM - 1) * block_len
    seg_pad = jnp.pad(seg_rows, ((0, 0), (pad_rows, pad_rows)), constant_values=-1)
    own_seg = lax.dynamic_slice_in_dim(seg_pad, position * block_len + pad_rows, block_len, 1)
    rank = lax.rem(position, TEAM)
    team_seg = lax.dynamic_slice(
        jnp.concatenate(
            [seg_pad[:, : pad_rows + seg_rows.shape[1]],
             jnp.full((seq_count, pad_rows), 2**24, seg_pad.dtype)], axis=1
        ),
        (lax.div(rank, 2), (position - rank) * block_len),
        (1, (3 * TEAM - 2) * block_len),
    )
    query_seg = team_seg[:, pad_rows : pad_rows + TEAM * block_len]
    lows = query_seg[0, ::TILE]
    highs = query_seg[0, TILE - 1 :: TILE]
    before = jnp.sum(team_seg < lows[:, None], axis=1, dtype=jnp.int32)
    through = jnp.sum(team_seg <= highs[:, None], axis=1, dtype=jnp.int32)
    bounds = jnp.stack([before // TILE, (through + TILE - 1) // TILE])
    seg_keys = team_seg.astype(jnp.float32)
    seg_queries = query_seg.astype(jnp.float32)
    rim_seg = lax.dynamic_slice_in_dim(
        seg_pad, position * block_len + pad_rows - RIM, block_len + 2 * RIM, 1
    )
    tap_mask = jnp.stack(
        [
            rim_seg[:, RIM - half_taps + j : RIM - half_taps + j + block_len] == own_seg
            for j in range(KERNEL)
        ],
        axis=1,
    ).astype(jnp.float32)
    seg_rim = jnp.pad(
        rim_seg.astype(jnp.float32), ((0, 0), (0, -rim_seg.shape[1] % LANES)), constant_values=-1
    )
    side = lax.axis_index("wsh")
    tap_rows = jnp.pad(tap_mask, ((0, 0), (0, 16 - KERNEL), (0, 0)))
    hidden = hidden_in.reshape(seq_count, block_len, model_width)
    (key_mat, value_mat, small_full, query_mat, point_mat, conv_mat, output_mat, inner_mat,
     window, query_team, queries, xrim, depth_low, span_keys, kern, ext, convolved,
     outer_half) = front(
        hidden, seg_rim, tap_rows, depth_kernel, kernel_w.T, kernel_b,
        [output_b, norm1_gain, norm1_bias, outer_b, norm2_gain, norm2_bias, inner_b],
        [query_b, value_b, point_b, conv_b],
        [key_w, value_w, query_w, point_w, conv_w, output_w, inner_w], outer_w,
    )
    outer_came = lax.ppermute(outer_half, "wsh", [(0, 1), (1, 0)])
    query_team = query_team.reshape(TEAM * block_len, 2 * LANES)
    attended_team, attended_t, log_sums = attend(
        bounds, query_team, window, seg_keys, seg_queries
    )
    (output, grad_sum1, grad_conv, grad_team, keep, xsend, vec_grads, bias_grads) = middle(
        attended_team.reshape(TEAM, block_len, -1), convolved, hidden, small_full,
        out_grad.reshape(seq_count, block_len, model_width),
        output_mat, inner_mat, outer_w, outer_came,
    )
    came = lax.ppermute(xsend, "ctx", [(i, i ^ 2) for i in range(lax.axis_size("ctx"))])
    grad_query_team, grad_window = attend_back(
        bounds, query_team, window, seg_keys, seg_queries,
        grad_team.reshape(TEAM * block_len, 2 * LANES), attended_t, log_sums,
    )
    grad_input, fin_ff, fin_a, fin_b = back(
        dict(seg=seg_rim, mask=tap_rows, small=small_full, vec=vec_grads, bias=bias_grads),
        grad_window, grad_query_team.reshape(TEAM, block_len, -1),
        dict(keep=keep, came=came, dconv=grad_conv, ext=ext, kern=kern, point=point_mat,
             queries=queries, spans=span_keys, depth=depth_low, xrim=xrim, x=hidden,
             convw=conv_mat, ds=grad_sum1, key=key_mat, value=value_mat, query=query_mat),
    )
    (grad_input, output, grad_query, grad_key, grad_value, grad_point, grad_conv, grad_output,
     grad_inner, grad_outer, grad_depth, grad_kernel, g_query_b, g_value_b, g_point_b, g_conv_b,
     g_output_b, gain1, shift1, g_outer_b, gain2, shift2, g_inner_b, g_kernel_b) = finish(
        side.astype(jnp.int32).reshape(1), fin_ff, fin_a, fin_b, grad_input, output,
        inner_w.shape, outer_w.shape,
    )
    return (
        output.reshape(hidden_in.shape), grad_input.reshape(hidden_in.shape),
        grad_query, g_query_b, grad_key, grad_value, g_value_b, grad_depth, grad_point,
        g_point_b, grad_kernel.T, g_kernel_b, grad_conv, g_conv_b, grad_output, g_output_b,
        gain1, shift1, grad_inner, g_inner_b, grad_outer, g_outer_b, gain2, shift2,
    )


def solution(mesh):
    in_specs = (
        P(None, "wsh", "ctx", None),
        P(None, "wsh", None),
        P(None, "wsh", "ctx", None),
        P("wsh", None),
        P("wsh"),
        P("wsh", None),
        P("wsh", None),
        P("wsh"),
        P(None, "wsh"),
        P("wsh", None),
        P("wsh"),
        P("wsh", None),
        P("wsh"),
        P("wsh", None),
        P("wsh"),
        P("wsh", None),
        P("wsh"),
        P("wsh"),
        P("wsh"),
        P(None, "wsh", None),
        P("wsh"),
        P(None, "wsh", None),
        P("wsh"),
        P("wsh"),
        P("wsh"),
    )
    out_specs = (
        P(None, "wsh", "ctx", None),
        P(None, "wsh", "ctx", None),
        P("wsh", None),
        P("wsh"),
        P("wsh", None),
        P("wsh", None),
        P("wsh"),
        P(None, "wsh"),
        P("wsh", None),
        P("wsh"),
        P("wsh", None),
        P("wsh"),
        P("wsh", None),
        P("wsh"),
        P("wsh", None),
        P("wsh"),
        P("wsh"),
        P("wsh"),
        P(None, "wsh", None),
        P("wsh"),
        P(None, "wsh", None),
        P("wsh"),
        P("wsh"),
        P("wsh"),
    )
    return jax.shard_map(
        on_device, mesh=mesh, in_specs=in_specs, out_specs=out_specs, check_vma=False
    )
```

```python
import functools
import types

import jax
import jax.numpy as jnp
from jax import lax
from jax.experimental import pallas as pl
from jax.experimental.pallas import tpu as pltpu
from jax.sharding import PartitionSpec as P

HEADS = 6
HEAD_DIM = 64
KERNEL = 9
GROUPS = 2


TILE = 256
NEG = -1000000000.0
LANES = 128
HEADS_HERE = HEADS // 2


def rows_nt(left, right):
    return lax.dot_general(
        left, right, (((1,), (1,)), ((), ())), preferred_element_type=jnp.float32
    )


def lane_half(block, upper):
    lane = lax.broadcasted_iota(jnp.int32, block.shape, 1)
    keep = lane >= HEAD_DIM if upper else lane < HEAD_DIM
    return jnp.where(keep, block, jnp.zeros_like(block))


def same_document(segk_ref, segq_ref, rows):
    row = segk_ref[0:1, rows]
    column = jnp.broadcast_to(row, (LANES, row.shape[1])).T
    wide = jnp.concatenate([column] * (TILE // LANES), axis=1)
    return wide == segq_ref[0:1, :]


def load_queries(q_ref, qm_ref):
    scale = jnp.asarray(HEAD_DIM ** (-0.5), q_ref.dtype)
    first = q_ref[:, 0:LANES] * scale
    qm_ref[0] = lane_half(first, False)
    qm_ref[1] = lane_half(first, True)
    qm_ref[2] = lane_half(q_ref[:, LANES : 2 * LANES] * scale, False)


KEY_GROUP = (0, 0, 1)
VALUE_GROUP = (2, 2, 1)


def lane_group(group):
    return slice(group * LANES, (group + 1) * LANES)


def over_tiles(first, last, step):
    fours = lax.div(last - first, 4)

    def four(p, carry):
        step(first + 4 * p, 4)
        return carry

    lax.fori_loop(0, fours, four, 0)
    rest = last - first - 4 * fours
    at = first + 4 * fours

    @pl.when(rest >= 2)
    def _():
        step(at, 2)

    @pl.when(lax.rem(rest, 2) == 1)
    def _():
        step(last - 1, 1)


def attend_kernel(bounds, q_ref, kv_ref, segk_ref, segq_ref, out_ref, outt_ref, lse_ref,
                  qm_ref, m_ref, l_ref, acc_ref):
    tile = pl.program_id(0)
    load_queries(q_ref, qm_ref)
    m_ref[...] = jnp.full_like(m_ref, -jnp.inf)
    l_ref[...] = jnp.zeros_like(l_ref)
    acc_ref[...] = jnp.zeros_like(acc_ref)

    def step(j, tiles):
        rows = pl.ds(pl.multiple_of(j * TILE, TILE), tiles * TILE)
        same = same_document(segk_ref, segq_ref, rows)
        values_t = kv_ref[rows, LANES : 3 * LANES].T
        value_rows = (2 * HEAD_DIM, 3 * HEAD_DIM, HEAD_DIM)
        raw = [
            rows_nt(kv_ref[rows, lane_group(KEY_GROUP[head])], qm_ref[head])
            for head in range(HEADS_HERE)
        ]
        highs, alphas = [], []
        for head in range(HEADS_HERE):
            scores = jnp.where(same, raw[head], NEG)
            old = m_ref[head : head + 1, :]
            top = jnp.maximum(old, jnp.max(scores, axis=0, keepdims=True))
            expo = jnp.exp(scores - top)
            alpha = jnp.exp(old - top)
            m_ref[head : head + 1, :] = top
            l_ref[head : head + 1, :] = l_ref[head : head + 1, :] * alpha + jnp.sum(
                expo, axis=0, keepdims=True
            )
            high = expo.astype(jnp.bfloat16)
            highs.append(high)
            alphas.append(alpha)
        for head in range(HEADS_HERE):
            span = slice(head * HEAD_DIM, (head + 1) * HEAD_DIM)
            vals = values_t[value_rows[head] : value_rows[head] + HEAD_DIM, :]
            acc_ref[span, :] = acc_ref[span, :] * alphas[head] + jnp.dot(
                vals, highs[head], preferred_element_type=jnp.float32
            )

    over_tiles(bounds[0, tile], bounds[1, tile], step)
    lse_ref[...] = m_ref[...] + jnp.log(l_ref[...])
    used = HEADS_HERE * HEAD_DIM
    for head in range(HEADS_HERE):
        span = slice(head * HEAD_DIM, (head + 1) * HEAD_DIM)
        inv = 1.0 / l_ref[head : head + 1, :]
        acc_ref[span, :] = acc_ref[span, :] * inv
    outt_ref[...] = acc_ref[...]
    out_ref[...] = acc_ref[...].T.astype(jnp.bfloat16)


def attend(bounds, queries, window, seg_keys, seg_queries):
    rows, wide = queries.shape
    span, width = window.shape
    return pl.pallas_call(
        attend_kernel,
        grid_spec=pltpu.PrefetchScalarGridSpec(
            num_scalar_prefetch=1,
            grid=(rows // TILE,),
            in_specs=[
                pl.BlockSpec((TILE, wide), lambda i, b: (i, 0)),
                pl.BlockSpec((span, width), lambda i, b: (0, 0)),
                pl.BlockSpec((1, span), lambda i, b: (0, 0)),
                pl.BlockSpec((1, TILE), lambda i, b: (0, i)),
            ],
            out_specs=[
                pl.BlockSpec((TILE, wide), lambda i, b: (i, 0)),
                pl.BlockSpec((wide, TILE), lambda i, b: (0, i)),
                pl.BlockSpec((8, TILE), lambda i, b: (0, i)),
            ],
            scratch_shapes=[
                pltpu.VMEM((HEADS_HERE, TILE, LANES), jnp.bfloat16),
                pltpu.VMEM((8, TILE), jnp.float32),
                pltpu.VMEM((8, TILE), jnp.float32),
                pltpu.VMEM((wide, TILE), jnp.float32),
            ],
        ),
        out_shape=[
            jax.ShapeDtypeStruct((rows, wide), jnp.bfloat16),
            jax.ShapeDtypeStruct((wide, rows), jnp.float32),
            jax.ShapeDtypeStruct((8, rows), jnp.float32),
        ],
        compiler_params=pltpu.CompilerParams(vmem_limit_bytes=63 * 2**20),
        name="attend",
    )(bounds, queries, window, seg_keys, seg_queries)


def attend_back_kernel(bounds, q_ref, kv_ref, segk_ref, segq_ref, grad_ref, outt_ref, lse_ref,
                       dq_ref, dkv_ref, qm_ref, gm_ref, delta_ref, dq_acc, dkv_acc):
    tile = pl.program_id(0)

    @pl.when(tile == 0)
    def _():
        dkv_acc[...] = jnp.zeros_like(dkv_acc)

    load_queries(q_ref, qm_ref)
    gm_ref[0] = lane_half(grad_ref[:, 0:LANES], False)
    gm_ref[1] = lane_half(grad_ref[:, 0:LANES], True)
    gm_ref[2] = lane_half(grad_ref[:, LANES : 2 * LANES], True)
    grads_t = grad_ref[...].astype(jnp.float32).T
    grad_rows = (0, HEAD_DIM, 3 * HEAD_DIM)
    for head in range(HEADS_HERE):
        span = slice(head * HEAD_DIM, (head + 1) * HEAD_DIM)
        delta_ref[head : head + 1, :] = jnp.sum(
            grads_t[grad_rows[head] : grad_rows[head] + HEAD_DIM, :] * outt_ref[span, :],
            axis=0, keepdims=True,
        )
    dq_acc[...] = jnp.zeros_like(dq_acc)

    def step(j, tiles):
        rows = pl.ds(pl.multiple_of(j * TILE, TILE), tiles * TILE)
        same = same_document(segk_ref, segq_ref, rows)
        keys_t = kv_ref[rows, 0 : 2 * LANES].T
        sums = [dkv_acc[rows, lane_group(g)] for g in range(3)]
        raw = [
            rows_nt(kv_ref[rows, lane_group(KEY_GROUP[head])], qm_ref[head])
            for head in range(HEADS_HERE)
        ]
        draw = [
            rows_nt(kv_ref[rows, lane_group(VALUE_GROUP[head])], gm_ref[head])
            for head in range(HEADS_HERE)
        ]
        ps, dss = [], []
        for head in range(HEADS_HERE):
            probs = jnp.where(same, jnp.exp(raw[head] - lse_ref[head : head + 1, :]), 0.0)
            dss.append((probs * (draw[head] - delta_ref[head : head + 1, :])).astype(jnp.bfloat16))
            ps.append(probs.astype(jnp.bfloat16))
        for head in range(HEADS_HERE):
            span = slice(head * HEAD_DIM, (head + 1) * HEAD_DIM)
            dq_acc[span, :] += jnp.dot(
                keys_t[span, :], dss[head], preferred_element_type=jnp.float32
            )
            sums[KEY_GROUP[head]] += jnp.dot(
                dss[head], qm_ref[head], preferred_element_type=jnp.float32
            )
            sums[VALUE_GROUP[head]] += jnp.dot(
                ps[head], gm_ref[head], preferred_element_type=jnp.float32
            )
        for g in range(3):
            dkv_acc[rows, lane_group(g)] = sums[g]

    over_tiles(bounds[0, tile], bounds[1, tile], step)
    dq_ref[...] = (dq_acc[...].T * HEAD_DIM ** (-0.5)).astype(dq_ref.dtype)

    @pl.when(tile == pl.num_programs(0) - 1)
    def _():
        dkv_ref[...] = dkv_acc[...].astype(dkv_ref.dtype)


def attend_back(bounds, queries, window, seg_keys, seg_queries, grads, outt, lse):
    rows, wide = queries.shape
    span, width = window.shape
    return pl.pallas_call(
        attend_back_kernel,
        grid_spec=pltpu.PrefetchScalarGridSpec(
            num_scalar_prefetch=1,
            grid=(rows // TILE,),
            in_specs=[
                pl.BlockSpec((TILE, wide), lambda i, b: (i, 0)),
                pl.BlockSpec((span, width), lambda i, b: (0, 0)),
                pl.BlockSpec((1, span), lambda i, b: (0, 0)),
                pl.BlockSpec((1, TILE), lambda i, b: (0, i)),
                pl.BlockSpec((TILE, wide), lambda i, b: (i, 0)),
                pl.BlockSpec((wide, TILE), lambda i, b: (0, i)),
                pl.BlockSpec((8, TILE), lambda i, b: (0, i)),
            ],
            out_specs=[
                pl.BlockSpec((TILE, wide), lambda i, b: (i, 0)),
                pl.BlockSpec((span, width), lambda i, b: (0, 0)),
            ],
            scratch_shapes=[
                pltpu.VMEM((HEADS_HERE, TILE, LANES), jnp.bfloat16),
                pltpu.VMEM((HEADS_HERE, TILE, LANES), jnp.bfloat16),
                pltpu.VMEM((8, TILE), jnp.float32),
                pltpu.VMEM((wide, TILE), jnp.float32),
                pltpu.VMEM((span, width), jnp.float32),
            ],
        ),
        out_shape=[
            jax.ShapeDtypeStruct((rows, wide), jnp.bfloat16),
            jax.ShapeDtypeStruct((span, width), jnp.bfloat16),
        ],
        compiler_params=pltpu.CompilerParams(vmem_limit_bytes=63 * 2**20),
        name="attend_back",
    )(bounds, queries, window, seg_keys, seg_queries, grads, outt, lse)


def rolled(part):
    return jnp.concatenate([part[..., HEAD_DIM:], part[..., :HEAD_DIM]], axis=-1)


def joined_halves(lower, upper):
    return jnp.concatenate([lower[..., :HEAD_DIM], upper[..., HEAD_DIM:]], axis=-1)


def lanes_of(values):
    return [values[..., lane_group(g)] for g in range(3)]


def parts_of_queries(queries, upper):
    one, two, three = lanes_of(queries)
    swapped = rolled(two)
    first, second = (swapped, two) if upper else (two, swapped)
    return jnp.stack(
        [jnp.concatenate([one, first], axis=-1), jnp.concatenate([three, second], axis=-1)], axis=1
    ).reshape(TEAM, queries.shape[1], 2 * LANES)


def parts_of_keys(keys, values):
    k = lanes_of(keys)
    v = lanes_of(values)
    low = jnp.concatenate([k[0], joined_halves(k[1], rolled(v[1])), v[0]], axis=-1)
    high = jnp.concatenate([k[2], joined_halves(rolled(k[1]), v[1]), v[2]], axis=-1)
    return jnp.stack([low, high], axis=1).reshape(TEAM, keys.shape[1], 3 * LANES)


def natural_rows(parts):
    pairs = parts.reshape(TEAM // 2, 2, parts.shape[1], 2 * LANES)
    low, high = pairs[:, 0], pairs[:, 1]
    middle = joined_halves(low[..., LANES:], rolled(high[..., LANES:]))
    return jnp.concatenate([low[..., :LANES], middle, high[..., :LANES]], axis=-1)


def natural_keys(parts):
    pairs = parts.reshape(TEAM // 2, 2, parts.shape[1], 3 * LANES)
    low, high = lanes_of(pairs[:, 0]), lanes_of(pairs[:, 1])
    keys = jnp.concatenate([low[0], joined_halves(low[1], rolled(high[1])), high[0]], axis=-1)
    values = jnp.concatenate([low[2], joined_halves(rolled(low[1]), high[1]), high[2]], axis=-1)
    return keys, values


TEAM = 4


def flip(index, step):
    return index + step * (1 - 2 * lax.rem(lax.div(index, step), 2))


def mate(rank, offset):
    if offset % 2:
        rank = flip(rank, 1)
    if offset // 2:
        rank = flip(rank, 2)
    return rank


def greet(peers):
    barrier = pltpu.get_barrier_semaphore()
    for peer in peers:
        pl.semaphore_signal(
            barrier, inc=1, device_id=peer, device_id_type=pl.DeviceIdType.MESH
        )
    pl.semaphore_wait(barrier, len(peers))


def remote(src, dst, send, recv, peer):
    return pltpu.make_async_remote_copy(
        src_ref=src,
        dst_ref=dst,
        send_sem=send,
        recv_sem=recv,
        device_id=peer,
        device_id_type=pl.DeviceIdType.MESH,
    )


RIM = 16
SMALL_ROWS = 128
SMALL_IN = 128
ROW_IN_KERNEL_W = 32
ROW_PAIR_QV, ROW_PAIR_PC, ROW_IN_KERNEL_B = 19, 20, 21
ROW_OUTPUT_B, ROW_GAIN1, ROW_SHIFT1, ROW_OUTER_B, ROW_GAIN2, ROW_SHIFT2 = range(9, 15)
ROW_INNER_B = 15
ROW_QUERY_B, ROW_VALUE_B, ROW_POINT_B, ROW_CONV_B = range(19, 23)
ROW_KERNEL_B = 24
ROW_KERNEL_W = 48
TAP_ROWS = 8 * KERNEL


def dot(left, right):
    return jnp.dot(left, right, preferred_element_type=jnp.float32)


def dot_tn(left, right):
    return lax.dot_general(
        left, right, (((0,), (0,)), ((), ())), preferred_element_type=jnp.float32
    )


def half_turn(block):
    return pltpu.roll(block, HEAD_DIM, axis=1)


def mixed_lanes(lower, upper):
    lane = lax.broadcasted_iota(jnp.int32, lower.shape, 1)
    return jnp.where(lane < HEAD_DIM, lower, upper)


def pair_row(small_ref, row, second):
    first = jnp.broadcast_to(small_ref[0, row : row + 1, :], (8, 384))
    other = jnp.broadcast_to(small_ref[1, row : row + 1, :], (8, 384))
    lane = lax.broadcasted_iota(jnp.int32, first.shape, 1)
    if second:
        first = pltpu.roll(first, 192, axis=1)
    else:
        other = pltpu.roll(other, 192, axis=1)
    return jnp.where(lane < 192, first, other)[0:1, :]


def tap_major(shape, offset):
    row = lax.broadcasted_iota(jnp.int32, shape, 0)
    column = lax.broadcasted_iota(jnp.int32, shape, 1) + offset
    head = lax.rem(row, 8)
    wanted = (head * KERNEL + lax.div(row, 8) == column) & (head < HEADS)
    return wanted & (row < TAP_ROWS)


def kernel_rows(first, other):
    lane = lax.broadcasted_iota(jnp.int32, first.shape, 1)
    rows = jnp.where(lane < 192, first, pltpu.roll(other, 192, axis=1))
    return jnp.concatenate(
        [rows, jnp.zeros((LANES - TAP_ROWS, rows.shape[1]), jnp.float32)], axis=0
    ).astype(jnp.bfloat16)


def kernel_bias(small_ref):
    half = HEADS * KERNEL // 2
    total = jnp.zeros((LANES, 1), jnp.float32)
    for w in range(2):
        row = small_ref[w, ROW_IN_KERNEL_B : ROW_IN_KERNEL_B + 1, 0:LANES]
        lane = lax.broadcasted_iota(jnp.int32, (LANES, LANES), 1)
        wanted = tap_major((LANES, LANES), w * half) & (lane < half)
        total = total + jnp.sum(jnp.where(wanted, row, 0.0), axis=1, keepdims=True)
    return total


def rows_of(ref, base, count):
    view = pl.ds(pl.multiple_of(base, 16), count)
    return ref.at[:, view, :] if len(ref.shape) == 3 else ref.at[view, :]


CHUNKS = 4


def front_kernel(count, *refs):
    x_ref, seg_ref, mask_ref, depth_in, kernel_in, kernel_b_in = refs[:6]
    vectors, pairs = refs[6:13], refs[13:17]
    shards = list(refs[17 : 16 + count])
    outer_any = refs[16 + count]
    rest = refs[17 + count :]
    outs = rest[: count + 9]
    half_any = rest[count + 9]
    win_ref, qteam_ref = outs[count : count + 2]
    holds = rest[count + 10 : 2 * count + 17]
    fulls = holds[:count]
    queries_ref, xrim_ref, depth_ref, spans_ref, kern_ref, ext_ref, conv_ref = holds[count:]
    (kv_part, q_part, seg_col, halo_low, halo_high, spread_ref, taps_ref, wide_ref,
     send_y, recv_y, send_c, recv_c, local, send_h, recv_h, send_kv, recv_kv, send_q, recv_q,
     send_l, recv_l, send_r, recv_r, emit_sem, small_f32, small_own, outer_half, half_sem) = rest[
        2 * count + 17 :
    ]
    shards.insert(2, small_own)
    key_ref, value_ref, small2d, query_ref, point_ref, convw_ref = fulls[:6]
    me, side = lax.axis_index("ctx"), lax.axis_index("wsh")
    size = lax.axis_size("ctx")
    core = lax.rem(me, 2)
    rank = lax.rem(me, TEAM)
    chip = lax.div(rank, 2)
    base = me - rank
    team = lax.div(me, TEAM)
    teams = size // TEAM
    right, left = lax.rem(me + TEAM, size), lax.rem(me + size - TEAM, size)
    after, prior = lax.rem(me + 1, size), lax.rem(me + size - 1, size)
    twin, across = {"ctx": flip(me, 1)}, {"wsh": 1 - side}
    seqs, block, model = x_ref.shape
    halo = (TEAM - 1) * block
    width = HEADS * HEAD_DIM
    chunk_rows = block // CHUNKS
    greet(
        [{"ctx": base + mate(rank, o)} for o in range(1, TEAM)]
        + [across, {"ctx": right}, {"ctx": left}, {"ctx": after}, {"ctx": prior}]
    )

    to_y, passed, own, emitted = [], [], [], []
    for i in range(count):
        rows = shards[i].shape[-2]
        to_y.append(
            remote(
                rows_of(shards[i], core * (rows // 2), rows // 2),
                rows_of(fulls[i], side * rows + core * (rows // 2), rows // 2),
                send_y.at[i], recv_y.at[i], across,
            )
        )
        came = rows_of(fulls[i], (1 - side) * rows + core * (rows // 2), rows // 2)
        passed.append(remote(came, came, send_c.at[i], recv_c.at[i], twin))
        own.append(
            pltpu.make_async_copy(shards[i], rows_of(fulls[i], side * rows, rows), local.at[i])
        )

    def emit(hold, out):
        copy = pltpu.make_async_copy(hold, out, emit_sem.at[len(emitted)])
        copy.start()
        emitted.append(copy)

    def emit_named(k):
        emit(holds[count + k], outs[count + 2 + k])

    urgent = 3
    for i in range(2):
        to_y[i].start()
    for i in range(2):
        own[i].start()
    half_rows = outer_half.shape[1]
    load_half = pltpu.make_async_copy(
        outer_any.at[:, part_rows(core * half_rows, half_rows), :], outer_half, half_sem.at[0]
    )
    load_half.start()
    small_f32[...] = jnp.zeros_like(small_f32)
    small_f32[0:KERNEL, :] = depth_in[...].astype(jnp.float32)

    def as_row(ref):
        return ref[...].astype(jnp.float32).reshape(1, ref.shape[0])

    at = KERNEL
    for ref in vectors:
        row = as_row(ref)
        for k in range(ref.shape[0] // 384):
            small_f32[at : at + 1, :] = row[:, k * 384 : (k + 1) * 384]
            at += 1
    for k in range(2):
        small_f32[at : at + 1, 0:192] = as_row(pairs[2 * k])
        small_f32[at : at + 1, 192:384] = as_row(pairs[2 * k + 1])
        at += 1
    small_f32[at : at + 1, 0 : kernel_b_in.shape[0]] = as_row(kernel_b_in)
    pick = jnp.where(tap_major((LANES, HEADS * KERNEL), 0), 1.0, 0.0).astype(jnp.bfloat16)
    small_f32[ROW_IN_KERNEL_W : ROW_IN_KERNEL_W + TAP_ROWS, 0:192] = dot(pick, kernel_in[...])[
        0:TAP_ROWS, :
    ]
    small_own[...] = small_f32[...].astype(jnp.bfloat16)
    to_y[2].start()
    own[2].start()
    to_after = remote(x_ref.at[:, pl.ds(block - RIM, RIM), :], halo_low, send_h.at[0],
                      recv_h.at[0], {"ctx": after})
    to_prior = remote(x_ref.at[:, pl.ds(0, RIM), :], halo_high, send_h.at[1], recv_h.at[1],
                      {"ctx": prior})
    pl.when(me < size - 1)(to_after.start)
    pl.when(me > 0)(to_prior.start)
    to_y[urgent].start()
    own[urgent].start()

    @pl.when(me == 0)
    def _():
        halo_low[...] = jnp.zeros_like(halo_low)

    @pl.when(me == size - 1)
    def _():
        halo_high[...] = jnp.zeros_like(halo_high)

    for s in range(seqs):
        seg_col[s] = jnp.broadcast_to(seg_ref[s : s + 1, :], (LANES, seg_ref.shape[1])).T
        for g in range(model // LANES):
            xrim_ref[s, g, pl.ds(RIM, block), :] = x_ref[s, :, lane_group(g)].astype(jnp.float32)

    def arrive(i):
        to_y[i].wait_recv()
        passed[i].start()

    def settle(i):
        own[i].wait()
        passed[i].wait_recv()
        emit(fulls[i], outs[i])

    for i in range(urgent):
        arrive(i)
    for i in (4, 5, 6, 7):
        to_y[i].start()
        own[i].start()
    for i in range(urgent):
        settle(i)
    small_ref = taps_ref
    for w in range(2):
        small_ref[w] = small2d[pl.ds(w * SMALL_IN, SMALL_IN), :].astype(jnp.float32)
    value_bias = pair_row(small_ref, ROW_PAIR_QV, True)
    query_bias = pair_row(small_ref, ROW_PAIR_QV, False)

    def piece(r, c):
        return win_ref.at[
            pl.ds(pl.multiple_of(halo + r * block + c * chunk_rows, 16), chunk_rows), :
        ]

    def part(r, c):
        return kv_part.at[r, pl.ds(c * chunk_rows, chunk_rows), :]

    def kv_copy(r, c):
        return (
            pltpu.make_async_copy(part(r, c), piece(rank, c), recv_kv.at[rank * CHUNKS + c]),
            remote(part(r, c), piece(rank, c), send_kv.at[r * CHUNKS + c],
                   recv_kv.at[rank * CHUNKS + c], {"ctx": base + r}),
        )

    def q_copy(r):
        return (
            pltpu.make_async_copy(q_part.at[r], qteam_ref.at[rank], recv_q.at[rank]),
            remote(q_part.at[r], qteam_ref.at[rank], send_q.at[r], recv_q.at[rank],
                   {"ctx": base + r}),
        )

    def begin(pair, r):
        pl.when(rank == r)(pair[0].start)
        pl.when(rank != r)(pair[1].start)

    for s in (1 - chip, chip):
        rows = x_ref[s]
        keys = dot(rows, key_ref[...])
        values = dot(rows, value_ref[...]) + value_bias
        k = [keys[:, lane_group(g)] for g in range(3)]
        v = [values[:, lane_group(g)] for g in range(3)]
        for half, groups in enumerate((
            (k[0], mixed_lanes(k[1], half_turn(v[1])), v[0]),
            (k[2], mixed_lanes(half_turn(k[1]), v[1]), v[2]),
        )):
            for g in range(3):
                kv_part[2 * s + half, :, lane_group(g)] = groups[g].astype(jnp.bfloat16)
        for c in range(CHUNKS):
            for half in range(2):
                begin(kv_copy(2 * s + half, c), 2 * s + half)

    def onward(r, c):
        to_right = remote(
            piece(r, c),
            win_ref.at[
                pl.ds(pl.multiple_of(lax.rem(r + TEAM - 1, TEAM) * block + c * chunk_rows, 16),
                      chunk_rows), :
            ],
            send_r.at[r * CHUNKS + c], recv_r.at[r * CHUNKS + c], {"ctx": right},
        )
        to_left = remote(
            piece(r, c),
            win_ref.at[
                pl.ds(
                    pl.multiple_of(
                        halo + TEAM * block + lax.rem(r, TEAM - 1) * block + c * chunk_rows, 16
                    ),
                    chunk_rows,
                ), :
            ],
            send_l.at[r * CHUNKS + c], recv_l.at[r * CHUNKS + c], {"ctx": left},
        )
        return to_right, to_left

    def relay(o, c):
        r = mate(rank, o)
        if o == 0:
            kv_copy(r, c)[0].wait()
        else:
            remote(part(rank, c), piece(r, c), send_kv.at[rank * CHUNKS + c],
                   recv_kv.at[r * CHUNKS + c], {"ctx": base + r}).wait_recv()
        to_right, to_left = onward(r, c)
        pl.when((r >= 1) & (team < teams - 1))(to_right.start)
        pl.when((r <= TEAM - 2) & (team > 0))(to_left.start)

    for c in range(CHUNKS):
        relay(0, c)
        relay(1, c)
    arrive(urgent)
    settle(urgent)
    for s in range(seqs):
        queries = dot(x_ref[s], query_ref[...]) + query_bias
        queries_ref[s] = queries.astype(jnp.bfloat16)
        q = [queries[:, lane_group(g)] for g in range(3)]
        for half, groups in enumerate(((q[0], q[1]), (q[2], half_turn(q[1])))):
            for g in range(2):
                q_part[2 * s + half, :, lane_group(g)] = groups[g].astype(jnp.bfloat16)
        for half in range(2):
            begin(q_copy(2 * s + half), 2 * s + half)
    emit_named(0)

    pl.when(me > 0)(to_after.wait_recv)
    pl.when(me < size - 1)(to_prior.wait_recv)
    for s in range(seqs):
        for g in range(model // LANES):
            xrim_ref[s, g, pl.ds(0, RIM), :] = halo_low[s, :, lane_group(g)].astype(jnp.float32)
            xrim_ref[s, g, pl.ds(RIM + block, RIM), :] = halo_high[s, :, lane_group(g)].astype(
                jnp.float32
            )
    emit_named(1)
    strip = 32
    lead = RIM - KERNEL // 2

    def taps_row(j, g):
        return small_ref[g // 3, j : j + 1, lane_group(g % 3)]

    def depth_strip(c, s):
        start = c * strip
        here = seg_col[s, pl.ds(RIM + start, strip), :]
        sums = [jnp.zeros((strip, LANES), jnp.float32) for _ in range(model // LANES)]
        for j in range(KERNEL):
            same = seg_col[s, pl.ds(lead + j + start, strip), :] == here
            for g in range(model // LANES):
                near = xrim_ref[s, g, pl.ds(lead + j + start, strip), :]
                sums[g] = sums[g] + jnp.where(same, near, 0.0) * taps_row(j, g)
        for g in range(model // LANES):
            depth_ref[s, pl.ds(pl.multiple_of(start, strip), strip), lane_group(g)] = sums[
                g
            ].astype(jnp.bfloat16)
        return s

    relay(2, 0)
    relay(3, 0)
    lax.fori_loop(0, block // strip, depth_strip, 0)
    relay(2, 1)
    relay(3, 1)
    lax.fori_loop(0, block // strip, depth_strip, 1)
    emit_named(2)
    for c in range(2, CHUNKS):
        relay(2, c)
        relay(3, c)
    for j in range(KERNEL):
        row = lax.broadcasted_iota(jnp.int32, (2 * LANES, width), 0)
        col = lax.broadcasted_iota(jnp.int32, (2 * LANES, width), 1)
        row = jnp.where(row >= LANES, row - LANES, row)
        spread_ref[j] = jnp.where(row == 8 * j + col // HEAD_DIM, 1.0, 0.0).astype(jnp.bfloat16)
    for i in (4, 5):
        arrive(i)
    for i in (4, 5):
        settle(i)
    load_half.wait()
    emit(outer_half, half_any)
    point_bias = pair_row(small_ref, ROW_PAIR_PC, False)
    conv_bias = pair_row(small_ref, ROW_PAIR_PC, True)
    tap_view = slice(ROW_IN_KERNEL_W, ROW_IN_KERNEL_W + TAP_ROWS)
    kernel_w = kernel_rows(small_ref[0, tap_view, :], small_ref[1, tap_view, :])
    kernel_b = kernel_bias(small_ref)
    for s in range(seqs):
        spans = dot(depth_ref[s], point_ref[...]) + point_bias
        spans_ref[s] = spans
        mixed = (spans * queries_ref[s].astype(jnp.float32)).astype(jnp.bfloat16)
        logits = rows_nt(kernel_w, mixed) + kernel_b
        cut = [logits[8 * j : 8 * j + 8, :] for j in range(KERNEL)]
        top = functools.reduce(jnp.maximum, cut)
        expo = [jnp.exp(part - top) for part in cut]
        inverse = 1.0 / sum(expo)
        for j in range(KERNEL):
            kern = expo[j] * inverse
            kern_ref[s, 8 * j : 8 * j + 8, :] = kern
            wide_ref[8 * j : 8 * j + 8, :] = kern * mask_ref[s, j : j + 1, :]
        wide_ref[TAP_ROWS:, :] = jnp.zeros((LANES - TAP_ROWS, block), jnp.float32)
        tall = wide_ref[...].T
        high = tall.astype(jnp.bfloat16)
        low = (tall - high.astype(jnp.float32)).astype(jnp.bfloat16)
        both = jnp.concatenate([high, low], axis=1)
        for g in range(3):
            row_ext = [xrim_ref[s, k] for k in range(model // LANES)]
        ext = dot(
            jnp.concatenate([part.astype(jnp.bfloat16) for part in row_ext], axis=1),
            convw_ref[...],
        ) + conv_bias
        for g in range(3):
            ext_ref[s, g] = ext[:, lane_group(g)]
        chunk = 128
        for c in range(block // chunk):
            sums = [jnp.zeros((chunk, LANES), jnp.float32) for _ in range(3)]
            for j in range(KERNEL):
                weight = dot(both[c * chunk : (c + 1) * chunk, :], spread_ref[j])
                for g in range(3):
                    near = ext_ref[s, g, pl.ds(lead + j + c * chunk, chunk), :]
                    sums[g] = sums[g] + weight[:, lane_group(g)] * near
            for g in range(3):
                conv_ref[s, pl.ds(c * chunk, chunk), lane_group(g)] = sums[g].astype(jnp.bfloat16)

    for k in range(3, 7):
        emit_named(k)
    for i in (6, 7):
        arrive(i)
    for i in (6, 7):
        settle(i)
    for r in range(TEAM):
        for c in range(CHUNKS):
            pl.when(rank != r)(kv_copy(r, c)[1].wait_send)
        pl.when(rank != r)(q_copy(r)[1].wait_send)
    for o in range(TEAM):
        r = mate(rank, o)
        if o == 0:
            q_copy(r)[0].wait()
        else:
            remote(q_part.at[rank], qteam_ref.at[r], send_q.at[rank], recv_q.at[r],
                   {"ctx": base + r}).wait_recv()
    for r in range(TEAM):
        for c in range(CHUNKS):
            to_right, to_left = onward(jnp.int32(r), c)
            if r >= 1:
                pl.when(team < teams - 1)(to_right.wait_send)
                pl.when(team > 0)(to_right.wait_recv)
            if r <= TEAM - 2:
                pl.when(team > 0)(to_left.wait_send)
                pl.when(team < teams - 1)(to_left.wait_recv)
    for i in range(count):
        to_y[i].wait_send()
        passed[i].wait_send()
    pl.when(me < size - 1)(to_after.wait_send)
    pl.when(me > 0)(to_prior.wait_send)
    for copy in emitted:
        copy.wait()


def front(hidden, seg_rim, tap_mask, depth, kernel, kernel_b, vectors, pairs, shards, outer):
    seqs, block, model = hidden.shape
    small = jax.ShapeDtypeStruct((SMALL_IN, 384), hidden.dtype)
    gathered = list(shards[:2]) + [small] + list(shards[2:])
    count = len(gathered)
    half = jax.ShapeDtypeStruct((outer.shape[0], outer.shape[1] // 2, outer.shape[2]), outer.dtype)
    width = HEADS * HEAD_DIM
    wide = block + 2 * RIM
    fulls = [
        jax.ShapeDtypeStruct(s.shape[:-2] + (2 * s.shape[-2], s.shape[-1]), s.dtype) for s in gathered
    ]
    vmem = pl.BlockSpec(memory_space=pltpu.VMEM)
    anywhere = pl.BlockSpec(memory_space=pl.ANY)
    low, full = jnp.bfloat16, jnp.float32
    outs = [
        jax.ShapeDtypeStruct(((3 * TEAM - 2) * block, width), low),
        jax.ShapeDtypeStruct((TEAM, block, 2 * LANES), low),
        jax.ShapeDtypeStruct((seqs, block, width), low),
        jax.ShapeDtypeStruct((seqs, model // LANES, wide, LANES), full),
        jax.ShapeDtypeStruct((seqs, block, model), low),
        jax.ShapeDtypeStruct((seqs, block, width), full),
        jax.ShapeDtypeStruct((seqs, TAP_ROWS, block), full),
        jax.ShapeDtypeStruct((seqs, 3, wide, LANES), full),
        jax.ShapeDtypeStruct((seqs, block, width), low),
    ]
    dma = pltpu.SemaphoreType.DMA
    return pl.pallas_call(
        functools.partial(front_kernel, count),
        out_shape=fulls + outs + [half],
        in_specs=[vmem] * 17 + [anywhere] * count,
        out_specs=[anywhere] * (count + 10),
        scratch_shapes=[pltpu.VMEM(s.shape, s.dtype) for s in fulls + outs[2:]] + [
            pltpu.VMEM((TEAM, block, width), low),
            pltpu.VMEM((TEAM, block, 2 * LANES), low),
            pltpu.VMEM((seqs, seg_rim.shape[1], LANES), full),
            pltpu.VMEM((seqs, RIM, model), low),
            pltpu.VMEM((seqs, RIM, model), low),
            pltpu.VMEM((KERNEL, 2 * LANES, width), low),
            pltpu.VMEM((2, SMALL_IN, 384), full),
            pltpu.VMEM((LANES, block), full),
            dma((count,)), dma((count,)), dma((count,)), dma((count,)), dma((count,)),
            dma((2,)), dma((2,)),
            dma((TEAM * CHUNKS,)), dma((TEAM * CHUNKS,)), dma((TEAM,)), dma((TEAM,)),
            dma((TEAM * CHUNKS,)), dma((TEAM * CHUNKS,)), dma((TEAM * CHUNKS,)),
            dma((TEAM * CHUNKS,)), dma((count + 8,)),
            pltpu.VMEM((SMALL_IN, 384), full), pltpu.VMEM((SMALL_IN, 384), low),
            pltpu.VMEM(half.shape, low), dma((1,)),
        ],
        compiler_params=pltpu.CompilerParams(
            collective_id=0, has_side_effects=True, vmem_limit_bytes=56 * 2**20
        ),
        name="front",
    )(hidden, seg_rim, tap_mask, depth, kernel, kernel_b, *vectors, *pairs, *shards, outer)
PACK_A = 1280
PACK_B = 768
SMALL_AT = 1152


def chips_of(me, size):
    core = lax.rem(me, 2)
    count = size // 2
    index = lax.div(me, 2)
    return index, count, lambda other: other * 2 + core


def pair_of(me, size):
    index = lax.rem(lax.div(me, 2), 2)
    return index, 2, lambda other: flip(me, 2)


def column_of(me, size):
    index = lax.div(me, TEAM)
    rest = lax.rem(me, TEAM)
    return index, size // TEAM, lambda other: other * TEAM + rest


def part_rows(base, count):
    return pl.ds(pl.multiple_of(base, 16), count)


def others(index, count):
    return [lax.rem(index + o, count) for o in range(1, count)]


def scatter_copies(stage, me, size, staged, came, send, recv):
    index, count, device = stage(me, size)
    piece = staged.shape[0] // count
    return [
        remote(staged.at[part_rows(other * piece, piece), :], came.at[index], send.at[other],
               recv.at[index], {"ctx": device(other)})
        for other in others(index, count)
    ]


def scatter_wait(stage, me, size, staged, came, send, recv):
    index, count, device = stage(me, size)
    piece = staged.shape[0] // count
    for other in others(index, count):
        remote(staged.at[part_rows(index * piece, piece), :], came.at[other], send.at[index],
               recv.at[other], {"ctx": device(other)}).wait_recv()


def share_copies(stage, me, size, fin, base, piece, send, recv):
    index, count, device = stage(me, size)
    view = fin.at[part_rows(base + index * piece, piece), :]
    return [
        remote(view, view, send.at[other], recv.at[index], {"ctx": device(other)})
        for other in others(index, count)
    ]


def share_wait(stage, me, size, fin, base, piece, send, recv):
    index, count, device = stage(me, size)
    for other in others(index, count):
        view = fin.at[part_rows(base + other * piece, piece), :]
        remote(view, view, send.at[index], recv.at[other], {"ctx": device(other)}).wait_recv()


def in_chunks(rows, body):
    chunk = max(c for c in range(16, 241, 16) if rows % c == 0)

    def step(i, carry):
        body(pl.multiple_of(i * chunk, 16), chunk)
        return carry

    lax.fori_loop(0, rows // chunk, step, 0)


def wide(value):
    return value.astype(jnp.float32)


def back_kernel(names, a_names, b_names, loaded, *refs):
    count_a, count_b = len(a_names), len(b_names)
    r = types.SimpleNamespace(**dict(zip(names, refs)))
    late = refs[len(names) :]
    block_a = types.SimpleNamespace(**dict(zip(a_names, late[:count_a])))
    block_b = types.SimpleNamespace(**dict(zip(b_names, late[count_a : count_a + count_b])))
    fetch_refs = late[count_a + count_b :]
    v = types.SimpleNamespace(**dict(zip(loaded, fetch_refs[len(loaded) :])))
    me, side = lax.axis_index("ctx"), lax.axis_index("wsh")
    size = lax.axis_size("ctx")
    core = lax.rem(me, 2)
    rank = lax.rem(me, TEAM)
    chip = lax.div(rank, 2)
    base = me - rank
    team = lax.div(me, TEAM)
    teams = size // TEAM
    twin, across = {"ctx": flip(me, 1)}, {"wsh": 1 - side}
    right, left = lax.rem(me + TEAM, size), lax.rem(me + size - TEAM, size)
    after, prior = lax.rem(me + 1, size), lax.rem(me + size - 1, size)
    seqs, block, model = v.x.shape
    width = HEADS * HEAD_DIM
    halo = (TEAM - 1) * block
    groups = model // LANES
    low = jnp.bfloat16
    index, count, device = chips_of(me, size)
    greet(
        [twin, across, {"ctx": base + mate(rank, 3)}, {"ctx": after}, {"ctx": prior}]
        + [{"ctx": device(other)} for other in others(index, count)]
    )

    def block_of(k):
        return pl.ds(pl.multiple_of(k * block, 16), block)

    def halo_left(c):
        return remote(r.window.at[block_of(2 * TEAM - 1 + c), :], r.from_left.at[block_of(c), :],
                      r.send_l.at[c], r.recv_l.at[c], {"ctx": right})

    def halo_right(c):
        return remote(r.window.at[block_of(c), :], r.from_right.at[block_of(c + 1), :],
                      r.send_r.at[c], r.recv_r.at[c], {"ctx": left})

    for k in range(TEAM - 1):
        to_right = halo_left(chip * k + (1 - chip) * (TEAM - 2 - k))
        to_left = halo_right(chip * k + (1 - chip) * ((k + 1) % (TEAM - 1)))
        pl.when(team < teams - 1)(to_right.start)
        pl.when(team > 0)(to_left.start)

    fetched = types.SimpleNamespace()
    for k, name in enumerate(loaded):
        copy = pltpu.make_async_copy(fetch_refs[k], fetch_refs[len(loaded) + k], r.load.at[k])
        setattr(fetched, name, copy)
    center = pltpu.make_async_copy(r.window.at[pl.ds(halo, TEAM * block), :], r.mine,
                                   r.load.at[len(loaded)])
    fetched.keep.start()
    fetched.came.start()
    center.start()

    def q_copy(o):
        other = mate(rank, o)
        return remote(r.dq.at[other], r.q_parts.at[rank], r.send_q.at[o], r.recv_q.at[o],
                      {"ctx": base + other})

    own_q = pltpu.make_async_copy(r.dq.at[rank], r.q_parts.at[rank], r.recv_q.at[0])
    for o in (3, 2, 1):
        q_copy(o).start()
    own_q.start()
    for name in loaded[2:]:
        getattr(fetched, name).start()

    def have(*copies):
        for copy in copies:
            copy.wait()

    half_ff = v.keep.shape[1]
    pair_index, _, _ = pair_of(me, size)
    have(fetched.keep, fetched.came)

    def stage_across(at, n):
        rows = part_rows(at, n)
        r.ff_send[rows, :] = (v.keep[1 - side, rows, :] + wide(v.came[1 - side, rows, :])).astype(low)
        v.keep[side, rows, :] = v.keep[side, rows, :] + wide(v.came[side, rows, :])

    in_chunks(half_ff, stage_across)
    ff_across = remote(r.ff_send, r.ff_came, r.send_p.at[0], r.recv_p.at[0], across)
    ff_across.start()

    small = r.sums
    small[...] = jnp.zeros_like(small)
    for j in range(KERNEL):
        row = lax.broadcasted_iota(jnp.int32, (2 * LANES, width), 0)
        col = lax.broadcasted_iota(jnp.int32, (2 * LANES, width), 1)
        row = jnp.where(row >= LANES, row - LANES, row)
        r.spread[j] = jnp.where(row == 8 * j + col // HEAD_DIM, 1.0, 0.0).astype(low)

    zero_block = jnp.zeros((block, width), low)
    r.from_left[pl.ds((TEAM - 1) * block, block), :] = zero_block
    r.from_right[0:block, :] = zero_block

    @pl.when(team == 0)
    def _():
        for k in range(TEAM - 1):
            r.from_left[pl.ds(k * block, block), :] = zero_block

    @pl.when(team == teams - 1)
    def _():
        for k in range(1, TEAM):
            r.from_right[pl.ds(k * block, block), :] = zero_block

    @pl.when(me == 0)
    def _():
        r.dd_low[...] = jnp.zeros_like(r.dd_low)
        r.rim_low[...] = jnp.zeros_like(r.rim_low)

    @pl.when(me == size - 1)
    def _():
        r.dd_high[...] = jnp.zeros_like(r.dd_high)
        r.rim_high[...] = jnp.zeros_like(r.rim_high)

    small_ref = r.small
    kernel_w = kernel_rows(
        wide(small_ref[ROW_IN_KERNEL_W : ROW_IN_KERNEL_W + TAP_ROWS, :]),
        wide(small_ref[SMALL_IN + ROW_IN_KERNEL_W : SMALL_IN + ROW_IN_KERNEL_W + TAP_ROWS, :]),
    )
    lead = RIM - KERNEL // 2
    chunk = 128
    r.d_ext[...] = jnp.zeros_like(r.d_ext)
    have(fetched.dconv, fetched.ext, fetched.kern, fetched.point, fetched.queries, fetched.spans)
    wide_ref, tall_ref = r.wide, r.tall

    def conv_back(s):
        r.seg_col[s] = jnp.broadcast_to(r.seg[s : s + 1, :], (LANES, r.seg.shape[1])).T
        for j in range(KERNEL):
            wide_ref[8 * j : 8 * j + 8, :] = (
                v.kern[s, 8 * j : 8 * j + 8, :] * r.mask[s, j : j + 1, :]
            )
        wide_ref[TAP_ROWS:, :] = jnp.zeros((LANES - TAP_ROWS, block), jnp.float32)
        tall = wide_ref[...].T
        high = tall.astype(low)
        both = jnp.concatenate([high, (tall - wide(high)).astype(low)], axis=1)
        for c in range(block // chunk):
            rows = slice(c * chunk, (c + 1) * chunk)
            grad = wide(v.dconv[s, rows, :])
            taps = jnp.zeros((chunk, LANES), jnp.float32)
            for j in range(KERNEL):
                near = jnp.concatenate(
                    [v.ext[s, g, pl.ds(lead + j + c * chunk, chunk), :] for g in range(3)],
                    axis=1,
                )
                term = near * grad
                first = term.astype(low)
                second = (term - wide(first)).astype(low)
                taps = taps + rows_nt(first, r.spread[j, 0:LANES, :])
                taps = taps + rows_nt(second, r.spread[j, 0:LANES, :])
                weight = dot(both[rows, :], r.spread[j]) * grad
                for g in range(3):
                    r.d_ext[s, g, pl.ds(lead + j + c * chunk, chunk), :] += weight[
                        :, lane_group(g)
                    ]
            tall_ref[rows, :] = taps
        back = tall_ref[...].T
        inner = jnp.zeros((8, block), jnp.float32)
        for j in range(KERNEL):
            inner = inner + v.kern[s, 8 * j : 8 * j + 8, :] * (
                back[8 * j : 8 * j + 8, :] * r.mask[s, j : j + 1, :]
            )
        for j in range(KERNEL):
            wide_ref[8 * j : 8 * j + 8, :] = v.kern[s, 8 * j : 8 * j + 8, :] * (
                back[8 * j : 8 * j + 8, :] * r.mask[s, j : j + 1, :] - inner
            )
        d_logits = wide_ref[0:TAP_ROWS, :].astype(low)
        mixed = (v.spans[s] * wide(v.queries[s])).astype(low)
        kernel_grad = dot(d_logits, mixed)
        kernel_bias = dot(d_logits, jnp.ones((block, LANES), low))
        for w in range(2):
            small[w, ROW_KERNEL_W : ROW_KERNEL_W + TAP_ROWS, :] += kernel_grad
            for g in range(3):
                small[w, ROW_KERNEL_B : ROW_KERNEL_B + 24, lane_group(g)] += kernel_bias[
                    24 * g : 24 * g + 24, :
                ]
        d_mixed = dot(wide_ref[...].T.astype(low), kernel_w)
        d_spans = (d_mixed * wide(v.queries[s])).astype(low)
        v.spans[s] = d_mixed * v.spans[s]
        v.dconv[s] = d_spans
        bias = jnp.sum(wide(d_spans), axis=0, keepdims=True)
        for w in range(2):
            small[w, ROW_POINT_B : ROW_POINT_B + 1, :] += bias
        d_depth = rows_nt(d_spans, v.point[...])
        for g in range(groups):
            r.dd[s, g, pl.ds(RIM, block), :] = d_depth[:, lane_group(g)]
        r.dd_first[s] = d_depth[0:RIM, :].astype(low)
        r.dd_last[s] = d_depth[block - RIM : block, :].astype(low)
        for g in range(3):
            r.rim_first[s, :, lane_group(g)] = r.d_ext[s, g, 0:RIM, :].astype(low)
            r.rim_last[s, :, lane_group(g)] = r.d_ext[
                s, g, RIM + block : 2 * RIM + block, :
            ].astype(low)


    def kv_copy(k):
        return (
            pltpu.make_async_copy(r.mine.at[block_of(k), :], r.kv_parts.at[rank], r.recv_kv.at[rank]),
            remote(r.mine.at[block_of(k), :], r.kv_parts.at[rank], r.send_kv.at[k],
                   r.recv_kv.at[rank], {"ctx": base + k}),
        )

    def return_block(k):
        pl.when((k <= TEAM - 2) & (team > 0))(lambda: halo_left(lax.rem(k, TEAM - 1)).wait_recv())
        pl.when((k >= 1) & (team < teams - 1))(
            lambda: halo_right(lax.rem(k + TEAM - 2, TEAM - 1)).wait_recv()
        )
        rows = block_of(k)
        r.mine[rows, :] = (
            wide(r.mine[rows, :]) + wide(r.from_left[rows, :]) + wide(r.from_right[rows, :])
        ).astype(low)
        pair = kv_copy(k)
        pl.when(k == rank)(pair[0].start)
        pl.when(k != rank)(pair[1].start)


    ff_base = core * (2 * half_ff) + pair_index * half_ff
    column_index, column_count, _ = column_of(me, size)
    column_piece = half_ff // column_count
    column_args = (column_of, me, size, r.ff_send, r.ff_column, r.send_c, r.recv_c)
    column_share = (column_of, me, size, r.fin_ff, ff_base, column_piece, r.send_cg, r.recv_cg)

    def piece_copy(fin, start, pair_rows, rows, k, mine, send, recv):
        side_of_pair = pair_index if mine else 1 - pair_index
        view = fin.at[part_rows(start + side_of_pair * pair_rows + k * rows, rows), :]
        return remote(view, view, send.at[k], recv.at[k], {"ctx": flip(me, 2)})

    def ff_piece(k, mine):
        return piece_copy(r.fin_ff, core * (2 * half_ff), half_ff, column_piece, k, mine,
                          r.send_pg, r.recv_pg)

    def wait_piece(spec, other):
        stage, _, _, fin, start, rows, send, recv = spec
        place, _, device_of = stage(me, size)
        view = fin.at[part_rows(start + other * rows, rows), :]
        remote(view, view, send.at[place], recv.at[other], {"ctx": device_of(other)}).wait_recv()

    def ff_to_column():
        ff_across.wait()

        def body(at, n):
            rows = part_rows(at, n)
            value = v.keep[side, rows, :] + wide(r.ff_came[rows, :])
            v.keep[side, rows, :] = value
            r.ff_send[rows, :] = value.astype(low)

        in_chunks(half_ff, body)
        for copy in scatter_copies(*column_args):
            copy.start()

    def ff_to_share():
        scatter_wait(*column_args)
        rows = part_rows(column_index * column_piece, column_piece)
        total = v.keep[side, rows, :]
        for other in others(column_index, column_count):
            total = total + wide(r.ff_column[other])
        r.ff_send[rows, :] = total.astype(low)
        own = pltpu.make_async_copy(
            r.ff_send.at[rows, :],
            r.fin_ff.at[part_rows(ff_base + column_index * column_piece, column_piece), :],
            r.load.at[0],
        )
        own.start()
        own.wait()
        for copy in share_copies(*column_share):
            copy.start()
        ff_piece(column_index, True).start()

    def ff_to_pair():
        for other in others(column_index, column_count):
            wait_piece(column_share, other)
            ff_piece(other, True).start()

    def ff_twin():
        view = r.fin_ff.at[part_rows(core * (2 * half_ff), 2 * half_ff), :]
        return remote(view, view, r.send_pg.at[column_count], r.recv_pg.at[column_count], twin)

    def ff_to_twin():
        for k in range(column_count):
            ff_piece(k, False).wait_recv()
        ff_twin().start()


    conv_back(0)
    center.wait()
    there = (1 - chip) * (TEAM // 2)
    here = chip * (TEAM // 2)
    return_block(there)
    conv_back(1)
    rims = [
        (remote(r.dd_last, r.dd_low, r.send_h.at[0], r.recv_h.at[0], {"ctx": after}), 1),
        (remote(r.rim_last, r.rim_low, r.send_h.at[1], r.recv_h.at[1], {"ctx": after}), 1),
        (remote(r.dd_first, r.dd_high, r.send_h.at[2], r.recv_h.at[2], {"ctx": prior}), 0),
        (remote(r.rim_first, r.rim_high, r.send_h.at[3], r.recv_h.at[3], {"ctx": prior}), 0),
    ]
    for copy, forward in rims:
        pl.when(me < size - 1 if forward else me > 0)(copy.start)

    return_block(there + 1)
    ff_to_column()
    have(fetched.depth, fetched.xrim)
    strip = 32

    def flat_rows(ref):
        return ref[...].reshape(seqs * block, ref.shape[2])

    point_grad = dot_tn(flat_rows(v.depth), flat_rows(v.dconv)).astype(low)
    for w in range(2):
        block_a.pack[w, 0:width, :] = point_grad[w * width : (w + 1) * width, :]
    for g in range(groups):
        def tap_step(c, sums, g=g):
            out = list(sums)
            for s in range(seqs):
                start = c * strip
                here = r.seg_col[s, pl.ds(RIM + start, strip), :]
                grad = r.dd[s, g, pl.ds(RIM + start, strip), :]
                for j in range(KERNEL):
                    same = r.seg_col[s, pl.ds(lead + j + start, strip), :] == here
                    near = v.xrim[s, g, pl.ds(lead + j + start, strip), :]
                    out[j] = out[j] + fold_rows(jnp.where(same, near, 0.0) * grad)
            return tuple(out)

        sums = lax.fori_loop(
            0, block // strip, tap_step,
            tuple(jnp.zeros((8, LANES), jnp.float32) for _ in range(KERNEL)),
        )
        for j in range(KERNEL):
            small[g // 3, j : j + 1, lane_group(g % 3)] = jnp.sum(sums[j], axis=0, keepdims=True)

    return_block(here + 1 - chip)
    return_block(here + chip)
    have(fetched.convw, fetched.x)
    for copy, forward in rims:
        pl.when(me > 0 if forward else me < size - 1)(copy.wait_recv)
    near_taps = KERNEL // 2
    for s in range(seqs):
        for g in range(3):
            head = pl.ds(RIM, RIM)
            tail = pl.ds(block, RIM)
            r.d_ext[s, g, head, :] += wide(r.rim_low[s, :, lane_group(g)])
            r.d_ext[s, g, tail, :] += wide(r.rim_high[s, :, lane_group(g)])
            v.queries[s, :, lane_group(g)] = r.d_ext[s, g, pl.ds(RIM, block), :].astype(low)
        for g in range(groups):
            r.dd[s, g, 0:RIM, :] = wide(r.dd_low[s, :, lane_group(g)])
            r.dd[s, g, pl.ds(RIM + block, RIM), :] = wide(r.dd_high[s, :, lane_group(g)])
        bias = jnp.sum(wide(v.queries[s]), axis=0, keepdims=True)
        for w in range(2):
            small[w, ROW_CONV_B : ROW_CONV_B + 1, :] += bias
    conv_grad = dot_tn(flat_rows(v.x), flat_rows(v.queries)).astype(low)
    for w in range(2):
        block_a.pack[w, width : 2 * width, :] = conv_grad[w * width : (w + 1) * width, :]

    def core_copy(blk):
        pack = blk.pack
        half = pack.shape[1] // 2
        return remote(pack.at[:, part_rows((1 - core) * half, half), :], blk.twin,
                      blk.send_core.at[0], blk.recv_core.at[0], twin)

    def y_copy(blk):
        return remote(blk.ysend, blk.ycame, blk.send_core.at[1],
                      blk.recv_core.at[1], across)

    def core_done(blk):
        core_copy(blk).wait()
        pack, came = blk.pack, blk.twin
        half = pack.shape[1] // 2

        def body(at, n):
            rows, there = part_rows(at, n), part_rows(core * half + at, n)
            blk.ysend[rows, :] = (
                wide(pack[1 - side, there, :]) + wide(came[1 - side, rows, :])
            ).astype(low)
            blk.acc[rows, :] = wide(pack[side, there, :]) + wide(came[side, rows, :])

        in_chunks(half, body)
        y_copy(blk).start()

    def chips_args(blk):
        return (chips_of, me, size, blk.ysend, blk.chips,
                blk.send_s, blk.recv_s)

    def y_done(blk):
        y_copy(blk).wait()

        def body(at, n):
            rows = part_rows(at, n)
            value = blk.acc[rows, :] + wide(blk.ycame[rows, :])
            blk.acc[rows, :] = value
            blk.ysend[rows, :] = value.astype(low)

        in_chunks(blk.ysend.shape[0], body)
        for copy in scatter_copies(*chips_args(blk)):
            copy.start()

    def pair_copy_a():
        rows = block_a.ysend.shape[0] // 2
        return remote(block_a.ysend.at[part_rows((1 - pair_index) * rows, rows), :], block_a.pair,
                      block_a.send_core.at[3], block_a.recv_core.at[3], {"ctx": flip(me, 2)})

    def y_done_a():
        y_copy(block_a).wait()

        def body(at, n):
            rows = part_rows(at, n)
            value = block_a.acc[rows, :] + wide(block_a.ycame[rows, :])
            block_a.acc[rows, :] = value
            block_a.ysend[rows, :] = value.astype(low)

        in_chunks(block_a.ysend.shape[0], body)
        pair_copy_a().start()

    def column_args_a():
        rows = block_a.ysend.shape[0] // 2
        return (column_of, me, size, block_a.ysend.at[pl.ds(0, rows), :], block_a.column,
                block_a.send_s, block_a.recv_s)

    def pair_done_a():
        pair_copy_a().wait()
        half = block_a.ysend.shape[0] // 2

        def body(at, n):
            rows = part_rows(at, n)
            value = block_a.acc[part_rows(pair_index * half + at, n), :] + wide(
                block_a.pair[rows, :]
            )
            block_a.acc[rows, :] = value
            block_a.ysend[rows, :] = value.astype(low)

        in_chunks(half, body)
        for copy in scatter_copies(*column_args_a()):
            copy.start()

    def column_share_a():
        half = block_a.ysend.shape[0]
        return (column_of, me, size, block_a.fin, core * half + pair_index * (half // 2),
                half // 2 // (size // TEAM), block_a.send_g, block_a.recv_g)

    def piece_a(k, mine):
        half = block_a.ysend.shape[0]
        return piece_copy(block_a.fin, core * half, half // 2, half // 2 // column_count, k, mine,
                          block_a.send_p, block_a.recv_p)

    def column_done_a():
        scatter_wait(*column_args_a())
        place, number, _ = column_of(me, size)
        half = block_a.ysend.shape[0]
        piece_rows = half // 2 // number
        value = block_a.acc[part_rows(place * piece_rows, piece_rows), :]
        for other in others(place, number):
            value = value + wide(block_a.column[other])
        at = core * half + pair_index * (half // 2) + place * piece_rows
        block_a.fin[part_rows(at, piece_rows), :] = value.astype(low)
        for copy in share_copies(*column_share_a()):
            copy.start()
        piece_a(column_index, True).start()

    def share_done_a():
        for other in others(column_index, column_count):
            wait_piece(column_share_a(), other)
            piece_a(other, True).start()

    def last_done_a():
        for k in range(column_count):
            piece_a(k, False).wait_recv()
        twin_copy(block_a).start()

    def finish_a():
        for copy in scatter_copies(*column_args_a()):
            copy.wait_send()
        for copy in share_copies(*column_share_a()):
            copy.wait_send()
        for k in range(column_count):
            piece_a(k, True).wait_send()
        twin_copy(block_a).wait()

    def share_args(blk):
        half = blk.ysend.shape[0]
        return (chips_of, me, size, blk.fin, core * half, half // count,
                blk.send_g, blk.recv_g)

    def chips_done(blk):
        scatter_wait(*chips_args(blk))
        half = blk.ysend.shape[0]
        piece = half // count
        value = blk.acc[part_rows(index * piece, piece), :]
        for other in others(index, count):
            value = value + wide(blk.chips[other])
        blk.fin[part_rows(core * half + index * piece, piece), :] = value.astype(low)
        for copy in share_copies(*share_args(blk)):
            copy.start()

    def twin_copy(blk):
        fin = blk.fin
        half = fin.shape[0] // 2
        view = fin.at[part_rows(core * half, half), :]
        return remote(view, view, blk.send_core.at[2], blk.recv_core.at[2], twin)

    def share_done(blk):
        share_wait(*share_args(blk))
        twin_copy(blk).start()

    def finish(blk):
        for copy in scatter_copies(*chips_args(blk)):
            copy.wait_send()
        for copy in share_copies(*share_args(blk)):
            copy.wait_send()
        twin_copy(blk).wait()

    own_q.wait()
    for o in range(1, TEAM):
        q_copy(o).wait_send()
        remote(r.dq.at[rank], r.q_parts.at[mate(rank, o)], r.send_q.at[o], r.recv_q.at[o],
               {"ctx": base + mate(rank, o)}).wait_recv()
    for s in range(seqs):
        one, two = r.q_parts.at[2 * s], r.q_parts.at[2 * s + 1]
        queries = (
            one[:, lane_group(0)],
            mixed_lanes(wide(one[:, lane_group(1)]), half_turn(wide(two[:, lane_group(1)]))),
            two[:, lane_group(0)],
        )
        for g in range(3):
            r.d_cat[s, :, lane_group(6 + g)] = (
                wide(queries[g]) + v.spans[s, :, lane_group(g)]
            ).astype(low)
    for s in range(seqs):
        bias = jnp.sum(wide(r.d_cat[s, :, 2 * width :]), axis=0, keepdims=True)
        for w in range(2):
            small[w, ROW_QUERY_B : ROW_QUERY_B + 1, :] += bias
    query_grad = dot_tn(
        flat_rows(v.x), r.d_cat[:, :, 2 * width :].reshape(seqs * block, width)
    ).astype(low)
    for w in range(2):
        block_a.pack[w, 2 * width : 3 * width, :] = query_grad[w * width : (w + 1) * width, :]
    for k, row in enumerate((ROW_GAIN2, ROW_SHIFT2, ROW_OUTER_B, ROW_GAIN1, ROW_SHIFT1, ROW_OUTPUT_B)):
        for w in range(2):
            small[w, row : row + 1, :] = r.vec[k : k + 1, w * 384 : (w + 1) * 384]
    for w in range(2):
        for k in range(4):
            at = (4 * w + k) * 384
            small[w, ROW_INNER_B + k : ROW_INNER_B + k + 1, :] = r.bias[0:1, at : at + 384]

    upper = lax.rem(rank, 2) == 1
    heads = jnp.sum(wide(r.mine[...]), axis=0, keepdims=True)
    heads = jnp.broadcast_to(heads, (8, width))
    middle, outer_pair = heads[:, lane_group(1)], heads[:, lane_group(2)]
    none = jnp.zeros_like(middle)
    bias = (
        jnp.where(upper, none, outer_pair),
        jnp.where(upper, mixed_lanes(none, middle), mixed_lanes(half_turn(middle), none)),
        jnp.where(upper, outer_pair, none),
    )
    for w in range(2):
        for g in range(3):
            small[w, ROW_VALUE_B : ROW_VALUE_B + 1, lane_group(g)] = bias[g][0:1, :]
    for w in range(2):
        block_a.pack[w, SMALL_AT : SMALL_AT + SMALL_ROWS, :] = small[w].astype(low)
    core_copy(block_a).start()
    core_done(block_a)
    ff_to_share()
    for k in range(TEAM):
        pl.when(k == rank)(kv_copy(k)[0].wait)
        pl.when(k != rank)(kv_copy(k)[1].wait_send)
    for o in range(1, TEAM):
        other = mate(rank, o)
        remote(r.mine.at[block_of(rank), :], r.kv_parts.at[other], r.send_kv.at[rank],
               r.recv_kv.at[other], {"ctx": base + other}).wait_recv()
    for s in range(seqs):
        one, two = r.kv_parts.at[2 * s], r.kv_parts.at[2 * s + 1]
        mid_one, mid_two = wide(one[:, lane_group(1)]), wide(two[:, lane_group(1)])
        r.d_cat[s, :, lane_group(0)] = one[:, lane_group(0)]
        r.d_cat[s, :, lane_group(1)] = mixed_lanes(mid_one, half_turn(mid_two)).astype(low)
        r.d_cat[s, :, lane_group(2)] = two[:, lane_group(0)]
        r.d_cat[s, :, lane_group(3)] = one[:, lane_group(2)]
        r.d_cat[s, :, lane_group(4)] = mixed_lanes(half_turn(mid_one), mid_two).astype(low)
        r.d_cat[s, :, lane_group(5)] = two[:, lane_group(2)]
    grads = r.d_cat[:, :, 0 : 2 * width].reshape(seqs * block, 2 * width)
    for w in range(2):
        piece = dot_tn(
            v.x[:, :, w * width : (w + 1) * width].reshape(seqs * block, width), grads
        ).astype(low)
        for k in range(2):
            block_b.pack[w, k * width : (k + 1) * width, :] = piece[:, k * width : (k + 1) * width]
    core_copy(block_b).start()
    core_done(block_b)
    y_done_a()
    have(fetched.ds, fetched.key, fetched.value, fetched.query)
    def taps_row(j, g):
        return wide(small_ref[(g // 3) * SMALL_IN + j : (g // 3) * SMALL_IN + j + 1,
                              lane_group(g % 3)])

    def depth_strip(c, s):
        start = c * strip
        here = r.seg_col[s, pl.ds(RIM + start, strip), :]
        rows = pl.ds(pl.multiple_of(start, strip), strip)
        sums = [v.ds[s, rows, lane_group(g)] for g in range(groups)]
        for j in range(KERNEL):
            same = r.seg_col[s, pl.ds(RIM + near_taps - j + start, strip), :] == here
            for g in range(groups):
                near = r.dd[s, g, pl.ds(RIM + near_taps - j + start, strip), :]
                sums[g] = sums[g] + jnp.where(same, near, 0.0) * taps_row(j, g)
        for g in range(groups):
            v.ds[s, rows, lane_group(g)] = sums[g]
        return s

    for s in range(seqs):
        lax.fori_loop(0, block // strip, depth_strip, s)
    pair_done_a()
    y_done(block_b)
    ff_to_pair()
    column_done_a()
    for s in range(seqs):
        v.ds[s] += (
            rows_nt(v.queries[s], v.convw[...])
            + rows_nt(r.d_cat[s, :, 0:width], v.key[...])
            + rows_nt(r.d_cat[s, :, width : 2 * width], v.value[...])
            + rows_nt(r.d_cat[s, :, 2 * width :], v.query[...])
        )
    out_copy = pltpu.make_async_copy(v.ds, r.input_grad, r.load.at[1])
    out_copy.start()
    ff_to_twin()
    chips_done(block_b)
    share_done_a()
    last_done_a()
    share_done(block_b)
    finish_a()
    finish(block_b)
    ff_twin().wait()
    for copy in scatter_copies(*column_args):
        copy.wait_send()
    for copy in share_copies(*column_share):
        copy.wait_send()
    for k in range(column_count):
        ff_piece(k, True).wait_send()
    for copy, forward in rims:
        pl.when(me < size - 1 if forward else me > 0)(copy.wait_send)
    for k in range(TEAM - 1):
        pl.when(team < teams - 1)(halo_left(k).wait_send)
        pl.when(team > 0)(halo_right(k).wait_send)
    out_copy.wait()


def padded(rows, unit):
    return -(-rows // unit) * unit


def back(held, window, dq_parts, loaded):
    size = lax.axis_size("ctx")
    unit = 16 * size
    seqs, block, model = loaded["x"].shape
    width = HEADS * HEAD_DIM
    halo = (TEAM - 1) * block
    span = block + 2 * RIM
    chips, column = size // 2, size // TEAM
    low, full = jnp.bfloat16, jnp.float32
    dma = pltpu.SemaphoreType.DMA
    half_ff = loaded["keep"].shape[1]
    outs = dict(
        input_grad=jax.ShapeDtypeStruct((seqs, block, model), full),
        fin_ff=jax.ShapeDtypeStruct((4 * half_ff, width), low),
    )
    scratch = dict(
        mine=pltpu.VMEM((TEAM * block, width), low),
        from_right=pltpu.VMEM((TEAM * block, width), low),
        from_left=pltpu.VMEM((TEAM * block, width), low),
        kv_parts=pltpu.VMEM((TEAM, block, width), low),
        q_parts=pltpu.VMEM((TEAM, block, 2 * LANES), low),
        ff_send=pltpu.VMEM((half_ff, width), low),
        ff_came=pltpu.VMEM((half_ff, width), low),
        ff_column=pltpu.VMEM((column, half_ff // column, width), low),
        spread=pltpu.VMEM((KERNEL, 2 * LANES, width), low),
        sums=pltpu.VMEM((2, SMALL_ROWS, width), full),
        wide=pltpu.VMEM((LANES, block), full),
        tall=pltpu.VMEM((block, LANES), full),
        seg_col=pltpu.VMEM((seqs, held["seg"].shape[1], LANES), full),
        d_ext=pltpu.VMEM((seqs, 3, span, LANES), full),
        dd=pltpu.VMEM((seqs, model // LANES, span, LANES), full),
        d_cat=pltpu.VMEM((seqs, block, 3 * width), low),
        dd_first=pltpu.VMEM((seqs, RIM, model), low),
        dd_last=pltpu.VMEM((seqs, RIM, model), low),
        dd_low=pltpu.VMEM((seqs, RIM, model), low),
        dd_high=pltpu.VMEM((seqs, RIM, model), low),
        rim_first=pltpu.VMEM((seqs, RIM, width), low),
        rim_last=pltpu.VMEM((seqs, RIM, width), low),
        rim_low=pltpu.VMEM((seqs, RIM, width), low),
        rim_high=pltpu.VMEM((seqs, RIM, width), low),
        send_l=dma((TEAM,)), recv_l=dma((TEAM,)), send_r=dma((TEAM,)), recv_r=dma((TEAM,)),
        send_q=dma((TEAM,)), recv_q=dma((TEAM,)), send_kv=dma((TEAM,)), recv_kv=dma((TEAM,)),
        send_h=dma((4,)), recv_h=dma((4,)), send_p=dma((1,)), recv_p=dma((1,)),
        send_c=dma((column,)), recv_c=dma((column,)), send_cg=dma((column,)),
        recv_cg=dma((column,)), send_pg=dma((column + 1,)),
        recv_pg=dma((column + 1,)),
        load=dma((len(loaded) + 1,)),
    )

    def block_scratch(rows):
        rows = padded(rows, unit)
        return dict(
            pack=pltpu.VMEM((2, rows, width), low),
            twin=pltpu.VMEM((2, rows // 2, width), low),
            ysend=pltpu.VMEM((rows // 2, width), low),
            ycame=pltpu.VMEM((rows // 2, width), low),
            acc=pltpu.VMEM((rows // 2, width), full),
            chips=pltpu.VMEM((chips, rows // 2 // chips, width), low),
            fin=pltpu.VMEM((rows, width), low),
            send_s=dma((chips,)), recv_s=dma((chips,)), send_g=dma((chips,)),
            recv_g=dma((chips,)), send_core=dma((4,)), recv_core=dma((4,)),
        )

    a_scratch, b_scratch = block_scratch(PACK_A), block_scratch(PACK_B)
    quarter = padded(PACK_A, unit) // 4
    del a_scratch["chips"]
    a_scratch.update(
        pair=pltpu.VMEM((quarter, width), low),
        column=pltpu.VMEM((column, quarter // column, width), low),
        send_p=dma((column,)), recv_p=dma((column,)),
    )
    del a_scratch["fin"], b_scratch["fin"]
    fin_shapes = [jax.ShapeDtypeStruct((padded(n, unit), width), low) for n in (PACK_A, PACK_B)]
    vmem = pl.BlockSpec(memory_space=pltpu.VMEM)
    anywhere = pl.BlockSpec(memory_space=pl.ANY)
    names = tuple(held) + ("window", "dq") + tuple(outs) + tuple(scratch)
    total_in = len(held) + 2
    fetch_count = len(loaded)

    def kernel(*refs):
        ins, loads = refs[:total_in], refs[total_in : total_in + fetch_count]
        at = total_in + fetch_count
        results = refs[at : at + len(outs)]
        fin_a, fin_b = refs[at + len(outs) : at + len(outs) + 2]
        late = refs[at + len(outs) + 2 :]
        first, late = late[: len(scratch)], late[len(scratch) :]
        a_refs, late = late[: len(a_scratch)], late[len(a_scratch) :]
        b_refs, holds = late[: len(b_scratch)], late[len(b_scratch) :]
        back_kernel(
            names, tuple(a_scratch) + ("fin",), tuple(b_scratch) + ("fin",), tuple(loaded),
            *ins, *results, *first, *a_refs, fin_a, *b_refs, fin_b, *loads, *holds,
        )

    holds = [pltpu.VMEM(a.shape, a.dtype) for a in loaded.values()]
    return pl.pallas_call(
        kernel,
        out_shape=list(outs.values()) + fin_shapes,
        in_specs=[vmem] * len(held) + [anywhere] * (2 + len(loaded)),
        out_specs=[anywhere] * 2 + [vmem] * 2,
        scratch_shapes=list(scratch.values()) + list(a_scratch.values())
        + list(b_scratch.values()) + holds,
        compiler_params=pltpu.CompilerParams(
            collective_id=5, has_side_effects=True, vmem_limit_bytes=65400 * 2**10
        ),
        name="back",
    )(*held.values(), window, dq_parts, *loaded.values())


STEP = 256
FF_CHUNK = 512
PACK_FF = 3840


def gelu_pair(value):
    share = 0.5 + 0.5 * lax.erf(value * 0.7071067811865476)
    bell = jnp.exp(-0.5 * value * value)
    return value * share, share + value * bell * 0.3989422804014327


def fold_rows(block):
    return jnp.sum(block.reshape(block.shape[0] // 8, 8, block.shape[1]), axis=0)


def norm_parts(value):
    center = value - jnp.mean(value, axis=-1, keepdims=True)
    spread = jnp.mean(center * center, axis=-1, keepdims=True)
    scale = lax.rsqrt(spread + 1e-05)
    return center * scale, scale


def norm_back(grad, unit, scale):
    return scale * (
        grad
        - jnp.mean(grad, axis=-1, keepdims=True)
        - unit * jnp.mean(grad * unit, axis=-1, keepdims=True)
    )


def middle_kernel(att_ref, conv_ref, x_ref, small_ref, og_any, ow_any, iw_any, uw_any, uw_came,
                  out_any, ds_any, dc_any, team_ref, keep_ref, xsend_ref, vec_ref, bias_ref,
                  og_ref, ow_ref, iw_ref, uw_ref, out_ref, ds_ref, dc_ref,
                  pack_ref, twin_ref, pieces, parts, joined_ref, low_ref, act_ref, slope_ref, do_ref, di_ref, db_ref,
                  sums_ref, wide_sums, send_a, recv_a, send_g, recv_g, send_t, recv_t, load, store):
    me = lax.axis_index("ctx")
    rank = lax.rem(me, TEAM)
    base = me - rank
    seqs, block, model = x_ref.shape
    width = HEADS * HEAD_DIM
    greet([{"ctx": base + mate(rank, o)} for o in range(1, TEAM)])

    def piece_copy(r):
        return (
            pltpu.make_async_copy(att_ref.at[r], pieces.at[rank], recv_a.at[rank]),
            remote(att_ref.at[r], pieces.at[rank], send_a.at[r], recv_a.at[rank],
                   {"ctx": base + r}),
        )

    def team_copy(r):
        return (
            pltpu.make_async_copy(parts.at[r], team_ref.at[rank], recv_g.at[rank]),
            remote(parts.at[r], team_ref.at[rank], send_g.at[r], recv_g.at[rank],
                   {"ctx": base + r}),
        )

    core, side = lax.rem(me, 2), lax.axis_index("wsh")
    for o in (1, 3, 2):
        piece_copy(mate(rank, o))[1].start()
    piece_copy(rank)[0].start()
    rows_in = uw_came.shape[1]
    came_at = part_rows((1 - side) * (2 * rows_in) + core * rows_in, rows_in)
    loads = [
        pltpu.make_async_copy(ow_any, ow_ref, load.at[0]),
        pltpu.make_async_copy(iw_any, iw_ref, load.at[1]),
        pltpu.make_async_copy(
            uw_any, uw_ref.at[:, part_rows(side * (2 * rows_in), 2 * rows_in), :], load.at[2]
        ),
        pltpu.make_async_copy(uw_came, uw_ref.at[:, came_at, :], load.at[3]),
        pltpu.make_async_copy(og_any, og_ref, load.at[4]),
    ]
    for copy in loads:
        copy.start()
    outer_twin = remote(uw_came, uw_ref.at[:, came_at, :], send_t.at[1], recv_t.at[1],
                        {"ctx": flip(me, 1)})
    outer_twin.start()
    sums_ref[...] = jnp.zeros_like(sums_ref)
    wide_sums[...] = jnp.zeros_like(wide_sums)
    own = lax.div(rank, 2)
    steps = block // STEP

    def row(index):
        return jnp.concatenate(
            [small_ref[index : index + 1, :], small_ref[SMALL_IN + index : SMALL_IN + index + 1, :]],
            axis=1,
        ).astype(jnp.float32)

    def body(i, carry):
        s = lax.rem(own + lax.div(i, steps), seqs)
        start = pl.multiple_of(lax.rem(i, steps) * STEP, STEP)
        rows = pl.ds(start, STEP)
        flat = pl.ds(pl.multiple_of(s * block + start, STEP), STEP)

        @pl.when(i == 0)
        def _():
            piece_copy(rank)[0].wait()
            remote(att_ref.at[rank], pieces.at[mate(rank, 1)], send_a.at[rank],
                   recv_a.at[mate(rank, 1)], {"ctx": base + mate(rank, 1)}).wait_recv()
            for copy in loads:
                copy.wait()
            outer_twin.wait()

        @pl.when(i == steps)
        def _():
            for o in (2, 3):
                remote(att_ref.at[rank], pieces.at[mate(rank, o)], send_a.at[rank],
                       recv_a.at[mate(rank, o)], {"ctx": base + mate(rank, o)}).wait_recv()

        first, second = pieces.at[2 * s], pieces.at[2 * s + 1]
        joined_ref[flat, lane_group(0)] = first[rows, lane_group(0)]
        joined_ref[flat, lane_group(1)] = mixed_lanes(
            first[rows, lane_group(1)].astype(jnp.float32),
            half_turn(second[rows, lane_group(1)].astype(jnp.float32)),
        ).astype(jnp.bfloat16)
        joined_ref[flat, lane_group(2)] = second[rows, lane_group(0)]
        joined_ref[flat, width:] = conv_ref[s, rows, :]
        branch = dot(joined_ref[flat, :], ow_ref[...]) + row(ROW_OUTPUT_B)
        unit1, scale1 = norm_parts(branch + x_ref[s, rows, :].astype(jnp.float32))
        gain1 = row(ROW_GAIN1)
        normed = unit1 * gain1 + row(ROW_SHIFT1)
        low_ref[flat, :] = normed.astype(jnp.bfloat16)
        outer = []
        part = model // GROUPS
        hidden = iw_ref.shape[2]
        for g in range(GROUPS):
            cols = slice(g * part, (g + 1) * part)
            for c in range(hidden // FF_CHUNK):
                span = slice(g * hidden + c * FF_CHUNK, g * hidden + (c + 1) * FF_CHUNK)
                near = slice(c * FF_CHUNK, (c + 1) * FF_CHUNK)
                bias = jnp.concatenate(
                    [
                        small_ref[
                            g * SMALL_IN + ROW_INNER_B + k // 3 : g * SMALL_IN + ROW_INNER_B + k // 3 + 1,
                            lane_group(k % 3),
                        ]
                        for k in range(c * FF_CHUNK // LANES, (c + 1) * FF_CHUNK // LANES)
                    ],
                    axis=1,
                ).astype(jnp.float32)
                inner = dot(low_ref[flat, cols], iw_ref[g, :, near]) + bias
                active, slope = gelu_pair(inner)
                act_ref[flat, span] = active.astype(jnp.bfloat16)
                slope_ref[:, span] = slope
            outer.append(dot(act_ref[flat, g * hidden : (g + 1) * hidden], uw_ref[g]))
        summed = jnp.concatenate(outer, axis=1) + row(ROW_OUTER_B) + normed
        unit2, scale2 = norm_parts(summed)
        gain2 = row(ROW_GAIN2)
        out_ref[s, rows, :] = (unit2 * gain2 + row(ROW_SHIFT2)).astype(jnp.bfloat16)
        grad = og_ref[s, rows, :].astype(jnp.float32)
        sums_ref[0] += fold_rows(grad * unit2)
        sums_ref[1] += fold_rows(grad)
        d_sum2 = norm_back(grad * gain2, unit2, scale2)
        d_outer = d_sum2.astype(jnp.bfloat16)
        do_ref[flat, :] = d_outer
        sums_ref[2] += fold_rows(d_outer.astype(jnp.float32))
        back = []
        for g in range(GROUPS):
            cols = slice(g * part, (g + 1) * part)
            for c in range(hidden // FF_CHUNK):
                span = slice(g * hidden + c * FF_CHUNK, g * hidden + (c + 1) * FF_CHUNK)
                near = slice(c * FF_CHUNK, (c + 1) * FF_CHUNK)
                d_inner = (
                    rows_nt(do_ref[flat, cols], uw_ref[g, near, :]) * slope_ref[:, span]
                ).astype(jnp.bfloat16)
                di_ref[flat, span] = d_inner
                wide_sums[:, span] += fold_rows(d_inner.astype(jnp.float32))
            back.append(rows_nt(di_ref[flat, g * hidden : (g + 1) * hidden], iw_ref[g]))
        d_normed = d_sum2 + jnp.concatenate(back, axis=1)
        sums_ref[3] += fold_rows(d_normed * unit1)
        sums_ref[4] += fold_rows(d_normed)
        d_sum1 = norm_back(d_normed * gain1, unit1, scale1)
        ds_ref[s, rows, :] = d_sum1
        d_branch = d_sum1.astype(jnp.bfloat16)
        db_ref[flat, :] = d_branch
        sums_ref[5] += fold_rows(d_branch.astype(jnp.float32))
        d_joined = rows_nt(d_branch, ow_ref[...])
        dc_ref[s, rows, :] = d_joined[:, width:].astype(jnp.bfloat16)
        parts[2 * s, rows, lane_group(0)] = d_joined[:, lane_group(0)].astype(jnp.bfloat16)
        parts[2 * s, rows, lane_group(1)] = half_turn(d_joined[:, lane_group(1)]).astype(
            jnp.bfloat16
        )
        parts[2 * s + 1, rows, lane_group(0)] = d_joined[:, lane_group(2)].astype(jnp.bfloat16)
        parts[2 * s + 1, rows, lane_group(1)] = d_joined[:, lane_group(1)].astype(jnp.bfloat16)

        @pl.when(i == steps - 1)
        def _():
            team_copy(rank)[0].start()
            team_copy(mate(rank, 1))[1].start()

        @pl.when(i == 2 * steps - 1)
        def _():
            team_copy(mate(rank, 2))[1].start()
            team_copy(mate(rank, 3))[1].start()

        return carry

    lax.fori_loop(0, seqs * steps, body, 0)
    stores = [
        pltpu.make_async_copy(out_ref, out_any, store.at[0]),
        pltpu.make_async_copy(ds_ref, ds_any, store.at[1]),
        pltpu.make_async_copy(dc_ref, dc_any, store.at[2]),
    ]
    for copy in stores:
        copy.start()

    half = width
    part = model // GROUPS
    hidden = iw_ref.shape[2]
    half_ff = pack_ref.shape[1] // 2
    early = half + part // 2 * (hidden // half)

    def exchange(at, rows, sem):
        return remote(
            pack_ref.at[:, part_rows((1 - core) * half_ff + at, rows), :],
            twin_ref.at[:, pl.ds(at, rows), :], send_t.at[sem], recv_t.at[sem],
            {"ctx": flip(me, 1)},
        )

    for w in range(2):
        for k in range(2):
            pack_ref[w, pl.ds(k * half_ff, half), :] = dot_tn(
                joined_ref[:, w * half : (w + 1) * half], db_ref[:, k * half : (k + 1) * half]
            ).astype(jnp.bfloat16)
    for g in range(GROUPS):
        for k in range(hidden // half):
            grads = dot_tn(
                low_ref[:, g * part : (g + 1) * part],
                di_ref[:, g * hidden + k * half : g * hidden + (k + 1) * half],
            ).astype(jnp.bfloat16)
            for w in range(2):
                pack_ref[w, pl.ds(g * half_ff + half + k * (part // 2), part // 2), :] = grads[
                    w * (part // 2) : (w + 1) * (part // 2), :
                ]
    exchange(0, early, 0).start()
    for g in range(GROUPS):
        for k in range(hidden // half):
            w, lower = k // 2, k % 2
            grads = dot_tn(
                act_ref[:, g * hidden + k * half : g * hidden + (k + 1) * half],
                do_ref[:, g * part : (g + 1) * part],
            ).astype(jnp.bfloat16)
            pack_ref[w, pl.ds(g * half_ff + early + lower * half, half), :] = grads
    exchange(early, half_ff - early, 2).start()
    for k in range(6):
        vec_ref[k : k + 1, :] = jnp.sum(sums_ref[k], axis=0, keepdims=True)
    vec_ref[6:, :] = jnp.zeros((2, model), jnp.float32)
    bias_ref[...] = jnp.broadcast_to(jnp.sum(wide_sums[...], axis=0, keepdims=True), bias_ref.shape)

    exchange(0, early, 0).wait()
    exchange(early, half_ff - early, 2).wait()
    pair_index, _, _ = pair_of(me, lax.axis_size("ctx"))
    quarter = half_ff // 2

    def add(at, n):
        here = part_rows(at, n)
        keep, give = pair_index * quarter, (1 - pair_index) * quarter
        for w in range(2):
            xsend_ref[w, here, :] = (
                wide(pack_ref[w, part_rows(core * half_ff + give + at, n), :])
                + wide(twin_ref[w, part_rows(give + at, n), :])
            ).astype(jnp.bfloat16)
            keep_ref[w, here, :] = wide(
                pack_ref[w, part_rows(core * half_ff + keep + at, n), :]
            ) + wide(twin_ref[w, part_rows(keep + at, n), :])

    in_chunks(quarter, add)
    team_copy(rank)[0].wait()
    for o in range(1, TEAM):
        other = mate(rank, o)
        piece_copy(other)[1].wait_send()
        team_copy(other)[1].wait_send()
        remote(parts.at[rank], team_ref.at[other], send_g.at[rank], recv_g.at[other],
               {"ctx": base + other}).wait_recv()
    for copy in stores:
        copy.wait()


def middle(attended, convolved, hidden, small, out_grad, output_w, inner_w, outer_w, outer_came):
    seqs, block, model = hidden.shape
    rows = seqs * block
    width = convolved.shape[2]
    inner = GROUPS * inner_w.shape[2]
    pack_rows = padded(PACK_FF, 16 * lax.axis_size("ctx"))
    vmem = pl.BlockSpec(memory_space=pltpu.VMEM)
    anywhere = pl.BlockSpec(memory_space=pl.ANY)
    low, full = jnp.bfloat16, jnp.float32
    dma = pltpu.SemaphoreType.DMA
    return pl.pallas_call(
        middle_kernel,
        out_shape=[
            jax.ShapeDtypeStruct((seqs, block, model), low),
            jax.ShapeDtypeStruct((seqs, block, model), full),
            jax.ShapeDtypeStruct((seqs, block, width), low),
            jax.ShapeDtypeStruct((TEAM, block, 2 * LANES), low),
            jax.ShapeDtypeStruct((2, pack_rows // 4, width), full),
            jax.ShapeDtypeStruct((2, pack_rows // 4, width), low),
            jax.ShapeDtypeStruct((8, model), full),
            jax.ShapeDtypeStruct((8, inner), full),
        ],
        in_specs=[anywhere] + [vmem] * 3 + [anywhere] * 5,
        out_specs=[anywhere] * 4 + [vmem] * 4,
        scratch_shapes=[
            pltpu.VMEM((seqs, block, model), low),
            pltpu.VMEM(output_w.shape, low),
            pltpu.VMEM(inner_w.shape, low),
            pltpu.VMEM((GROUPS, 2 * outer_w.shape[1], outer_w.shape[2]), low),
            pltpu.VMEM((seqs, block, model), low),
            pltpu.VMEM((seqs, block, model), full),
            pltpu.VMEM((seqs, block, width), low),
            pltpu.VMEM((2, pack_rows, width), low),
            pltpu.VMEM((2, pack_rows // 2, width), low),
            pltpu.VMEM((TEAM, block, 2 * LANES), low),
            pltpu.VMEM((TEAM, block, 2 * LANES), low),
            pltpu.VMEM((rows, model), low),
            pltpu.VMEM((rows, model), low),
            pltpu.VMEM((rows, inner), low),
            pltpu.VMEM((STEP, inner), full),
            pltpu.VMEM((rows, model), low),
            pltpu.VMEM((rows, inner), low),
            pltpu.VMEM((rows, model), low),
            pltpu.VMEM((6, 8, model), full),
            pltpu.VMEM((8, inner), full),
            dma((TEAM,)), dma((TEAM,)), dma((TEAM,)), dma((TEAM,)), dma((3,)), dma((3,)),
            dma((5,)), dma((3,)),
        ],
        compiler_params=pltpu.CompilerParams(
            collective_id=2, has_side_effects=True, vmem_limit_bytes=63 * 2**20
        ),
        name="middle",
    )(attended, convolved, hidden, small, out_grad, output_w, inner_w, outer_w, outer_came)


def finish_kernel(side_ref, ff_any, a_any, b_any, grad_any, out_any,
                  grad_out, out_out, query_out, key_out, value_out, point_out, conv_out,
                  output_out, inner_out, outer_out, depth_out, kernel_out, query_b, value_b, point_b, conv_b,
                  output_b, gain1, shift1, outer_b, gain2, shift2, inner_b, kernel_b,
                  ff, a, b, grad, out, wide_a, wide_b, wide_output, wide_inner, wide_outer,
                  load, store):
    width = HEADS * HEAD_DIM
    loads = [
        pltpu.make_async_copy(a_any.at[pl.ds(0, a.shape[0]), :], a, load.at[0]),
        pltpu.make_async_copy(b_any.at[pl.ds(0, b.shape[0]), :], b, load.at[1]),
        pltpu.make_async_copy(ff_any.at[pl.ds(0, ff.shape[0]), :], ff, load.at[2]),
        pltpu.make_async_copy(grad_any, grad, load.at[3]),
        pltpu.make_async_copy(out_any, out, load.at[4]),
    ]
    for copy in loads:
        copy.start()
    stores = []

    def put(src, dst):
        copy = pltpu.make_async_copy(src, dst, store.at[len(stores)])
        copy.start()
        stores.append(copy)

    loads[0].wait()
    for k, place in enumerate((point_out, conv_out, query_out)):
        rows = pl.ds(k * width, width)
        wide_a[rows, :] = a[rows, :].astype(jnp.float32)
        put(wide_a.at[rows, :], place)
    small = a[pl.ds(SMALL_AT, SMALL_ROWS), :].astype(jnp.float32)
    depth_out[...] = small[0:KERNEL, :]
    first = side_ref[0] == 0
    for ref, row in ((output_b, ROW_OUTPUT_B), (gain1, ROW_GAIN1), (shift1, ROW_SHIFT1),
                     (outer_b, ROW_OUTER_B), (gain2, ROW_GAIN2), (shift2, ROW_SHIFT2)):
        ref[...] = small[row : row + 1, :].reshape(width)
    inner_b[...] = jnp.concatenate(
        [small[ROW_INNER_B + k : ROW_INNER_B + k + 1, :] for k in range(4)], axis=1
    ).reshape(4 * width)
    block = small[16:24, :]
    turned = jnp.where(first, block, pltpu.roll(block, 192, axis=1))
    for ref, row in ((query_b, ROW_QUERY_B), (value_b, ROW_VALUE_B), (point_b, ROW_POINT_B),
                     (conv_b, ROW_CONV_B)):
        ref[...] = turned[row - 16 : row - 15, 0:192].reshape(192)
    taps = small[ROW_KERNEL_W : ROW_KERNEL_W + TAP_ROWS, :]
    half = jnp.where(first, taps, pltpu.roll(taps, 192, axis=1))[:, 0:192]
    pick = jnp.where(tap_major((TAP_ROWS, HEADS * KERNEL), 0), 1.0, 0.0)
    kernel_out[...] = dot_tn(pick.astype(jnp.bfloat16), half.astype(jnp.bfloat16))
    lanes = small[ROW_KERNEL_B : ROW_KERNEL_B + 24, :]
    column = jnp.concatenate([lanes[:, lane_group(g)] for g in range(3)], axis=0)
    wide_pick = jnp.where(
        first,
        jnp.where(tap_major((TAP_ROWS, LANES), 0), 1.0, 0.0),
        jnp.where(tap_major((TAP_ROWS, LANES), HEADS * KERNEL // 2), 1.0, 0.0),
    )
    count = HEADS * KERNEL // 2
    kernel_b[...] = jnp.sum(column * wide_pick, axis=0, keepdims=True)[:, 0:count].reshape(count)
    loads[1].wait()
    for k, place in enumerate((key_out, value_out)):
        rows = pl.ds(k * width, width)
        wide_b[rows, :] = b[rows, :].astype(jnp.float32)
        put(wide_b.at[rows, :], place)
    loads[2].wait()
    half_ff = ff.shape[0] // 2
    count = inner_out.shape[1]
    blocks = inner_out.shape[2] // width
    rows = outer_out.shape[1]
    for g in range(GROUPS):
        cols = slice(g * width, (g + 1) * width)
        wide_output[:, cols] = ff[pl.ds(g * half_ff, width), :].astype(jnp.float32)
        for k in range(blocks):
            at = g * half_ff + width + k * count
            wide_inner[g, :, k * width : (k + 1) * width] = ff[pl.ds(at, count), :].astype(
                jnp.float32
            )
        wide_outer[g] = ff[pl.ds(g * half_ff + width + blocks * count, rows), :].astype(
            jnp.float32
        )
    put(wide_output, output_out)
    put(wide_inner, inner_out)
    put(wide_outer, outer_out)
    loads[3].wait()
    put(grad, grad_out)
    loads[4].wait()
    put(out, out_out)
    for copy in stores:
        copy.wait()


def finish(side, fin_ff, fin_a, fin_b, grad_input, output, inner_shape, outer_shape):
    width = HEADS * HEAD_DIM
    full, low = jnp.float32, jnp.bfloat16
    anywhere = pl.BlockSpec(memory_space=pl.ANY)
    vmem = pl.BlockSpec(memory_space=pltpu.VMEM)
    square = jax.ShapeDtypeStruct((width, width), full)
    lengths = [width // 2] * 4 + [width] * 6 + [4 * width, HEADS * KERNEL // 2]
    return pl.pallas_call(
        finish_kernel,
        out_shape=[
            jax.ShapeDtypeStruct(grad_input.shape, full),
            jax.ShapeDtypeStruct(output.shape, low),
            square, square, square, square, square,
            jax.ShapeDtypeStruct((width, 2 * width), full),
            jax.ShapeDtypeStruct(inner_shape, full),
            jax.ShapeDtypeStruct(outer_shape, full),
            jax.ShapeDtypeStruct((KERNEL, width), full),
            jax.ShapeDtypeStruct((HEADS * KERNEL, width // 2), full),
        ] + [jax.ShapeDtypeStruct((n,), full) for n in lengths],
        in_specs=[pl.BlockSpec(memory_space=pltpu.SMEM)] + [anywhere] * 5,
        out_specs=[anywhere] * 10 + [vmem] * 14,
        scratch_shapes=[
            pltpu.VMEM(fin_ff.shape, low),
            pltpu.VMEM((PACK_A, width), low),
            pltpu.VMEM((PACK_B, width), low),
            pltpu.VMEM(grad_input.shape, full),
            pltpu.VMEM(output.shape, low),
            pltpu.VMEM((SMALL_AT, width), full),
            pltpu.VMEM((PACK_B, width), full),
            pltpu.VMEM((width, 2 * width), full),
            pltpu.VMEM(inner_shape, full),
            pltpu.VMEM(outer_shape, full),
            pltpu.SemaphoreType.DMA((5,)),
            pltpu.SemaphoreType.DMA((10,)),
        ],
        compiler_params=pltpu.CompilerParams(vmem_limit_bytes=60 * 2**20),
        name="finish",
    )(side, fin_ff, fin_a, fin_b, grad_input, output)


def on_device(
    hidden_in,
    segment_ids,
    out_grad,
    query_w,
    query_b,
    key_w,
    value_w,
    value_b,
    depth_kernel,
    point_w,
    point_b,
    kernel_w,
    kernel_b,
    conv_w,
    conv_b,
    output_w,
    output_b,
    norm1_gain,
    norm1_bias,
    inner_w,
    inner_b,
    outer_w,
    outer_b,
    norm2_gain,
    norm2_bias,
):
    micro_count, seq_local, block_len, model_width = hidden_in.shape
    seq_count = micro_count * seq_local
    att_width = HEADS * HEAD_DIM
    half_taps = KERNEL // 2
    position = lax.axis_index("ctx")
    seg_rows = segment_ids.reshape(seq_count, segment_ids.shape[2])
    pad_rows = (TEAM - 1) * block_len
    seg_pad = jnp.pad(seg_rows, ((0, 0), (pad_rows, pad_rows)), constant_values=-1)
    own_seg = lax.dynamic_slice_in_dim(seg_pad, position * block_len + pad_rows, block_len, 1)
    rank = lax.rem(position, TEAM)
    first_key = (position - rank) * block_len
    team_seg = lax.dynamic_slice(
        seg_pad, (lax.div(rank, 2), first_key), (1, (3 * TEAM - 2) * block_len)
    )
    key_place = first_key - pad_rows + lax.broadcasted_iota(jnp.int32, team_seg.shape, 1)
    team_seg = jnp.where(key_place >= seg_rows.shape[1], 2**24, team_seg)
    query_seg = team_seg[:, pad_rows : pad_rows + TEAM * block_len]
    lows = query_seg[0, ::TILE]
    highs = query_seg[0, TILE - 1 :: TILE]
    before = jnp.sum(team_seg < lows[:, None], axis=1, dtype=jnp.int32)
    through = jnp.sum(team_seg <= highs[:, None], axis=1, dtype=jnp.int32)
    bounds = jnp.stack([before // TILE, (through + TILE - 1) // TILE])
    seg_keys = team_seg.astype(jnp.float32)
    seg_queries = query_seg.astype(jnp.float32)
    rim_seg = lax.dynamic_slice_in_dim(
        seg_pad, position * block_len + pad_rows - RIM, block_len + 2 * RIM, 1
    )
    tap_mask = jnp.stack(
        [
            rim_seg[:, RIM - half_taps + j : RIM - half_taps + j + block_len] == own_seg
            for j in range(KERNEL)
        ],
        axis=1,
    ).astype(jnp.float32)
    seg_rim = jnp.pad(
        rim_seg.astype(jnp.float32), ((0, 0), (0, -rim_seg.shape[1] % LANES)), constant_values=-1
    )
    side = lax.axis_index("wsh")
    tap_rows = jnp.pad(tap_mask, ((0, 0), (0, 16 - KERNEL), (0, 0)))
    hidden = hidden_in.reshape(seq_count, block_len, model_width)
    (key_mat, value_mat, small_full, query_mat, point_mat, conv_mat, output_mat, inner_mat,
     window, query_team, queries, xrim, depth_low, span_keys, kern, ext, convolved,
     outer_half) = front(
        hidden, seg_rim, tap_rows, depth_kernel, kernel_w.T, kernel_b,
        [output_b, norm1_gain, norm1_bias, outer_b, norm2_gain, norm2_bias, inner_b],
        [query_b, value_b, point_b, conv_b],
        [key_w, value_w, query_w, point_w, conv_w, output_w, inner_w], outer_w,
    )
    outer_came = lax.ppermute(outer_half, "wsh", [(0, 1), (1, 0)])
    query_team = query_team.reshape(TEAM * block_len, 2 * LANES)
    attended_team, attended_t, log_sums = attend(
        bounds, query_team, window, seg_keys, seg_queries
    )
    (output, grad_sum1, grad_conv, grad_team, keep, xsend, vec_grads, bias_grads) = middle(
        attended_team.reshape(TEAM, block_len, -1), convolved, hidden, small_full,
        out_grad.reshape(seq_count, block_len, model_width),
        output_mat, inner_mat, outer_w, outer_came,
    )
    came = lax.ppermute(xsend, "ctx", [(i, i ^ 2) for i in range(lax.axis_size("ctx"))])
    grad_query_team, grad_window = attend_back(
        bounds, query_team, window, seg_keys, seg_queries,
        grad_team.reshape(TEAM * block_len, 2 * LANES), attended_t, log_sums,
    )
    grad_input, fin_ff, fin_a, fin_b = back(
        dict(seg=seg_rim, mask=tap_rows, small=small_full, vec=vec_grads, bias=bias_grads),
        grad_window, grad_query_team.reshape(TEAM, block_len, -1),
        dict(keep=keep, came=came, dconv=grad_conv, ext=ext, kern=kern, point=point_mat,
             queries=queries, spans=span_keys, depth=depth_low, xrim=xrim, x=hidden,
             convw=conv_mat, ds=grad_sum1, key=key_mat, value=value_mat, query=query_mat),
    )
    (grad_input, output, grad_query, grad_key, grad_value, grad_point, grad_conv, grad_output,
     grad_inner, grad_outer, grad_depth, grad_kernel, g_query_b, g_value_b, g_point_b, g_conv_b,
     g_output_b, gain1, shift1, g_outer_b, gain2, shift2, g_inner_b, g_kernel_b) = finish(
        side.astype(jnp.int32).reshape(1), fin_ff, fin_a, fin_b, grad_input, output,
        inner_w.shape, outer_w.shape,
    )
    return (
        output.reshape(hidden_in.shape), grad_input.reshape(hidden_in.shape),
        grad_query, g_query_b, grad_key, grad_value, g_value_b, grad_depth, grad_point,
        g_point_b, grad_kernel.T, g_kernel_b, grad_conv, g_conv_b, grad_output, g_output_b,
        gain1, shift1, grad_inner, g_inner_b, grad_outer, g_outer_b, gain2, shift2,
    )


def solution(mesh):
    in_specs = (
        P(None, "wsh", "ctx", None),
        P(None, "wsh", None),
        P(None, "wsh", "ctx", None),
        P("wsh", None),
        P("wsh"),
        P("wsh", None),
        P("wsh", None),
        P("wsh"),
        P(None, "wsh"),
        P("wsh", None),
        P("wsh"),
        P("wsh", None),
        P("wsh"),
        P("wsh", None),
        P("wsh"),
        P("wsh", None),
        P("wsh"),
        P("wsh"),
        P("wsh"),
        P(None, "wsh", None),
        P("wsh"),
        P(None, "wsh", None),
        P("wsh"),
        P("wsh"),
        P("wsh"),
    )
    out_specs = (
        P(None, "wsh", "ctx", None),
        P(None, "wsh", "ctx", None),
        P("wsh", None),
        P("wsh"),
        P("wsh", None),
        P("wsh", None),
        P("wsh"),
        P(None, "wsh"),
        P("wsh", None),
        P("wsh"),
        P("wsh", None),
        P("wsh"),
        P("wsh", None),
        P("wsh"),
        P("wsh", None),
        P("wsh"),
        P("wsh"),
        P("wsh"),
        P(None, "wsh", None),
        P("wsh"),
        P(None, "wsh", None),
        P("wsh"),
        P("wsh"),
        P("wsh"),
    )
    return jax.shard_map(
        on_device, mesh=mesh, in_specs=in_specs, out_specs=out_specs, check_vma=False
    )
```

```python
import functools
import types

import jax
import jax.numpy as jnp
from jax import lax
from jax.experimental import pallas as pl
from jax.experimental.pallas import tpu as pltpu
from jax.sharding import PartitionSpec as P

HEADS = 6
HEAD_DIM = 64
KERNEL = 9
GROUPS = 2


TILE = 256
NEG = -1000000000.0
LANES = 128
HEADS_HERE = HEADS // 2


def rows_nt(left, right):
    return lax.dot_general(
        left, right, (((1,), (1,)), ((), ())), preferred_element_type=jnp.float32
    )


def lane_half(block, upper):
    lane = lax.broadcasted_iota(jnp.int32, block.shape, 1)
    keep = lane >= HEAD_DIM if upper else lane < HEAD_DIM
    return jnp.where(keep, block, jnp.zeros_like(block))


def same_document(segk_ref, segq_ref, rows):
    row = segk_ref[0:1, rows]
    column = jnp.broadcast_to(row, (LANES, row.shape[1])).T
    wide = jnp.concatenate([column] * (TILE // LANES), axis=1)
    return wide == segq_ref[0:1, :]


def load_queries(q_ref, qm_ref):
    scale = jnp.asarray(HEAD_DIM ** (-0.5), q_ref.dtype)
    first = q_ref[:, 0:LANES] * scale
    qm_ref[0] = lane_half(first, False)
    qm_ref[1] = lane_half(first, True)
    qm_ref[2] = lane_half(q_ref[:, LANES : 2 * LANES] * scale, False)


KEY_GROUP = (0, 0, 1)
VALUE_GROUP = (2, 2, 1)


def lane_group(group):
    return slice(group * LANES, (group + 1) * LANES)


def over_tiles(first, last, step):
    sixes = lax.div(last - first, 6)

    def six(p, carry):
        step(first + 6 * p, 6)
        return carry

    lax.fori_loop(0, sixes, six, 0)
    rest = last - first - 6 * sixes
    at = first + 6 * sixes

    @pl.when(rest >= 4)
    def _():
        step(at, 4)

    @pl.when((rest == 2) | (rest == 3))
    def _():
        step(at, 2)

    @pl.when(lax.rem(rest, 2) == 1)
    def _():
        step(last - 1, 1)


def attend_kernel(bounds, q_ref, kv_ref, segk_ref, segq_ref, out_ref, outt_ref, lse_ref,
                  qm_ref, m_ref, l_ref, acc_ref):
    tile = pl.program_id(0)
    load_queries(q_ref, qm_ref)
    m_ref[...] = jnp.full_like(m_ref, -jnp.inf)
    l_ref[...] = jnp.zeros_like(l_ref)
    acc_ref[...] = jnp.zeros_like(acc_ref)

    def step(j, tiles):
        rows = pl.ds(pl.multiple_of(j * TILE, TILE), tiles * TILE)
        same = same_document(segk_ref, segq_ref, rows)
        values_t = kv_ref[rows, LANES : 3 * LANES].T
        value_rows = (2 * HEAD_DIM, 3 * HEAD_DIM, HEAD_DIM)
        raw = [
            rows_nt(kv_ref[rows, lane_group(KEY_GROUP[head])], qm_ref[head])
            for head in range(HEADS_HERE)
        ]
        highs, alphas = [], []
        for head in range(HEADS_HERE):
            scores = jnp.where(same, raw[head], NEG)
            old = m_ref[head : head + 1, :]
            top = jnp.maximum(old, jnp.max(scores, axis=0, keepdims=True))
            expo = jnp.exp(scores - top)
            alpha = jnp.exp(old - top)
            m_ref[head : head + 1, :] = top
            l_ref[head : head + 1, :] = l_ref[head : head + 1, :] * alpha + jnp.sum(
                expo, axis=0, keepdims=True
            )
            high = expo.astype(jnp.bfloat16)
            highs.append(high)
            alphas.append(alpha)
        for head in range(HEADS_HERE):
            span = slice(head * HEAD_DIM, (head + 1) * HEAD_DIM)
            vals = values_t[value_rows[head] : value_rows[head] + HEAD_DIM, :]
            acc_ref[span, :] = acc_ref[span, :] * alphas[head] + jnp.dot(
                vals, highs[head], preferred_element_type=jnp.float32
            )

    over_tiles(bounds[0, tile], bounds[1, tile], step)
    lse_ref[...] = m_ref[...] + jnp.log(l_ref[...])
    used = HEADS_HERE * HEAD_DIM
    for head in range(HEADS_HERE):
        span = slice(head * HEAD_DIM, (head + 1) * HEAD_DIM)
        inv = 1.0 / l_ref[head : head + 1, :]
        acc_ref[span, :] = acc_ref[span, :] * inv
    outt_ref[...] = acc_ref[...]
    out_ref[...] = acc_ref[...].T.astype(jnp.bfloat16)


def attend(bounds, queries, window, seg_keys, seg_queries):
    rows, wide = queries.shape
    span, width = window.shape
    return pl.pallas_call(
        attend_kernel,
        grid_spec=pltpu.PrefetchScalarGridSpec(
            num_scalar_prefetch=1,
            grid=(rows // TILE,),
            in_specs=[
                pl.BlockSpec((TILE, wide), lambda i, b: (i, 0)),
                pl.BlockSpec((span, width), lambda i, b: (0, 0)),
                pl.BlockSpec((1, span), lambda i, b: (0, 0)),
                pl.BlockSpec((1, TILE), lambda i, b: (0, i)),
            ],
            out_specs=[
                pl.BlockSpec((TILE, wide), lambda i, b: (i, 0)),
                pl.BlockSpec((wide, TILE), lambda i, b: (0, i)),
                pl.BlockSpec((8, TILE), lambda i, b: (0, i)),
            ],
            scratch_shapes=[
                pltpu.VMEM((HEADS_HERE, TILE, LANES), jnp.bfloat16),
                pltpu.VMEM((8, TILE), jnp.float32),
                pltpu.VMEM((8, TILE), jnp.float32),
                pltpu.VMEM((wide, TILE), jnp.float32),
            ],
        ),
        out_shape=[
            jax.ShapeDtypeStruct((rows, wide), jnp.bfloat16),
            jax.ShapeDtypeStruct((wide, rows), jnp.float32),
            jax.ShapeDtypeStruct((8, rows), jnp.float32),
        ],
        compiler_params=pltpu.CompilerParams(vmem_limit_bytes=63 * 2**20),
        name="attend",
    )(bounds, queries, window, seg_keys, seg_queries)


def attend_back_kernel(bounds, q_ref, kv_ref, segk_ref, segq_ref, grad_ref, outt_ref, lse_ref,
                       dq_ref, dkv_ref, qm_ref, gm_ref, delta_ref, dq_acc, dkv_acc):
    tile = pl.program_id(0)

    @pl.when(tile == 0)
    def _():
        dkv_acc[...] = jnp.zeros_like(dkv_acc)

    load_queries(q_ref, qm_ref)
    gm_ref[0] = lane_half(grad_ref[:, 0:LANES], False)
    gm_ref[1] = lane_half(grad_ref[:, 0:LANES], True)
    gm_ref[2] = lane_half(grad_ref[:, LANES : 2 * LANES], True)
    grads_t = grad_ref[...].astype(jnp.float32).T
    grad_rows = (0, HEAD_DIM, 3 * HEAD_DIM)
    for head in range(HEADS_HERE):
        span = slice(head * HEAD_DIM, (head + 1) * HEAD_DIM)
        delta_ref[head : head + 1, :] = jnp.sum(
            grads_t[grad_rows[head] : grad_rows[head] + HEAD_DIM, :] * outt_ref[span, :],
            axis=0, keepdims=True,
        )
    dq_acc[...] = jnp.zeros_like(dq_acc)

    def step(j, tiles):
        rows = pl.ds(pl.multiple_of(j * TILE, TILE), tiles * TILE)
        same = same_document(segk_ref, segq_ref, rows)
        keys_t = kv_ref[rows, 0 : 2 * LANES].T
        sums = [dkv_acc[rows, lane_group(g)] for g in range(3)]
        raw = [
            rows_nt(kv_ref[rows, lane_group(KEY_GROUP[head])], qm_ref[head])
            for head in range(HEADS_HERE)
        ]
        draw = [
            rows_nt(kv_ref[rows, lane_group(VALUE_GROUP[head])], gm_ref[head])
            for head in range(HEADS_HERE)
        ]
        ps, dss = [], []
        for head in range(HEADS_HERE):
            probs = jnp.where(same, jnp.exp(raw[head] - lse_ref[head : head + 1, :]), 0.0)
            dss.append((probs * (draw[head] - delta_ref[head : head + 1, :])).astype(jnp.bfloat16))
            ps.append(probs.astype(jnp.bfloat16))
        for head in range(HEADS_HERE):
            span = slice(head * HEAD_DIM, (head + 1) * HEAD_DIM)
            dq_acc[span, :] += jnp.dot(
                keys_t[span, :], dss[head], preferred_element_type=jnp.float32
            )
            sums[KEY_GROUP[head]] += jnp.dot(
                dss[head], qm_ref[head], preferred_element_type=jnp.float32
            )
            sums[VALUE_GROUP[head]] += jnp.dot(
                ps[head], gm_ref[head], preferred_element_type=jnp.float32
            )
        for g in range(3):
            dkv_acc[rows, lane_group(g)] = sums[g]

    over_tiles(bounds[0, tile], bounds[1, tile], step)
    dq_ref[...] = (dq_acc[...].T * HEAD_DIM ** (-0.5)).astype(dq_ref.dtype)

    @pl.when(tile == pl.num_programs(0) - 1)
    def _():
        dkv_ref[...] = dkv_acc[...].astype(dkv_ref.dtype)


def attend_back(bounds, queries, window, seg_keys, seg_queries, grads, outt, lse):
    rows, wide = queries.shape
    span, width = window.shape
    return pl.pallas_call(
        attend_back_kernel,
        grid_spec=pltpu.PrefetchScalarGridSpec(
            num_scalar_prefetch=1,
            grid=(rows // TILE,),
            in_specs=[
                pl.BlockSpec((TILE, wide), lambda i, b: (i, 0)),
                pl.BlockSpec((span, width), lambda i, b: (0, 0)),
                pl.BlockSpec((1, span), lambda i, b: (0, 0)),
                pl.BlockSpec((1, TILE), lambda i, b: (0, i)),
                pl.BlockSpec((TILE, wide), lambda i, b: (i, 0)),
                pl.BlockSpec((wide, TILE), lambda i, b: (0, i)),
                pl.BlockSpec((8, TILE), lambda i, b: (0, i)),
            ],
            out_specs=[
                pl.BlockSpec((TILE, wide), lambda i, b: (i, 0)),
                pl.BlockSpec((span, width), lambda i, b: (0, 0)),
            ],
            scratch_shapes=[
                pltpu.VMEM((HEADS_HERE, TILE, LANES), jnp.bfloat16),
                pltpu.VMEM((HEADS_HERE, TILE, LANES), jnp.bfloat16),
                pltpu.VMEM((8, TILE), jnp.float32),
                pltpu.VMEM((wide, TILE), jnp.float32),
                pltpu.VMEM((span, width), jnp.float32),
            ],
        ),
        out_shape=[
            jax.ShapeDtypeStruct((rows, wide), jnp.bfloat16),
            jax.ShapeDtypeStruct((span, width), jnp.bfloat16),
        ],
        compiler_params=pltpu.CompilerParams(vmem_limit_bytes=63 * 2**20),
        name="attend_back",
    )(bounds, queries, window, seg_keys, seg_queries, grads, outt, lse)


def rolled(part):
    return jnp.concatenate([part[..., HEAD_DIM:], part[..., :HEAD_DIM]], axis=-1)


def joined_halves(lower, upper):
    return jnp.concatenate([lower[..., :HEAD_DIM], upper[..., HEAD_DIM:]], axis=-1)


def lanes_of(values):
    return [values[..., lane_group(g)] for g in range(3)]


def parts_of_queries(queries, upper):
    one, two, three = lanes_of(queries)
    swapped = rolled(two)
    first, second = (swapped, two) if upper else (two, swapped)
    return jnp.stack(
        [jnp.concatenate([one, first], axis=-1), jnp.concatenate([three, second], axis=-1)], axis=1
    ).reshape(TEAM, queries.shape[1], 2 * LANES)


def parts_of_keys(keys, values):
    k = lanes_of(keys)
    v = lanes_of(values)
    low = jnp.concatenate([k[0], joined_halves(k[1], rolled(v[1])), v[0]], axis=-1)
    high = jnp.concatenate([k[2], joined_halves(rolled(k[1]), v[1]), v[2]], axis=-1)
    return jnp.stack([low, high], axis=1).reshape(TEAM, keys.shape[1], 3 * LANES)


def natural_rows(parts):
    pairs = parts.reshape(TEAM // 2, 2, parts.shape[1], 2 * LANES)
    low, high = pairs[:, 0], pairs[:, 1]
    middle = joined_halves(low[..., LANES:], rolled(high[..., LANES:]))
    return jnp.concatenate([low[..., :LANES], middle, high[..., :LANES]], axis=-1)


def natural_keys(parts):
    pairs = parts.reshape(TEAM // 2, 2, parts.shape[1], 3 * LANES)
    low, high = lanes_of(pairs[:, 0]), lanes_of(pairs[:, 1])
    keys = jnp.concatenate([low[0], joined_halves(low[1], rolled(high[1])), high[0]], axis=-1)
    values = jnp.concatenate([low[2], joined_halves(rolled(low[1]), high[1]), high[2]], axis=-1)
    return keys, values


TEAM = 4


def flip(index, step):
    return index + step * (1 - 2 * lax.rem(lax.div(index, step), 2))


def mate(rank, offset):
    if offset % 2:
        rank = flip(rank, 1)
    if offset // 2:
        rank = flip(rank, 2)
    return rank


def greet(peers):
    barrier = pltpu.get_barrier_semaphore()
    for peer in peers:
        pl.semaphore_signal(
            barrier, inc=1, device_id=peer, device_id_type=pl.DeviceIdType.MESH
        )
    pl.semaphore_wait(barrier, len(peers))


def remote(src, dst, send, recv, peer):
    return pltpu.make_async_remote_copy(
        src_ref=src,
        dst_ref=dst,
        send_sem=send,
        recv_sem=recv,
        device_id=peer,
        device_id_type=pl.DeviceIdType.MESH,
    )


RIM = 16
SMALL_ROWS = 128
SMALL_IN = 128
ROW_IN_KERNEL_W = 32
ROW_PAIR_QV, ROW_PAIR_PC, ROW_IN_KERNEL_B = 19, 20, 21
ROW_OUTPUT_B, ROW_GAIN1, ROW_SHIFT1, ROW_OUTER_B, ROW_GAIN2, ROW_SHIFT2 = range(9, 15)
ROW_INNER_B = 15
ROW_QUERY_B, ROW_VALUE_B, ROW_POINT_B, ROW_CONV_B = range(19, 23)
ROW_KERNEL_B = 24
ROW_KERNEL_W = 48
TAP_ROWS = 8 * KERNEL


def dot(left, right):
    return jnp.dot(left, right, preferred_element_type=jnp.float32)


def dot_tn(left, right):
    return lax.dot_general(
        left, right, (((0,), (0,)), ((), ())), preferred_element_type=jnp.float32
    )


def half_turn(block):
    return pltpu.roll(block, HEAD_DIM, axis=1)


def mixed_lanes(lower, upper):
    lane = lax.broadcasted_iota(jnp.int32, lower.shape, 1)
    return jnp.where(lane < HEAD_DIM, lower, upper)


def pair_row(small_ref, row, second):
    first = jnp.broadcast_to(small_ref[0, row : row + 1, :], (8, 384))
    other = jnp.broadcast_to(small_ref[1, row : row + 1, :], (8, 384))
    lane = lax.broadcasted_iota(jnp.int32, first.shape, 1)
    if second:
        first = pltpu.roll(first, 192, axis=1)
    else:
        other = pltpu.roll(other, 192, axis=1)
    return jnp.where(lane < 192, first, other)[0:1, :]


def tap_major(shape, offset):
    row = lax.broadcasted_iota(jnp.int32, shape, 0)
    column = lax.broadcasted_iota(jnp.int32, shape, 1) + offset
    head = lax.rem(row, 8)
    wanted = (head * KERNEL + lax.div(row, 8) == column) & (head < HEADS)
    return wanted & (row < TAP_ROWS)


def kernel_rows(first, other):
    lane = lax.broadcasted_iota(jnp.int32, first.shape, 1)
    rows = jnp.where(lane < 192, first, pltpu.roll(other, 192, axis=1))
    return jnp.concatenate(
        [rows, jnp.zeros((LANES - TAP_ROWS, rows.shape[1]), jnp.float32)], axis=0
    ).astype(jnp.bfloat16)


def kernel_bias(small_ref):
    half = HEADS * KERNEL // 2
    total = jnp.zeros((LANES, 1), jnp.float32)
    for w in range(2):
        row = small_ref[w, ROW_IN_KERNEL_B : ROW_IN_KERNEL_B + 1, 0:LANES]
        lane = lax.broadcasted_iota(jnp.int32, (LANES, LANES), 1)
        wanted = tap_major((LANES, LANES), w * half) & (lane < half)
        total = total + jnp.sum(jnp.where(wanted, row, 0.0), axis=1, keepdims=True)
    return total


def rows_of(ref, base, count):
    view = pl.ds(pl.multiple_of(base, 16), count)
    return ref.at[:, view, :] if len(ref.shape) == 3 else ref.at[view, :]


CHUNKS = 4


def front_kernel(count, *refs):
    x_ref, seg_ref, mask_ref, depth_in, kernel_in, kernel_b_in = refs[:6]
    vectors, pairs = refs[6:13], refs[13:17]
    shards = list(refs[17 : 16 + count])
    outer_any = refs[16 + count]
    rest = refs[17 + count :]
    outs = rest[: count + 9]
    half_any = rest[count + 9]
    win_ref, qteam_ref = outs[count : count + 2]
    holds = rest[count + 10 : 2 * count + 17]
    fulls = holds[:count]
    queries_ref, xrim_ref, depth_ref, spans_ref, kern_ref, ext_ref, conv_ref = holds[count:]
    (kv_part, q_part, seg_col, halo_low, halo_high, spread_ref, taps_ref, wide_ref,
     send_y, recv_y, send_c, recv_c, local, send_h, recv_h, send_kv, recv_kv, send_q, recv_q,
     send_l, recv_l, send_r, recv_r, emit_sem, small_f32, small_own, outer_half, half_sem) = rest[
        2 * count + 17 :
    ]
    shards.insert(2, small_own)
    key_ref, value_ref, small2d, query_ref, point_ref, convw_ref = fulls[:6]
    me, side = lax.axis_index("ctx"), lax.axis_index("wsh")
    size = lax.axis_size("ctx")
    core = lax.rem(me, 2)
    rank = lax.rem(me, TEAM)
    chip = lax.div(rank, 2)
    base = me - rank
    team = lax.div(me, TEAM)
    teams = size // TEAM
    right, left = lax.rem(me + TEAM, size), lax.rem(me + size - TEAM, size)
    after, prior = lax.rem(me + 1, size), lax.rem(me + size - 1, size)
    twin, across = {"ctx": flip(me, 1)}, {"wsh": 1 - side}
    seqs, block, model = x_ref.shape
    halo = (TEAM - 1) * block
    width = HEADS * HEAD_DIM
    chunk_rows = block // CHUNKS
    greet(
        [{"ctx": base + mate(rank, o)} for o in range(1, TEAM)]
        + [across, {"ctx": right}, {"ctx": left}, {"ctx": after}, {"ctx": prior}]
    )

    to_y, passed, own, emitted = [], [], [], []
    for i in range(count):
        rows = shards[i].shape[-2]
        to_y.append(
            remote(
                rows_of(shards[i], core * (rows // 2), rows // 2),
                rows_of(fulls[i], side * rows + core * (rows // 2), rows // 2),
                send_y.at[i], recv_y.at[i], across,
            )
        )
        came = rows_of(fulls[i], (1 - side) * rows + core * (rows // 2), rows // 2)
        passed.append(remote(came, came, send_c.at[i], recv_c.at[i], twin))
        own.append(
            pltpu.make_async_copy(shards[i], rows_of(fulls[i], side * rows, rows), local.at[i])
        )

    def emit(hold, out):
        copy = pltpu.make_async_copy(hold, out, emit_sem.at[len(emitted)])
        copy.start()
        emitted.append(copy)

    def emit_named(k):
        emit(holds[count + k], outs[count + 2 + k])

    urgent = 3
    for i in range(2):
        to_y[i].start()
    for i in range(2):
        own[i].start()
    half_rows = outer_half.shape[1]
    load_half = pltpu.make_async_copy(
        outer_any.at[:, part_rows(core * half_rows, half_rows), :], outer_half, half_sem.at[0]
    )
    load_half.start()
    small_f32[...] = jnp.zeros_like(small_f32)
    small_f32[0:KERNEL, :] = depth_in[...].astype(jnp.float32)

    def as_row(ref):
        return ref[...].astype(jnp.float32).reshape(1, ref.shape[0])

    at = KERNEL
    for ref in vectors:
        row = as_row(ref)
        for k in range(ref.shape[0] // 384):
            small_f32[at : at + 1, :] = row[:, k * 384 : (k + 1) * 384]
            at += 1
    for k in range(2):
        small_f32[at : at + 1, 0:192] = as_row(pairs[2 * k])
        small_f32[at : at + 1, 192:384] = as_row(pairs[2 * k + 1])
        at += 1
    small_f32[at : at + 1, 0 : kernel_b_in.shape[0]] = as_row(kernel_b_in)
    pick = jnp.where(tap_major((LANES, HEADS * KERNEL), 0), 1.0, 0.0).astype(jnp.bfloat16)
    small_f32[ROW_IN_KERNEL_W : ROW_IN_KERNEL_W + TAP_ROWS, 0:192] = dot(pick, kernel_in[...])[
        0:TAP_ROWS, :
    ]
    small_own[...] = small_f32[...].astype(jnp.bfloat16)
    to_y[2].start()
    own[2].start()
    to_after = remote(x_ref.at[:, pl.ds(block - RIM, RIM), :], halo_low, send_h.at[0],
                      recv_h.at[0], {"ctx": after})
    to_prior = remote(x_ref.at[:, pl.ds(0, RIM), :], halo_high, send_h.at[1], recv_h.at[1],
                      {"ctx": prior})
    pl.when(me < size - 1)(to_after.start)
    pl.when(me > 0)(to_prior.start)
    to_y[urgent].start()
    own[urgent].start()

    @pl.when(me == 0)
    def _():
        halo_low[...] = jnp.zeros_like(halo_low)

    @pl.when(me == size - 1)
    def _():
        halo_high[...] = jnp.zeros_like(halo_high)

    for s in range(seqs):
        seg_col[s] = jnp.broadcast_to(seg_ref[s : s + 1, :], (LANES, seg_ref.shape[1])).T
        for g in range(model // LANES):
            xrim_ref[s, g, pl.ds(RIM, block), :] = x_ref[s, :, lane_group(g)].astype(jnp.float32)

    def arrive(i):
        to_y[i].wait_recv()
        passed[i].start()

    def settle(i):
        own[i].wait()
        passed[i].wait_recv()
        emit(fulls[i], outs[i])

    for i in range(urgent):
        arrive(i)
    for i in (4, 5, 6, 7):
        to_y[i].start()
        own[i].start()
    for i in range(urgent):
        settle(i)
    small_ref = taps_ref
    for w in range(2):
        small_ref[w] = small2d[pl.ds(w * SMALL_IN, SMALL_IN), :].astype(jnp.float32)
    value_bias = pair_row(small_ref, ROW_PAIR_QV, True)
    query_bias = pair_row(small_ref, ROW_PAIR_QV, False)

    def piece(r, c):
        return win_ref.at[
            pl.ds(pl.multiple_of(halo + r * block + c * chunk_rows, 16), chunk_rows), :
        ]

    def part(r, c):
        return kv_part.at[r, pl.ds(c * chunk_rows, chunk_rows), :]

    def kv_copy(r, c):
        return (
            pltpu.make_async_copy(part(r, c), piece(rank, c), recv_kv.at[rank * CHUNKS + c]),
            remote(part(r, c), piece(rank, c), send_kv.at[r * CHUNKS + c],
                   recv_kv.at[rank * CHUNKS + c], {"ctx": base + r}),
        )

    def q_copy(r):
        return (
            pltpu.make_async_copy(q_part.at[r], qteam_ref.at[rank], recv_q.at[rank]),
            remote(q_part.at[r], qteam_ref.at[rank], send_q.at[r], recv_q.at[rank],
                   {"ctx": base + r}),
        )

    def begin(pair, r):
        pl.when(rank == r)(pair[0].start)
        pl.when(rank != r)(pair[1].start)

    for s in (1 - chip, chip):
        rows = x_ref[s]
        keys = dot(rows, key_ref[...])
        values = dot(rows, value_ref[...]) + value_bias
        k = [keys[:, lane_group(g)] for g in range(3)]
        v = [values[:, lane_group(g)] for g in range(3)]
        for half, groups in enumerate((
            (k[0], mixed_lanes(k[1], half_turn(v[1])), v[0]),
            (k[2], mixed_lanes(half_turn(k[1]), v[1]), v[2]),
        )):
            for g in range(3):
                kv_part[2 * s + half, :, lane_group(g)] = groups[g].astype(jnp.bfloat16)
        for c in range(CHUNKS):
            for half in range(2):
                begin(kv_copy(2 * s + half, c), 2 * s + half)

    def onward(r, c):
        to_right = remote(
            piece(r, c),
            win_ref.at[
                pl.ds(pl.multiple_of(lax.rem(r + TEAM - 1, TEAM) * block + c * chunk_rows, 16),
                      chunk_rows), :
            ],
            send_r.at[r * CHUNKS + c], recv_r.at[r * CHUNKS + c], {"ctx": right},
        )
        to_left = remote(
            piece(r, c),
            win_ref.at[
                pl.ds(
                    pl.multiple_of(
                        halo + TEAM * block + lax.rem(r, TEAM - 1) * block + c * chunk_rows, 16
                    ),
                    chunk_rows,
                ), :
            ],
            send_l.at[r * CHUNKS + c], recv_l.at[r * CHUNKS + c], {"ctx": left},
        )
        return to_right, to_left

    def relay(o, c):
        r = mate(rank, o)
        if o == 0:
            kv_copy(r, c)[0].wait()
        else:
            remote(part(rank, c), piece(r, c), send_kv.at[rank * CHUNKS + c],
                   recv_kv.at[r * CHUNKS + c], {"ctx": base + r}).wait_recv()
        to_right, to_left = onward(r, c)
        pl.when((r >= 1) & (team < teams - 1))(to_right.start)
        pl.when((r <= TEAM - 2) & (team > 0))(to_left.start)

    for c in range(CHUNKS):
        relay(0, c)
        relay(1, c)
    arrive(urgent)
    settle(urgent)
    for s in range(seqs):
        queries = dot(x_ref[s], query_ref[...]) + query_bias
        queries_ref[s] = queries.astype(jnp.bfloat16)
        q = [queries[:, lane_group(g)] for g in range(3)]
        for half, groups in enumerate(((q[0], q[1]), (q[2], half_turn(q[1])))):
            for g in range(2):
                q_part[2 * s + half, :, lane_group(g)] = groups[g].astype(jnp.bfloat16)
        for half in range(2):
            begin(q_copy(2 * s + half), 2 * s + half)
    emit_named(0)

    pl.when(me > 0)(to_after.wait_recv)
    pl.when(me < size - 1)(to_prior.wait_recv)
    for s in range(seqs):
        for g in range(model // LANES):
            xrim_ref[s, g, pl.ds(0, RIM), :] = halo_low[s, :, lane_group(g)].astype(jnp.float32)
            xrim_ref[s, g, pl.ds(RIM + block, RIM), :] = halo_high[s, :, lane_group(g)].astype(
                jnp.float32
            )
    emit_named(1)
    strip = 32
    lead = RIM - KERNEL // 2

    def taps_row(j, g):
        return small_ref[g // 3, j : j + 1, lane_group(g % 3)]

    def depth_strip(c, s):
        start = c * strip
        here = seg_col[s, pl.ds(RIM + start, strip), :]
        sums = [jnp.zeros((strip, LANES), jnp.float32) for _ in range(model // LANES)]
        for j in range(KERNEL):
            same = seg_col[s, pl.ds(lead + j + start, strip), :] == here
            for g in range(model // LANES):
                near = xrim_ref[s, g, pl.ds(lead + j + start, strip), :]
                sums[g] = sums[g] + jnp.where(same, near, 0.0) * taps_row(j, g)
        for g in range(model // LANES):
            depth_ref[s, pl.ds(pl.multiple_of(start, strip), strip), lane_group(g)] = sums[
                g
            ].astype(jnp.bfloat16)
        return s

    relay(2, 0)
    relay(3, 0)
    lax.fori_loop(0, block // strip, depth_strip, 0)
    relay(2, 1)
    relay(3, 1)
    lax.fori_loop(0, block // strip, depth_strip, 1)
    emit_named(2)
    for c in range(2, CHUNKS):
        relay(2, c)
        relay(3, c)
    for j in range(KERNEL):
        row = lax.broadcasted_iota(jnp.int32, (2 * LANES, width), 0)
        col = lax.broadcasted_iota(jnp.int32, (2 * LANES, width), 1)
        row = jnp.where(row >= LANES, row - LANES, row)
        spread_ref[j] = jnp.where(row == 8 * j + col // HEAD_DIM, 1.0, 0.0).astype(jnp.bfloat16)
    for i in (4, 5):
        arrive(i)
    for i in (4, 5):
        settle(i)
    load_half.wait()
    emit(outer_half, half_any)
    point_bias = pair_row(small_ref, ROW_PAIR_PC, False)
    conv_bias = pair_row(small_ref, ROW_PAIR_PC, True)
    tap_view = slice(ROW_IN_KERNEL_W, ROW_IN_KERNEL_W + TAP_ROWS)
    kernel_w = kernel_rows(small_ref[0, tap_view, :], small_ref[1, tap_view, :])
    kernel_b = kernel_bias(small_ref)
    for s in range(seqs):
        spans = dot(depth_ref[s], point_ref[...]) + point_bias
        spans_ref[s] = spans
        mixed = (spans * queries_ref[s].astype(jnp.float32)).astype(jnp.bfloat16)
        logits = rows_nt(kernel_w, mixed) + kernel_b
        cut = [logits[8 * j : 8 * j + 8, :] for j in range(KERNEL)]
        top = functools.reduce(jnp.maximum, cut)
        expo = [jnp.exp(part - top) for part in cut]
        inverse = 1.0 / sum(expo)
        for j in range(KERNEL):
            kern = expo[j] * inverse
            kern_ref[s, 8 * j : 8 * j + 8, :] = kern
            wide_ref[8 * j : 8 * j + 8, :] = kern * mask_ref[s, j : j + 1, :]
        wide_ref[TAP_ROWS:, :] = jnp.zeros((LANES - TAP_ROWS, block), jnp.float32)
        tall = wide_ref[...].T
        high = tall.astype(jnp.bfloat16)
        low = (tall - high.astype(jnp.float32)).astype(jnp.bfloat16)
        both = jnp.concatenate([high, low], axis=1)
        for g in range(3):
            row_ext = [xrim_ref[s, k] for k in range(model // LANES)]
        ext = dot(
            jnp.concatenate([part.astype(jnp.bfloat16) for part in row_ext], axis=1),
            convw_ref[...],
        ) + conv_bias
        for g in range(3):
            ext_ref[s, g] = ext[:, lane_group(g)]
        chunk = 128
        for c in range(block // chunk):
            sums = [jnp.zeros((chunk, LANES), jnp.float32) for _ in range(3)]
            for j in range(KERNEL):
                weight = dot(both[c * chunk : (c + 1) * chunk, :], spread_ref[j])
                for g in range(3):
                    near = ext_ref[s, g, pl.ds(lead + j + c * chunk, chunk), :]
                    sums[g] = sums[g] + weight[:, lane_group(g)] * near
            for g in range(3):
                conv_ref[s, pl.ds(c * chunk, chunk), lane_group(g)] = sums[g].astype(jnp.bfloat16)

    for k in range(3, 7):
        emit_named(k)
    for i in (6, 7):
        arrive(i)
    for i in (6, 7):
        settle(i)
    for r in range(TEAM):
        for c in range(CHUNKS):
            pl.when(rank != r)(kv_copy(r, c)[1].wait_send)
        pl.when(rank != r)(q_copy(r)[1].wait_send)
    for o in range(TEAM):
        r = mate(rank, o)
        if o == 0:
            q_copy(r)[0].wait()
        else:
            remote(q_part.at[rank], qteam_ref.at[r], send_q.at[rank], recv_q.at[r],
                   {"ctx": base + r}).wait_recv()
    for r in range(TEAM):
        for c in range(CHUNKS):
            to_right, to_left = onward(jnp.int32(r), c)
            if r >= 1:
                pl.when(team < teams - 1)(to_right.wait_send)
                pl.when(team > 0)(to_right.wait_recv)
            if r <= TEAM - 2:
                pl.when(team > 0)(to_left.wait_send)
                pl.when(team < teams - 1)(to_left.wait_recv)
    for i in range(count):
        to_y[i].wait_send()
        passed[i].wait_send()
    pl.when(me < size - 1)(to_after.wait_send)
    pl.when(me > 0)(to_prior.wait_send)
    for copy in emitted:
        copy.wait()


def front(hidden, seg_rim, tap_mask, depth, kernel, kernel_b, vectors, pairs, shards, outer):
    seqs, block, model = hidden.shape
    small = jax.ShapeDtypeStruct((SMALL_IN, 384), hidden.dtype)
    gathered = list(shards[:2]) + [small] + list(shards[2:])
    count = len(gathered)
    half = jax.ShapeDtypeStruct((outer.shape[0], outer.shape[1] // 2, outer.shape[2]), outer.dtype)
    width = HEADS * HEAD_DIM
    wide = block + 2 * RIM
    fulls = [
        jax.ShapeDtypeStruct(s.shape[:-2] + (2 * s.shape[-2], s.shape[-1]), s.dtype) for s in gathered
    ]
    vmem = pl.BlockSpec(memory_space=pltpu.VMEM)
    anywhere = pl.BlockSpec(memory_space=pl.ANY)
    low, full = jnp.bfloat16, jnp.float32
    outs = [
        jax.ShapeDtypeStruct(((3 * TEAM - 2) * block, width), low),
        jax.ShapeDtypeStruct((TEAM, block, 2 * LANES), low),
        jax.ShapeDtypeStruct((seqs, block, width), low),
        jax.ShapeDtypeStruct((seqs, model // LANES, wide, LANES), full),
        jax.ShapeDtypeStruct((seqs, block, model), low),
        jax.ShapeDtypeStruct((seqs, block, width), full),
        jax.ShapeDtypeStruct((seqs, TAP_ROWS, block), full),
        jax.ShapeDtypeStruct((seqs, 3, wide, LANES), full),
        jax.ShapeDtypeStruct((seqs, block, width), low),
    ]
    dma = pltpu.SemaphoreType.DMA
    return pl.pallas_call(
        functools.partial(front_kernel, count),
        out_shape=fulls + outs + [half],
        in_specs=[vmem] * 17 + [anywhere] * count,
        out_specs=[anywhere] * (count + 10),
        scratch_shapes=[pltpu.VMEM(s.shape, s.dtype) for s in fulls + outs[2:]] + [
            pltpu.VMEM((TEAM, block, width), low),
            pltpu.VMEM((TEAM, block, 2 * LANES), low),
            pltpu.VMEM((seqs, seg_rim.shape[1], LANES), full),
            pltpu.VMEM((seqs, RIM, model), low),
            pltpu.VMEM((seqs, RIM, model), low),
            pltpu.VMEM((KERNEL, 2 * LANES, width), low),
            pltpu.VMEM((2, SMALL_IN, 384), full),
            pltpu.VMEM((LANES, block), full),
            dma((count,)), dma((count,)), dma((count,)), dma((count,)), dma((count,)),
            dma((2,)), dma((2,)),
            dma((TEAM * CHUNKS,)), dma((TEAM * CHUNKS,)), dma((TEAM,)), dma((TEAM,)),
            dma((TEAM * CHUNKS,)), dma((TEAM * CHUNKS,)), dma((TEAM * CHUNKS,)),
            dma((TEAM * CHUNKS,)), dma((count + 8,)),
            pltpu.VMEM((SMALL_IN, 384), full), pltpu.VMEM((SMALL_IN, 384), low),
            pltpu.VMEM(half.shape, low), dma((1,)),
        ],
        compiler_params=pltpu.CompilerParams(
            collective_id=0, has_side_effects=True, vmem_limit_bytes=56 * 2**20
        ),
        name="front",
    )(hidden, seg_rim, tap_mask, depth, kernel, kernel_b, *vectors, *pairs, *shards, outer)
PACK_A = 1280
PACK_B = 768
SMALL_AT = 1152


def chips_of(me, size):
    core = lax.rem(me, 2)
    count = size // 2
    index = lax.div(me, 2)
    return index, count, lambda other: other * 2 + core


def pair_of(me, size):
    index = lax.rem(lax.div(me, 2), 2)
    return index, 2, lambda other: flip(me, 2)


def column_of(me, size):
    index = lax.div(me, TEAM)
    rest = lax.rem(me, TEAM)
    return index, size // TEAM, lambda other: other * TEAM + rest


def part_rows(base, count):
    return pl.ds(pl.multiple_of(base, 16), count)


def others(index, count):
    return [lax.rem(index + o, count) for o in range(1, count)]


def scatter_copies(stage, me, size, staged, came, send, recv):
    index, count, device = stage(me, size)
    piece = staged.shape[0] // count
    return [
        remote(staged.at[part_rows(other * piece, piece), :], came.at[index], send.at[other],
               recv.at[index], {"ctx": device(other)})
        for other in others(index, count)
    ]


def scatter_wait(stage, me, size, staged, came, send, recv):
    index, count, device = stage(me, size)
    piece = staged.shape[0] // count
    for other in others(index, count):
        remote(staged.at[part_rows(index * piece, piece), :], came.at[other], send.at[index],
               recv.at[other], {"ctx": device(other)}).wait_recv()


def share_copies(stage, me, size, fin, base, piece, send, recv):
    index, count, device = stage(me, size)
    view = fin.at[part_rows(base + index * piece, piece), :]
    return [
        remote(view, view, send.at[other], recv.at[index], {"ctx": device(other)})
        for other in others(index, count)
    ]


def share_wait(stage, me, size, fin, base, piece, send, recv):
    index, count, device = stage(me, size)
    for other in others(index, count):
        view = fin.at[part_rows(base + other * piece, piece), :]
        remote(view, view, send.at[index], recv.at[other], {"ctx": device(other)}).wait_recv()


def in_chunks(rows, body):
    chunk = max(c for c in range(16, 241, 16) if rows % c == 0)

    def step(i, carry):
        body(pl.multiple_of(i * chunk, 16), chunk)
        return carry

    lax.fori_loop(0, rows // chunk, step, 0)


def wide(value):
    return value.astype(jnp.float32)


def back_kernel(names, a_names, b_names, loaded, *refs):
    count_a, count_b = len(a_names), len(b_names)
    r = types.SimpleNamespace(**dict(zip(names, refs)))
    late = refs[len(names) :]
    block_a = types.SimpleNamespace(**dict(zip(a_names, late[:count_a])))
    block_b = types.SimpleNamespace(**dict(zip(b_names, late[count_a : count_a + count_b])))
    fetch_refs = late[count_a + count_b :]
    v = types.SimpleNamespace(**dict(zip(loaded, fetch_refs[len(loaded) :])))
    me, side = lax.axis_index("ctx"), lax.axis_index("wsh")
    size = lax.axis_size("ctx")
    core = lax.rem(me, 2)
    rank = lax.rem(me, TEAM)
    chip = lax.div(rank, 2)
    base = me - rank
    team = lax.div(me, TEAM)
    teams = size // TEAM
    twin, across = {"ctx": flip(me, 1)}, {"wsh": 1 - side}
    right, left = lax.rem(me + TEAM, size), lax.rem(me + size - TEAM, size)
    after, prior = lax.rem(me + 1, size), lax.rem(me + size - 1, size)
    seqs, block, model = v.x.shape
    width = HEADS * HEAD_DIM
    halo = (TEAM - 1) * block
    groups = model // LANES
    low = jnp.bfloat16
    index, count, device = chips_of(me, size)
    greet(
        [twin, across, {"ctx": base + mate(rank, 3)}, {"ctx": after}, {"ctx": prior}]
        + [{"ctx": device(other)} for other in others(index, count)]
    )

    def block_of(k):
        return pl.ds(pl.multiple_of(k * block, 16), block)

    def halo_left(c):
        return remote(r.window.at[block_of(2 * TEAM - 1 + c), :], r.from_left.at[block_of(c), :],
                      r.send_l.at[c], r.recv_l.at[c], {"ctx": right})

    def halo_right(c):
        return remote(r.window.at[block_of(c), :], r.from_right.at[block_of(c + 1), :],
                      r.send_r.at[c], r.recv_r.at[c], {"ctx": left})

    for k in range(TEAM - 1):
        to_right = halo_left(chip * k + (1 - chip) * (TEAM - 2 - k))
        to_left = halo_right(chip * k + (1 - chip) * ((k + 1) % (TEAM - 1)))
        pl.when(team < teams - 1)(to_right.start)
        pl.when(team > 0)(to_left.start)

    fetched = types.SimpleNamespace()
    for k, name in enumerate(loaded):
        copy = pltpu.make_async_copy(fetch_refs[k], fetch_refs[len(loaded) + k], r.load.at[k])
        setattr(fetched, name, copy)
    center = pltpu.make_async_copy(r.window.at[pl.ds(halo, TEAM * block), :], r.mine,
                                   r.load.at[len(loaded)])
    fetched.keep.start()
    fetched.came.start()
    center.start()

    def q_copy(o):
        other = mate(rank, o)
        return remote(r.dq.at[other], r.q_parts.at[rank], r.send_q.at[o], r.recv_q.at[o],
                      {"ctx": base + other})

    own_q = pltpu.make_async_copy(r.dq.at[rank], r.q_parts.at[rank], r.recv_q.at[0])
    for o in (3, 2, 1):
        q_copy(o).start()
    own_q.start()
    for name in loaded[2:]:
        getattr(fetched, name).start()

    def have(*copies):
        for copy in copies:
            copy.wait()

    half_ff = v.keep.shape[1]
    pair_index, _, _ = pair_of(me, size)
    have(fetched.keep, fetched.came)

    def stage_across(at, n):
        rows = part_rows(at, n)
        r.ff_send[rows, :] = (v.keep[1 - side, rows, :] + wide(v.came[1 - side, rows, :])).astype(low)
        v.keep[side, rows, :] = v.keep[side, rows, :] + wide(v.came[side, rows, :])

    in_chunks(half_ff, stage_across)
    ff_across = remote(r.ff_send, r.ff_came, r.send_p.at[0], r.recv_p.at[0], across)
    ff_across.start()

    small = r.sums
    small[...] = jnp.zeros_like(small)
    for j in range(KERNEL):
        row = lax.broadcasted_iota(jnp.int32, (2 * LANES, width), 0)
        col = lax.broadcasted_iota(jnp.int32, (2 * LANES, width), 1)
        row = jnp.where(row >= LANES, row - LANES, row)
        r.spread[j] = jnp.where(row == 8 * j + col // HEAD_DIM, 1.0, 0.0).astype(low)

    zero_block = jnp.zeros((block, width), low)
    r.from_left[pl.ds((TEAM - 1) * block, block), :] = zero_block
    r.from_right[0:block, :] = zero_block

    @pl.when(team == 0)
    def _():
        for k in range(TEAM - 1):
            r.from_left[pl.ds(k * block, block), :] = zero_block

    @pl.when(team == teams - 1)
    def _():
        for k in range(1, TEAM):
            r.from_right[pl.ds(k * block, block), :] = zero_block

    @pl.when(me == 0)
    def _():
        r.dd_low[...] = jnp.zeros_like(r.dd_low)
        r.rim_low[...] = jnp.zeros_like(r.rim_low)

    @pl.when(me == size - 1)
    def _():
        r.dd_high[...] = jnp.zeros_like(r.dd_high)
        r.rim_high[...] = jnp.zeros_like(r.rim_high)

    small_ref = r.small
    kernel_w = kernel_rows(
        wide(small_ref[ROW_IN_KERNEL_W : ROW_IN_KERNEL_W + TAP_ROWS, :]),
        wide(small_ref[SMALL_IN + ROW_IN_KERNEL_W : SMALL_IN + ROW_IN_KERNEL_W + TAP_ROWS, :]),
    )
    lead = RIM - KERNEL // 2
    chunk = 128
    r.d_ext[...] = jnp.zeros_like(r.d_ext)
    have(fetched.dconv, fetched.ext, fetched.kern, fetched.point, fetched.queries, fetched.spans)
    wide_ref, tall_ref = r.wide, r.tall

    def conv_back(s):
        r.seg_col[s] = jnp.broadcast_to(r.seg[s : s + 1, :], (LANES, r.seg.shape[1])).T
        for j in range(KERNEL):
            wide_ref[8 * j : 8 * j + 8, :] = (
                v.kern[s, 8 * j : 8 * j + 8, :] * r.mask[s, j : j + 1, :]
            )
        wide_ref[TAP_ROWS:, :] = jnp.zeros((LANES - TAP_ROWS, block), jnp.float32)
        tall = wide_ref[...].T
        high = tall.astype(low)
        both = jnp.concatenate([high, (tall - wide(high)).astype(low)], axis=1)
        for c in range(block // chunk):
            rows = slice(c * chunk, (c + 1) * chunk)
            grad = wide(v.dconv[s, rows, :])
            taps = jnp.zeros((chunk, LANES), jnp.float32)
            for j in range(KERNEL):
                near = jnp.concatenate(
                    [v.ext[s, g, pl.ds(lead + j + c * chunk, chunk), :] for g in range(3)],
                    axis=1,
                )
                term = near * grad
                first = term.astype(low)
                second = (term - wide(first)).astype(low)
                taps = taps + rows_nt(first, r.spread[j, 0:LANES, :])
                taps = taps + rows_nt(second, r.spread[j, 0:LANES, :])
                weight = dot(both[rows, :], r.spread[j]) * grad
                for g in range(3):
                    r.d_ext[s, g, pl.ds(lead + j + c * chunk, chunk), :] += weight[
                        :, lane_group(g)
                    ]
            tall_ref[rows, :] = taps
        back = tall_ref[...].T
        inner = jnp.zeros((8, block), jnp.float32)
        for j in range(KERNEL):
            inner = inner + v.kern[s, 8 * j : 8 * j + 8, :] * (
                back[8 * j : 8 * j + 8, :] * r.mask[s, j : j + 1, :]
            )
        for j in range(KERNEL):
            wide_ref[8 * j : 8 * j + 8, :] = v.kern[s, 8 * j : 8 * j + 8, :] * (
                back[8 * j : 8 * j + 8, :] * r.mask[s, j : j + 1, :] - inner
            )
        d_logits = wide_ref[0:TAP_ROWS, :].astype(low)
        mixed = (v.spans[s] * wide(v.queries[s])).astype(low)
        kernel_grad = dot(d_logits, mixed)
        kernel_bias = dot(d_logits, jnp.ones((block, LANES), low))
        for w in range(2):
            small[w, ROW_KERNEL_W : ROW_KERNEL_W + TAP_ROWS, :] += kernel_grad
            for g in range(3):
                small[w, ROW_KERNEL_B : ROW_KERNEL_B + 24, lane_group(g)] += kernel_bias[
                    24 * g : 24 * g + 24, :
                ]
        d_mixed = dot(wide_ref[...].T.astype(low), kernel_w)
        d_spans = (d_mixed * wide(v.queries[s])).astype(low)
        v.spans[s] = d_mixed * v.spans[s]
        v.dconv[s] = d_spans
        bias = jnp.sum(wide(d_spans), axis=0, keepdims=True)
        for w in range(2):
            small[w, ROW_POINT_B : ROW_POINT_B + 1, :] += bias
        d_depth = rows_nt(d_spans, v.point[...])
        for g in range(groups):
            r.dd[s, g, pl.ds(RIM, block), :] = d_depth[:, lane_group(g)]
        r.dd_first[s] = d_depth[0:RIM, :].astype(low)
        r.dd_last[s] = d_depth[block - RIM : block, :].astype(low)
        for g in range(3):
            r.rim_first[s, :, lane_group(g)] = r.d_ext[s, g, 0:RIM, :].astype(low)
            r.rim_last[s, :, lane_group(g)] = r.d_ext[
                s, g, RIM + block : 2 * RIM + block, :
            ].astype(low)


    def kv_copy(k):
        return (
            pltpu.make_async_copy(r.mine.at[block_of(k), :], r.kv_parts.at[rank], r.recv_kv.at[rank]),
            remote(r.mine.at[block_of(k), :], r.kv_parts.at[rank], r.send_kv.at[k],
                   r.recv_kv.at[rank], {"ctx": base + k}),
        )

    def return_block(k):
        pl.when((k <= TEAM - 2) & (team > 0))(lambda: halo_left(lax.rem(k, TEAM - 1)).wait_recv())
        pl.when((k >= 1) & (team < teams - 1))(
            lambda: halo_right(lax.rem(k + TEAM - 2, TEAM - 1)).wait_recv()
        )
        rows = block_of(k)
        r.mine[rows, :] = (
            wide(r.mine[rows, :]) + wide(r.from_left[rows, :]) + wide(r.from_right[rows, :])
        ).astype(low)
        pair = kv_copy(k)
        pl.when(k == rank)(pair[0].start)
        pl.when(k != rank)(pair[1].start)


    ff_base = core * (2 * half_ff) + pair_index * half_ff
    column_index, column_count, _ = column_of(me, size)
    column_piece = half_ff // column_count
    column_args = (column_of, me, size, r.ff_send, r.ff_column, r.send_c, r.recv_c)
    column_share = (column_of, me, size, r.fin_ff, ff_base, column_piece, r.send_cg, r.recv_cg)

    def piece_copy(fin, start, pair_rows, rows, k, mine, send, recv):
        side_of_pair = pair_index if mine else 1 - pair_index
        view = fin.at[part_rows(start + side_of_pair * pair_rows + k * rows, rows), :]
        return remote(view, view, send.at[k], recv.at[k], {"ctx": flip(me, 2)})

    def ff_piece(k, mine):
        return piece_copy(r.fin_ff, core * (2 * half_ff), half_ff, column_piece, k, mine,
                          r.send_pg, r.recv_pg)

    def wait_piece(spec, other):
        stage, _, _, fin, start, rows, send, recv = spec
        place, _, device_of = stage(me, size)
        view = fin.at[part_rows(start + other * rows, rows), :]
        remote(view, view, send.at[place], recv.at[other], {"ctx": device_of(other)}).wait_recv()

    def ff_to_column():
        ff_across.wait()

        def body(at, n):
            rows = part_rows(at, n)
            value = v.keep[side, rows, :] + wide(r.ff_came[rows, :])
            v.keep[side, rows, :] = value
            r.ff_send[rows, :] = value.astype(low)

        in_chunks(half_ff, body)
        for copy in scatter_copies(*column_args):
            copy.start()

    def ff_to_share():
        scatter_wait(*column_args)
        rows = part_rows(column_index * column_piece, column_piece)
        total = v.keep[side, rows, :]
        for other in others(column_index, column_count):
            total = total + wide(r.ff_column[other])
        r.ff_send[rows, :] = total.astype(low)
        own = pltpu.make_async_copy(
            r.ff_send.at[rows, :],
            r.fin_ff.at[part_rows(ff_base + column_index * column_piece, column_piece), :],
            r.load.at[0],
        )
        own.start()
        own.wait()
        for copy in share_copies(*column_share):
            copy.start()
        ff_piece(column_index, True).start()

    def ff_to_pair():
        for other in others(column_index, column_count):
            wait_piece(column_share, other)
            ff_piece(other, True).start()

    def ff_twin():
        view = r.fin_ff.at[part_rows(core * (2 * half_ff), 2 * half_ff), :]
        return remote(view, view, r.send_pg.at[column_count], r.recv_pg.at[column_count], twin)

    def ff_to_twin():
        for k in range(column_count):
            ff_piece(k, False).wait_recv()
        ff_twin().start()


    conv_back(0)
    center.wait()
    there = (1 - chip) * (TEAM // 2)
    here = chip * (TEAM // 2)
    return_block(there)
    conv_back(1)
    rims = [
        (remote(r.dd_last, r.dd_low, r.send_h.at[0], r.recv_h.at[0], {"ctx": after}), 1),
        (remote(r.rim_last, r.rim_low, r.send_h.at[1], r.recv_h.at[1], {"ctx": after}), 1),
        (remote(r.dd_first, r.dd_high, r.send_h.at[2], r.recv_h.at[2], {"ctx": prior}), 0),
        (remote(r.rim_first, r.rim_high, r.send_h.at[3], r.recv_h.at[3], {"ctx": prior}), 0),
    ]
    for copy, forward in rims:
        pl.when(me < size - 1 if forward else me > 0)(copy.start)

    return_block(there + 1)
    ff_to_column()
    have(fetched.depth, fetched.xrim)
    strip = 32

    def flat_rows(ref):
        return ref[...].reshape(seqs * block, ref.shape[2])

    point_grad = dot_tn(flat_rows(v.depth), flat_rows(v.dconv)).astype(low)
    for w in range(2):
        block_a.pack[w, 0:width, :] = point_grad[w * width : (w + 1) * width, :]
    for g in range(groups):
        def tap_step(c, sums, g=g):
            out = list(sums)
            for s in range(seqs):
                start = c * strip
                here = r.seg_col[s, pl.ds(RIM + start, strip), :]
                grad = r.dd[s, g, pl.ds(RIM + start, strip), :]
                for j in range(KERNEL):
                    same = r.seg_col[s, pl.ds(lead + j + start, strip), :] == here
                    near = v.xrim[s, g, pl.ds(lead + j + start, strip), :]
                    out[j] = out[j] + fold_rows(jnp.where(same, near, 0.0) * grad)
            return tuple(out)

        sums = lax.fori_loop(
            0, block // strip, tap_step,
            tuple(jnp.zeros((8, LANES), jnp.float32) for _ in range(KERNEL)),
        )
        for j in range(KERNEL):
            small[g // 3, j : j + 1, lane_group(g % 3)] = jnp.sum(sums[j], axis=0, keepdims=True)

    return_block(here + 1 - chip)
    return_block(here + chip)
    have(fetched.convw, fetched.x)
    for copy, forward in rims:
        pl.when(me > 0 if forward else me < size - 1)(copy.wait_recv)
    near_taps = KERNEL // 2
    for s in range(seqs):
        for g in range(3):
            head = pl.ds(RIM, RIM)
            tail = pl.ds(block, RIM)
            r.d_ext[s, g, head, :] += wide(r.rim_low[s, :, lane_group(g)])
            r.d_ext[s, g, tail, :] += wide(r.rim_high[s, :, lane_group(g)])
            v.queries[s, :, lane_group(g)] = r.d_ext[s, g, pl.ds(RIM, block), :].astype(low)
        for g in range(groups):
            r.dd[s, g, 0:RIM, :] = wide(r.dd_low[s, :, lane_group(g)])
            r.dd[s, g, pl.ds(RIM + block, RIM), :] = wide(r.dd_high[s, :, lane_group(g)])
        bias = jnp.sum(wide(v.queries[s]), axis=0, keepdims=True)
        for w in range(2):
            small[w, ROW_CONV_B : ROW_CONV_B + 1, :] += bias
    conv_grad = dot_tn(flat_rows(v.x), flat_rows(v.queries)).astype(low)
    for w in range(2):
        block_a.pack[w, width : 2 * width, :] = conv_grad[w * width : (w + 1) * width, :]

    def core_copy(blk):
        pack = blk.pack
        half = pack.shape[1] // 2
        return remote(pack.at[:, part_rows((1 - core) * half, half), :], blk.twin,
                      blk.send_core.at[0], blk.recv_core.at[0], twin)

    def y_copy(blk):
        return remote(blk.ysend, blk.ycame, blk.send_core.at[1],
                      blk.recv_core.at[1], across)

    def core_done(blk):
        core_copy(blk).wait()
        pack, came = blk.pack, blk.twin
        half = pack.shape[1] // 2

        def body(at, n):
            rows, there = part_rows(at, n), part_rows(core * half + at, n)
            blk.ysend[rows, :] = (
                wide(pack[1 - side, there, :]) + wide(came[1 - side, rows, :])
            ).astype(low)
            blk.acc[rows, :] = wide(pack[side, there, :]) + wide(came[side, rows, :])

        in_chunks(half, body)
        y_copy(blk).start()

    def chips_args(blk):
        return (chips_of, me, size, blk.ysend, blk.chips,
                blk.send_s, blk.recv_s)

    def y_done(blk):
        y_copy(blk).wait()

        def body(at, n):
            rows = part_rows(at, n)
            value = blk.acc[rows, :] + wide(blk.ycame[rows, :])
            blk.acc[rows, :] = value
            blk.ysend[rows, :] = value.astype(low)

        in_chunks(blk.ysend.shape[0], body)
        for copy in scatter_copies(*chips_args(blk)):
            copy.start()

    def pair_copy_a():
        rows = block_a.ysend.shape[0] // 2
        return remote(block_a.ysend.at[part_rows((1 - pair_index) * rows, rows), :], block_a.pair,
                      block_a.send_core.at[3], block_a.recv_core.at[3], {"ctx": flip(me, 2)})

    def y_done_a():
        y_copy(block_a).wait()

        def body(at, n):
            rows = part_rows(at, n)
            value = block_a.acc[rows, :] + wide(block_a.ycame[rows, :])
            block_a.acc[rows, :] = value
            block_a.ysend[rows, :] = value.astype(low)

        in_chunks(block_a.ysend.shape[0], body)
        pair_copy_a().start()

    def column_args_a():
        rows = block_a.ysend.shape[0] // 2
        return (column_of, me, size, block_a.ysend.at[pl.ds(0, rows), :], block_a.column,
                block_a.send_s, block_a.recv_s)

    def pair_done_a():
        pair_copy_a().wait()
        half = block_a.ysend.shape[0] // 2

        def body(at, n):
            rows = part_rows(at, n)
            value = block_a.acc[part_rows(pair_index * half + at, n), :] + wide(
                block_a.pair[rows, :]
            )
            block_a.acc[rows, :] = value
            block_a.ysend[rows, :] = value.astype(low)

        in_chunks(half, body)
        for copy in scatter_copies(*column_args_a()):
            copy.start()

    def column_share_a():
        half = block_a.ysend.shape[0]
        return (column_of, me, size, block_a.fin, core * half + pair_index * (half // 2),
                half // 2 // (size // TEAM), block_a.send_g, block_a.recv_g)

    def piece_a(k, mine):
        half = block_a.ysend.shape[0]
        return piece_copy(block_a.fin, core * half, half // 2, half // 2 // column_count, k, mine,
                          block_a.send_p, block_a.recv_p)

    def column_done_a():
        scatter_wait(*column_args_a())
        place, number, _ = column_of(me, size)
        half = block_a.ysend.shape[0]
        piece_rows = half // 2 // number
        value = block_a.acc[part_rows(place * piece_rows, piece_rows), :]
        for other in others(place, number):
            value = value + wide(block_a.column[other])
        at = core * half + pair_index * (half // 2) + place * piece_rows
        block_a.fin[part_rows(at, piece_rows), :] = value.astype(low)
        for copy in share_copies(*column_share_a()):
            copy.start()
        piece_a(column_index, True).start()

    def share_done_a():
        for other in others(column_index, column_count):
            wait_piece(column_share_a(), other)
            piece_a(other, True).start()

    def last_done_a():
        for k in range(column_count):
            piece_a(k, False).wait_recv()
        twin_copy(block_a).start()

    def finish_a():
        for copy in scatter_copies(*column_args_a()):
            copy.wait_send()
        for copy in share_copies(*column_share_a()):
            copy.wait_send()
        for k in range(column_count):
            piece_a(k, True).wait_send()
        twin_copy(block_a).wait()

    def share_args(blk):
        half = blk.ysend.shape[0]
        return (chips_of, me, size, blk.fin, core * half, half // count,
                blk.send_g, blk.recv_g)

    def chips_done(blk):
        scatter_wait(*chips_args(blk))
        half = blk.ysend.shape[0]
        piece = half // count
        value = blk.acc[part_rows(index * piece, piece), :]
        for other in others(index, count):
            value = value + wide(blk.chips[other])
        blk.fin[part_rows(core * half + index * piece, piece), :] = value.astype(low)
        for copy in share_copies(*share_args(blk)):
            copy.start()

    def twin_copy(blk):
        fin = blk.fin
        half = fin.shape[0] // 2
        view = fin.at[part_rows(core * half, half), :]
        return remote(view, view, blk.send_core.at[2], blk.recv_core.at[2], twin)

    def share_done(blk):
        share_wait(*share_args(blk))
        twin_copy(blk).start()

    def finish(blk):
        for copy in scatter_copies(*chips_args(blk)):
            copy.wait_send()
        for copy in share_copies(*share_args(blk)):
            copy.wait_send()
        twin_copy(blk).wait()

    own_q.wait()
    for o in range(1, TEAM):
        q_copy(o).wait_send()
        remote(r.dq.at[rank], r.q_parts.at[mate(rank, o)], r.send_q.at[o], r.recv_q.at[o],
               {"ctx": base + mate(rank, o)}).wait_recv()
    for s in range(seqs):
        one, two = r.q_parts.at[2 * s], r.q_parts.at[2 * s + 1]
        queries = (
            one[:, lane_group(0)],
            mixed_lanes(wide(one[:, lane_group(1)]), half_turn(wide(two[:, lane_group(1)]))),
            two[:, lane_group(0)],
        )
        for g in range(3):
            r.d_cat[s, :, lane_group(6 + g)] = (
                wide(queries[g]) + v.spans[s, :, lane_group(g)]
            ).astype(low)
    for s in range(seqs):
        bias = jnp.sum(wide(r.d_cat[s, :, 2 * width :]), axis=0, keepdims=True)
        for w in range(2):
            small[w, ROW_QUERY_B : ROW_QUERY_B + 1, :] += bias
    query_grad = dot_tn(
        flat_rows(v.x), r.d_cat[:, :, 2 * width :].reshape(seqs * block, width)
    ).astype(low)
    for w in range(2):
        block_a.pack[w, 2 * width : 3 * width, :] = query_grad[w * width : (w + 1) * width, :]
    for k, row in enumerate((ROW_GAIN2, ROW_SHIFT2, ROW_OUTER_B, ROW_GAIN1, ROW_SHIFT1, ROW_OUTPUT_B)):
        for w in range(2):
            small[w, row : row + 1, :] = r.vec[k : k + 1, w * 384 : (w + 1) * 384]
    for w in range(2):
        for k in range(4):
            at = (4 * w + k) * 384
            small[w, ROW_INNER_B + k : ROW_INNER_B + k + 1, :] = r.bias[0:1, at : at + 384]

    upper = lax.rem(rank, 2) == 1
    heads = jnp.sum(wide(r.mine[...]), axis=0, keepdims=True)
    heads = jnp.broadcast_to(heads, (8, width))
    middle, outer_pair = heads[:, lane_group(1)], heads[:, lane_group(2)]
    none = jnp.zeros_like(middle)
    bias = (
        jnp.where(upper, none, outer_pair),
        jnp.where(upper, mixed_lanes(none, middle), mixed_lanes(half_turn(middle), none)),
        jnp.where(upper, outer_pair, none),
    )
    for w in range(2):
        for g in range(3):
            small[w, ROW_VALUE_B : ROW_VALUE_B + 1, lane_group(g)] = bias[g][0:1, :]
    for w in range(2):
        block_a.pack[w, SMALL_AT : SMALL_AT + SMALL_ROWS, :] = small[w].astype(low)
    core_copy(block_a).start()
    core_done(block_a)
    ff_to_share()
    for k in range(TEAM):
        pl.when(k == rank)(kv_copy(k)[0].wait)
        pl.when(k != rank)(kv_copy(k)[1].wait_send)
    for o in range(1, TEAM):
        other = mate(rank, o)
        remote(r.mine.at[block_of(rank), :], r.kv_parts.at[other], r.send_kv.at[rank],
               r.recv_kv.at[other], {"ctx": base + other}).wait_recv()
    for s in range(seqs):
        one, two = r.kv_parts.at[2 * s], r.kv_parts.at[2 * s + 1]
        mid_one, mid_two = wide(one[:, lane_group(1)]), wide(two[:, lane_group(1)])
        r.d_cat[s, :, lane_group(0)] = one[:, lane_group(0)]
        r.d_cat[s, :, lane_group(1)] = mixed_lanes(mid_one, half_turn(mid_two)).astype(low)
        r.d_cat[s, :, lane_group(2)] = two[:, lane_group(0)]
        r.d_cat[s, :, lane_group(3)] = one[:, lane_group(2)]
        r.d_cat[s, :, lane_group(4)] = mixed_lanes(half_turn(mid_one), mid_two).astype(low)
        r.d_cat[s, :, lane_group(5)] = two[:, lane_group(2)]
    grads = r.d_cat[:, :, 0 : 2 * width].reshape(seqs * block, 2 * width)
    for w in range(2):
        piece = dot_tn(
            v.x[:, :, w * width : (w + 1) * width].reshape(seqs * block, width), grads
        ).astype(low)
        for k in range(2):
            block_b.pack[w, k * width : (k + 1) * width, :] = piece[:, k * width : (k + 1) * width]
    core_copy(block_b).start()
    core_done(block_b)
    y_done_a()
    have(fetched.ds, fetched.key, fetched.value, fetched.query)
    def taps_row(j, g):
        return wide(small_ref[(g // 3) * SMALL_IN + j : (g // 3) * SMALL_IN + j + 1,
                              lane_group(g % 3)])

    def depth_strip(c, s):
        start = c * strip
        here = r.seg_col[s, pl.ds(RIM + start, strip), :]
        rows = pl.ds(pl.multiple_of(start, strip), strip)
        sums = [v.ds[s, rows, lane_group(g)] for g in range(groups)]
        for j in range(KERNEL):
            same = r.seg_col[s, pl.ds(RIM + near_taps - j + start, strip), :] == here
            for g in range(groups):
                near = r.dd[s, g, pl.ds(RIM + near_taps - j + start, strip), :]
                sums[g] = sums[g] + jnp.where(same, near, 0.0) * taps_row(j, g)
        for g in range(groups):
            v.ds[s, rows, lane_group(g)] = sums[g]
        return s

    for s in range(seqs):
        lax.fori_loop(0, block // strip, depth_strip, s)
    pair_done_a()
    y_done(block_b)
    ff_to_pair()
    column_done_a()
    for s in range(seqs):
        v.ds[s] += (
            rows_nt(v.queries[s], v.convw[...])
            + rows_nt(r.d_cat[s, :, 0:width], v.key[...])
            + rows_nt(r.d_cat[s, :, width : 2 * width], v.value[...])
            + rows_nt(r.d_cat[s, :, 2 * width :], v.query[...])
        )
    out_copy = pltpu.make_async_copy(v.ds, r.input_grad, r.load.at[1])
    out_copy.start()
    ff_to_twin()
    chips_done(block_b)
    share_done_a()
    last_done_a()
    share_done(block_b)
    finish_a()
    finish(block_b)
    ff_twin().wait()
    for copy in scatter_copies(*column_args):
        copy.wait_send()
    for copy in share_copies(*column_share):
        copy.wait_send()
    for k in range(column_count):
        ff_piece(k, True).wait_send()
    for copy, forward in rims:
        pl.when(me < size - 1 if forward else me > 0)(copy.wait_send)
    for k in range(TEAM - 1):
        pl.when(team < teams - 1)(halo_left(k).wait_send)
        pl.when(team > 0)(halo_right(k).wait_send)
    out_copy.wait()


def padded(rows, unit):
    return -(-rows // unit) * unit


def back(held, window, dq_parts, loaded):
    size = lax.axis_size("ctx")
    unit = 16 * size
    seqs, block, model = loaded["x"].shape
    width = HEADS * HEAD_DIM
    halo = (TEAM - 1) * block
    span = block + 2 * RIM
    chips, column = size // 2, size // TEAM
    low, full = jnp.bfloat16, jnp.float32
    dma = pltpu.SemaphoreType.DMA
    half_ff = loaded["keep"].shape[1]
    outs = dict(
        input_grad=jax.ShapeDtypeStruct((seqs, block, model), full),
        fin_ff=jax.ShapeDtypeStruct((4 * half_ff, width), low),
    )
    scratch = dict(
        mine=pltpu.VMEM((TEAM * block, width), low),
        from_right=pltpu.VMEM((TEAM * block, width), low),
        from_left=pltpu.VMEM((TEAM * block, width), low),
        kv_parts=pltpu.VMEM((TEAM, block, width), low),
        q_parts=pltpu.VMEM((TEAM, block, 2 * LANES), low),
        ff_send=pltpu.VMEM((half_ff, width), low),
        ff_came=pltpu.VMEM((half_ff, width), low),
        ff_column=pltpu.VMEM((column, half_ff // column, width), low),
        spread=pltpu.VMEM((KERNEL, 2 * LANES, width), low),
        sums=pltpu.VMEM((2, SMALL_ROWS, width), full),
        wide=pltpu.VMEM((LANES, block), full),
        tall=pltpu.VMEM((block, LANES), full),
        seg_col=pltpu.VMEM((seqs, held["seg"].shape[1], LANES), full),
        d_ext=pltpu.VMEM((seqs, 3, span, LANES), full),
        dd=pltpu.VMEM((seqs, model // LANES, span, LANES), full),
        d_cat=pltpu.VMEM((seqs, block, 3 * width), low),
        dd_first=pltpu.VMEM((seqs, RIM, model), low),
        dd_last=pltpu.VMEM((seqs, RIM, model), low),
        dd_low=pltpu.VMEM((seqs, RIM, model), low),
        dd_high=pltpu.VMEM((seqs, RIM, model), low),
        rim_first=pltpu.VMEM((seqs, RIM, width), low),
        rim_last=pltpu.VMEM((seqs, RIM, width), low),
        rim_low=pltpu.VMEM((seqs, RIM, width), low),
        rim_high=pltpu.VMEM((seqs, RIM, width), low),
        send_l=dma((TEAM,)), recv_l=dma((TEAM,)), send_r=dma((TEAM,)), recv_r=dma((TEAM,)),
        send_q=dma((TEAM,)), recv_q=dma((TEAM,)), send_kv=dma((TEAM,)), recv_kv=dma((TEAM,)),
        send_h=dma((4,)), recv_h=dma((4,)), send_p=dma((1,)), recv_p=dma((1,)),
        send_c=dma((column,)), recv_c=dma((column,)), send_cg=dma((column,)),
        recv_cg=dma((column,)), send_pg=dma((column + 1,)),
        recv_pg=dma((column + 1,)),
        load=dma((len(loaded) + 1,)),
    )

    def block_scratch(rows):
        rows = padded(rows, unit)
        return dict(
            pack=pltpu.VMEM((2, rows, width), low),
            twin=pltpu.VMEM((2, rows // 2, width), low),
            ysend=pltpu.VMEM((rows // 2, width), low),
            ycame=pltpu.VMEM((rows // 2, width), low),
            acc=pltpu.VMEM((rows // 2, width), full),
            chips=pltpu.VMEM((chips, rows // 2 // chips, width), low),
            fin=pltpu.VMEM((rows, width), low),
            send_s=dma((chips,)), recv_s=dma((chips,)), send_g=dma((chips,)),
            recv_g=dma((chips,)), send_core=dma((4,)), recv_core=dma((4,)),
        )

    a_scratch, b_scratch = block_scratch(PACK_A), block_scratch(PACK_B)
    quarter = padded(PACK_A, unit) // 4
    del a_scratch["chips"]
    a_scratch.update(
        pair=pltpu.VMEM((quarter, width), low),
        column=pltpu.VMEM((column, quarter // column, width), low),
        send_p=dma((column,)), recv_p=dma((column,)),
    )
    del a_scratch["fin"], b_scratch["fin"]
    fin_shapes = [jax.ShapeDtypeStruct((padded(n, unit), width), low) for n in (PACK_A, PACK_B)]
    vmem = pl.BlockSpec(memory_space=pltpu.VMEM)
    anywhere = pl.BlockSpec(memory_space=pl.ANY)
    names = tuple(held) + ("window", "dq") + tuple(outs) + tuple(scratch)
    total_in = len(held) + 2
    fetch_count = len(loaded)

    def kernel(*refs):
        ins, loads = refs[:total_in], refs[total_in : total_in + fetch_count]
        at = total_in + fetch_count
        results = refs[at : at + len(outs)]
        fin_a, fin_b = refs[at + len(outs) : at + len(outs) + 2]
        late = refs[at + len(outs) + 2 :]
        first, late = late[: len(scratch)], late[len(scratch) :]
        a_refs, late = late[: len(a_scratch)], late[len(a_scratch) :]
        b_refs, holds = late[: len(b_scratch)], late[len(b_scratch) :]
        back_kernel(
            names, tuple(a_scratch) + ("fin",), tuple(b_scratch) + ("fin",), tuple(loaded),
            *ins, *results, *first, *a_refs, fin_a, *b_refs, fin_b, *loads, *holds,
        )

    holds = [pltpu.VMEM(a.shape, a.dtype) for a in loaded.values()]
    return pl.pallas_call(
        kernel,
        out_shape=list(outs.values()) + fin_shapes,
        in_specs=[vmem] * len(held) + [anywhere] * (2 + len(loaded)),
        out_specs=[anywhere] * 2 + [vmem] * 2,
        scratch_shapes=list(scratch.values()) + list(a_scratch.values())
        + list(b_scratch.values()) + holds,
        compiler_params=pltpu.CompilerParams(
            collective_id=5, has_side_effects=True, vmem_limit_bytes=65400 * 2**10
        ),
        name="back",
    )(*held.values(), window, dq_parts, *loaded.values())


STEP = 256
FF_CHUNK = 512
PACK_FF = 3840


def gelu_pair(value):
    share = 0.5 + 0.5 * lax.erf(value * 0.7071067811865476)
    bell = jnp.exp(-0.5 * value * value)
    return value * share, share + value * bell * 0.3989422804014327


def fold_rows(block):
    return jnp.sum(block.reshape(block.shape[0] // 8, 8, block.shape[1]), axis=0)


def norm_parts(value):
    center = value - jnp.mean(value, axis=-1, keepdims=True)
    spread = jnp.mean(center * center, axis=-1, keepdims=True)
    scale = lax.rsqrt(spread + 1e-05)
    return center * scale, scale


def norm_back(grad, unit, scale):
    return scale * (
        grad
        - jnp.mean(grad, axis=-1, keepdims=True)
        - unit * jnp.mean(grad * unit, axis=-1, keepdims=True)
    )


def middle_kernel(att_ref, conv_ref, x_ref, small_ref, og_any, ow_any, iw_any, uw_any, uw_came,
                  out_any, ds_any, dc_any, team_ref, keep_ref, xsend_ref, vec_ref, bias_ref,
                  og_ref, ow_ref, iw_ref, uw_ref, out_ref, ds_ref, dc_ref,
                  pack_ref, twin_ref, pieces, parts, joined_ref, low_ref, act_ref, slope_ref, do_ref, di_ref, db_ref,
                  sums_ref, wide_sums, send_a, recv_a, send_g, recv_g, send_t, recv_t, load, store):
    me = lax.axis_index("ctx")
    rank = lax.rem(me, TEAM)
    base = me - rank
    seqs, block, model = x_ref.shape
    width = HEADS * HEAD_DIM
    greet([{"ctx": base + mate(rank, o)} for o in range(1, TEAM)])

    def piece_copy(r):
        return (
            pltpu.make_async_copy(att_ref.at[r], pieces.at[rank], recv_a.at[rank]),
            remote(att_ref.at[r], pieces.at[rank], send_a.at[r], recv_a.at[rank],
                   {"ctx": base + r}),
        )

    def team_copy(r):
        return (
            pltpu.make_async_copy(parts.at[r], team_ref.at[rank], recv_g.at[rank]),
            remote(parts.at[r], team_ref.at[rank], send_g.at[r], recv_g.at[rank],
                   {"ctx": base + r}),
        )

    core, side = lax.rem(me, 2), lax.axis_index("wsh")
    for o in (1, 3, 2):
        piece_copy(mate(rank, o))[1].start()
    piece_copy(rank)[0].start()
    rows_in = uw_came.shape[1]
    came_at = part_rows((1 - side) * (2 * rows_in) + core * rows_in, rows_in)
    loads = [
        pltpu.make_async_copy(ow_any, ow_ref, load.at[0]),
        pltpu.make_async_copy(iw_any, iw_ref, load.at[1]),
        pltpu.make_async_copy(
            uw_any, uw_ref.at[:, part_rows(side * (2 * rows_in), 2 * rows_in), :], load.at[2]
        ),
        pltpu.make_async_copy(uw_came, uw_ref.at[:, came_at, :], load.at[3]),
        pltpu.make_async_copy(og_any, og_ref, load.at[4]),
    ]
    for copy in loads:
        copy.start()
    outer_twin = remote(uw_came, uw_ref.at[:, came_at, :], send_t.at[1], recv_t.at[1],
                        {"ctx": flip(me, 1)})
    outer_twin.start()
    sums_ref[...] = jnp.zeros_like(sums_ref)
    wide_sums[...] = jnp.zeros_like(wide_sums)
    own = lax.div(rank, 2)
    steps = block // STEP

    def row(index):
        return jnp.concatenate(
            [small_ref[index : index + 1, :], small_ref[SMALL_IN + index : SMALL_IN + index + 1, :]],
            axis=1,
        ).astype(jnp.float32)

    def body(i, carry):
        s = lax.rem(own + lax.div(i, steps), seqs)
        start = pl.multiple_of(lax.rem(i, steps) * STEP, STEP)
        rows = pl.ds(start, STEP)
        flat = pl.ds(pl.multiple_of(s * block + start, STEP), STEP)

        @pl.when(i == 0)
        def _():
            piece_copy(rank)[0].wait()
            remote(att_ref.at[rank], pieces.at[mate(rank, 1)], send_a.at[rank],
                   recv_a.at[mate(rank, 1)], {"ctx": base + mate(rank, 1)}).wait_recv()
            for copy in loads:
                copy.wait()
            outer_twin.wait()

        @pl.when(i == steps)
        def _():
            for o in (2, 3):
                remote(att_ref.at[rank], pieces.at[mate(rank, o)], send_a.at[rank],
                       recv_a.at[mate(rank, o)], {"ctx": base + mate(rank, o)}).wait_recv()

        first, second = pieces.at[2 * s], pieces.at[2 * s + 1]
        joined_ref[flat, lane_group(0)] = first[rows, lane_group(0)]
        joined_ref[flat, lane_group(1)] = mixed_lanes(
            first[rows, lane_group(1)].astype(jnp.float32),
            half_turn(second[rows, lane_group(1)].astype(jnp.float32)),
        ).astype(jnp.bfloat16)
        joined_ref[flat, lane_group(2)] = second[rows, lane_group(0)]
        joined_ref[flat, width:] = conv_ref[s, rows, :]
        branch = dot(joined_ref[flat, :], ow_ref[...]) + row(ROW_OUTPUT_B)
        unit1, scale1 = norm_parts(branch + x_ref[s, rows, :].astype(jnp.float32))
        gain1 = row(ROW_GAIN1)
        normed = unit1 * gain1 + row(ROW_SHIFT1)
        low_ref[flat, :] = normed.astype(jnp.bfloat16)
        outer = []
        part = model // GROUPS
        hidden = iw_ref.shape[2]
        for g in range(GROUPS):
            cols = slice(g * part, (g + 1) * part)
            for c in range(hidden // FF_CHUNK):
                span = slice(g * hidden + c * FF_CHUNK, g * hidden + (c + 1) * FF_CHUNK)
                near = slice(c * FF_CHUNK, (c + 1) * FF_CHUNK)
                bias = jnp.concatenate(
                    [
                        small_ref[
                            g * SMALL_IN + ROW_INNER_B + k // 3 : g * SMALL_IN + ROW_INNER_B + k // 3 + 1,
                            lane_group(k % 3),
                        ]
                        for k in range(c * FF_CHUNK // LANES, (c + 1) * FF_CHUNK // LANES)
                    ],
                    axis=1,
                ).astype(jnp.float32)
                inner = dot(low_ref[flat, cols], iw_ref[g, :, near]) + bias
                active, slope = gelu_pair(inner)
                act_ref[flat, span] = active.astype(jnp.bfloat16)
                slope_ref[:, span] = slope
            outer.append(dot(act_ref[flat, g * hidden : (g + 1) * hidden], uw_ref[g]))
        summed = jnp.concatenate(outer, axis=1) + row(ROW_OUTER_B) + normed
        unit2, scale2 = norm_parts(summed)
        gain2 = row(ROW_GAIN2)
        out_ref[s, rows, :] = (unit2 * gain2 + row(ROW_SHIFT2)).astype(jnp.bfloat16)
        grad = og_ref[s, rows, :].astype(jnp.float32)
        sums_ref[0] += fold_rows(grad * unit2)
        sums_ref[1] += fold_rows(grad)
        d_sum2 = norm_back(grad * gain2, unit2, scale2)
        d_outer = d_sum2.astype(jnp.bfloat16)
        do_ref[flat, :] = d_outer
        sums_ref[2] += fold_rows(d_outer.astype(jnp.float32))
        back = []
        for g in range(GROUPS):
            cols = slice(g * part, (g + 1) * part)
            for c in range(hidden // FF_CHUNK):
                span = slice(g * hidden + c * FF_CHUNK, g * hidden + (c + 1) * FF_CHUNK)
                near = slice(c * FF_CHUNK, (c + 1) * FF_CHUNK)
                d_inner = (
                    rows_nt(do_ref[flat, cols], uw_ref[g, near, :]) * slope_ref[:, span]
                ).astype(jnp.bfloat16)
                di_ref[flat, span] = d_inner
                wide_sums[:, span] += fold_rows(d_inner.astype(jnp.float32))
            back.append(rows_nt(di_ref[flat, g * hidden : (g + 1) * hidden], iw_ref[g]))
        d_normed = d_sum2 + jnp.concatenate(back, axis=1)
        sums_ref[3] += fold_rows(d_normed * unit1)
        sums_ref[4] += fold_rows(d_normed)
        d_sum1 = norm_back(d_normed * gain1, unit1, scale1)
        ds_ref[s, rows, :] = d_sum1
        d_branch = d_sum1.astype(jnp.bfloat16)
        db_ref[flat, :] = d_branch
        sums_ref[5] += fold_rows(d_branch.astype(jnp.float32))
        d_joined = rows_nt(d_branch, ow_ref[...])
        dc_ref[s, rows, :] = d_joined[:, width:].astype(jnp.bfloat16)
        parts[2 * s, rows, lane_group(0)] = d_joined[:, lane_group(0)].astype(jnp.bfloat16)
        parts[2 * s, rows, lane_group(1)] = half_turn(d_joined[:, lane_group(1)]).astype(
            jnp.bfloat16
        )
        parts[2 * s + 1, rows, lane_group(0)] = d_joined[:, lane_group(2)].astype(jnp.bfloat16)
        parts[2 * s + 1, rows, lane_group(1)] = d_joined[:, lane_group(1)].astype(jnp.bfloat16)

        @pl.when(i == steps - 1)
        def _():
            team_copy(rank)[0].start()
            team_copy(mate(rank, 1))[1].start()

        @pl.when(i == 2 * steps - 1)
        def _():
            team_copy(mate(rank, 2))[1].start()
            team_copy(mate(rank, 3))[1].start()

        return carry

    lax.fori_loop(0, seqs * steps, body, 0)
    stores = [
        pltpu.make_async_copy(out_ref, out_any, store.at[0]),
        pltpu.make_async_copy(ds_ref, ds_any, store.at[1]),
        pltpu.make_async_copy(dc_ref, dc_any, store.at[2]),
    ]
    for copy in stores:
        copy.start()

    half = width
    part = model // GROUPS
    hidden = iw_ref.shape[2]
    half_ff = pack_ref.shape[1] // 2
    early = half + part // 2 * (hidden // half)

    def exchange(at, rows, sem):
        return remote(
            pack_ref.at[:, part_rows((1 - core) * half_ff + at, rows), :],
            twin_ref.at[:, pl.ds(at, rows), :], send_t.at[sem], recv_t.at[sem],
            {"ctx": flip(me, 1)},
        )

    for w in range(2):
        for k in range(2):
            pack_ref[w, pl.ds(k * half_ff, half), :] = dot_tn(
                joined_ref[:, w * half : (w + 1) * half], db_ref[:, k * half : (k + 1) * half]
            ).astype(jnp.bfloat16)
    for g in range(GROUPS):
        for k in range(hidden // half):
            grads = dot_tn(
                low_ref[:, g * part : (g + 1) * part],
                di_ref[:, g * hidden + k * half : g * hidden + (k + 1) * half],
            ).astype(jnp.bfloat16)
            for w in range(2):
                pack_ref[w, pl.ds(g * half_ff + half + k * (part // 2), part // 2), :] = grads[
                    w * (part // 2) : (w + 1) * (part // 2), :
                ]
    exchange(0, early, 0).start()
    for g in range(GROUPS):
        for k in range(hidden // half):
            w, lower = k // 2, k % 2
            grads = dot_tn(
                act_ref[:, g * hidden + k * half : g * hidden + (k + 1) * half],
                do_ref[:, g * part : (g + 1) * part],
            ).astype(jnp.bfloat16)
            pack_ref[w, pl.ds(g * half_ff + early + lower * half, half), :] = grads
    exchange(early, half_ff - early, 2).start()
    for k in range(6):
        vec_ref[k : k + 1, :] = jnp.sum(sums_ref[k], axis=0, keepdims=True)
    vec_ref[6:, :] = jnp.zeros((2, model), jnp.float32)
    bias_ref[...] = jnp.broadcast_to(jnp.sum(wide_sums[...], axis=0, keepdims=True), bias_ref.shape)

    exchange(0, early, 0).wait()
    exchange(early, half_ff - early, 2).wait()
    pair_index, _, _ = pair_of(me, lax.axis_size("ctx"))
    quarter = half_ff // 2

    def add(at, n):
        here = part_rows(at, n)
        keep, give = pair_index * quarter, (1 - pair_index) * quarter
        for w in range(2):
            xsend_ref[w, here, :] = (
                wide(pack_ref[w, part_rows(core * half_ff + give + at, n), :])
                + wide(twin_ref[w, part_rows(give + at, n), :])
            ).astype(jnp.bfloat16)
            keep_ref[w, here, :] = wide(
                pack_ref[w, part_rows(core * half_ff + keep + at, n), :]
            ) + wide(twin_ref[w, part_rows(keep + at, n), :])

    in_chunks(quarter, add)
    team_copy(rank)[0].wait()
    for o in range(1, TEAM):
        other = mate(rank, o)
        piece_copy(other)[1].wait_send()
        team_copy(other)[1].wait_send()
        remote(parts.at[rank], team_ref.at[other], send_g.at[rank], recv_g.at[other],
               {"ctx": base + other}).wait_recv()
    for copy in stores:
        copy.wait()


def middle(attended, convolved, hidden, small, out_grad, output_w, inner_w, outer_w, outer_came):
    seqs, block, model = hidden.shape
    rows = seqs * block
    width = convolved.shape[2]
    inner = GROUPS * inner_w.shape[2]
    pack_rows = padded(PACK_FF, 16 * lax.axis_size("ctx"))
    vmem = pl.BlockSpec(memory_space=pltpu.VMEM)
    anywhere = pl.BlockSpec(memory_space=pl.ANY)
    low, full = jnp.bfloat16, jnp.float32
    dma = pltpu.SemaphoreType.DMA
    return pl.pallas_call(
        middle_kernel,
        out_shape=[
            jax.ShapeDtypeStruct((seqs, block, model), low),
            jax.ShapeDtypeStruct((seqs, block, model), full),
            jax.ShapeDtypeStruct((seqs, block, width), low),
            jax.ShapeDtypeStruct((TEAM, block, 2 * LANES), low),
            jax.ShapeDtypeStruct((2, pack_rows // 4, width), full),
            jax.ShapeDtypeStruct((2, pack_rows // 4, width), low),
            jax.ShapeDtypeStruct((8, model), full),
            jax.ShapeDtypeStruct((8, inner), full),
        ],
        in_specs=[anywhere] + [vmem] * 3 + [anywhere] * 5,
        out_specs=[anywhere] * 4 + [vmem] * 4,
        scratch_shapes=[
            pltpu.VMEM((seqs, block, model), low),
            pltpu.VMEM(output_w.shape, low),
            pltpu.VMEM(inner_w.shape, low),
            pltpu.VMEM((GROUPS, 2 * outer_w.shape[1], outer_w.shape[2]), low),
            pltpu.VMEM((seqs, block, model), low),
            pltpu.VMEM((seqs, block, model), full),
            pltpu.VMEM((seqs, block, width), low),
            pltpu.VMEM((2, pack_rows, width), low),
            pltpu.VMEM((2, pack_rows // 2, width), low),
            pltpu.VMEM((TEAM, block, 2 * LANES), low),
            pltpu.VMEM((TEAM, block, 2 * LANES), low),
            pltpu.VMEM((rows, model), low),
            pltpu.VMEM((rows, model), low),
            pltpu.VMEM((rows, inner), low),
            pltpu.VMEM((STEP, inner), full),
            pltpu.VMEM((rows, model), low),
            pltpu.VMEM((rows, inner), low),
            pltpu.VMEM((rows, model), low),
            pltpu.VMEM((6, 8, model), full),
            pltpu.VMEM((8, inner), full),
            dma((TEAM,)), dma((TEAM,)), dma((TEAM,)), dma((TEAM,)), dma((3,)), dma((3,)),
            dma((5,)), dma((3,)),
        ],
        compiler_params=pltpu.CompilerParams(
            collective_id=2, has_side_effects=True, vmem_limit_bytes=63 * 2**20
        ),
        name="middle",
    )(attended, convolved, hidden, small, out_grad, output_w, inner_w, outer_w, outer_came)


def finish_kernel(side_ref, ff_any, a_any, b_any, grad_any, out_any,
                  grad_out, out_out, query_out, key_out, value_out, point_out, conv_out,
                  output_out, inner_out, outer_out, depth_out, kernel_out, query_b, value_b, point_b, conv_b,
                  output_b, gain1, shift1, outer_b, gain2, shift2, inner_b, kernel_b,
                  ff, a, b, grad, out, wide_a, wide_b, wide_output, wide_inner, wide_outer,
                  load, store):
    width = HEADS * HEAD_DIM
    loads = [
        pltpu.make_async_copy(a_any.at[pl.ds(0, a.shape[0]), :], a, load.at[0]),
        pltpu.make_async_copy(b_any.at[pl.ds(0, b.shape[0]), :], b, load.at[1]),
        pltpu.make_async_copy(ff_any.at[pl.ds(0, ff.shape[0]), :], ff, load.at[2]),
        pltpu.make_async_copy(grad_any, grad, load.at[3]),
        pltpu.make_async_copy(out_any, out, load.at[4]),
    ]
    for copy in loads:
        copy.start()
    stores = []

    def put(src, dst):
        copy = pltpu.make_async_copy(src, dst, store.at[len(stores)])
        copy.start()
        stores.append(copy)

    loads[0].wait()
    for k, place in enumerate((point_out, conv_out, query_out)):
        rows = pl.ds(k * width, width)
        wide_a[rows, :] = a[rows, :].astype(jnp.float32)
        put(wide_a.at[rows, :], place)
    small = a[pl.ds(SMALL_AT, SMALL_ROWS), :].astype(jnp.float32)
    depth_out[...] = small[0:KERNEL, :]
    first = side_ref[0] == 0
    for ref, row in ((output_b, ROW_OUTPUT_B), (gain1, ROW_GAIN1), (shift1, ROW_SHIFT1),
                     (outer_b, ROW_OUTER_B), (gain2, ROW_GAIN2), (shift2, ROW_SHIFT2)):
        ref[...] = small[row : row + 1, :].reshape(width)
    inner_b[...] = jnp.concatenate(
        [small[ROW_INNER_B + k : ROW_INNER_B + k + 1, :] for k in range(4)], axis=1
    ).reshape(4 * width)
    block = small[16:24, :]
    turned = jnp.where(first, block, pltpu.roll(block, 192, axis=1))
    for ref, row in ((query_b, ROW_QUERY_B), (value_b, ROW_VALUE_B), (point_b, ROW_POINT_B),
                     (conv_b, ROW_CONV_B)):
        ref[...] = turned[row - 16 : row - 15, 0:192].reshape(192)
    taps = small[ROW_KERNEL_W : ROW_KERNEL_W + TAP_ROWS, :]
    half = jnp.where(first, taps, pltpu.roll(taps, 192, axis=1))[:, 0:192]
    pick = jnp.where(tap_major((TAP_ROWS, HEADS * KERNEL), 0), 1.0, 0.0)
    kernel_out[...] = dot_tn(pick.astype(jnp.bfloat16), half.astype(jnp.bfloat16))
    lanes = small[ROW_KERNEL_B : ROW_KERNEL_B + 24, :]
    column = jnp.concatenate([lanes[:, lane_group(g)] for g in range(3)], axis=0)
    wide_pick = jnp.where(
        first,
        jnp.where(tap_major((TAP_ROWS, LANES), 0), 1.0, 0.0),
        jnp.where(tap_major((TAP_ROWS, LANES), HEADS * KERNEL // 2), 1.0, 0.0),
    )
    count = HEADS * KERNEL // 2
    kernel_b[...] = jnp.sum(column * wide_pick, axis=0, keepdims=True)[:, 0:count].reshape(count)
    loads[1].wait()
    for k, place in enumerate((key_out, value_out)):
        rows = pl.ds(k * width, width)
        wide_b[rows, :] = b[rows, :].astype(jnp.float32)
        put(wide_b.at[rows, :], place)
    loads[2].wait()
    half_ff = ff.shape[0] // 2
    count = inner_out.shape[1]
    blocks = inner_out.shape[2] // width
    rows = outer_out.shape[1]
    for g in range(GROUPS):
        cols = slice(g * width, (g + 1) * width)
        wide_output[:, cols] = ff[pl.ds(g * half_ff, width), :].astype(jnp.float32)
        for k in range(blocks):
            at = g * half_ff + width + k * count
            wide_inner[g, :, k * width : (k + 1) * width] = ff[pl.ds(at, count), :].astype(
                jnp.float32
            )
        wide_outer[g] = ff[pl.ds(g * half_ff + width + blocks * count, rows), :].astype(
            jnp.float32
        )
    put(wide_output, output_out)
    put(wide_inner, inner_out)
    put(wide_outer, outer_out)
    loads[3].wait()
    put(grad, grad_out)
    loads[4].wait()
    put(out, out_out)
    for copy in stores:
        copy.wait()


def finish(side, fin_ff, fin_a, fin_b, grad_input, output, inner_shape, outer_shape):
    width = HEADS * HEAD_DIM
    full, low = jnp.float32, jnp.bfloat16
    anywhere = pl.BlockSpec(memory_space=pl.ANY)
    vmem = pl.BlockSpec(memory_space=pltpu.VMEM)
    square = jax.ShapeDtypeStruct((width, width), full)
    lengths = [width // 2] * 4 + [width] * 6 + [4 * width, HEADS * KERNEL // 2]
    return pl.pallas_call(
        finish_kernel,
        out_shape=[
            jax.ShapeDtypeStruct(grad_input.shape, full),
            jax.ShapeDtypeStruct(output.shape, low),
            square, square, square, square, square,
            jax.ShapeDtypeStruct((width, 2 * width), full),
            jax.ShapeDtypeStruct(inner_shape, full),
            jax.ShapeDtypeStruct(outer_shape, full),
            jax.ShapeDtypeStruct((KERNEL, width), full),
            jax.ShapeDtypeStruct((HEADS * KERNEL, width // 2), full),
        ] + [jax.ShapeDtypeStruct((n,), full) for n in lengths],
        in_specs=[pl.BlockSpec(memory_space=pltpu.SMEM)] + [anywhere] * 5,
        out_specs=[anywhere] * 10 + [vmem] * 14,
        scratch_shapes=[
            pltpu.VMEM(fin_ff.shape, low),
            pltpu.VMEM((PACK_A, width), low),
            pltpu.VMEM((PACK_B, width), low),
            pltpu.VMEM(grad_input.shape, full),
            pltpu.VMEM(output.shape, low),
            pltpu.VMEM((SMALL_AT, width), full),
            pltpu.VMEM((PACK_B, width), full),
            pltpu.VMEM((width, 2 * width), full),
            pltpu.VMEM(inner_shape, full),
            pltpu.VMEM(outer_shape, full),
            pltpu.SemaphoreType.DMA((5,)),
            pltpu.SemaphoreType.DMA((10,)),
        ],
        compiler_params=pltpu.CompilerParams(vmem_limit_bytes=60 * 2**20),
        name="finish",
    )(side, fin_ff, fin_a, fin_b, grad_input, output)


def on_device(
    hidden_in,
    segment_ids,
    out_grad,
    query_w,
    query_b,
    key_w,
    value_w,
    value_b,
    depth_kernel,
    point_w,
    point_b,
    kernel_w,
    kernel_b,
    conv_w,
    conv_b,
    output_w,
    output_b,
    norm1_gain,
    norm1_bias,
    inner_w,
    inner_b,
    outer_w,
    outer_b,
    norm2_gain,
    norm2_bias,
):
    micro_count, seq_local, block_len, model_width = hidden_in.shape
    seq_count = micro_count * seq_local
    att_width = HEADS * HEAD_DIM
    half_taps = KERNEL // 2
    position = lax.axis_index("ctx")
    seg_rows = segment_ids.reshape(seq_count, segment_ids.shape[2])
    pad_rows = (TEAM - 1) * block_len
    seg_pad = jnp.pad(seg_rows, ((0, 0), (pad_rows, pad_rows)), constant_values=-1)
    own_seg = lax.dynamic_slice_in_dim(seg_pad, position * block_len + pad_rows, block_len, 1)
    rank = lax.rem(position, TEAM)
    first_key = (position - rank) * block_len
    team_seg = lax.dynamic_slice(
        seg_pad, (lax.div(rank, 2), first_key), (1, (3 * TEAM - 2) * block_len)
    )
    key_place = first_key - pad_rows + lax.broadcasted_iota(jnp.int32, team_seg.shape, 1)
    team_seg = jnp.where(key_place >= seg_rows.shape[1], 2**24, team_seg)
    query_seg = team_seg[:, pad_rows : pad_rows + TEAM * block_len]
    lows = query_seg[0, ::TILE]
    highs = query_seg[0, TILE - 1 :: TILE]
    before = jnp.sum(team_seg < lows[:, None], axis=1, dtype=jnp.int32)
    through = jnp.sum(team_seg <= highs[:, None], axis=1, dtype=jnp.int32)
    bounds = jnp.stack([before // TILE, (through + TILE - 1) // TILE])
    seg_keys = team_seg.astype(jnp.float32)
    seg_queries = query_seg.astype(jnp.float32)
    rim_seg = lax.dynamic_slice_in_dim(
        seg_pad, position * block_len + pad_rows - RIM, block_len + 2 * RIM, 1
    )
    tap_mask = jnp.stack(
        [
            rim_seg[:, RIM - half_taps + j : RIM - half_taps + j + block_len] == own_seg
            for j in range(KERNEL)
        ],
        axis=1,
    ).astype(jnp.float32)
    seg_rim = jnp.pad(
        rim_seg.astype(jnp.float32), ((0, 0), (0, -rim_seg.shape[1] % LANES)), constant_values=-1
    )
    side = lax.axis_index("wsh")
    tap_rows = jnp.pad(tap_mask, ((0, 0), (0, 16 - KERNEL), (0, 0)))
    hidden = hidden_in.reshape(seq_count, block_len, model_width)
    (key_mat, value_mat, small_full, query_mat, point_mat, conv_mat, output_mat, inner_mat,
     window, query_team, queries, xrim, depth_low, span_keys, kern, ext, convolved,
     outer_half) = front(
        hidden, seg_rim, tap_rows, depth_kernel, kernel_w.T, kernel_b,
        [output_b, norm1_gain, norm1_bias, outer_b, norm2_gain, norm2_bias, inner_b],
        [query_b, value_b, point_b, conv_b],
        [key_w, value_w, query_w, point_w, conv_w, output_w, inner_w], outer_w,
    )
    outer_came = lax.ppermute(outer_half, "wsh", [(0, 1), (1, 0)])
    query_team = query_team.reshape(TEAM * block_len, 2 * LANES)
    attended_team, attended_t, log_sums = attend(
        bounds, query_team, window, seg_keys, seg_queries
    )
    (output, grad_sum1, grad_conv, grad_team, keep, xsend, vec_grads, bias_grads) = middle(
        attended_team.reshape(TEAM, block_len, -1), convolved, hidden, small_full,
        out_grad.reshape(seq_count, block_len, model_width),
        output_mat, inner_mat, outer_w, outer_came,
    )
    came = lax.ppermute(xsend, "ctx", [(i, i ^ 2) for i in range(lax.axis_size("ctx"))])
    grad_query_team, grad_window = attend_back(
        bounds, query_team, window, seg_keys, seg_queries,
        grad_team.reshape(TEAM * block_len, 2 * LANES), attended_t, log_sums,
    )
    grad_input, fin_ff, fin_a, fin_b = back(
        dict(seg=seg_rim, mask=tap_rows, small=small_full, vec=vec_grads, bias=bias_grads),
        grad_window, grad_query_team.reshape(TEAM, block_len, -1),
        dict(keep=keep, came=came, dconv=grad_conv, ext=ext, kern=kern, point=point_mat,
             queries=queries, spans=span_keys, depth=depth_low, xrim=xrim, x=hidden,
             convw=conv_mat, ds=grad_sum1, key=key_mat, value=value_mat, query=query_mat),
    )
    (grad_input, output, grad_query, grad_key, grad_value, grad_point, grad_conv, grad_output,
     grad_inner, grad_outer, grad_depth, grad_kernel, g_query_b, g_value_b, g_point_b, g_conv_b,
     g_output_b, gain1, shift1, g_outer_b, gain2, shift2, g_inner_b, g_kernel_b) = finish(
        side.astype(jnp.int32).reshape(1), fin_ff, fin_a, fin_b, grad_input, output,
        inner_w.shape, outer_w.shape,
    )
    return (
        output.reshape(hidden_in.shape), grad_input.reshape(hidden_in.shape),
        grad_query, g_query_b, grad_key, grad_value, g_value_b, grad_depth, grad_point,
        g_point_b, grad_kernel.T, g_kernel_b, grad_conv, g_conv_b, grad_output, g_output_b,
        gain1, shift1, grad_inner, g_inner_b, grad_outer, g_outer_b, gain2, shift2,
    )


def solution(mesh):
    in_specs = (
        P(None, "wsh", "ctx", None),
        P(None, "wsh", None),
        P(None, "wsh", "ctx", None),
        P("wsh", None),
        P("wsh"),
        P("wsh", None),
        P("wsh", None),
        P("wsh"),
        P(None, "wsh"),
        P("wsh", None),
        P("wsh"),
        P("wsh", None),
        P("wsh"),
        P("wsh", None),
        P("wsh"),
        P("wsh", None),
        P("wsh"),
        P("wsh"),
        P("wsh"),
        P(None, "wsh", None),
        P("wsh"),
        P(None, "wsh", None),
        P("wsh"),
        P("wsh"),
        P("wsh"),
    )
    out_specs = (
        P(None, "wsh", "ctx", None),
        P(None, "wsh", "ctx", None),
        P("wsh", None),
        P("wsh"),
        P("wsh", None),
        P("wsh", None),
        P("wsh"),
        P(None, "wsh"),
        P("wsh", None),
        P("wsh"),
        P("wsh", None),
        P("wsh"),
        P("wsh", None),
        P("wsh"),
        P("wsh", None),
        P("wsh"),
        P("wsh"),
        P("wsh"),
        P(None, "wsh", None),
        P("wsh"),
        P(None, "wsh", None),
        P("wsh"),
        P("wsh"),
        P("wsh"),
    )
    return jax.shard_map(
        on_device, mesh=mesh, in_specs=in_specs, out_specs=out_specs, check_vma=False
    )
```
